32 devices in a mesh: blk: 4 (over y, core), uly: 2 (over x), dp: 4 (over z).
Axes of the slice: x: 2, y: 2, z: 4, core: 2. Of those that a mesh axis runs over, the one named last changes fastest.
Arguments:
- queries: bfloat16 [4, 1024, 4096], P(None, ('blk', 'uly', 'dp')), may hold values from -16 to 16
- keys: bfloat16 [4, 1024, 512], P(None, ('blk', 'uly', 'dp')), may hold values from -16 to 16
- values: bfloat16 [4, 1024, 512], P(None, ('blk', 'uly', 'dp')), may hold values from -6 to 6
- grad_out: bfloat16 [4, 1024, 4096], P(None, ('blk', 'uly', 'dp')), may hold values from -6 to 6
- segment_ids: int32 [4, 1024], replicated, may hold values from 0 to 7, never falling along the last dimension, each value on 1 to 256 neighbouring positions
- assignment: int32 [4], replicated, may hold values from 0 to 3, each once
Outputs:
- grad_queries: bfloat16 [4, 1024, 32, 128], P('dp', ('blk', 'uly'))
- grad_keys: bfloat16 [4, 1024, 512], P('dp', ('blk', 'uly'))
- grad_values: bfloat16 [4, 1024, 512], P('dp', ('blk', 'uly'))
The draws below stay inside these ranges and needn't reach their ends.
Inputs may be any that keep to these rules, and one draw needn't show every extreme that they name: `segment_ids`: no document holds more than 256 tokens, and some document holds exactly 256.
All inputs are finite; a program needn't handle non-finite values.
Results may differ from the reference program's by a relative error of at most 0.008.
Values may be sent and summed in bfloat16 or wider, within the bound.
No kernel may reach another device: no remote copies, remote signals or barrier semaphores. Data moves between devices by JAX's collectives and lax.ppermute only.
A program may use at most 64 MiB of HBM per device.

```python
import math
import jax
import jax.numpy as jnp
import numpy as np
from jax import lax

QH = 32
KVH = 4
HD = 128
SEQS = 4
S = 1024
DOC_MAX = 256
DOCS = 8


def draw_queries(key, part):
    base = jnp.clip(jax.random.normal(jax.random.fold_in(key, 1), (SEQS, S, QH * HD), jnp.float32), -6.0, 6.0)
    return base.astype(jnp.bfloat16)


def draw_keys(key, part):
    base = jnp.clip(jax.random.normal(jax.random.fold_in(key, 2), (SEQS, S, KVH * HD), jnp.float32), -6.0, 6.0)
    return base.astype(jnp.bfloat16)


def block_levels(key, shape, split, low, high):
    def one(dim, parts):
        steps = jax.random.uniform(jax.random.fold_in(jax.random.fold_in(key, 6), dim), (parts,), jnp.float32, low / len(split), high / len(split))
        return jnp.repeat(jnp.exp(steps), shape[dim] // parts).reshape((-1,) + (1,) * (len(shape) - dim - 1))

    loudness = one(*split[0])
    for cut in split[1:]:
        loudness = loudness * one(*cut)
    return loudness


def length_profile(number_of, total, bound, skew):
    loads = [(1 << 20) // math.isqrt(rank ** skew) + 1 for rank in range(2, number_of + 1)]
    surplus, holding = total - bound - (number_of - 1), [1] * (number_of - 1)
    while surplus > 0:
        free = [i for i in range(number_of - 1) if holding[i] < bound]
        pool, budget = sum([loads[i] for i in free]), surplus
        for i in free:
            more = min(bound - holding[i], max(1, budget * loads[i] // pool), surplus)
            holding[i] = holding[i] + more
            surplus = surplus - more
    return np.array([bound] + holding)


def uneven(key, count, total, limit, lean):
    if count == 2:
        one = jax.random.randint(key, (), max(1, total - limit), min(limit, total - 1) + 1)
        return jnp.stack([one, total - one])
    sizes = jnp.asarray(length_profile(count, total, limit, lean), jnp.int32)
    couples = (count - 1) // 2
    giver, receiver = sizes[1:1 + 2 * couples:2], sizes[2:2 + 2 * couples:2]
    room = jnp.minimum(giver - 1, limit - receiver)
    moved = jax.random.randint(jax.random.fold_in(key, 1), (couples,), 0, 1 << 20) % (room + 1)
    sizes = sizes.at[1:1 + 2 * couples:2].set(giver - moved).at[2:2 + 2 * couples:2].set(receiver + moved)
    return sizes[jax.random.permutation(jax.random.fold_in(key, 2), count)]


def noise(key, dims, scale, reach, split=(), kind=jnp.bfloat16):
    result = jax.random.normal(key, dims, jnp.float32) * scale
    if len(split) > 0:
        result = block_levels(key, dims, split, -0.22, 0.18) * result
    return jnp.clip(result, min=-reach, max=reach).astype(kind)


def setup_inputs(seed: int = 0) -> dict:
    seeds = jax.random.split(jax.random.key(seed), 7)
    queries = draw_queries(jax.random.fold_in(seeds[6], 71), 0)
    keys = draw_keys(jax.random.fold_in(seeds[6], 71), 0)
    values = noise(seeds[2], (SEQS, S, KVH * HD), 1.0, 6.0, ((1, 32),))
    grad_out = noise(seeds[3], (SEQS, S, QH * HD), 1.0, 6.0, ((1, 32),))
    segment_ids = jax.vmap(lambda own: jnp.searchsorted(jnp.cumsum(uneven(own, DOCS, S, DOC_MAX, 2)), jnp.arange(S), side="right"))(jax.random.split(seeds[4], SEQS)).reshape((SEQS, S)).astype(jnp.int32)
    assignment = jax.random.permutation(seeds[5], SEQS).astype(jnp.int32)
    return dict(queries=queries, keys=keys, values=values, grad_out=grad_out, segment_ids=segment_ids, assignment=assignment)


def block_grads(query_block, grad_block, key_window, value_window, allowed, softmax_scale):
    scores = jnp.dot(query_block, key_window.T, preferred_element_type=jnp.float32) * softmax_scale
    scores = jnp.where(allowed, scores, -jnp.inf)
    top_score = jnp.max(scores, axis=1, keepdims=True)
    weights = jnp.where(allowed, jnp.exp(scores - top_score), 0.0)
    probs = weights / jnp.sum(weights, axis=1, keepdims=True)
    probs_half = probs.astype(jnp.bfloat16)
    grad_value = jnp.dot(probs_half.T, grad_block, preferred_element_type=jnp.float32)
    grad_probs = jnp.dot(grad_block, value_window.T, preferred_element_type=jnp.float32)
    row_delta = jnp.sum(probs * grad_probs, axis=1, keepdims=True)
    grad_scores = (softmax_scale * probs * (grad_probs - row_delta)).astype(jnp.bfloat16)
    grad_query = jnp.dot(grad_scores, key_window, preferred_element_type=jnp.float32).astype(jnp.bfloat16)
    grad_key = jnp.dot(grad_scores.T, query_block, preferred_element_type=jnp.float32)
    return grad_query, grad_key, grad_value


def head_grads(query_head, key_head, value_head, grad_head, segment_row):
    block_rows = DOC_MAX
    nblocks = S // block_rows
    softmax_scale = 1.0 / (HD ** 0.5)
    key_pad = jnp.concatenate([jnp.zeros((block_rows, HD), jnp.bfloat16), key_head], axis=0)
    value_pad = jnp.concatenate([jnp.zeros((block_rows, HD), jnp.bfloat16), value_head], axis=0)
    segment_pad = jnp.concatenate([jnp.full((block_rows,), -1, jnp.int32), segment_row.astype(jnp.int32)], axis=0)
    row_pos = jnp.arange(block_rows, dtype=jnp.int32) + block_rows
    col_pos = jnp.arange(2 * block_rows, dtype=jnp.int32)

    def step(carry, index):
        key_acc, value_acc = carry
        start = (index * block_rows).astype(jnp.int32)
        query_block = lax.dynamic_slice_in_dim(query_head, start, block_rows, 0)
        grad_block = lax.dynamic_slice_in_dim(grad_head, start, block_rows, 0)
        key_window = lax.dynamic_slice_in_dim(key_pad, start, 2 * block_rows, 0)
        value_window = lax.dynamic_slice_in_dim(value_pad, start, 2 * block_rows, 0)
        segment_query = lax.dynamic_slice_in_dim(segment_pad, start + block_rows, block_rows, 0)
        segment_key = lax.dynamic_slice_in_dim(segment_pad, start, 2 * block_rows, 0)
        allowed = (segment_query[:, None] == segment_key[None, :]) & (col_pos[None, :] <= row_pos[:, None])
        grad_query, grad_key, grad_value = block_grads(query_block, grad_block, key_window, value_window, allowed, softmax_scale)
        old_key = lax.dynamic_slice_in_dim(key_acc, start, 2 * block_rows, 0)
        old_value = lax.dynamic_slice_in_dim(value_acc, start, 2 * block_rows, 0)
        key_acc = lax.dynamic_update_slice_in_dim(key_acc, old_key + grad_key, start, 0)
        value_acc = lax.dynamic_update_slice_in_dim(value_acc, old_value + grad_value, start, 0)
        return (key_acc, value_acc), grad_query

    start_acc = jnp.zeros((S + block_rows, HD), jnp.float32)
    (key_acc, value_acc), grad_blocks = lax.scan(step, (start_acc, start_acc), jnp.arange(nblocks, dtype=jnp.int32))
    return grad_blocks.reshape(S, HD), key_acc[block_rows:], value_acc[block_rows:]


def one_sequence(query_seq, key_seq, value_seq, grad_seq, segment_row):
    group_size = QH // KVH
    query_split = query_seq.reshape(S, KVH, group_size, HD).transpose(1, 2, 0, 3)
    grad_split = grad_seq.reshape(S, KVH, group_size, HD).transpose(1, 2, 0, 3)
    key_split = key_seq.reshape(S, KVH, HD).transpose(1, 0, 2)
    value_split = value_seq.reshape(S, KVH, HD).transpose(1, 0, 2)

    def kv_group(items):
        query_group, grad_group, key_head, value_head = items

        def single(pair):
            return head_grads(pair[0], key_head, value_head, pair[1], segment_row)

        grad_query, grad_key, grad_value = lax.map(single, (query_group, grad_group))
        return grad_query, jnp.sum(grad_key, axis=0), jnp.sum(grad_value, axis=0)

    grad_query, grad_key, grad_value = lax.map(kv_group, (query_split, grad_split, key_split, value_split))
    grad_query = grad_query.transpose(2, 0, 1, 3).reshape(S, QH, HD)
    grad_key = grad_key.transpose(1, 0, 2).reshape(S, KVH * HD).astype(jnp.bfloat16)
    grad_value = grad_value.transpose(1, 0, 2).reshape(S, KVH * HD).astype(jnp.bfloat16)
    return grad_query, grad_key, grad_value


def reference(queries, keys, values, grad_out, segment_ids, assignment):
    query_list = []
    key_list = []
    value_list = []
    for group_index in range(SEQS):
        chosen = assignment[group_index]
        grad_query, grad_key, grad_value = one_sequence(queries[chosen], keys[chosen], values[chosen], grad_out[chosen], segment_ids[chosen])
        query_list.append(grad_query)
        key_list.append(grad_key)
        value_list.append(grad_value)
    return jnp.stack(query_list), jnp.stack(key_list), jnp.stack(value_list)
```

```python
import functools

import jax
import jax.numpy as jnp
from jax import lax
from jax.experimental import pallas as pl
from jax.experimental.pallas import tpu as pltpu
from jax.sharding import PartitionSpec as P

HD = 128
LOG2E = 1.4426950408889634
BIG_NEGATIVE = -1e30
VMEM_BYTES = 32 * 1024 * 1024
HEADS_STEP = 2


def partner(index, step, count):
    if count & (count - 1) == 0:
        return index ^ step, index ^ step
    return (index + step) % count, (index + count - step) % count


def exchanged(value, axis, step):
    count = lax.axis_size(axis)
    return lax.ppermute(value, axis, [(i, partner(i, step, count)[0]) for i in range(count)])


def shifted(value, axis, by):
    length = lax.axis_size(axis)
    pairs = [(i, i + by) for i in range(length) if 0 <= i + by < length]
    return lax.ppermute(value, axis, pairs)


def stage_kv_kernel(assign_ref, key_ref, value_ref, out_ref, sems):
    copies = []
    for group in range(out_ref.shape[0]):
        chosen = assign_ref[group]
        for which, source in enumerate((key_ref, value_ref)):
            copies.append(
                pltpu.make_async_copy(
                    source.at[chosen], out_ref.at[group, which], sems.at[2 * group + which]
                )
            )
    for copy in copies:
        copy.start()
    for copy in copies:
        copy.wait()


def stage_kv(assignment, keys, values):
    count, rows, width = keys.shape
    return pl.pallas_call(
        stage_kv_kernel,
        out_shape=jax.ShapeDtypeStruct((count, 2, rows, width), keys.dtype),
        in_specs=[
            pl.BlockSpec(memory_space=pltpu.SMEM),
            pl.BlockSpec(memory_space=pl.ANY),
            pl.BlockSpec(memory_space=pl.ANY),
        ],
        out_specs=pl.BlockSpec(memory_space=pl.ANY),
        scratch_shapes=[pltpu.SemaphoreType.DMA((2 * count,))],
        name="stage_kv",
    )(assignment, keys, values)


def stage_rows_kernel(picks_ref, query_ref, grad_ref, *refs):
    out_refs, sems = refs[:-1], refs[-1]
    copies = []
    for step, out_ref in enumerate(out_refs):
        chosen = picks_ref[step]
        for which, source in enumerate((query_ref, grad_ref)):
            copies.append(
                pltpu.make_async_copy(
                    source.at[chosen], out_ref.at[which], sems.at[2 * step + which]
                )
            )
    for copy in copies:
        copy.start()
    for copy in copies:
        copy.wait()


def stage_rows(picks, queries, grad_out):
    count, rows, width = queries.shape
    return pl.pallas_call(
        stage_rows_kernel,
        out_shape=[jax.ShapeDtypeStruct((2, rows, width), queries.dtype)] * count,
        in_specs=[
            pl.BlockSpec(memory_space=pltpu.SMEM),
            pl.BlockSpec(memory_space=pl.ANY),
            pl.BlockSpec(memory_space=pl.ANY),
        ],
        out_specs=[pl.BlockSpec(memory_space=pl.ANY)] * count,
        scratch_shapes=[pltpu.SemaphoreType.DMA((2 * count,))],
        name="stage_rows",
    )(picks, queries, grad_out)


def build_bias(meta_ref, segment_ref, bias_ref, rows, tok_dev, ratio):
    source, sequence, line = meta_ref[0], meta_ref[1], meta_ref[2]
    pieces = bias_ref.shape[0] // tok_dev
    lanes = ratio * rows
    eye = lax.broadcasted_iota(jnp.int32, (tok_dev, tok_dev), 0) == lax.broadcasted_iota(
        jnp.int32, (tok_dev, tok_dev), 1
    )
    token = lax.broadcasted_iota(jnp.int32, (tok_dev, lanes), 0)
    place = source * rows + lax.rem(
        lax.broadcasted_iota(jnp.int32, (tok_dev, lanes), 1), jnp.int32(rows)
    )

    def column(back):
        start = pl.multiple_of(jnp.maximum(line - back, 0) * tok_dev, tok_dev)
        every = segment_ref[:, pl.ds(start, tok_dev)].astype(jnp.float32)
        mine = lax.broadcasted_iota(jnp.int32, every.shape, 0) == sequence
        row = jnp.sum(jnp.where(mine, every, 0.0), axis=0, keepdims=True)
        return jnp.sum(jnp.where(eye, row, 0.0), axis=1, keepdims=True)

    own = column(0)
    asked = jnp.sum(jnp.where(token == place, own, 0.0), axis=0, keepdims=True)
    allowed = (own == asked) & (token <= place)
    bias_ref[:tok_dev, :] = jnp.where(allowed, 0.0, BIG_NEGATIVE)
    for back in range(1, pieces):
        held = jnp.where(line >= back, column(back), -1.0)
        bias_ref[back * tok_dev : (back + 1) * tok_dev, :] = jnp.where(
            held == asked, 0.0, BIG_NEGATIVE
        )


def attend_kernel(first, last, pieces, ratio, meta_ref, segment_ref, rows_ref, *refs):
    refs = list(refs)
    kv_refs = [refs.pop(0) for _ in range(pieces)]
    if not first:
        acc_in_ref = refs.pop(0)
        refs.pop(0)
    query_out_ref = refs.pop(0)
    if last:
        own_ref, halo_ref = refs.pop(0), refs.pop(0)
    else:
        acc_out_ref = refs.pop(0)
    bias_ref = refs.pop(0)

    rows = rows_ref.shape[1]
    count = kv_refs[0].shape[0]
    tok_dev = count * rows
    scale = 1.0 / HD**0.5

    @pl.when(pl.program_id(0) == 0)
    def _():
        build_bias(meta_ref, segment_ref, bias_ref, rows, tok_dev, ratio)

    grads = []
    for head in range(HEADS_STEP):
        columns = slice(head * HD, (head + 1) * HD)

        def stacked(which):
            base = head * ratio * HD
            return jnp.concatenate(
                [rows_ref[which, :, base + r * HD : base + (r + 1) * HD] for r in range(ratio)],
                axis=0,
            )

        def window(which):
            return jnp.concatenate(
                [ref[:, which, :, columns].reshape(tok_dev, HD) for ref in kv_refs], axis=0
            )

        query, grad = stacked(0), stacked(1)
        key, value = window(0), window(1)
        turned = (((1,), (1,)), ((), ()))
        scores = lax.dot_general(key, query, turned, preferred_element_type=jnp.float32)
        scores = scores * (scale * LOG2E) + bias_ref[...]
        top = jnp.max(scores, axis=0, keepdims=True)
        weights = jnp.exp2(scores - top)
        probs = weights * (1.0 / jnp.sum(weights, axis=0, keepdims=True))
        grad_probs = lax.dot_general(value, grad, turned, preferred_element_type=jnp.float32)
        product = probs * grad_probs
        delta = jnp.sum(product, axis=0, keepdims=True)
        grad_scores = (product - probs * delta).astype(jnp.bfloat16)
        grad_value = jnp.dot(
            probs.astype(jnp.bfloat16), grad, preferred_element_type=jnp.float32
        )
        grad_key = jnp.dot(grad_scores, query, preferred_element_type=jnp.float32)
        grad_query = lax.dot_general(
            grad_scores, key, (((0,), (0,)), ((), ())), preferred_element_type=jnp.float32
        )
        grads.append((grad_query * scale).reshape(ratio, rows, HD))
        if not first:
            grad_key = grad_key + acc_in_ref[0, :, columns]
            grad_value = grad_value + acc_in_ref[1, :, columns]
        if last:
            grad_key = grad_key * scale
            own_ref[0, :, columns] = grad_key[:tok_dev]
            own_ref[1, :, columns] = grad_value[:tok_dev]
            for back in range(1, pieces):
                span = slice(back * tok_dev, (back + 1) * tok_dev)
                halo_ref[back - 1, 0, :, columns] = grad_key[span].astype(jnp.bfloat16)
                halo_ref[back - 1, 1, :, columns] = grad_value[span].astype(jnp.bfloat16)
        else:
            acc_out_ref[0, :, columns] = grad_key
            acc_out_ref[1, :, columns] = grad_value
    query_out_ref[...] = jnp.swapaxes(jnp.concatenate(grads, axis=0), 0, 1).astype(jnp.bfloat16)


def attend(meta, segments, rows_pair, kv_pieces, carried, last):
    first = carried is None
    rows, width = rows_pair.shape[1:]
    count, _, _, kv_width = kv_pieces[0].shape
    pieces = len(kv_pieces)
    kv_heads, heads = kv_width // HD, width // HD
    ratio = heads // kv_heads
    tok_dev = count * rows
    keys = pieces * tok_dev
    step_heads, step_lanes = HEADS_STEP * ratio, HEADS_STEP * HD
    acc_spec = pl.BlockSpec((2, keys, step_lanes), lambda c, m: (0, 0, c))
    query_spec = pl.BlockSpec((rows, step_heads, HD), lambda c, m: (m[0], c, 0))
    in_specs = [
        pl.BlockSpec(segments.shape, lambda c, m: (0, 0)),
        pl.BlockSpec((2, rows, step_heads * HD), lambda c, m: (0, 0, c)),
    ]
    in_specs += [
        pl.BlockSpec((count, 2, rows, step_lanes), lambda c, m: (0, 0, 0, c)) for _ in kv_pieces
    ]
    query_shape = jax.ShapeDtypeStruct((tok_dev, heads, HD), jnp.bfloat16)
    out_shape, out_specs = [query_shape], [query_spec]
    operands = [meta, segments, rows_pair, *kv_pieces]
    aliases = {}
    if not first:
        acc, query_full = carried
        aliases[len(operands) + 1] = 0
        if not last:
            aliases[len(operands)] = 1
        operands += [acc, query_full]
        in_specs += [acc_spec, pl.BlockSpec(memory_space=pl.ANY)]
    if last:
        out_shape += [
            jax.ShapeDtypeStruct((2, tok_dev, kv_width), jnp.float32),
            jax.ShapeDtypeStruct((pieces - 1, 2, tok_dev, kv_width), jnp.bfloat16),
        ]
        out_specs += [
            pl.BlockSpec((2, tok_dev, step_lanes), lambda c, m: (0, 0, c)),
            pl.BlockSpec((pieces - 1, 2, tok_dev, step_lanes), lambda c, m: (0, 0, 0, c)),
        ]
    else:
        out_shape.append(jax.ShapeDtypeStruct((2, keys, kv_width), jnp.float32))
        out_specs.append(acc_spec)
    flops = 10 * heads * rows * keys * HD
    return pl.pallas_call(
        functools.partial(attend_kernel, first, last, pieces, ratio),
        out_shape=out_shape,
        grid_spec=pltpu.PrefetchScalarGridSpec(
            num_scalar_prefetch=1,
            grid=(kv_heads // HEADS_STEP,),
            in_specs=in_specs,
            out_specs=out_specs,
            scratch_shapes=[pltpu.VMEM((keys, ratio * rows), jnp.float32)],
        ),
        input_output_aliases=aliases,
        compiler_params=pltpu.CompilerParams(
            dimension_semantics=("arbitrary",), vmem_limit_bytes=VMEM_BYTES
        ),
        cost_estimate=pl.CostEstimate(
            flops=flops, bytes_accessed=4 * keys * kv_width * 4, transcendentals=flops // 1280
        ),
        name="attend",
    )(*operands)


def shards(queries, keys, values, grad_out, segment_ids, assignment):
    count = lax.axis_size("dp")
    uly = lax.axis_size("uly")
    group = lax.axis_index("dp")
    line = lax.axis_index("blk") * uly + lax.axis_index("uly")
    tok_dev = count * queries.shape[1]
    doc_most = min(512, tok_dev * uly)
    hops = -(-doc_most // tok_dev)
    targets = [partner(group, step, count)[0] for step in range(count)]
    sources = [partner(group, step, count)[1] for step in range(count)]
    picks = jnp.take(assignment, jnp.stack(targets))
    sequence = picks[0]
    metas = [jnp.stack([source, sequence, line]).astype(jnp.int32) for source in sources]

    kv_out = stage_kv(assignment, keys, values)
    kv_own = lax.all_to_all(kv_out, "dp", split_axis=0, concat_axis=0, tiled=True)
    staged = stage_rows(picks, queries, grad_out)
    order = [0] + sorted(range(1, count), key=lambda step: (step == count - 1, step))
    arrived = {0: staged[0]}
    for step in reversed(order[1:]):
        arrived[step] = exchanged(staged[step], "dp", step)
    pieces = [kv_own]
    for back in range(1, hops + 1):
        pieces.append(shifted(kv_own, ("blk", "uly"), back))

    carried = None
    for step in order[:-1]:
        query_full, acc = attend(metas[step], segment_ids, arrived[step], pieces, carried, False)
        carried = (acc, query_full)
    step = order[-1]
    query_full, own, halo = attend(metas[step], segment_ids, arrived[step], pieces, carried, True)
    total = own
    for back in range(1, hops + 1):
        total = total + shifted(halo[back - 1], ("blk", "uly"), -back).astype(jnp.float32)
    total = total.astype(jnp.bfloat16)
    return query_full[None], total[0][None], total[1][None]


def solution(mesh):
    in_specs = (
        P(None, ("blk", "uly", "dp"), None),
        P(None, ("blk", "uly", "dp"), None),
        P(None, ("blk", "uly", "dp"), None),
        P(None, ("blk", "uly", "dp"), None),
        P(),
        P(),
    )
    out_specs = (
        P("dp", ("blk", "uly"), None, None),
        P("dp", ("blk", "uly"), None),
        P("dp", ("blk", "uly"), None),
    )
    return jax.shard_map(shards, mesh=mesh, in_specs=in_specs, out_specs=out_specs, check_vma=False)
```

```python
import functools

import jax
import jax.numpy as jnp
from jax import lax
from jax.experimental import pallas as pl
from jax.experimental.pallas import tpu as pltpu
from jax.sharding import PartitionSpec as P

HD = 128
LOG2E = 1.4426950408889634
BIG_NEGATIVE = -1e30
VMEM_BYTES = 32 * 1024 * 1024
HEADS_STEP = 2


def partner(index, step, count):
    if count & (count - 1) == 0:
        return index ^ step, index ^ step
    return (index + step) % count, (index + count - step) % count


def exchanged(value, axis, step):
    count = lax.axis_size(axis)
    return lax.ppermute(value, axis, [(i, partner(i, step, count)[0]) for i in range(count)])


def shifted(value, axis, by):
    length = lax.axis_size(axis)
    pairs = [(i, i + by) for i in range(length) if 0 <= i + by < length]
    return lax.ppermute(value, axis, pairs)


def stage_kernel(count, parts, meta_ref, assign_ref, query_ref, grad_ref, key_ref, value_ref, *refs):
    group = meta_ref[0]
    kv_out_ref, row_out_refs = refs[0], refs[1 : 1 + len(parts)]
    kv_held_ref, row_held_refs = refs[1 + len(parts)], refs[2 + len(parts) : 2 + 2 * len(parts)]
    in_sems, out_sems = refs[-2:]
    loads, stores = [], []

    def hop(source, held, target):
        slot = len(loads)
        loads.append(pltpu.make_async_copy(source, held, in_sems.at[slot]))
        stores.append(pltpu.make_async_copy(held, target, out_sems.at[slot]))

    for other in range(count):
        chosen = assign_ref[other]
        for which, source in enumerate((key_ref, value_ref)):
            hop(source.at[chosen], kv_held_ref.at[other, which], kv_out_ref.at[other, which])
    for (step, start, width), out_ref, held_ref in zip(parts, row_out_refs, row_held_refs):
        chosen = assign_ref[partner(group, step, count)[0]]
        for which, source in enumerate((query_ref, grad_ref)):
            hop(
                source.at[chosen, :, start : start + width], held_ref.at[which], out_ref.at[which]
            )
    for load in loads:
        load.start()
    for load, store in zip(loads, stores):
        load.wait()
        store.start()
    for store in stores:
        store.wait()


def stage(meta, assignment, queries, grad_out, keys, values, parts):
    count, rows, _ = queries.shape
    kv_shape = (count, 2, rows, keys.shape[2])
    shapes = [kv_shape] + [(2, rows, width) for _, _, width in parts]
    copies = 2 * count + 2 * len(parts)
    anywhere, scalars = pl.BlockSpec(memory_space=pl.ANY), pl.BlockSpec(memory_space=pltpu.SMEM)
    return pl.pallas_call(
        functools.partial(stage_kernel, count, parts),
        out_shape=[jax.ShapeDtypeStruct(shape, queries.dtype) for shape in shapes],
        in_specs=[scalars] * 2 + [anywhere] * 4,
        out_specs=[anywhere] * len(shapes),
        scratch_shapes=[pltpu.VMEM(shape, queries.dtype) for shape in shapes]
        + [pltpu.SemaphoreType.DMA((copies,))] * 2,
        compiler_params=pltpu.CompilerParams(vmem_limit_bytes=VMEM_BYTES),
        name="stage",
    )(meta, assignment, queries, grad_out, keys, values)


def build_bias(source, sequence, line, segment_ref, bias_ref, rows, tok_dev, ratio):
    pieces = bias_ref.shape[0] // tok_dev
    lanes = ratio * rows
    eye = lax.broadcasted_iota(jnp.int32, (tok_dev, tok_dev), 0) == lax.broadcasted_iota(
        jnp.int32, (tok_dev, tok_dev), 1
    )
    token = lax.broadcasted_iota(jnp.int32, (tok_dev, lanes), 0)
    place = source * rows + lax.rem(
        lax.broadcasted_iota(jnp.int32, (tok_dev, lanes), 1), jnp.int32(rows)
    )

    def column(back):
        start = pl.multiple_of(jnp.maximum(line - back, 0) * tok_dev, tok_dev)
        every = segment_ref[:, pl.ds(start, tok_dev)].astype(jnp.float32)
        mine = lax.broadcasted_iota(jnp.int32, every.shape, 0) == sequence
        row = jnp.sum(jnp.where(mine, every, 0.0), axis=0, keepdims=True)
        return jnp.sum(jnp.where(eye, row, 0.0), axis=1, keepdims=True)

    own = column(0)
    asked = jnp.sum(jnp.where(token == place, own, 0.0), axis=0, keepdims=True)
    allowed = (own == asked) & (token <= place)
    bias_ref[:tok_dev, :] = jnp.where(allowed, 0.0, BIG_NEGATIVE)
    for back in range(1, pieces):
        held = jnp.where(line >= back, column(back), -1.0)
        bias_ref[back * tok_dev : (back + 1) * tok_dev, :] = jnp.where(
            held == asked, 0.0, BIG_NEGATIVE
        )


def attend_kernel(
    step, first, filled, last, pieces, ratio, meta_ref, assign_ref, segment_ref, query_ref, grad_ref, *refs
):
    refs = list(refs)
    kv_refs = [refs.pop(0) for _ in range(pieces)]
    if not first:
        acc_in_ref = refs.pop(0)
    if filled:
        refs.pop(0)
    query_out_ref = refs.pop(0)
    if last:
        own_ref, halo_refs = refs.pop(0), [refs.pop(0) for _ in range(pieces - 1)]
    else:
        acc_out_ref = refs.pop(0)
    bias_ref, held_ref = refs

    rows = query_ref.shape[0]
    count = kv_refs[0].shape[0]
    tok_dev = count * rows
    scale = 1.0 / HD**0.5
    head = pl.program_id(0)

    @pl.when(head == 0)
    def _():
        group = meta_ref[0]
        source = partner(group, step, count)[1]
        build_bias(
            source, assign_ref[group], meta_ref[1], segment_ref, bias_ref, rows, tok_dev, ratio
        )

    def stacked(ref):
        return jnp.concatenate([ref[:, r * HD : (r + 1) * HD] for r in range(ratio)], axis=0)

    def window(which):
        return jnp.concatenate([ref[:, which].reshape(tok_dev, HD) for ref in kv_refs], axis=0)

    query, grad = stacked(query_ref), stacked(grad_ref)
    key, value = window(0), window(1)
    turned = (((1,), (1,)), ((), ()))
    scores = lax.dot_general(key, query, turned, preferred_element_type=jnp.float32)
    scores = scores * (scale * LOG2E) + bias_ref[...]
    top = jnp.max(scores, axis=0, keepdims=True)
    weights = jnp.exp2(scores - top)
    probs = weights * (1.0 / jnp.sum(weights, axis=0, keepdims=True))
    grad_probs = lax.dot_general(value, grad, turned, preferred_element_type=jnp.float32)
    product = probs * grad_probs
    delta = jnp.sum(product, axis=0, keepdims=True)
    grad_scores = (product - probs * delta).astype(jnp.bfloat16)
    grad_value = jnp.dot(probs.astype(jnp.bfloat16), grad, preferred_element_type=jnp.float32)
    grad_key = jnp.dot(grad_scores, query, preferred_element_type=jnp.float32)
    grad_query = lax.dot_general(
        grad_scores, key, (((0,), (0,)), ((), ())), preferred_element_type=jnp.float32
    )
    held_ref[head] = (grad_query * scale).reshape(ratio, rows, HD)
    if not first:
        grad_key = grad_key + acc_in_ref[0]
        grad_value = grad_value + acc_in_ref[1]
    if last:
        grad_key = grad_key * scale
        own_ref[0] = grad_key[:tok_dev]
        own_ref[1] = grad_value[:tok_dev]
        for back, halo_ref in enumerate(halo_refs, 1):
            span = slice(back * tok_dev, (back + 1) * tok_dev)
            halo_ref[0] = grad_key[span].astype(jnp.bfloat16)
            halo_ref[1] = grad_value[span].astype(jnp.bfloat16)
    else:
        acc_out_ref[0] = grad_key
        acc_out_ref[1] = grad_value

    @pl.when(head == HEADS_STEP - 1)
    def _():
        held = held_ref[...].reshape(HEADS_STEP * ratio, rows, HD)
        query_out_ref[...] = jnp.swapaxes(held, 0, 1).astype(jnp.bfloat16)


def attend(step, half, lanes_from, heads, meta, assignment, segments, query, grad, kv_pieces, acc, full, last):
    first, filled = acc is None, full is not None
    rows, (count, _, _, kv_width) = query[0].shape[1], kv_pieces[0].shape
    pieces = len(kv_pieces)
    ratio = heads // (kv_width // HD)
    tok_dev = count * rows
    keys = pieces * tok_dev
    step_lanes = HEADS_STEP * HD
    base = half * HEADS_STEP

    def rows_spec(pick):
        return pl.BlockSpec(
            (None, rows, ratio * HD), lambda c, m, a: (pick(m, a), 0, lanes_from + c)
        )

    acc_spec = pl.BlockSpec((2, keys, HD), lambda c, m, a: (0, 0, c))
    in_specs = [
        pl.BlockSpec(segments.shape, lambda c, m, a: (0, 0)),
        rows_spec(query[1]),
        rows_spec(grad[1]),
    ]
    in_specs += [
        pl.BlockSpec((count, 2, rows, HD), lambda c, m, a: (0, 0, 0, base + c)) for _ in kv_pieces
    ]
    operands = [meta, assignment, segments, query[0], grad[0], *kv_pieces]
    aliases = {}
    if not first:
        if not last:
            aliases[len(operands)] = 1
        operands.append(acc)
        in_specs.append(acc_spec)
    if filled:
        aliases[len(operands)] = 0
        operands.append(full)
        in_specs.append(pl.BlockSpec(memory_space=pl.ANY))
    out_shape = [jax.ShapeDtypeStruct((tok_dev, heads, HD), jnp.bfloat16)]
    out_specs = [
        pl.BlockSpec(
            (rows, HEADS_STEP * ratio, HD),
            lambda c, m, a: (partner(m[0], step, count)[1], half, 0),
        )
    ]
    if last:
        span_spec = pl.BlockSpec((2, tok_dev, HD), lambda c, m, a: (0, 0, c))
        out_shape.append(jax.ShapeDtypeStruct((2, tok_dev, step_lanes), jnp.float32))
        out_shape += [jax.ShapeDtypeStruct((2, tok_dev, step_lanes), jnp.bfloat16)] * (pieces - 1)
        out_specs += [span_spec] * pieces
    else:
        out_shape.append(jax.ShapeDtypeStruct((2, keys, step_lanes), jnp.float32))
        out_specs.append(acc_spec)
    pairs = HEADS_STEP * ratio * rows * keys
    return pl.pallas_call(
        functools.partial(attend_kernel, step, first, filled, last, pieces, ratio),
        out_shape=out_shape,
        grid_spec=pltpu.PrefetchScalarGridSpec(
            num_scalar_prefetch=2,
            grid=(HEADS_STEP,),
            in_specs=in_specs,
            out_specs=out_specs,
            scratch_shapes=[
                pltpu.VMEM((keys, ratio * rows), jnp.float32),
                pltpu.VMEM((HEADS_STEP, ratio, rows, HD), jnp.float32),
            ],
        ),
        input_output_aliases=aliases,
        compiler_params=pltpu.CompilerParams(
            dimension_semantics=("arbitrary",), vmem_limit_bytes=VMEM_BYTES
        ),
        cost_estimate=pl.CostEstimate(
            flops=10 * pairs * HD, bytes_accessed=8 * keys * step_lanes, transcendentals=pairs
        ),
        name="attend",
    )(*operands)


def shards(queries, keys, values, grad_out, segment_ids, assignment):
    count = lax.axis_size("dp")
    uly = lax.axis_size("uly")
    group = lax.axis_index("dp")
    line = lax.axis_index("blk") * uly + lax.axis_index("uly")
    width, kv_width = queries.shape[2], keys.shape[2]
    heads, kv_heads = width // HD, kv_width // HD
    halves = kv_heads // HEADS_STEP
    part = width // halves
    tok_dev = count * queries.shape[1]
    doc_most = min(512, tok_dev * uly)
    hops = -(-doc_most // tok_dev)
    meta = jnp.stack([group, line]).astype(jnp.int32)
    final = count - 1

    parts = [(step, 0, width) for step in range(1, final)]
    parts += [(final, half * part, part) for half in range(halves)]
    kv_out, *staged = stage(meta, assignment, queries, grad_out, keys, values, parts)
    kv_own = lax.all_to_all(kv_out, "dp", split_axis=0, concat_axis=0, tiled=True)
    whole = {step: exchanged(staged[step - 1], "dp", step) for step in range(final - 1, 0, -1)}
    split = [exchanged(staged[final - 1], "dp", final)]
    for half in range(1, halves):
        after, _ = lax.optimization_barrier((staged[final - 1 + half], split[-1]))
        split.append(exchanged(after, "dp", final))
    pieces = [kv_own]
    for back in range(1, hops + 1):
        pieces.append(shifted(kv_own, ("blk", "uly"), back))

    accs, full, own, halos = [None] * halves, None, [None] * halves, [None] * halves

    def visit(step, half, last):
        nonlocal full
        kv_step = HEADS_STEP * half
        if step == 0:
            query = (queries, lambda m, a: a[m[0]])
            grad = (grad_out, lambda m, a: a[m[0]])
        else:
            both = split[half] if step == final else whole[step]
            query, grad = (both, lambda m, a: 0), (both, lambda m, a: 1)
            if step == final:
                kv_step = 0
        full, *rest = attend(
            step, half, kv_step, heads, meta, assignment, segment_ids, query, grad, pieces,
            accs[half], full, last,
        )
        if last:
            own[half], halos[half] = rest[0], rest[1:]
        else:
            accs[half] = rest[0]

    for step in range(final - 1):
        for half in range(halves):
            visit(step, half, False)
    for half in range(halves - 1):
        visit(final, half, False)
        visit(final - 1, half, True)
    visit(final - 1, halves - 1, False)
    visit(final, halves - 1, True)

    totals = []
    for half in range(halves):
        total = own[half]
        for back in range(1, hops + 1):
            total = total + shifted(halos[half][back - 1], ("blk", "uly"), -back).astype(
                jnp.float32
            )
        totals.append(total.astype(jnp.bfloat16))
    total = jnp.concatenate(totals, axis=2)
    return full[None], total[0][None], total[1][None]


def solution(mesh):
    in_specs = (
        P(None, ("blk", "uly", "dp"), None),
        P(None, ("blk", "uly", "dp"), None),
        P(None, ("blk", "uly", "dp"), None),
        P(None, ("blk", "uly", "dp"), None),
        P(),
        P(),
    )
    out_specs = (
        P("dp", ("blk", "uly"), None, None),
        P("dp", ("blk", "uly"), None),
        P("dp", ("blk", "uly"), None),
    )
    return jax.shard_map(shards, mesh=mesh, in_specs=in_specs, out_specs=out_specs, check_vma=False)
```

```python
import functools

import jax
import jax.numpy as jnp
from jax import lax
from jax.experimental import pallas as pl
from jax.experimental.pallas import tpu as pltpu
from jax.sharding import PartitionSpec as P

HD = 128
LOG2E = 1.4426950408889634
BIG_NEGATIVE = -1e30
VMEM_BYTES = 32 * 1024 * 1024
HEADS_STEP = 2


def target_of(index, step, count):
    return lax.rem(index + step, count)


def source_of(index, step, count):
    return lax.rem(index + count - step, count)


def exchanged(value, axis, step):
    count = lax.axis_size(axis)
    return lax.ppermute(value, axis, [(i, (i + step) % count) for i in range(count)])


def shifted(value, axis, by):
    length = lax.axis_size(axis)
    pairs = [(i, i + by) for i in range(length) if 0 <= i + by < length]
    return lax.ppermute(value, axis, pairs)


def stage_kernel(count, parts, meta_ref, assign_ref, query_ref, grad_ref, key_ref, value_ref, *refs):
    group = meta_ref[0]
    kv_out_ref, row_out_refs = refs[0], refs[1 : 1 + len(parts)]
    kv_held_ref, row_held_refs = refs[1 + len(parts)], refs[2 + len(parts) : 2 + 2 * len(parts)]
    in_sems, out_sems = refs[-2:]
    loads, stores = [], []

    def hop(source, held, target):
        slot = len(loads)
        loads.append(pltpu.make_async_copy(source, held, in_sems.at[slot]))
        stores.append(pltpu.make_async_copy(held, target, out_sems.at[slot]))

    for other in range(count):
        chosen = assign_ref[other]
        for which, source in enumerate((key_ref, value_ref)):
            hop(source.at[chosen], kv_held_ref.at[other, which], kv_out_ref.at[other, which])
    for (step, start, width), out_ref, held_ref in zip(parts, row_out_refs, row_held_refs):
        chosen = assign_ref[target_of(group, step, count)]
        for which, source in enumerate((query_ref, grad_ref)):
            hop(
                source.at[chosen, :, start : start + width], held_ref.at[which], out_ref.at[which]
            )
    for load in loads:
        load.start()
    for load, store in zip(loads, stores):
        load.wait()
        store.start()
    for store in stores:
        store.wait()


def stage(meta, assignment, queries, grad_out, keys, values, parts):
    count, rows, _ = queries.shape
    kv_shape = (count, 2, rows, keys.shape[2])
    shapes = [kv_shape] + [(2, rows, width) for _, _, width in parts]
    copies = 2 * count + 2 * len(parts)
    far, scalars = pl.BlockSpec(memory_space=pltpu.HBM), pl.BlockSpec(memory_space=pltpu.SMEM)
    return pl.pallas_call(
        functools.partial(stage_kernel, count, parts),
        out_shape=[jax.ShapeDtypeStruct(shape, queries.dtype) for shape in shapes],
        in_specs=[scalars] * 2 + [far] * 4,
        out_specs=[far] * len(shapes),
        scratch_shapes=[pltpu.VMEM(shape, queries.dtype) for shape in shapes]
        + [pltpu.SemaphoreType.DMA((copies,))] * 2,
        compiler_params=pltpu.CompilerParams(vmem_limit_bytes=VMEM_BYTES),
        name="stage",
    )(meta, assignment, queries, grad_out, keys, values)


def build_bias(source, sequence, line, segment_ref, bias_ref, rows, tok_dev, ratio):
    pieces = bias_ref.shape[0] // tok_dev
    lanes = ratio * rows
    eye = lax.broadcasted_iota(jnp.int32, (tok_dev, tok_dev), 0) == lax.broadcasted_iota(
        jnp.int32, (tok_dev, tok_dev), 1
    )
    token = lax.broadcasted_iota(jnp.int32, (tok_dev, lanes), 0)
    place = source * rows + lax.rem(
        lax.broadcasted_iota(jnp.int32, (tok_dev, lanes), 1), jnp.int32(rows)
    )

    def column(back):
        start = pl.multiple_of(jnp.maximum(line - back, 0) * tok_dev, tok_dev)
        every = segment_ref[:, pl.ds(start, tok_dev)].astype(jnp.float32)
        mine = lax.broadcasted_iota(jnp.int32, every.shape, 0) == sequence
        row = jnp.sum(jnp.where(mine, every, 0.0), axis=0, keepdims=True)
        return jnp.sum(jnp.where(eye, row, 0.0), axis=1, keepdims=True)

    own = column(0)
    asked = jnp.sum(jnp.where(token == place, own, 0.0), axis=0, keepdims=True)
    allowed = (own == asked) & (token <= place)
    bias_ref[:tok_dev, :] = jnp.where(allowed, 0.0, BIG_NEGATIVE)
    for back in range(1, pieces):
        held = jnp.where(line >= back, column(back), -1.0)
        bias_ref[back * tok_dev : (back + 1) * tok_dev, :] = jnp.where(
            held == asked, 0.0, BIG_NEGATIVE
        )


def attend_kernel(
    step, first, filled, last, pieces, ratio, meta_ref, assign_ref, segment_ref, query_ref, grad_ref, *refs
):
    refs = list(refs)
    kv_refs = [refs.pop(0) for _ in range(pieces)]
    if not first:
        acc_in_ref = refs.pop(0)
    if filled:
        refs.pop(0)
    query_out_ref = refs.pop(0)
    if last:
        own_ref, halo_refs = refs.pop(0), [refs.pop(0) for _ in range(pieces - 1)]
    else:
        acc_out_ref = refs.pop(0)
    bias_ref, held_ref = refs

    rows = query_ref.shape[0]
    count = kv_refs[0].shape[0]
    tok_dev = count * rows
    scale = 1.0 / HD**0.5
    head = pl.program_id(0)
    slot = lax.rem(head, HEADS_STEP)

    @pl.when(head == 0)
    def _():
        group = meta_ref[0]
        source = source_of(group, step, count)
        build_bias(
            source, assign_ref[group], meta_ref[1], segment_ref, bias_ref, rows, tok_dev, ratio
        )

    def stacked(ref):
        return jnp.concatenate([ref[:, r * HD : (r + 1) * HD] for r in range(ratio)], axis=0)

    def window(which):
        return jnp.concatenate([ref[:, which].reshape(tok_dev, HD) for ref in kv_refs], axis=0)

    query, grad = stacked(query_ref), stacked(grad_ref)
    key, value = window(0), window(1)
    turned = (((1,), (1,)), ((), ()))
    scores = lax.dot_general(key, query, turned, preferred_element_type=jnp.float32)
    scores = scores * (scale * LOG2E) + bias_ref[...]
    top = jnp.max(scores, axis=0, keepdims=True)
    weights = jnp.exp2(scores - top)
    probs = weights * (1.0 / jnp.sum(weights, axis=0, keepdims=True))
    grad_probs = lax.dot_general(value, grad, turned, preferred_element_type=jnp.float32)
    product = probs * grad_probs
    delta = jnp.sum(product, axis=0, keepdims=True)
    grad_scores = (product - probs * delta).astype(jnp.bfloat16)
    grad_value = jnp.dot(probs.astype(jnp.bfloat16), grad, preferred_element_type=jnp.float32)
    grad_key = jnp.dot(grad_scores, query, preferred_element_type=jnp.float32)
    grad_query = lax.dot_general(
        grad_scores, key, (((0,), (0,)), ((), ())), preferred_element_type=jnp.float32
    )
    held_ref[slot] = (grad_query * scale).reshape(ratio, rows, HD)
    if not first:
        grad_key = grad_key + acc_in_ref[0]
        grad_value = grad_value + acc_in_ref[1]
    if last:
        grad_key = grad_key * scale
        own_ref[0] = grad_key[:tok_dev]
        own_ref[1] = grad_value[:tok_dev]
        for back, halo_ref in enumerate(halo_refs, 1):
            span = slice(back * tok_dev, (back + 1) * tok_dev)
            halo_ref[0] = grad_key[span].astype(jnp.bfloat16)
            halo_ref[1] = grad_value[span].astype(jnp.bfloat16)
    else:
        acc_out_ref[0] = grad_key
        acc_out_ref[1] = grad_value

    @pl.when(slot == HEADS_STEP - 1)
    def _():
        held = held_ref[...].reshape(HEADS_STEP * ratio, rows, HD)
        query_out_ref[...] = jnp.swapaxes(held, 0, 1).astype(jnp.bfloat16)


def attend(step, base, span, heads, meta, assignment, segments, query, grad, kv_pieces, acc, full, last):
    first, filled = acc is None, full is not None
    rows, (count, _, _, kv_width) = query[0].shape[1], kv_pieces[0].shape
    pieces = len(kv_pieces)
    ratio = heads // (kv_width // HD)
    tok_dev = count * rows
    keys = pieces * tok_dev

    def rows_spec(array, pick):
        start = base if array.shape[2] == heads * HD else 0
        return pl.BlockSpec((None, rows, ratio * HD), lambda c, m, a: (pick(m, a), 0, start + c))

    in_specs = [
        pl.BlockSpec(segments.shape, lambda c, m, a: (0, 0)),
        rows_spec(*query),
        rows_spec(*grad),
    ]
    in_specs += [
        pl.BlockSpec((count, 2, rows, HD), lambda c, m, a: (0, 0, 0, base + c)) for _ in kv_pieces
    ]
    operands = [meta, assignment, segments, query[0], grad[0], *kv_pieces]
    aliases = {}
    acc_spec = pl.BlockSpec((2, keys, HD), lambda c, m, a: (0, 0, base + c))
    if not first:
        if not last:
            aliases[len(operands)] = 1
        operands.append(acc)
        in_specs.append(acc_spec)
    if filled:
        aliases[len(operands)] = 0
        operands.append(full)
        in_specs.append(pl.BlockSpec(memory_space=pl.ANY))
    out_shape = [jax.ShapeDtypeStruct((tok_dev, heads, HD), jnp.bfloat16)]
    out_specs = [
        pl.BlockSpec(
            (rows, HEADS_STEP * ratio, HD),
            lambda c, m, a: (source_of(m[0], step, count), (base + c) // HEADS_STEP, 0),
        )
    ]
    if last:
        span_spec = pl.BlockSpec((2, tok_dev, HD), lambda c, m, a: (0, 0, c))
        out_shape.append(jax.ShapeDtypeStruct((2, tok_dev, span * HD), jnp.float32))
        out_shape += [jax.ShapeDtypeStruct((2, tok_dev, span * HD), jnp.bfloat16)] * (pieces - 1)
        out_specs += [span_spec] * pieces
    else:
        out_shape.append(jax.ShapeDtypeStruct((2, keys, kv_width), jnp.float32))
        out_specs.append(acc_spec)
    pairs = span * ratio * rows * keys
    return pl.pallas_call(
        functools.partial(attend_kernel, step, first, filled, last, pieces, ratio),
        out_shape=out_shape,
        grid_spec=pltpu.PrefetchScalarGridSpec(
            num_scalar_prefetch=2,
            grid=(span,),
            in_specs=in_specs,
            out_specs=out_specs,
            scratch_shapes=[
                pltpu.VMEM((keys, ratio * rows), jnp.float32),
                pltpu.VMEM((HEADS_STEP, ratio, rows, HD), jnp.float32),
            ],
        ),
        input_output_aliases=aliases,
        compiler_params=pltpu.CompilerParams(
            dimension_semantics=("arbitrary",), vmem_limit_bytes=VMEM_BYTES
        ),
        cost_estimate=pl.CostEstimate(
            flops=100 * pairs * HD, bytes_accessed=8 * keys * span * HD, transcendentals=pairs
        ),
        name="attend",
    )(*operands)


def shards(queries, keys, values, grad_out, segment_ids, assignment):
    count = lax.axis_size("dp")
    uly = lax.axis_size("uly")
    group = lax.axis_index("dp")
    line = lax.axis_index("blk") * uly + lax.axis_index("uly")
    width, kv_width = queries.shape[2], keys.shape[2]
    heads, kv_heads = width // HD, kv_width // HD
    halves = kv_heads // HEADS_STEP
    part = width // halves
    tok_dev = count * queries.shape[1]
    doc_most = min(512, tok_dev * uly)
    hops = -(-doc_most // tok_dev)
    meta = jnp.stack([group, line]).astype(jnp.int32)
    final = count - 1

    parts = [(step, 0, width) for step in range(1, final)]
    parts += [(final, half * part, part) for half in range(halves)]
    kv_out, *staged = stage(meta, assignment, queries, grad_out, keys, values, parts)
    kv_own = lax.all_to_all(kv_out, "dp", split_axis=0, concat_axis=0, tiled=True)
    arrived = [exchanged(rows, "dp", step) for rows, (step, _, _) in zip(staged, parts)]
    pieces = [kv_own]
    for back in range(1, hops + 1):
        pieces.append(shifted(kv_own, ("blk", "uly"), back))

    fixed = (heads, meta, assignment, segment_ids)
    query, grad = (queries, lambda m, a: a[m[0]]), (grad_out, lambda m, a: a[m[0]])
    full, acc = attend(0, 0, kv_heads, *fixed, query, grad, pieces, None, None, False)
    for both, (step, _, _) in zip(arrived[:-halves], parts):
        query, grad = (both, lambda m, a: 0), (both, lambda m, a: 1)
        full, acc = attend(step, 0, kv_heads, *fixed, query, grad, pieces, acc, full, False)
    totals = []
    for half, both in enumerate(arrived[-halves:]):
        query, grad = (both, lambda m, a: 0), (both, lambda m, a: 1)
        base = half * HEADS_STEP
        full, own, *halos = attend(
            final, base, HEADS_STEP, *fixed, query, grad, pieces, acc, full, True
        )
        for back, halo in enumerate(halos, 1):
            own = own + shifted(halo, ("blk", "uly"), -back).astype(jnp.float32)
        totals.append(own.astype(jnp.bfloat16))
    total = jnp.concatenate(totals, axis=2)
    return full[None], total[0][None], total[1][None]


def solution(mesh):
    in_specs = (
        P(None, ("blk", "uly", "dp"), None),
        P(None, ("blk", "uly", "dp"), None),
        P(None, ("blk", "uly", "dp"), None),
        P(None, ("blk", "uly", "dp"), None),
        P(),
        P(),
    )
    out_specs = (
        P("dp", ("blk", "uly"), None, None),
        P("dp", ("blk", "uly"), None),
        P("dp", ("blk", "uly"), None),
    )
    return jax.shard_map(shards, mesh=mesh, in_specs=in_specs, out_specs=out_specs, check_vma=False)
```

```python
import functools

import jax
import jax.numpy as jnp
from jax import lax
from jax.experimental import pallas as pl
from jax.experimental.pallas import tpu as pltpu
from jax.sharding import PartitionSpec as P

HD = 128
LOG2E = 1.4426950408889634
BIG_NEGATIVE = -1e30
VMEM_BYTES = 32 * 1024 * 1024
HEADS_STEP = 2


def target_of(index, step, count):
    return lax.rem(index + step, count)


def source_of(index, step, count):
    return lax.rem(index + count - step, count)


def exchanged(value, axis, step):
    count = lax.axis_size(axis)
    return lax.ppermute(value, axis, [(i, (i + step) % count) for i in range(count)])


def shifted(value, axis, by):
    length = lax.axis_size(axis)
    pairs = [(i, i + by) for i in range(length) if 0 <= i + by < length]
    return lax.ppermute(value, axis, pairs)


def stage_kernel(count, parts, copies, meta_ref, assign_ref, *refs):
    group = meta_ref[0]
    sources = refs[:2]
    out_refs, held_refs = refs[-2 - 2 * len(parts) : -2 - len(parts)], refs[-2 - len(parts) : -2]
    in_sems, out_sems = refs[-2:]
    loads, stores = [], []
    for (step, start, width), out_ref, held_ref in zip(parts, out_refs, held_refs):
        chosen = assign_ref[target_of(group, step, count)]
        for which, source in enumerate(sources):
            slot = len(loads)
            loads.append(
                pltpu.make_async_copy(
                    source.at[chosen, :, start : start + width],
                    held_ref.at[which],
                    in_sems.at[slot],
                )
            )
            stores.append(
                pltpu.make_async_copy(held_ref.at[which], out_ref.at[which], out_sems.at[slot])
            )
    for load in loads:
        load.start()
    for load, store in zip(loads, stores):
        load.wait()
        store.start()
    for store in stores:
        store.wait()


def stage_kv_kernel(assign_ref, key_ref, value_ref, out_ref, held_ref, in_sems, out_sems):
    loads, stores = [], []
    for group in range(out_ref.shape[0]):
        chosen = assign_ref[group]
        for which, source in enumerate((key_ref, value_ref)):
            slot = len(loads)
            held = held_ref.at[group, which]
            loads.append(pltpu.make_async_copy(source.at[chosen], held, in_sems.at[slot]))
            stores.append(
                pltpu.make_async_copy(held, out_ref.at[group, which], out_sems.at[slot])
            )
    for load in loads:
        load.start()
    for load, store in zip(loads, stores):
        load.wait()
        store.start()
    for store in stores:
        store.wait()


def stage_kv(assignment, keys, values):
    count, rows, width = keys.shape
    shape = (count, 2, rows, width)
    far = pl.BlockSpec(memory_space=pltpu.HBM)
    return pl.pallas_call(
        stage_kv_kernel,
        out_shape=jax.ShapeDtypeStruct(shape, keys.dtype),
        in_specs=[pl.BlockSpec(memory_space=pltpu.SMEM), far, far],
        out_specs=far,
        scratch_shapes=[pltpu.VMEM(shape, keys.dtype)]
        + [pltpu.SemaphoreType.DMA((2 * count,))] * 2,
        name="stage_kv",
    )(assignment, keys, values)


def stage(meta, assignment, first, second, parts, after=()):
    count, rows, _ = first.shape
    shapes = [(2, rows, width) for _, _, width in parts]
    copies = 2 * len(parts)
    far, scalars = pl.BlockSpec(memory_space=pltpu.HBM), pl.BlockSpec(memory_space=pltpu.SMEM)
    return pl.pallas_call(
        functools.partial(stage_kernel, count, parts, copies),
        out_shape=[jax.ShapeDtypeStruct(shape, first.dtype) for shape in shapes],
        in_specs=[scalars] * 2 + [far] * 2 + [pl.BlockSpec(memory_space=pl.ANY)] * len(after),
        out_specs=[far] * len(shapes),
        scratch_shapes=[pltpu.VMEM(shape, first.dtype) for shape in shapes]
        + [pltpu.SemaphoreType.DMA((copies,))] * 2,
        name="stage",
    )(meta, assignment, first, second, *after)


def build_bias(source, sequence, line, segment_ref, bias_ref, rows, tok_dev, ratio):
    pieces = bias_ref.shape[0] // tok_dev
    lanes = ratio * rows
    eye = lax.broadcasted_iota(jnp.int32, (tok_dev, tok_dev), 0) == lax.broadcasted_iota(
        jnp.int32, (tok_dev, tok_dev), 1
    )
    token = lax.broadcasted_iota(jnp.int32, (tok_dev, lanes), 0)
    place = source * rows + lax.rem(
        lax.broadcasted_iota(jnp.int32, (tok_dev, lanes), 1), jnp.int32(rows)
    )

    def column(back):
        start = pl.multiple_of(jnp.maximum(line - back, 0) * tok_dev, tok_dev)
        every = segment_ref[:, pl.ds(start, tok_dev)].astype(jnp.float32)
        mine = lax.broadcasted_iota(jnp.int32, every.shape, 0) == sequence
        row = jnp.sum(jnp.where(mine, every, 0.0), axis=0, keepdims=True)
        return jnp.sum(jnp.where(eye, row, 0.0), axis=1, keepdims=True)

    own = column(0)
    asked = jnp.sum(jnp.where(token == place, own, 0.0), axis=0, keepdims=True)
    allowed = (own == asked) & (token <= place)
    bias_ref[:tok_dev, :] = jnp.where(allowed, 0.0, BIG_NEGATIVE)
    for back in range(1, pieces):
        held = jnp.where(line >= back, column(back), -1.0)
        bias_ref[back * tok_dev : (back + 1) * tok_dev, :] = jnp.where(
            held == asked, 0.0, BIG_NEGATIVE
        )


def attend_kernel(
    step, first, filled, last, pieces, ratio, meta_ref, assign_ref, segment_ref, query_ref, grad_ref, *refs
):
    refs = list(refs)
    kv_refs = [refs.pop(0) for _ in range(pieces)]
    if not first:
        acc_in_ref = refs.pop(0)
    if filled:
        refs.pop(0)
    query_out_ref = refs.pop(0)
    if last:
        own_ref, halo_refs = refs.pop(0), [refs.pop(0) for _ in range(pieces - 1)]
    else:
        acc_out_ref = refs.pop(0)
    (bias_ref,) = refs

    rows = query_ref.shape[0]
    count = kv_refs[0].shape[0]
    tok_dev = count * rows
    scale = 1.0 / HD**0.5

    group = meta_ref[0]

    @pl.when(pl.program_id(0) == 0)
    def _():
        source = source_of(group, step, count)
        build_bias(
            source, assign_ref[group], meta_ref[1], segment_ref, bias_ref, rows, tok_dev, ratio
        )

    turned = (((1,), (1,)), ((), ()))
    grads = []
    for head in range(HEADS_STEP):
        lanes = slice(head * HD, (head + 1) * HD)

        def stacked(ref):
            start = head * ratio
            return jnp.concatenate(
                [ref[:, r * HD : (r + 1) * HD] for r in range(start, start + ratio)], axis=0
            )

        def window(which):
            return jnp.concatenate(
                [
                    ref[place, which, :, lanes]
                    for ref in kv_refs
                    for place in range(count)
                ],
                axis=0,
            )

        query, grad = stacked(query_ref), stacked(grad_ref)
        key, value = window(0), window(1)
        scores = lax.dot_general(key, query, turned, preferred_element_type=jnp.float32)
        scores = scores * (scale * LOG2E) + bias_ref[...]
        top = jnp.max(scores, axis=0, keepdims=True)
        weights = jnp.exp2(scores - top)
        probs = weights * (1.0 / jnp.sum(weights, axis=0, keepdims=True))
        grad_probs = lax.dot_general(value, grad, turned, preferred_element_type=jnp.float32)
        product = probs * grad_probs
        delta = jnp.sum(product, axis=0, keepdims=True)
        grad_scores = (product - probs * delta).astype(jnp.bfloat16)
        grad_value = jnp.dot(
            probs.astype(jnp.bfloat16), grad, preferred_element_type=jnp.float32
        )
        grad_key = jnp.dot(grad_scores, query, preferred_element_type=jnp.float32)
        grad_query = lax.dot_general(
            grad_scores, key, (((0,), (0,)), ((), ())), preferred_element_type=jnp.float32
        )
        grads.append((grad_query * scale).reshape(ratio, rows, HD))
        if not first:
            grad_key = grad_key + acc_in_ref[0, :, lanes]
            grad_value = grad_value + acc_in_ref[1, :, lanes]
        if last:
            grad_key = grad_key * scale
            own_ref[0, :, lanes] = grad_key[:tok_dev]
            own_ref[1, :, lanes] = grad_value[:tok_dev]
            for back, halo_ref in enumerate(halo_refs, 1):
                span = slice(back * tok_dev, (back + 1) * tok_dev)
                halo_ref[0, :, lanes] = grad_key[span].astype(jnp.bfloat16)
                halo_ref[1, :, lanes] = grad_value[span].astype(jnp.bfloat16)
        else:
            acc_out_ref[0, :, lanes] = grad_key
            acc_out_ref[1, :, lanes] = grad_value
    query_out_ref[...] = jnp.swapaxes(jnp.concatenate(grads, axis=0), 0, 1).astype(jnp.bfloat16)


def attend(step, base, span, cost, heads, meta, assignment, segments, query, grad, kv_pieces, acc, full, last):
    first, filled = acc is None, full is not None
    rows, (count, _, _, kv_width) = query[0].shape[1], kv_pieces[0].shape
    pieces = len(kv_pieces)
    ratio = heads // (kv_width // HD)
    tok_dev = count * rows
    keys = pieces * tok_dev
    lanes, place = HEADS_STEP * HD, base // HEADS_STEP

    def rows_spec(array, pick):
        start = place if array.shape[2] == heads * HD else 0
        return pl.BlockSpec(
            (None, rows, HEADS_STEP * ratio * HD), lambda c, m, a: (pick(m, a), 0, start + c)
        )

    in_specs = [
        pl.BlockSpec(segments.shape, lambda c, m, a: (0, 0)),
        rows_spec(*query),
        rows_spec(*grad),
    ]
    in_specs += [
        pl.BlockSpec((count, 2, rows, lanes), lambda c, m, a: (0, 0, 0, place + c))
        for _ in kv_pieces
    ]
    operands = [meta, assignment, segments, query[0], grad[0], *kv_pieces]
    aliases = {}
    acc_spec = pl.BlockSpec((2, keys, lanes), lambda c, m, a: (0, 0, place + c))
    if not first:
        if not last:
            aliases[len(operands)] = 1
        operands.append(acc)
        in_specs.append(acc_spec)
    if filled:
        aliases[len(operands)] = 0
        operands.append(full)
        in_specs.append(pl.BlockSpec(memory_space=pl.ANY))
    out_shape = [jax.ShapeDtypeStruct((tok_dev, heads, HD), jnp.bfloat16)]
    out_specs = [
        pl.BlockSpec(
            (rows, HEADS_STEP * ratio, HD),
            lambda c, m, a: (source_of(m[0], step, count), place + c, 0),
        )
    ]
    if last:
        span_spec = pl.BlockSpec((2, tok_dev, lanes), lambda c, m, a: (0, 0, c))
        out_shape.append(jax.ShapeDtypeStruct((2, tok_dev, span * HD), jnp.float32))
        out_shape += [jax.ShapeDtypeStruct((2, tok_dev, span * HD), jnp.bfloat16)] * (pieces - 1)
        out_specs += [span_spec] * pieces
    else:
        out_shape.append(jax.ShapeDtypeStruct((2, keys, kv_width), jnp.float32))
        out_specs.append(acc_spec)
    pairs = span * ratio * rows * keys
    return pl.pallas_call(
        functools.partial(attend_kernel, step, first, filled, last, pieces, ratio),
        out_shape=out_shape,
        grid_spec=pltpu.PrefetchScalarGridSpec(
            num_scalar_prefetch=2,
            grid=(span // HEADS_STEP,),
            in_specs=in_specs,
            out_specs=out_specs,
            scratch_shapes=[
                pltpu.VMEM((keys, ratio * rows), jnp.float32),
            ],
        ),
        input_output_aliases=aliases,
        compiler_params=pltpu.CompilerParams(
            dimension_semantics=("arbitrary",), vmem_limit_bytes=VMEM_BYTES
        ),
        cost_estimate=pl.CostEstimate(
            flops=cost * pairs * HD, bytes_accessed=cost * pairs, transcendentals=0
        ),
        name="attend",
    )(*operands)


def shards(queries, keys, values, grad_out, segment_ids, assignment):
    count = lax.axis_size("dp")
    uly = lax.axis_size("uly")
    group = lax.axis_index("dp")
    line = lax.axis_index("blk") * uly + lax.axis_index("uly")
    width, kv_width = queries.shape[2], keys.shape[2]
    heads, kv_heads = width // HD, kv_width // HD
    tok_dev = count * queries.shape[1]
    doc_most = min(512, tok_dev * uly)
    hops = -(-doc_most // tok_dev)
    meta = jnp.stack([group, line]).astype(jnp.int32)
    final = count - 1

    kv_out = stage_kv(assignment, keys, values)
    parts = [(step, 0, width) for step in range(1, count)]
    staged = stage(meta, assignment, queries, grad_out, parts, after=(kv_out,))
    kv_own = lax.all_to_all(kv_out, "dp", split_axis=0, concat_axis=0, tiled=True)
    arrived = [exchanged(rows, "dp", step) for rows, (step, _, _) in zip(staged, parts)]
    pieces = [kv_own]
    for back in range(1, hops + 1):
        pieces.append(shifted(kv_own, ("blk", "uly"), back))

    fixed = (heads, meta, assignment, segment_ids)
    query, grad = (queries, lambda m, a: a[m[0]]), (grad_out, lambda m, a: a[m[0]])
    full, acc = attend(0, 0, kv_heads, 1, *fixed, query, grad, pieces, None, None, False)
    for both, (step, _, _) in zip(arrived, parts):
        query, grad = (both, lambda m, a: 0), (both, lambda m, a: 1)
        full, acc, *halos = attend(
            step, 0, kv_heads, 1, *fixed, query, grad, pieces, acc, full, step == final
        )
    total = acc
    for back, halo in enumerate(halos, 1):
        total = total + shifted(halo, ("blk", "uly"), -back).astype(jnp.float32)
    total = total.astype(jnp.bfloat16)
    return full[None], total[0][None], total[1][None]


def solution(mesh):
    in_specs = (
        P(None, ("blk", "uly", "dp"), None),
        P(None, ("blk", "uly", "dp"), None),
        P(None, ("blk", "uly", "dp"), None),
        P(None, ("blk", "uly", "dp"), None),
        P(),
        P(),
    )
    out_specs = (
        P("dp", ("blk", "uly"), None, None),
        P("dp", ("blk", "uly"), None),
        P("dp", ("blk", "uly"), None),
    )
    return jax.shard_map(shards, mesh=mesh, in_specs=in_specs, out_specs=out_specs, check_vma=False)
```

```python
import functools

import jax
import jax.numpy as jnp
from jax import lax
from jax.experimental import pallas as pl
from jax.experimental.pallas import tpu as pltpu
from jax.sharding import PartitionSpec as P

HD = 128
LOG2E = 1.4426950408889634
BIG_NEGATIVE = -1e30
VMEM_BYTES = 32 * 1024 * 1024
HEADS_STEP = 2


def target_of(index, step, count):
    return lax.rem(index + step, count)


def source_of(index, step, count):
    return lax.rem(index + count - step, count)


def exchanged(value, axis, step):
    count = lax.axis_size(axis)
    return lax.ppermute(value, axis, [(i, (i + step) % count) for i in range(count)])


def shifted(value, axis, by):
    length = lax.axis_size(axis)
    pairs = [(i, i + by) for i in range(length) if 0 <= i + by < length]
    return lax.ppermute(value, axis, pairs)


def stage_kernel(count, jobs, outs, meta_ref, assign_ref, *refs):
    group = meta_ref[0]
    sources, refs = refs[:4], refs[len(refs) - 2 * outs - 2 :]
    out_refs, held_refs, (in_sems, out_sems) = refs[:outs], refs[outs : 2 * outs], refs[-2:]
    loads, stores = [], []
    for slot, (source, step, start, width, out, place) in enumerate(jobs):
        other = step if len(place) > 1 else target_of(group, step, count)
        origin = sources[source].at[assign_ref[other], :, start : start + width]
        held, goal = held_refs[out].at[place], out_refs[out].at[place]
        loads.append(pltpu.make_async_copy(origin, held, in_sems.at[slot]))
        stores.append(pltpu.make_async_copy(held, goal, out_sems.at[slot]))
    for load in loads:
        load.start()
    for load, store in zip(loads, stores):
        load.wait()
        store.start()
    for store in stores:
        store.wait()


def stage(meta, assignment, arrays, parts, with_kv, after=()):
    count, rows, _ = arrays[0].shape
    kv_width = arrays[2].shape[2]
    shapes, jobs = [], []
    if with_kv:
        shapes.append((count, 2, rows, kv_width))
        for other in range(count):
            jobs += [(2 + which, other, 0, kv_width, 0, (other, which)) for which in range(2)]
    for step, start, width in parts:
        jobs += [(which, step, start, width, len(shapes), (which,)) for which in range(2)]
        shapes.append((2, rows, width))
    far, scalars = pl.BlockSpec(memory_space=pltpu.HBM), pl.BlockSpec(memory_space=pltpu.SMEM)
    return pl.pallas_call(
        functools.partial(stage_kernel, count, jobs, len(shapes)),
        out_shape=[jax.ShapeDtypeStruct(shape, arrays[0].dtype) for shape in shapes],
        in_specs=[scalars] * 2 + [far] * 4 + [pl.BlockSpec(memory_space=pl.ANY)] * len(after),
        out_specs=[far] * len(shapes),
        scratch_shapes=[pltpu.VMEM(shape, arrays[0].dtype) for shape in shapes]
        + [pltpu.SemaphoreType.DMA((len(jobs),))] * 2,
        name="stage",
    )(meta, assignment, *arrays, *after)


def build_bias(source, sequence, line, segment_ref, bias_ref, rows, tok_dev, ratio):
    pieces = bias_ref.shape[0] // tok_dev
    lanes = ratio * rows
    eye = lax.broadcasted_iota(jnp.int32, (tok_dev, tok_dev), 0) == lax.broadcasted_iota(
        jnp.int32, (tok_dev, tok_dev), 1
    )
    token = lax.broadcasted_iota(jnp.int32, (tok_dev, lanes), 0)
    place = source * rows + lax.rem(
        lax.broadcasted_iota(jnp.int32, (tok_dev, lanes), 1), jnp.int32(rows)
    )

    def column(back):
        start = pl.multiple_of(jnp.maximum(line - back, 0) * tok_dev, tok_dev)
        every = segment_ref[:, pl.ds(start, tok_dev)].astype(jnp.float32)
        mine = lax.broadcasted_iota(jnp.int32, every.shape, 0) == sequence
        row = jnp.sum(jnp.where(mine, every, 0.0), axis=0, keepdims=True)
        return jnp.sum(jnp.where(eye, row, 0.0), axis=1, keepdims=True)

    own = column(0)
    asked = jnp.sum(jnp.where(token == place, own, 0.0), axis=0, keepdims=True)
    allowed = (own == asked) & (token <= place)
    bias_ref[:tok_dev, :] = jnp.where(allowed, 0.0, BIG_NEGATIVE)
    for back in range(1, pieces):
        held = jnp.where(line >= back, column(back), -1.0)
        bias_ref[back * tok_dev : (back + 1) * tok_dev, :] = jnp.where(
            held == asked, 0.0, BIG_NEGATIVE
        )


def attend_kernel(
    step, first, filled, last, pieces, ratio, meta_ref, assign_ref, segment_ref, query_ref, grad_ref, *refs
):
    refs = list(refs)
    kv_refs = [refs.pop(0) for _ in range(pieces)]
    if not first:
        acc_in_ref = refs.pop(0)
    if filled:
        refs.pop(0)
    query_out_ref = refs.pop(0)
    if last:
        own_ref, halo_refs = refs.pop(0), [refs.pop(0) for _ in range(pieces - 1)]
    else:
        acc_out_ref = refs.pop(0)
    (bias_ref,) = refs

    rows = query_ref.shape[0]
    count = kv_refs[0].shape[0]
    tok_dev = count * rows
    scale = 1.0 / HD**0.5

    group = meta_ref[0]

    @pl.when(pl.program_id(0) == 0)
    def _():
        source = source_of(group, step, count)
        build_bias(
            source, assign_ref[group], meta_ref[1], segment_ref, bias_ref, rows, tok_dev, ratio
        )

    turned = (((1,), (1,)), ((), ()))
    grads = []
    for head in range(HEADS_STEP):
        lanes = slice(head * HD, (head + 1) * HD)

        def stacked(ref):
            start = head * ratio
            return jnp.concatenate(
                [ref[:, r * HD : (r + 1) * HD] for r in range(start, start + ratio)], axis=0
            )

        def window(which):
            return jnp.concatenate(
                [
                    ref[place, which, :, lanes]
                    for ref in kv_refs
                    for place in range(count)
                ],
                axis=0,
            )

        query, grad = stacked(query_ref), stacked(grad_ref)
        key, value = window(0), window(1)
        scores = lax.dot_general(key, query, turned, preferred_element_type=jnp.float32)
        scores = scores * (scale * LOG2E) + bias_ref[...]
        top = jnp.max(scores, axis=0, keepdims=True)
        weights = jnp.exp2(scores - top)
        probs = weights * (1.0 / jnp.sum(weights, axis=0, keepdims=True))
        grad_probs = lax.dot_general(value, grad, turned, preferred_element_type=jnp.float32)
        product = probs * grad_probs
        delta = jnp.sum(product, axis=0, keepdims=True)
        grad_scores = (product - probs * delta).astype(jnp.bfloat16)
        grad_value = jnp.dot(
            probs.astype(jnp.bfloat16), grad, preferred_element_type=jnp.float32
        )
        grad_key = jnp.dot(grad_scores, query, preferred_element_type=jnp.float32)
        grad_query = lax.dot_general(
            grad_scores, key, (((0,), (0,)), ((), ())), preferred_element_type=jnp.float32
        )
        grads.append((grad_query * scale).reshape(ratio, rows, HD))
        if not first:
            grad_key = grad_key + acc_in_ref[0, :, lanes]
            grad_value = grad_value + acc_in_ref[1, :, lanes]
        if last:
            grad_key = grad_key * scale
            own_ref[0, :, lanes] = grad_key[:tok_dev]
            own_ref[1, :, lanes] = grad_value[:tok_dev]
            for back, halo_ref in enumerate(halo_refs, 1):
                span = slice(back * tok_dev, (back + 1) * tok_dev)
                halo_ref[0, :, lanes] = grad_key[span].astype(jnp.bfloat16)
                halo_ref[1, :, lanes] = grad_value[span].astype(jnp.bfloat16)
        else:
            acc_out_ref[0, :, lanes] = grad_key
            acc_out_ref[1, :, lanes] = grad_value
    query_out_ref[...] = jnp.swapaxes(jnp.concatenate(grads, axis=0), 0, 1).astype(jnp.bfloat16)


def attend(step, base, span, cost, heads, meta, assignment, segments, query, grad, kv_pieces, acc, full, last):
    first, filled = acc is None, full is not None
    rows, (count, _, _, kv_width) = query[0].shape[1], kv_pieces[0].shape
    pieces = len(kv_pieces)
    ratio = heads // (kv_width // HD)
    tok_dev = count * rows
    keys = pieces * tok_dev
    lanes, place = HEADS_STEP * HD, base // HEADS_STEP

    def rows_spec(array, pick):
        start = place if array.shape[2] == heads * HD else 0
        return pl.BlockSpec(
            (None, rows, HEADS_STEP * ratio * HD), lambda c, m, a: (pick(m, a), 0, start + c)
        )

    in_specs = [
        pl.BlockSpec(segments.shape, lambda c, m, a: (0, 0)),
        rows_spec(*query),
        rows_spec(*grad),
    ]
    in_specs += [
        pl.BlockSpec((count, 2, rows, lanes), lambda c, m, a: (0, 0, 0, place + c))
        for _ in kv_pieces
    ]
    operands = [meta, assignment, segments, query[0], grad[0], *kv_pieces]
    aliases = {}
    acc_spec = pl.BlockSpec((2, keys, lanes), lambda c, m, a: (0, 0, place + c))
    if not first:
        if not last:
            aliases[len(operands)] = 1
        operands.append(acc)
        in_specs.append(acc_spec)
    if filled:
        aliases[len(operands)] = 0
        operands.append(full)
        in_specs.append(pl.BlockSpec(memory_space=pl.ANY))
    out_shape = [jax.ShapeDtypeStruct((tok_dev, heads, HD), jnp.bfloat16)]
    out_specs = [
        pl.BlockSpec(
            (rows, HEADS_STEP * ratio, HD),
            lambda c, m, a: (source_of(m[0], step, count), place + c, 0),
        )
    ]
    if last:
        span_spec = pl.BlockSpec((2, tok_dev, lanes), lambda c, m, a: (0, 0, c))
        out_shape.append(jax.ShapeDtypeStruct((2, tok_dev, span * HD), jnp.float32))
        out_shape += [jax.ShapeDtypeStruct((2, tok_dev, span * HD), jnp.bfloat16)] * (pieces - 1)
        out_specs += [span_spec] * pieces
    else:
        out_shape.append(jax.ShapeDtypeStruct((2, keys, kv_width), jnp.float32))
        out_specs.append(acc_spec)
    pairs = span * ratio * rows * keys
    return pl.pallas_call(
        functools.partial(attend_kernel, step, first, filled, last, pieces, ratio),
        out_shape=out_shape,
        grid_spec=pltpu.PrefetchScalarGridSpec(
            num_scalar_prefetch=2,
            grid=(span // HEADS_STEP,),
            in_specs=in_specs,
            out_specs=out_specs,
            scratch_shapes=[
                pltpu.VMEM((keys, ratio * rows), jnp.float32),
            ],
        ),
        input_output_aliases=aliases,
        compiler_params=pltpu.CompilerParams(
            dimension_semantics=("arbitrary",), vmem_limit_bytes=VMEM_BYTES
        ),
        cost_estimate=pl.CostEstimate(
            flops=cost * pairs * HD, bytes_accessed=cost * pairs, transcendentals=0
        ),
        name="attend",
    )(*operands)


def shards(queries, keys, values, grad_out, segment_ids, assignment):
    count = lax.axis_size("dp")
    uly = lax.axis_size("uly")
    group = lax.axis_index("dp")
    line = lax.axis_index("blk") * uly + lax.axis_index("uly")
    width, kv_width = queries.shape[2], keys.shape[2]
    heads, kv_heads = width // HD, kv_width // HD
    tok_dev = count * queries.shape[1]
    doc_most = min(512, tok_dev * uly)
    hops = -(-doc_most // tok_dev)
    meta = jnp.stack([group, line]).astype(jnp.int32)
    halves = kv_heads // HEADS_STEP
    part = width // halves
    final = count // 2
    others = [step for step in range(1, count) if step != final]

    arrays = (queries, grad_out, keys, values)
    parts = [(step, 0, width) for step in others]
    parts += [(final, half * part, part) for half in range(halves)]
    ahead = stage(meta, assignment, arrays, parts[:1], False)
    kv_out, *behind = stage(meta, assignment, arrays, parts[1:], True, after=ahead)
    kv_own = lax.all_to_all(kv_out, "dp", split_axis=0, concat_axis=0, tiled=True)
    early, late = [*ahead, *behind][: len(others) + 1], behind[len(others) :]
    arrived = [exchanged(rows, "dp", step) for rows, (step, _, _) in zip(early, parts)]
    pieces = [kv_own]
    for back in range(1, hops + 1):
        pieces.append(shifted(kv_own, ("blk", "uly"), back))

    fixed = (heads, meta, assignment, segment_ids)
    query, grad = (queries, lambda m, a: a[m[0]]), (grad_out, lambda m, a: a[m[0]])
    full, acc = attend(0, 0, kv_heads, 1, *fixed, query, grad, pieces, None, None, False)
    late, acc = lax.optimization_barrier((late, acc))
    arrived += [exchanged(rows, "dp", final) for rows in late]
    for both, step in zip(arrived, others):
        query, grad = (both, lambda m, a: 0), (both, lambda m, a: 1)
        full, acc = attend(step, 0, kv_heads, 1, *fixed, query, grad, pieces, acc, full, False)
    totals, returned = [], []
    for half, both in enumerate(arrived[len(others) :]):
        if half:
            both, returned = lax.optimization_barrier((both, returned))
        query, grad = (both, lambda m, a: 0), (both, lambda m, a: 1)
        full, total, *halos = attend(
            final, half * HEADS_STEP, HEADS_STEP, 1, *fixed, query, grad, pieces, acc, full, True
        )
        returned = [shifted(halo, ("blk", "uly"), -back) for back, halo in enumerate(halos, 1)]
        for halo in returned:
            total = total + halo.astype(jnp.float32)
        totals.append(total.astype(jnp.bfloat16))
    total = jnp.concatenate(totals, axis=2)
    return full[None], total[0][None], total[1][None]


def solution(mesh):
    in_specs = (
        P(None, ("blk", "uly", "dp"), None),
        P(None, ("blk", "uly", "dp"), None),
        P(None, ("blk", "uly", "dp"), None),
        P(None, ("blk", "uly", "dp"), None),
        P(),
        P(),
    )
    out_specs = (
        P("dp", ("blk", "uly"), None, None),
        P("dp", ("blk", "uly"), None),
        P("dp", ("blk", "uly"), None),
    )
    return jax.shard_map(shards, mesh=mesh, in_specs=in_specs, out_specs=out_specs, check_vma=False)
```

```python
import functools

import jax
import jax.numpy as jnp
from jax import lax
from jax.experimental import pallas as pl
from jax.experimental.pallas import tpu as pltpu
from jax.sharding import PartitionSpec as P

HD = 128
LOG2E = 1.4426950408889634
BIG_NEGATIVE = -1e30
VMEM_BYTES = 32 * 1024 * 1024
HEADS_STEP = 2
STAGE_COST = 30_000_000_000


def target_of(index, step, count):
    return lax.rem(index + step, count)


def source_of(index, step, count):
    return lax.rem(index + count - step, count)


def exchanged(value, axis, step):
    count = lax.axis_size(axis)
    return lax.ppermute(value, axis, [(i, (i + step) % count) for i in range(count)])


def shifted(value, axis, by):
    length = lax.axis_size(axis)
    pairs = [(i, i + by) for i in range(length) if 0 <= i + by < length]
    return lax.ppermute(value, axis, pairs)


def stage_kernel(count, jobs, outs, meta_ref, assign_ref, *refs):
    group = meta_ref[0]
    sources, refs = refs[:4], refs[len(refs) - 2 * outs - 2 :]
    out_refs, held_refs, (in_sems, out_sems) = refs[:outs], refs[outs : 2 * outs], refs[-2:]
    loads, stores = [], []
    for slot, (source, step, start, width, out, place) in enumerate(jobs):
        other = step if len(place) > 1 else target_of(group, step, count)
        origin = sources[source].at[assign_ref[other], :, start : start + width]
        held, goal = held_refs[out].at[place], out_refs[out].at[place]
        loads.append(pltpu.make_async_copy(origin, held, in_sems.at[slot]))
        stores.append(pltpu.make_async_copy(held, goal, out_sems.at[slot]))
    for load in loads:
        load.start()
    for load, store in zip(loads, stores):
        load.wait()
        store.start()
    for store in stores:
        store.wait()


def stage(meta, assignment, arrays, parts, with_kv, cost, after=()):
    count, rows, _ = arrays[0].shape
    kv_width = arrays[2].shape[2]
    shapes, jobs = [], []
    if with_kv:
        shapes.append((count, 2, rows, kv_width))
        for other in range(count):
            jobs += [(2 + which, other, 0, kv_width, 0, (other, which)) for which in range(2)]
    for step, start, width in parts:
        jobs += [(which, step, start, width, len(shapes), (which,)) for which in range(2)]
        shapes.append((2, rows, width))
    far, scalars = pl.BlockSpec(memory_space=pltpu.HBM), pl.BlockSpec(memory_space=pltpu.SMEM)
    return pl.pallas_call(
        functools.partial(stage_kernel, count, jobs, len(shapes)),
        out_shape=[jax.ShapeDtypeStruct(shape, arrays[0].dtype) for shape in shapes],
        in_specs=[scalars] * 2 + [far] * 4 + [pl.BlockSpec(memory_space=pl.ANY)] * len(after),
        out_specs=[far] * len(shapes),
        scratch_shapes=[pltpu.VMEM(shape, arrays[0].dtype) for shape in shapes]
        + [pltpu.SemaphoreType.DMA((len(jobs),))] * 2,
        cost_estimate=pl.CostEstimate(flops=cost, bytes_accessed=cost, transcendentals=0),
        name="stage",
    )(meta, assignment, *arrays, *after)


def build_bias(source, sequence, line, segment_ref, column_ref, bias_ref, rows, tok_dev, reach):
    keys, lanes = column_ref.shape
    pieces = keys // tok_dev
    window = bias_ref.shape[0]
    eye = lax.broadcasted_iota(jnp.int32, (tok_dev, tok_dev), 0) == lax.broadcasted_iota(
        jnp.int32, (tok_dev, tok_dev), 1
    )
    for place in range(pieces):
        back = pieces - 1 - place
        start = pl.multiple_of(jnp.maximum(line - back, 0) * tok_dev, tok_dev)
        every = segment_ref[:, pl.ds(start, tok_dev)].astype(jnp.float32)
        mine = lax.broadcasted_iota(jnp.int32, every.shape, 0) == sequence
        row = jnp.sum(jnp.where(mine, every, 0.0), axis=0, keepdims=True)
        column = jnp.sum(jnp.where(eye, row, 0.0), axis=1, keepdims=True)
        column = jnp.where(line >= back, column, -1.0)
        column_ref[place * tok_dev : (place + 1) * tok_dev, :] = jnp.broadcast_to(
            column, (tok_dev, lanes)
        )

    def token(shape):
        return lax.rem(lax.broadcasted_iota(jnp.int32, shape, 1), jnp.int32(rows))

    here = pl.multiple_of(keys - tok_dev + source * rows, rows)
    asked_rows = column_ref[pl.ds(here, rows), :]
    same = lax.broadcasted_iota(jnp.int32, (rows, lanes), 0) == token((rows, lanes))
    asked = jnp.sum(jnp.where(same, asked_rows, 0.0), axis=0, keepdims=True)
    held = column_ref[pl.ds(pl.multiple_of(here - reach, rows), window), :]
    place = lax.broadcasted_iota(jnp.int32, (window, lanes), 0)
    allowed = (held == asked) & (place <= token((window, lanes)) + reach)
    bias_ref[...] = jnp.where(allowed, 0.0, BIG_NEGATIVE)


def attend_kernel(
    step, first, filled, last, tok_dev, reach, ratio,
    meta_ref, assign_ref, segment_ref, query_ref, grad_ref, kv_ref, *refs,
):
    refs = list(refs)
    if not first:
        acc_in_ref = refs.pop(0)
    if filled:
        refs.pop(0)
    query_out_ref = refs.pop(0)
    column_ref, bias_ref = refs[-2 - last], refs[-1 - last]
    if last:
        own_ref, halo_refs, acc_ref = refs[0], refs[1:-3], refs[-1]
    else:
        acc_ref = refs[0]

    rows = query_ref.shape[0]
    window = bias_ref.shape[0]
    keys = column_ref.shape[0]
    scale = 1.0 / HD**0.5
    group = meta_ref[0]
    source = source_of(group, step, tok_dev // rows)
    block = (keys - tok_dev - reach) // rows + source
    span = pl.ds(pl.multiple_of(block * rows, rows), window)

    @pl.when(pl.program_id(0) == 0)
    def _():
        build_bias(
            source, assign_ref[group], meta_ref[1], segment_ref, column_ref, bias_ref, rows, tok_dev, reach
        )

    acc_ref[...] = jnp.zeros_like(acc_ref) if first else acc_in_ref[...]
    turned = (((1,), (1,)), ((), ()))
    grads = []
    for head in range(HEADS_STEP):
        lanes = slice(head * HD, (head + 1) * HD)

        def stacked(ref):
            start = head * ratio
            return jnp.concatenate(
                [ref[:, r * HD : (r + 1) * HD] for r in range(start, start + ratio)], axis=0
            )

        def windowed(which):
            return kv_ref[pl.ds(block, window // rows), which, :, lanes].reshape(window, HD)

        query, grad = stacked(query_ref), stacked(grad_ref)
        key, value = windowed(0), windowed(1)
        scores = lax.dot_general(key, query, turned, preferred_element_type=jnp.float32)
        scores = scores * (scale * LOG2E) + bias_ref[...]
        top = jnp.max(scores, axis=0, keepdims=True)
        weights = jnp.exp2(scores - top)
        probs = weights * (1.0 / jnp.sum(weights, axis=0, keepdims=True))
        grad_probs = lax.dot_general(value, grad, turned, preferred_element_type=jnp.float32)
        product = probs * grad_probs
        delta = jnp.sum(product, axis=0, keepdims=True)
        grad_scores = (product - probs * delta).astype(jnp.bfloat16)
        grad_value = jnp.dot(
            probs.astype(jnp.bfloat16), grad, preferred_element_type=jnp.float32
        )
        grad_key = jnp.dot(grad_scores, query, preferred_element_type=jnp.float32)
        grad_query = lax.dot_general(
            grad_scores, key, (((0,), (0,)), ((), ())), preferred_element_type=jnp.float32
        )
        grads.append((grad_query * scale).reshape(ratio, rows, HD))
        acc_ref[0, span, lanes] += grad_key
        acc_ref[1, span, lanes] += grad_value
    if last:
        own_ref[0] = acc_ref[0, keys - tok_dev :] * scale
        own_ref[1] = acc_ref[1, keys - tok_dev :]
        for back, halo_ref in enumerate(halo_refs, 1):
            part = slice(keys - (back + 1) * tok_dev, keys - back * tok_dev)
            halo_ref[0] = (acc_ref[0, part] * scale).astype(jnp.bfloat16)
            halo_ref[1] = acc_ref[1, part].astype(jnp.bfloat16)
    query_out_ref[...] = jnp.swapaxes(jnp.concatenate(grads, axis=0), 0, 1).astype(jnp.bfloat16)


def attend(step, base, span, reach, heads, meta, assignment, segments, query, grad, kv, acc, full, last):
    first, filled = acc is None, full is not None
    rows, (blocks, _, _, kv_width) = query[0].shape[1], kv.shape
    ratio = heads // (kv_width // HD)
    keys, tok_dev = blocks * rows, query[0].shape[1] * lax.axis_size("dp")
    pieces, window = keys // tok_dev, reach + rows
    lanes, place = HEADS_STEP * HD, base // HEADS_STEP

    def rows_spec(array, pick):
        start = place if array.shape[2] == heads * HD else 0
        return pl.BlockSpec(
            (None, rows, HEADS_STEP * ratio * HD), lambda c, m, a: (pick(m, a), 0, start + c)
        )

    in_specs = [
        pl.BlockSpec(segments.shape, lambda c, m, a: (0, 0)),
        rows_spec(*query),
        rows_spec(*grad),
    ]
    in_specs.append(pl.BlockSpec((blocks, 2, rows, lanes), lambda c, m, a: (0, 0, 0, place + c)))
    operands = [meta, assignment, segments, query[0], grad[0], kv]
    aliases = {}
    acc_spec = pl.BlockSpec((2, keys, lanes), lambda c, m, a: (0, 0, place + c))
    if not first:
        if not last:
            aliases[len(operands)] = 1
        operands.append(acc)
        in_specs.append(acc_spec)
    if filled:
        aliases[len(operands)] = 0
        operands.append(full)
        in_specs.append(pl.BlockSpec(memory_space=pl.ANY))
    out_shape = [jax.ShapeDtypeStruct((tok_dev, heads, HD), jnp.bfloat16)]
    out_specs = [
        pl.BlockSpec(
            (rows, HEADS_STEP * ratio, HD),
            lambda c, m, a: (source_of(m[0], step, tok_dev // rows), place + c, 0),
        )
    ]
    if last:
        span_spec = pl.BlockSpec((2, tok_dev, lanes), lambda c, m, a: (0, 0, c))
        out_shape.append(jax.ShapeDtypeStruct((2, tok_dev, span * HD), jnp.float32))
        out_shape += [jax.ShapeDtypeStruct((2, tok_dev, span * HD), jnp.bfloat16)] * (pieces - 1)
        out_specs += [span_spec] * pieces
    else:
        out_shape.append(jax.ShapeDtypeStruct((2, keys, kv_width), jnp.float32))
        out_specs.append(acc_spec)
    pairs = span * ratio * rows * window
    held = (keys, ratio * rows), (window, ratio * rows)
    held += ((2, keys, lanes),) * last
    return pl.pallas_call(
        functools.partial(attend_kernel, step, first, filled, last, tok_dev, reach, ratio),
        out_shape=out_shape,
        grid_spec=pltpu.PrefetchScalarGridSpec(
            num_scalar_prefetch=2,
            grid=(span // HEADS_STEP,),
            in_specs=in_specs,
            out_specs=out_specs,
            scratch_shapes=[pltpu.VMEM(shape, jnp.float32) for shape in held],
        ),
        input_output_aliases=aliases,
        compiler_params=pltpu.CompilerParams(
            dimension_semantics=("arbitrary",), vmem_limit_bytes=VMEM_BYTES
        ),
        cost_estimate=pl.CostEstimate(
            flops=pairs * HD, bytes_accessed=pairs, transcendentals=0
        ),
        name="attend",
    )(*operands)


def shards(queries, keys, values, grad_out, segment_ids, assignment):
    count = lax.axis_size("dp")
    uly = lax.axis_size("uly")
    group = lax.axis_index("dp")
    line = lax.axis_index("blk") * uly + lax.axis_index("uly")
    width, kv_width = queries.shape[2], keys.shape[2]
    heads, kv_heads = width // HD, kv_width // HD
    tok_dev = count * queries.shape[1]
    doc_most = min(512, tok_dev * uly)
    hops = -(-doc_most // tok_dev)
    meta = jnp.stack([group, line]).astype(jnp.int32)

    arrays = (queries, grad_out, keys, values)
    parts = [(step, 0, width) for step in range(1, count)]
    ahead = stage(meta, assignment, arrays, parts[:1], False, 1)
    kv_out, *behind = stage(meta, assignment, arrays, parts[1:], True, STAGE_COST, after=ahead)
    arrived = [exchanged(ahead[0], "dp", 1)]
    kv_own = lax.all_to_all(kv_out, "dp", split_axis=0, concat_axis=0, tiled=True)
    behind, kv_own = lax.optimization_barrier((behind, kv_own))
    arrived += [exchanged(rows, "dp", step) for rows, (step, _, _) in zip(behind, parts[1:])]
    halos = [shifted(kv_own, ("blk", "uly"), back) for back in range(hops, 0, -1)]
    kv = jnp.concatenate([*halos, kv_own], axis=0)

    fixed = (doc_most, heads, meta, assignment, segment_ids)
    query, grad = (queries, lambda m, a: a[m[0]]), (grad_out, lambda m, a: a[m[0]])
    full, acc = attend(0, 0, kv_heads, *fixed, query, grad, kv, None, None, False)
    for both, (step, _, _) in zip(arrived, parts):
        query, grad = (both, lambda m, a: 0), (both, lambda m, a: 1)
        full, acc, *returned = attend(
            step, 0, kv_heads, *fixed, query, grad, kv, acc, full, step == count - 1
        )
    for back, halo in enumerate(returned, 1):
        acc = acc + shifted(halo, ("blk", "uly"), -back).astype(jnp.float32)
    total = acc.astype(jnp.bfloat16)
    return full[None], total[0][None], total[1][None]


def solution(mesh):
    in_specs = (
        P(None, ("blk", "uly", "dp"), None),
        P(None, ("blk", "uly", "dp"), None),
        P(None, ("blk", "uly", "dp"), None),
        P(None, ("blk", "uly", "dp"), None),
        P(),
        P(),
    )
    out_specs = (
        P("dp", ("blk", "uly"), None, None),
        P("dp", ("blk", "uly"), None),
        P("dp", ("blk", "uly"), None),
    )
    return jax.shard_map(shards, mesh=mesh, in_specs=in_specs, out_specs=out_specs, check_vma=False)
```

```python
import functools

import jax
import jax.numpy as jnp
from jax import lax
from jax.experimental import pallas as pl
from jax.experimental.pallas import tpu as pltpu
from jax.sharding import PartitionSpec as P

HD = 128
LOG2E = 1.4426950408889634
BIG_NEGATIVE = -1e30
VMEM_BYTES = 32 * 1024 * 1024
HEADS_STEP = 2


def target_of(index, step, count):
    return lax.rem(index + step, count)


def source_of(index, step, count):
    return lax.rem(index + count - step, count)


def exchanged(value, axis, step):
    count = lax.axis_size(axis)
    return lax.ppermute(value, axis, [(i, (i + step) % count) for i in range(count)])


def shifted(value, axis, by):
    length = lax.axis_size(axis)
    pairs = [(i, i + by) for i in range(length) if 0 <= i + by < length]
    return lax.ppermute(value, axis, pairs)


def stage_kernel(count, jobs, outs, meta_ref, assign_ref, *refs):
    group = meta_ref[0]
    sources, refs = refs[:4], refs[4:]
    out_refs, held_refs, (in_sems, out_sems) = refs[:outs], refs[outs : 2 * outs], refs[-2:]
    loads, stores = [], []
    for slot, (source, step, out, which) in enumerate(jobs):
        origin = sources[source].at[assign_ref[target_of(group, step, count)]]
        held, goal = held_refs[out].at[which], out_refs[out].at[which]
        loads.append(pltpu.make_async_copy(origin, held, in_sems.at[slot]))
        stores.append(pltpu.make_async_copy(held, goal, out_sems.at[slot]))
    for load in loads:
        load.start()
    for load, store in zip(loads, stores):
        load.wait()
        store.start()
    for store in stores:
        store.wait()


def stage(meta, assignment, queries, grad_out, keys, values):
    count, rows, _ = queries.shape
    shapes, jobs = [], []
    for first, steps in ((2, range(count)), (0, range(1, count))):
        width = (queries, grad_out, keys, values)[first].shape[2]
        for step in steps:
            jobs += [(first + which, step, len(shapes), which) for which in range(2)]
            shapes.append((2, rows, width))
    far, scalars = pl.BlockSpec(memory_space=pltpu.HBM), pl.BlockSpec(memory_space=pltpu.SMEM)
    staged = pl.pallas_call(
        functools.partial(stage_kernel, count, jobs, len(shapes)),
        out_shape=[jax.ShapeDtypeStruct(shape, queries.dtype) for shape in shapes],
        in_specs=[scalars] * 2 + [far] * 4,
        out_specs=[far] * len(shapes),
        scratch_shapes=[pltpu.VMEM(shape, queries.dtype) for shape in shapes]
        + [pltpu.SemaphoreType.DMA((len(jobs),))] * 2,
        name="stage",
    )(meta, assignment, queries, grad_out, keys, values)
    return staged[:count], staged[count:]


def build_bias(source, sequence, line, segment_ref, column_ref, bias_ref, rows, tok_dev, reach):
    keys, lanes = column_ref.shape
    pieces = keys // tok_dev
    window = bias_ref.shape[0]
    eye = lax.broadcasted_iota(jnp.int32, (tok_dev, tok_dev), 0) == lax.broadcasted_iota(
        jnp.int32, (tok_dev, tok_dev), 1
    )
    for place in range(pieces):
        back = pieces - 1 - place
        start = pl.multiple_of(jnp.maximum(line - back, 0) * tok_dev, tok_dev)
        every = segment_ref[:, pl.ds(start, tok_dev)].astype(jnp.float32)
        mine = lax.broadcasted_iota(jnp.int32, every.shape, 0) == sequence
        row = jnp.sum(jnp.where(mine, every, 0.0), axis=0, keepdims=True)
        column = jnp.sum(jnp.where(eye, row, 0.0), axis=1, keepdims=True)
        column = jnp.where(line >= back, column, -1.0)
        column_ref[place * tok_dev : (place + 1) * tok_dev, :] = jnp.broadcast_to(
            column, (tok_dev, lanes)
        )

    def token(shape):
        return lax.rem(lax.broadcasted_iota(jnp.int32, shape, 1), jnp.int32(rows))

    here = pl.multiple_of(keys - tok_dev + source * rows, rows)
    asked_rows = column_ref[pl.ds(here, rows), :]
    same = lax.broadcasted_iota(jnp.int32, (rows, lanes), 0) == token((rows, lanes))
    asked = jnp.sum(jnp.where(same, asked_rows, 0.0), axis=0, keepdims=True)
    held = column_ref[pl.ds(pl.multiple_of(here - reach, rows), window), :]
    place = lax.broadcasted_iota(jnp.int32, (window, lanes), 0)
    allowed = (held == asked) & (place <= token((window, lanes)) + reach)
    bias_ref[...] = jnp.where(allowed, 0.0, BIG_NEGATIVE)


def attend_kernel(
    step, first, filled, last, tok_dev, reach, ratio,
    meta_ref, assign_ref, segment_ref, query_ref, grad_ref, kv_ref, *refs,
):
    refs = list(refs)
    if not first:
        acc_in_ref = refs.pop(0)
    if filled:
        refs.pop(0)
    query_out_ref = refs.pop(0)
    column_ref, bias_ref = refs[-2 - last], refs[-1 - last]
    if last:
        own_ref, halo_refs, acc_ref = refs[0], refs[1:-3], refs[-1]
    else:
        acc_ref = refs[0]

    rows = query_ref.shape[0]
    window = bias_ref.shape[0]
    keys = column_ref.shape[0]
    scale = 1.0 / HD**0.5
    group = meta_ref[0]
    source = source_of(group, step, tok_dev // rows)
    block = (keys - tok_dev - reach) // rows + source
    span = pl.ds(pl.multiple_of(block * rows, rows), window)

    @pl.when(pl.program_id(0) == 0)
    def _():
        build_bias(
            source, assign_ref[group], meta_ref[1], segment_ref, column_ref, bias_ref, rows, tok_dev, reach
        )

    acc_ref[...] = jnp.zeros_like(acc_ref) if first else acc_in_ref[...]
    turned = (((1,), (1,)), ((), ()))
    grads = []
    for head in range(HEADS_STEP):
        lanes = slice(head * HD, (head + 1) * HD)

        def stacked(ref):
            start = head * ratio
            return jnp.concatenate(
                [ref[:, r * HD : (r + 1) * HD] for r in range(start, start + ratio)], axis=0
            )

        def windowed(which):
            return kv_ref[pl.ds(block, window // rows), which, :, lanes].reshape(window, HD)

        query, grad = stacked(query_ref), stacked(grad_ref)
        key, value = windowed(0), windowed(1)
        scores = lax.dot_general(key, query, turned, preferred_element_type=jnp.float32)
        scores = scores * (scale * LOG2E) + bias_ref[...]
        top = jnp.max(scores, axis=0, keepdims=True)
        weights = jnp.exp2(scores - top)
        probs = weights * (1.0 / jnp.sum(weights, axis=0, keepdims=True))
        grad_probs = lax.dot_general(value, grad, turned, preferred_element_type=jnp.float32)
        product = probs * grad_probs
        delta = jnp.sum(product, axis=0, keepdims=True)
        grad_scores = (product - probs * delta).astype(jnp.bfloat16)
        grad_value = jnp.dot(
            probs.astype(jnp.bfloat16), grad, preferred_element_type=jnp.float32
        )
        grad_key = jnp.dot(grad_scores, query, preferred_element_type=jnp.float32)
        grad_query = lax.dot_general(
            grad_scores, key, (((0,), (0,)), ((), ())), preferred_element_type=jnp.float32
        )
        grads.append((grad_query * scale).reshape(ratio, rows, HD))
        acc_ref[0, span, lanes] += grad_key
        acc_ref[1, span, lanes] += grad_value
    if last:
        own_ref[0] = acc_ref[0, keys - tok_dev :] * scale
        own_ref[1] = acc_ref[1, keys - tok_dev :]
        for back, halo_ref in enumerate(halo_refs, 1):
            part = slice(keys - (back + 1) * tok_dev, keys - back * tok_dev)
            halo_ref[0] = (acc_ref[0, part] * scale).astype(jnp.bfloat16)
            halo_ref[1] = acc_ref[1, part].astype(jnp.bfloat16)
    query_out_ref[...] = jnp.swapaxes(jnp.concatenate(grads, axis=0), 0, 1).astype(jnp.bfloat16)


def attend(step, base, span, reach, heads, meta, assignment, segments, query, grad, kv, acc, full, last):
    first, filled = acc is None, full is not None
    rows, (blocks, _, _, kv_width) = query[0].shape[1], kv.shape
    ratio = heads // (kv_width // HD)
    keys, tok_dev = blocks * rows, query[0].shape[1] * lax.axis_size("dp")
    pieces, window = keys // tok_dev, reach + rows
    lanes, place = HEADS_STEP * HD, base // HEADS_STEP

    def rows_spec(array, pick):
        start = place if array.shape[2] == heads * HD else 0
        return pl.BlockSpec(
            (None, rows, HEADS_STEP * ratio * HD), lambda c, m, a: (pick(m, a), 0, start + c)
        )

    in_specs = [
        pl.BlockSpec(segments.shape, lambda c, m, a: (0, 0)),
        rows_spec(*query),
        rows_spec(*grad),
    ]
    in_specs.append(pl.BlockSpec((blocks, 2, rows, lanes), lambda c, m, a: (0, 0, 0, place + c)))
    operands = [meta, assignment, segments, query[0], grad[0], kv]
    aliases = {}
    acc_spec = pl.BlockSpec((2, keys, lanes), lambda c, m, a: (0, 0, place + c))
    if not first:
        if not last:
            aliases[len(operands)] = 1
        operands.append(acc)
        in_specs.append(acc_spec)
    if filled:
        aliases[len(operands)] = 0
        operands.append(full)
        in_specs.append(pl.BlockSpec(memory_space=pl.ANY))
    out_shape = [jax.ShapeDtypeStruct((tok_dev, heads, HD), jnp.bfloat16)]
    out_specs = [
        pl.BlockSpec(
            (rows, HEADS_STEP * ratio, HD),
            lambda c, m, a: (source_of(m[0], step, tok_dev // rows), place + c, 0),
        )
    ]
    if last:
        span_spec = pl.BlockSpec((2, tok_dev, lanes), lambda c, m, a: (0, 0, c))
        out_shape.append(jax.ShapeDtypeStruct((2, tok_dev, span * HD), jnp.float32))
        out_shape += [jax.ShapeDtypeStruct((2, tok_dev, span * HD), jnp.bfloat16)] * (pieces - 1)
        out_specs += [span_spec] * pieces
    else:
        out_shape.append(jax.ShapeDtypeStruct((2, keys, kv_width), jnp.float32))
        out_specs.append(acc_spec)
    pairs = span * ratio * rows * window
    held = (keys, ratio * rows), (window, ratio * rows)
    held += ((2, keys, lanes),) * last
    return pl.pallas_call(
        functools.partial(attend_kernel, step, first, filled, last, tok_dev, reach, ratio),
        out_shape=out_shape,
        grid_spec=pltpu.PrefetchScalarGridSpec(
            num_scalar_prefetch=2,
            grid=(span // HEADS_STEP,),
            in_specs=in_specs,
            out_specs=out_specs,
            scratch_shapes=[pltpu.VMEM(shape, jnp.float32) for shape in held],
        ),
        input_output_aliases=aliases,
        compiler_params=pltpu.CompilerParams(
            dimension_semantics=("arbitrary",), vmem_limit_bytes=VMEM_BYTES
        ),
        cost_estimate=pl.CostEstimate(
            flops=pairs * HD, bytes_accessed=pairs, transcendentals=0
        ),
        name="attend",
    )(*operands)


def shards(queries, keys, values, grad_out, segment_ids, assignment):
    count = lax.axis_size("dp")
    uly = lax.axis_size("uly")
    group = lax.axis_index("dp")
    line = lax.axis_index("blk") * uly + lax.axis_index("uly")
    width, kv_width = queries.shape[2], keys.shape[2]
    heads, kv_heads = width // HD, kv_width // HD
    tok_dev = count * queries.shape[1]
    doc_most = min(512, tok_dev * uly)
    hops = -(-doc_most // tok_dev)
    meta = jnp.stack([group, line]).astype(jnp.int32)

    kv_staged, staged = stage(meta, assignment, queries, grad_out, keys, values)
    kv_arrived = [exchanged(kv_staged[step], "dp", step) for step in range(1, count)]
    staged, kv_arrived = lax.optimization_barrier((staged, kv_arrived))
    arrived = [exchanged(rows, "dp", step) for step, rows in enumerate(staged, 1)]
    kv_own = jnp.zeros((count, *kv_staged[0].shape), keys.dtype)
    for step, piece in enumerate([kv_staged[0], *kv_arrived]):
        kv_own = lax.dynamic_update_index_in_dim(
            kv_own, piece, source_of(group, step, count), 0
        )
    halos = [shifted(kv_own, ("blk", "uly"), back) for back in range(hops, 0, -1)]
    kv = jnp.concatenate([*halos, kv_own], axis=0)

    fixed = (doc_most, heads, meta, assignment, segment_ids)
    query, grad = (queries, lambda m, a: a[m[0]]), (grad_out, lambda m, a: a[m[0]])
    full, acc = attend(0, 0, kv_heads, *fixed, query, grad, kv, None, None, False)
    for step, both in enumerate(arrived, 1):
        query, grad = (both, lambda m, a: 0), (both, lambda m, a: 1)
        full, acc, *returned = attend(
            step, 0, kv_heads, *fixed, query, grad, kv, acc, full, step == count - 1
        )
    for back, halo in enumerate(returned, 1):
        acc = acc + shifted(halo, ("blk", "uly"), -back).astype(jnp.float32)
    total = acc.astype(jnp.bfloat16)
    return full[None], total[0][None], total[1][None]


def solution(mesh):
    in_specs = (
        P(None, ("blk", "uly", "dp"), None),
        P(None, ("blk", "uly", "dp"), None),
        P(None, ("blk", "uly", "dp"), None),
        P(None, ("blk", "uly", "dp"), None),
        P(),
        P(),
    )
    out_specs = (
        P("dp", ("blk", "uly"), None, None),
        P("dp", ("blk", "uly"), None),
        P("dp", ("blk", "uly"), None),
    )
    return jax.shard_map(shards, mesh=mesh, in_specs=in_specs, out_specs=out_specs, check_vma=False)
```

```python
import functools

import jax
import jax.numpy as jnp
from jax import lax
from jax.experimental import pallas as pl
from jax.experimental.pallas import tpu as pltpu
from jax.sharding import PartitionSpec as P

HD = 128
LOG2E = 1.4426950408889634
BIG_NEGATIVE = -1e30
VMEM_BYTES = 32 * 1024 * 1024
HEADS_STEP = 2


def target_of(index, step, count):
    return lax.rem(index + step, count)


def source_of(index, step, count):
    return lax.rem(index + count - step, count)


def exchanged(value, axis, step):
    count = lax.axis_size(axis)
    return lax.ppermute(value, axis, [(i, (i + step) % count) for i in range(count)])


def shifted(value, axis, by):
    length = lax.axis_size(axis)
    pairs = [(i, i + by) for i in range(length) if 0 <= i + by < length]
    return lax.ppermute(value, axis, pairs)


def stage_kernel(count, jobs, outs, meta_ref, assign_ref, first_ref, second_ref, *refs):
    group = meta_ref[0]
    out_refs, held_refs, (in_sems, out_sems) = refs[-2 - 2 * outs : -2 - outs], refs[-2 - outs : -2], refs[-2:]
    loads, stores = [], []
    for out, (step, start, width) in enumerate(jobs):
        chosen = assign_ref[target_of(group, step, count)]
        for which, source in enumerate((first_ref, second_ref)):
            origin = source.at[chosen, :, start : start + width]
            held, goal, slot = held_refs[out].at[which], out_refs[out].at[which], 2 * out + which
            loads.append(pltpu.make_async_copy(origin, held, in_sems.at[slot]))
            stores.append(pltpu.make_async_copy(held, goal, out_sems.at[slot]))
    for load in loads:
        load.start()
    for load, store in zip(loads, stores):
        load.wait()
        store.start()
    for store in stores:
        store.wait()


def stage(meta, assignment, first, second, jobs, after=()):
    count, rows, _ = first.shape
    shapes = [(2, rows, width) for _, _, width in jobs]
    far, scalars = pl.BlockSpec(memory_space=pltpu.HBM), pl.BlockSpec(memory_space=pltpu.SMEM)
    return pl.pallas_call(
        functools.partial(stage_kernel, count, jobs, len(shapes)),
        out_shape=[jax.ShapeDtypeStruct(shape, first.dtype) for shape in shapes],
        in_specs=[scalars] * 2 + [far] * 2 + [pl.BlockSpec(memory_space=pl.ANY)] * len(after),
        out_specs=[far] * len(shapes),
        scratch_shapes=[pltpu.VMEM(shape, first.dtype) for shape in shapes]
        + [pltpu.SemaphoreType.DMA((2 * len(shapes),))] * 2,
        name="stage",
    )(meta, assignment, first, second, *after)


def build_bias(source, sequence, line, segment_ref, column_ref, bias_ref, rows, tok_dev, reach):
    keys, lanes = column_ref.shape
    pieces = keys // tok_dev
    window = bias_ref.shape[0]
    eye = lax.broadcasted_iota(jnp.int32, (tok_dev, tok_dev), 0) == lax.broadcasted_iota(
        jnp.int32, (tok_dev, tok_dev), 1
    )
    for place in range(pieces):
        back = pieces - 1 - place
        start = pl.multiple_of(jnp.maximum(line - back, 0) * tok_dev, tok_dev)
        every = segment_ref[:, pl.ds(start, tok_dev)].astype(jnp.float32)
        mine = lax.broadcasted_iota(jnp.int32, every.shape, 0) == sequence
        row = jnp.sum(jnp.where(mine, every, 0.0), axis=0, keepdims=True)
        column = jnp.sum(jnp.where(eye, row, 0.0), axis=1, keepdims=True)
        column = jnp.where(line >= back, column, -1.0)
        column_ref[place * tok_dev : (place + 1) * tok_dev, :] = jnp.broadcast_to(
            column, (tok_dev, lanes)
        )

    def token(shape):
        return lax.rem(lax.broadcasted_iota(jnp.int32, shape, 1), jnp.int32(rows))

    here = pl.multiple_of(keys - tok_dev + source * rows, rows)
    asked_rows = column_ref[pl.ds(here, rows), :]
    same = lax.broadcasted_iota(jnp.int32, (rows, lanes), 0) == token((rows, lanes))
    asked = jnp.sum(jnp.where(same, asked_rows, 0.0), axis=0, keepdims=True)
    held = column_ref[pl.ds(pl.multiple_of(here - reach, rows), window), :]
    place = lax.broadcasted_iota(jnp.int32, (window, lanes), 0)
    allowed = (held == asked) & (place <= token((window, lanes)) + reach)
    bias_ref[...] = jnp.where(allowed, 0.0, BIG_NEGATIVE)


def attend_kernel(
    step, first, filled, last, tok_dev, reach, ratio,
    meta_ref, assign_ref, segment_ref, query_ref, grad_ref, kv_ref, *refs,
):
    refs = list(refs)
    if not first:
        acc_in_ref = refs.pop(0)
    if filled:
        refs.pop(0)
    query_out_ref = refs.pop(0)
    column_ref, bias_ref = refs[-2 - last], refs[-1 - last]
    if last:
        own_ref, halo_refs, acc_ref = refs[0], refs[1:-3], refs[-1]
    else:
        acc_ref = refs[0]

    rows = query_ref.shape[0]
    window = bias_ref.shape[0]
    keys = column_ref.shape[0]
    scale = 1.0 / HD**0.5
    group = meta_ref[0]
    source = source_of(group, step, tok_dev // rows)
    block = (keys - tok_dev - reach) // rows + source
    span = pl.ds(pl.multiple_of(block * rows, rows), window)

    @pl.when(pl.program_id(0) == 0)
    def _():
        build_bias(
            source, assign_ref[group], meta_ref[1], segment_ref, column_ref, bias_ref, rows, tok_dev, reach
        )

    acc_ref[...] = jnp.zeros_like(acc_ref) if first else acc_in_ref[...]
    turned = (((1,), (1,)), ((), ()))
    grads = []
    for head in range(HEADS_STEP):
        lanes = slice(head * HD, (head + 1) * HD)

        def stacked(ref):
            start = head * ratio
            return jnp.concatenate(
                [ref[:, r * HD : (r + 1) * HD] for r in range(start, start + ratio)], axis=0
            )

        def windowed(which):
            return kv_ref[pl.ds(block, window // rows), which, :, lanes].reshape(window, HD)

        query, grad = stacked(query_ref), stacked(grad_ref)
        key, value = windowed(0), windowed(1)
        scores = lax.dot_general(key, query, turned, preferred_element_type=jnp.float32)
        scores = scores * (scale * LOG2E) + bias_ref[...]
        top = jnp.max(scores, axis=0, keepdims=True)
        weights = jnp.exp2(scores - top)
        probs = weights * (1.0 / jnp.sum(weights, axis=0, keepdims=True))
        grad_probs = lax.dot_general(value, grad, turned, preferred_element_type=jnp.float32)
        product = probs * grad_probs
        delta = jnp.sum(product, axis=0, keepdims=True)
        grad_scores = (product - probs * delta).astype(jnp.bfloat16)
        grad_value = jnp.dot(
            probs.astype(jnp.bfloat16), grad, preferred_element_type=jnp.float32
        )
        grad_key = jnp.dot(grad_scores, query, preferred_element_type=jnp.float32)
        grad_query = lax.dot_general(
            grad_scores, key, (((0,), (0,)), ((), ())), preferred_element_type=jnp.float32
        )
        grads.append((grad_query * scale).reshape(ratio, rows, HD))
        acc_ref[0, span, lanes] += grad_key
        acc_ref[1, span, lanes] += grad_value
    if last:
        own_ref[0] = acc_ref[0, keys - tok_dev :] * scale
        own_ref[1] = acc_ref[1, keys - tok_dev :]
        for back, halo_ref in enumerate(halo_refs, 1):
            part = slice(keys - (back + 1) * tok_dev, keys - back * tok_dev)
            halo_ref[0] = (acc_ref[0, part] * scale).astype(jnp.bfloat16)
            halo_ref[1] = acc_ref[1, part].astype(jnp.bfloat16)
    query_out_ref[...] = jnp.swapaxes(jnp.concatenate(grads, axis=0), 0, 1).astype(jnp.bfloat16)


def attend(step, base, span, reach, heads, meta, assignment, segments, query, grad, kv, acc, full, last):
    first, filled = acc is None, full is not None
    rows, (blocks, _, _, kv_width) = query[0].shape[1], kv.shape
    ratio = heads // (kv_width // HD)
    keys, tok_dev = blocks * rows, query[0].shape[1] * lax.axis_size("dp")
    pieces, window = keys // tok_dev, reach + rows
    lanes, place = HEADS_STEP * HD, base // HEADS_STEP

    def rows_spec(array, pick):
        start = place if array.shape[2] == heads * HD else 0
        return pl.BlockSpec(
            (None, rows, HEADS_STEP * ratio * HD), lambda c, m, a: (pick(m, a), 0, start + c)
        )

    in_specs = [
        pl.BlockSpec(segments.shape, lambda c, m, a: (0, 0)),
        rows_spec(*query),
        rows_spec(*grad),
    ]
    in_specs.append(pl.BlockSpec((blocks, 2, rows, lanes), lambda c, m, a: (0, 0, 0, place + c)))
    operands = [meta, assignment, segments, query[0], grad[0], kv]
    aliases = {}
    acc_spec = pl.BlockSpec((2, keys, lanes), lambda c, m, a: (0, 0, place + c))
    if not first:
        if not last:
            aliases[len(operands)] = 1
        operands.append(acc)
        in_specs.append(acc_spec)
    if filled:
        aliases[len(operands)] = 0
        operands.append(full)
        in_specs.append(pl.BlockSpec(memory_space=pl.ANY))
    out_shape = [jax.ShapeDtypeStruct((tok_dev, heads, HD), jnp.bfloat16)]
    out_specs = [
        pl.BlockSpec(
            (rows, HEADS_STEP * ratio, HD),
            lambda c, m, a: (source_of(m[0], step, tok_dev // rows), place + c, 0),
        )
    ]
    if last:
        span_spec = pl.BlockSpec((2, tok_dev, lanes), lambda c, m, a: (0, 0, c))
        out_shape.append(jax.ShapeDtypeStruct((2, tok_dev, span * HD), jnp.float32))
        out_shape += [jax.ShapeDtypeStruct((2, tok_dev, span * HD), jnp.bfloat16)] * (pieces - 1)
        out_specs += [span_spec] * pieces
    else:
        out_shape.append(jax.ShapeDtypeStruct((2, keys, kv_width), jnp.float32))
        out_specs.append(acc_spec)
    pairs = span * ratio * rows * window
    held = (keys, ratio * rows), (window, ratio * rows)
    held += ((2, keys, lanes),) * last
    return pl.pallas_call(
        functools.partial(attend_kernel, step, first, filled, last, tok_dev, reach, ratio),
        out_shape=out_shape,
        grid_spec=pltpu.PrefetchScalarGridSpec(
            num_scalar_prefetch=2,
            grid=(span // HEADS_STEP,),
            in_specs=in_specs,
            out_specs=out_specs,
            scratch_shapes=[pltpu.VMEM(shape, jnp.float32) for shape in held],
        ),
        input_output_aliases=aliases,
        compiler_params=pltpu.CompilerParams(
            dimension_semantics=("arbitrary",), vmem_limit_bytes=VMEM_BYTES
        ),
        cost_estimate=pl.CostEstimate(
            flops=pairs * HD, bytes_accessed=pairs, transcendentals=0
        ),
        name="attend",
    )(*operands)


def shards(queries, keys, values, grad_out, segment_ids, assignment):
    count = lax.axis_size("dp")
    uly = lax.axis_size("uly")
    group = lax.axis_index("dp")
    line = lax.axis_index("blk") * uly + lax.axis_index("uly")
    width, kv_width = queries.shape[2], keys.shape[2]
    heads, kv_heads = width // HD, kv_width // HD
    tok_dev = count * queries.shape[1]
    doc_most = min(512, tok_dev * uly)
    hops = -(-doc_most // tok_dev)
    meta = jnp.stack([group, line]).astype(jnp.int32)

    final, halves = count - 1, kv_heads // HEADS_STEP
    part = width // halves
    kv_jobs = [(step, 0, kv_width) for step in range(count)]
    kv_staged = stage(meta, assignment, keys, values, kv_jobs)
    jobs = [(step, 0, width) for step in range(1, final)]
    jobs += [(final, half * part, part) for half in range(halves)]
    staged = stage(meta, assignment, queries, grad_out, jobs, after=kv_staged[:1])
    kv_arrived = [exchanged(kv_staged[step], "dp", step) for step in range(1, count)]
    staged, kv_arrived = lax.optimization_barrier((staged, kv_arrived))
    arrived = [exchanged(staged[step - 1], "dp", step) for step in range(1, final)]
    split = [exchanged(staged[final - 1], "dp", final)]
    kv_own = jnp.zeros((count, *kv_staged[0].shape), keys.dtype)
    for step, piece in enumerate([kv_staged[0], *kv_arrived]):
        kv_own = lax.dynamic_update_index_in_dim(
            kv_own, piece, source_of(group, step, count), 0
        )
    halos = [shifted(kv_own, ("blk", "uly"), back) for back in range(hops, 0, -1)]
    kv = jnp.concatenate([*halos, kv_own], axis=0)

    fixed = (doc_most, heads, meta, assignment, segment_ids)
    query, grad = (queries, lambda m, a: a[m[0]]), (grad_out, lambda m, a: a[m[0]])
    full, acc = attend(0, 0, kv_heads, *fixed, query, grad, kv, None, None, False)
    rows, acc = lax.optimization_barrier((staged[final], acc))
    split.append(exchanged(rows, "dp", final))
    for step in range(1, final):
        both = arrived[step - 1]
        query, grad = (both, lambda m, a: 0), (both, lambda m, a: 1)
        full, acc = attend(step, 0, kv_heads, *fixed, query, grad, kv, acc, full, False)
    totals, returned = [], []
    for half, both in enumerate(split):
        query, grad = (both, lambda m, a: 0), (both, lambda m, a: 1)
        full, total, *halos = attend(
            final, half * HEADS_STEP, HEADS_STEP, *fixed, query, grad, kv, acc, full, True
        )
        if half:
            halos, returned = lax.optimization_barrier((halos, returned))
        returned = [shifted(halo, ("blk", "uly"), -back) for back, halo in enumerate(halos, 1)]
        for halo in returned:
            total = total + halo.astype(jnp.float32)
        totals.append(total.astype(jnp.bfloat16))
    total = jnp.concatenate(totals, axis=2)
    return full[None], total[0][None], total[1][None]


def solution(mesh):
    in_specs = (
        P(None, ("blk", "uly", "dp"), None),
        P(None, ("blk", "uly", "dp"), None),
        P(None, ("blk", "uly", "dp"), None),
        P(None, ("blk", "uly", "dp"), None),
        P(),
        P(),
    )
    out_specs = (
        P("dp", ("blk", "uly"), None, None),
        P("dp", ("blk", "uly"), None),
        P("dp", ("blk", "uly"), None),
    )
    return jax.shard_map(shards, mesh=mesh, in_specs=in_specs, out_specs=out_specs, check_vma=False)
```

```python
import functools

import jax
import jax.numpy as jnp
from jax import lax
from jax.experimental import pallas as pl
from jax.experimental.pallas import tpu as pltpu
from jax.sharding import PartitionSpec as P

HD = 128
LOG2E = 1.4426950408889634
BIG_NEGATIVE = -1e30
VMEM_BYTES = 32 * 1024 * 1024
HEADS_STEP = 2


def target_of(index, step, count):
    return lax.rem(index + step, count)


def source_of(index, step, count):
    return lax.rem(index + count - step, count)


def exchanged(value, axis, step):
    count = lax.axis_size(axis)
    return lax.ppermute(value, axis, [(i, (i + step) % count) for i in range(count)])


def shifted(value, axis, by):
    length = lax.axis_size(axis)
    pairs = [(i, i + by) for i in range(length) if 0 <= i + by < length]
    return lax.ppermute(value, axis, pairs)


def stage_kernel(count, jobs, outs, meta_ref, assign_ref, first_ref, second_ref, *refs):
    group = meta_ref[0]
    out_refs, held_refs, (in_sems, out_sems) = refs[-2 - 2 * outs : -2 - outs], refs[-2 - outs : -2], refs[-2:]
    loads, stores = [], []
    for out, (step, start, width) in enumerate(jobs):
        chosen = assign_ref[target_of(group, step, count)]
        for which, source in enumerate((first_ref, second_ref)):
            origin = source.at[chosen, :, start : start + width]
            held, goal, slot = held_refs[out].at[which], out_refs[out].at[which], 2 * out + which
            loads.append(pltpu.make_async_copy(origin, held, in_sems.at[slot]))
            stores.append(pltpu.make_async_copy(held, goal, out_sems.at[slot]))
    for load in loads:
        load.start()
    for load, store in zip(loads, stores):
        load.wait()
        store.start()
    for store in stores:
        store.wait()


def stage(meta, assignment, first, second, jobs, after=()):
    count, rows, _ = first.shape
    shapes = [(2, rows, width) for _, _, width in jobs]
    far, scalars = pl.BlockSpec(memory_space=pltpu.HBM), pl.BlockSpec(memory_space=pltpu.SMEM)
    return pl.pallas_call(
        functools.partial(stage_kernel, count, jobs, len(shapes)),
        out_shape=[jax.ShapeDtypeStruct(shape, first.dtype) for shape in shapes],
        in_specs=[scalars] * 2 + [far] * 2 + [pl.BlockSpec(memory_space=pl.ANY)] * len(after),
        out_specs=[far] * len(shapes),
        scratch_shapes=[pltpu.VMEM(shape, first.dtype) for shape in shapes]
        + [pltpu.SemaphoreType.DMA((2 * len(shapes),))] * 2,
        name="stage",
    )(meta, assignment, first, second, *after)


def build_bias(source, sequence, line, segment_ref, column_ref, bias_ref, rows, tok_dev, reach):
    keys, lanes = column_ref.shape
    pieces = keys // tok_dev
    window = bias_ref.shape[0]
    eye = lax.broadcasted_iota(jnp.int32, (tok_dev, tok_dev), 0) == lax.broadcasted_iota(
        jnp.int32, (tok_dev, tok_dev), 1
    )
    for place in range(pieces):
        back = pieces - 1 - place
        start = pl.multiple_of(jnp.maximum(line - back, 0) * tok_dev, tok_dev)
        every = segment_ref[:, pl.ds(start, tok_dev)].astype(jnp.float32)
        mine = lax.broadcasted_iota(jnp.int32, every.shape, 0) == sequence
        row = jnp.sum(jnp.where(mine, every, 0.0), axis=0, keepdims=True)
        column = jnp.sum(jnp.where(eye, row, 0.0), axis=1, keepdims=True)
        column = jnp.where(line >= back, column, -1.0)
        column_ref[place * tok_dev : (place + 1) * tok_dev, :] = jnp.broadcast_to(
            column, (tok_dev, lanes)
        )

    def token(shape):
        return lax.rem(lax.broadcasted_iota(jnp.int32, shape, 1), jnp.int32(rows))

    here = pl.multiple_of(keys - tok_dev + source * rows, rows)
    asked_rows = column_ref[pl.ds(here, rows), :]
    same = lax.broadcasted_iota(jnp.int32, (rows, lanes), 0) == token((rows, lanes))
    asked = jnp.sum(jnp.where(same, asked_rows, 0.0), axis=0, keepdims=True)
    held = column_ref[pl.ds(pl.multiple_of(here - reach, rows), window), :]
    place = lax.broadcasted_iota(jnp.int32, (window, lanes), 0)
    allowed = (held == asked) & (place <= token((window, lanes)) + reach)
    bias_ref[...] = jnp.where(allowed, 0.0, BIG_NEGATIVE)


def attend_kernel(
    step, first, filled, last, tok_dev, reach, ratio,
    meta_ref, assign_ref, segment_ref, query_ref, grad_ref, kv_ref, *refs,
):
    refs = list(refs)
    if not first:
        acc_in_ref = refs.pop(0)
    if filled:
        refs.pop(0)
    query_out_ref = refs.pop(0)
    column_ref, bias_ref = refs[-2 - last], refs[-1 - last]
    if last:
        own_ref, halo_refs, acc_ref = refs[0], refs[1:-3], refs[-1]
    else:
        acc_ref = refs[0]

    rows = query_ref.shape[0]
    window = bias_ref.shape[0]
    keys = column_ref.shape[0]
    scale = 1.0 / HD**0.5
    group = meta_ref[0]
    source = source_of(group, step, tok_dev // rows)
    block = (keys - tok_dev - reach) // rows + source
    span = pl.ds(pl.multiple_of(block * rows, rows), window)

    @pl.when(pl.program_id(0) == 0)
    def _():
        build_bias(
            source, assign_ref[group], meta_ref[1], segment_ref, column_ref, bias_ref, rows, tok_dev, reach
        )

    acc_ref[...] = jnp.zeros_like(acc_ref) if first else acc_in_ref[...]
    turned = (((1,), (1,)), ((), ()))
    grads = []
    for head in range(HEADS_STEP):
        lanes = slice(head * HD, (head + 1) * HD)

        def stacked(ref):
            start = head * ratio
            return jnp.concatenate(
                [ref[:, r * HD : (r + 1) * HD] for r in range(start, start + ratio)], axis=0
            )

        def windowed(which):
            return kv_ref[pl.ds(block, window // rows), which, :, lanes].reshape(window, HD)

        query, grad = stacked(query_ref), stacked(grad_ref)
        key, value = windowed(0), windowed(1)
        scores = lax.dot_general(key, query, turned, preferred_element_type=jnp.float32)
        scores = scores * (scale * LOG2E) + bias_ref[...]
        top = jnp.max(scores, axis=0, keepdims=True)
        weights = jnp.exp2(scores - top)
        probs = weights * (1.0 / jnp.sum(weights, axis=0, keepdims=True))
        grad_probs = lax.dot_general(value, grad, turned, preferred_element_type=jnp.float32)
        product = probs * grad_probs
        delta = jnp.sum(product, axis=0, keepdims=True)
        grad_scores = (product - probs * delta).astype(jnp.bfloat16)
        grad_value = jnp.dot(
            probs.astype(jnp.bfloat16), grad, preferred_element_type=jnp.float32
        )
        grad_key = jnp.dot(grad_scores, query, preferred_element_type=jnp.float32)
        grad_query = lax.dot_general(
            grad_scores, key, (((0,), (0,)), ((), ())), preferred_element_type=jnp.float32
        )
        grads.append((grad_query * scale).reshape(ratio, rows, HD))
        acc_ref[0, span, lanes] += grad_key
        acc_ref[1, span, lanes] += grad_value
    if last:
        own_ref[0] = acc_ref[0, keys - tok_dev :] * scale
        own_ref[1] = acc_ref[1, keys - tok_dev :]
        for back, halo_ref in enumerate(halo_refs, 1):
            part = slice(keys - (back + 1) * tok_dev, keys - back * tok_dev)
            halo_ref[0] = (acc_ref[0, part] * scale).astype(jnp.bfloat16)
            halo_ref[1] = acc_ref[1, part].astype(jnp.bfloat16)
    query_out_ref[...] = jnp.swapaxes(jnp.concatenate(grads, axis=0), 0, 1).astype(jnp.bfloat16)


def attend(step, base, span, reach, heads, meta, assignment, segments, query, grad, kv, acc, full, last):
    first, filled = acc is None, full is not None
    rows, (blocks, _, _, kv_width) = query[0].shape[1], kv.shape
    ratio = heads // (kv_width // HD)
    keys, tok_dev = blocks * rows, query[0].shape[1] * lax.axis_size("dp")
    pieces, window = keys // tok_dev, reach + rows
    lanes, place = HEADS_STEP * HD, base // HEADS_STEP

    def rows_spec(array, pick):
        start = place if array.shape[2] == heads * HD else 0
        return pl.BlockSpec(
            (None, rows, HEADS_STEP * ratio * HD), lambda c, m, a: (pick(m, a), 0, start + c)
        )

    in_specs = [
        pl.BlockSpec(segments.shape, lambda c, m, a: (0, 0)),
        rows_spec(*query),
        rows_spec(*grad),
    ]
    in_specs.append(pl.BlockSpec((blocks, 2, rows, lanes), lambda c, m, a: (0, 0, 0, place + c)))
    operands = [meta, assignment, segments, query[0], grad[0], kv]
    aliases = {}
    acc_spec = pl.BlockSpec((2, keys, lanes), lambda c, m, a: (0, 0, place + c))
    if not first:
        if not last:
            aliases[len(operands)] = 1
        operands.append(acc)
        in_specs.append(acc_spec)
    if filled:
        aliases[len(operands)] = 0
        operands.append(full)
        in_specs.append(pl.BlockSpec(memory_space=pl.ANY))
    out_shape = [jax.ShapeDtypeStruct((tok_dev, heads, HD), jnp.bfloat16)]
    out_specs = [
        pl.BlockSpec(
            (rows, HEADS_STEP * ratio, HD),
            lambda c, m, a: (source_of(m[0], step, tok_dev // rows), place + c, 0),
        )
    ]
    if last:
        span_spec = pl.BlockSpec((2, tok_dev, lanes), lambda c, m, a: (0, 0, c))
        out_shape.append(jax.ShapeDtypeStruct((2, tok_dev, span * HD), jnp.float32))
        out_shape += [jax.ShapeDtypeStruct((2, tok_dev, span * HD), jnp.bfloat16)] * (pieces - 1)
        out_specs += [span_spec] * pieces
    else:
        out_shape.append(jax.ShapeDtypeStruct((2, keys, kv_width), jnp.float32))
        out_specs.append(acc_spec)
    pairs = span * ratio * rows * window
    held = (keys, ratio * rows), (window, ratio * rows)
    held += ((2, keys, lanes),) * last
    return pl.pallas_call(
        functools.partial(attend_kernel, step, first, filled, last, tok_dev, reach, ratio),
        out_shape=out_shape,
        grid_spec=pltpu.PrefetchScalarGridSpec(
            num_scalar_prefetch=2,
            grid=(span // HEADS_STEP,),
            in_specs=in_specs,
            out_specs=out_specs,
            scratch_shapes=[pltpu.VMEM(shape, jnp.float32) for shape in held],
        ),
        input_output_aliases=aliases,
        compiler_params=pltpu.CompilerParams(
            dimension_semantics=("arbitrary",), vmem_limit_bytes=VMEM_BYTES
        ),
        cost_estimate=pl.CostEstimate(
            flops=pairs * HD, bytes_accessed=pairs, transcendentals=0
        ),
        name="attend",
    )(*operands)


def shards(queries, keys, values, grad_out, segment_ids, assignment):
    count = lax.axis_size("dp")
    uly = lax.axis_size("uly")
    group = lax.axis_index("dp")
    line = lax.axis_index("blk") * uly + lax.axis_index("uly")
    width, kv_width = queries.shape[2], keys.shape[2]
    heads, kv_heads = width // HD, kv_width // HD
    tok_dev = count * queries.shape[1]
    doc_most = min(512, tok_dev * uly)
    hops = -(-doc_most // tok_dev)
    meta = jnp.stack([group, line]).astype(jnp.int32)

    final, halves = count // 2, kv_heads // HEADS_STEP
    part = width // halves
    others = [step for step in range(1, count) if step != final]
    kv_jobs = [(step, 0, kv_width) for step in range(count)]
    kv_staged = stage(meta, assignment, keys, values, kv_jobs)
    jobs = [(step, 0, width) for step in others]
    jobs += [(final, half * part, part) for half in range(halves)]
    staged = stage(meta, assignment, queries, grad_out, jobs, after=kv_staged[:1])
    kv_arrived = [exchanged(kv_staged[step], "dp", step) for step in range(1, count)]
    staged, kv_arrived = lax.optimization_barrier((staged, kv_arrived))
    arrived = [exchanged(rows, "dp", step) for rows, step in zip(staged, others)]
    held = staged[len(others) :]
    kv_own = jnp.zeros((count, *kv_staged[0].shape), keys.dtype)
    for step, piece in enumerate([kv_staged[0], *kv_arrived]):
        kv_own = lax.dynamic_update_index_in_dim(
            kv_own, piece, source_of(group, step, count), 0
        )
    halos = [shifted(kv_own, ("blk", "uly"), back) for back in range(hops, 0, -1)]
    kv = jnp.concatenate([*halos, kv_own], axis=0)

    fixed = (doc_most, heads, meta, assignment, segment_ids)
    query, grad = (queries, lambda m, a: a[m[0]]), (grad_out, lambda m, a: a[m[0]])
    full, acc = attend(0, 0, kv_heads, *fixed, query, grad, kv, None, None, False)
    rows, acc = lax.optimization_barrier((held[0], acc))
    split = [exchanged(rows, "dp", final)]
    for step, both in zip(others, arrived):
        query, grad = (both, lambda m, a: 0), (both, lambda m, a: 1)
        full, acc = attend(step, 0, kv_heads, *fixed, query, grad, kv, acc, full, False)
    for rows in held[1:]:
        rows, acc = lax.optimization_barrier((rows, acc))
        split.append(exchanged(rows, "dp", final))
    totals, returned = [], []
    for half, both in enumerate(split):
        query, grad = (both, lambda m, a: 0), (both, lambda m, a: 1)
        full, total, *halos = attend(
            final, half * HEADS_STEP, HEADS_STEP, *fixed, query, grad, kv, acc, full, True
        )
        if half:
            halos, returned = lax.optimization_barrier((halos, returned))
        returned = [shifted(halo, ("blk", "uly"), -back) for back, halo in enumerate(halos, 1)]
        for halo in returned:
            total = total + halo.astype(jnp.float32)
        totals.append(total.astype(jnp.bfloat16))
    total = jnp.concatenate(totals, axis=2)
    return full[None], total[0][None], total[1][None]


def solution(mesh):
    in_specs = (
        P(None, ("blk", "uly", "dp"), None),
        P(None, ("blk", "uly", "dp"), None),
        P(None, ("blk", "uly", "dp"), None),
        P(None, ("blk", "uly", "dp"), None),
        P(),
        P(),
    )
    out_specs = (
        P("dp", ("blk", "uly"), None, None),
        P("dp", ("blk", "uly"), None),
        P("dp", ("blk", "uly"), None),
    )
    return jax.shard_map(shards, mesh=mesh, in_specs=in_specs, out_specs=out_specs, check_vma=False)
```

```python
import functools

import jax
import jax.numpy as jnp
from jax import lax
from jax.experimental import pallas as pl
from jax.experimental.pallas import tpu as pltpu
from jax.sharding import PartitionSpec as P

HD = 128
LOG2E = 1.4426950408889634
BIG_NEGATIVE = -1e30
VMEM_BYTES = 32 * 1024 * 1024
HEADS_STEP = 2


def target_of(index, step, count):
    return lax.rem(index + step, count)


def source_of(index, step, count):
    return lax.rem(index + count - step, count)


def exchanged(value, axis, step):
    count = lax.axis_size(axis)
    return lax.ppermute(value, axis, [(i, (i + step) % count) for i in range(count)])


def shifted(value, axis, by):
    length = lax.axis_size(axis)
    pairs = [(i, i + by) for i in range(length) if 0 <= i + by < length]
    return lax.ppermute(value, axis, pairs)


def stage_kernel(count, jobs, outs, assign_ref, *refs):
    group = lax.axis_index("dp")
    sources, refs = refs[:4], refs[4:]
    out_refs, held_refs, (in_sems, out_sems) = refs[:outs], refs[outs : 2 * outs], refs[-2:]
    loads, stores = [], []
    for out, (first, step, start, width) in enumerate(jobs):
        chosen = assign_ref[target_of(group, step, count)]
        goal = out_refs[out] if step else out_refs[out].at[group]
        for which in range(2):
            origin = sources[first + which].at[chosen, :, start : start + width]
            held, slot = held_refs[out].at[which], 2 * out + which
            loads.append(pltpu.make_async_copy(origin, held, in_sems.at[slot]))
            stores.append(pltpu.make_async_copy(held, goal.at[which], out_sems.at[slot]))
    for load in loads:
        load.start()
    for load, store in zip(loads, stores):
        load.wait()
        store.start()
    for store in stores:
        store.wait()


def stage(assignment, arrays, jobs):
    count, rows, _ = arrays[0].shape
    held = [(2, rows, width) for _, _, _, width in jobs]
    shapes = [shape if job[1] else (count, *shape) for shape, job in zip(held, jobs)]
    kind = arrays[0].dtype
    far = pl.BlockSpec(memory_space=pltpu.HBM)
    return pl.pallas_call(
        functools.partial(stage_kernel, count, jobs, len(jobs)),
        out_shape=[jax.ShapeDtypeStruct(shape, kind) for shape in shapes],
        in_specs=[pl.BlockSpec(memory_space=pltpu.SMEM)] + [far] * len(arrays),
        out_specs=[far] * len(jobs),
        scratch_shapes=[pltpu.VMEM(shape, kind) for shape in held]
        + [pltpu.SemaphoreType.DMA((2 * len(jobs),))] * 2,
        name="stage",
    )(assignment, *arrays)


def build_bias(source, sequence, line, segment_ref, column_ref, bias_ref, rows, tok_dev, reach):
    keys, lanes = column_ref.shape
    pieces = keys // tok_dev
    window = bias_ref.shape[0]
    eye = lax.broadcasted_iota(jnp.int32, (tok_dev, tok_dev), 0) == lax.broadcasted_iota(
        jnp.int32, (tok_dev, tok_dev), 1
    )
    for place in range(pieces):
        back = pieces - 1 - place
        start = pl.multiple_of(jnp.maximum(line - back, 0) * tok_dev, tok_dev)
        every = segment_ref[:, pl.ds(start, tok_dev)].astype(jnp.float32)
        mine = lax.broadcasted_iota(jnp.int32, every.shape, 0) == sequence
        row = jnp.sum(jnp.where(mine, every, 0.0), axis=0, keepdims=True)
        column = jnp.sum(jnp.where(eye, row, 0.0), axis=1, keepdims=True)
        column = jnp.where(line >= back, column, -1.0)
        column_ref[place * tok_dev : (place + 1) * tok_dev, :] = jnp.broadcast_to(
            column, (tok_dev, lanes)
        )

    def token(shape):
        return lax.rem(lax.broadcasted_iota(jnp.int32, shape, 1), jnp.int32(rows))

    here = pl.multiple_of(keys - tok_dev + source * rows, rows)
    asked_rows = column_ref[pl.ds(here, rows), :]
    same = lax.broadcasted_iota(jnp.int32, (rows, lanes), 0) == token((rows, lanes))
    asked = jnp.sum(jnp.where(same, asked_rows, 0.0), axis=0, keepdims=True)
    held = column_ref[pl.ds(pl.multiple_of(here - reach, rows), window), :]
    place = lax.broadcasted_iota(jnp.int32, (window, lanes), 0)
    allowed = (held == asked) & (place <= token((window, lanes)) + reach)
    bias_ref[...] = jnp.where(allowed, 0.0, BIG_NEGATIVE)


def attend_kernel(
    step, first, filled, last, tok_dev, reach, ratio,
    meta_ref, assign_ref, segment_ref, query_ref, grad_ref, kv_ref, *refs,
):
    refs = list(refs)
    if not first:
        acc_in_ref = refs.pop(0)
    if filled:
        refs.pop(0)
    query_out_ref = refs.pop(0)
    column_ref, bias_ref = refs[-2 - last], refs[-1 - last]
    if last:
        own_ref, halo_refs, acc_ref = refs[0], refs[1:-3], refs[-1]
    else:
        acc_ref = refs[0]

    rows = query_ref.shape[0]
    window = bias_ref.shape[0]
    keys = column_ref.shape[0]
    scale = 1.0 / HD**0.5
    group = meta_ref[0]
    source = source_of(group, step, tok_dev // rows)
    block = (keys - tok_dev - reach) // rows + source
    span = pl.ds(pl.multiple_of(block * rows, rows), window)

    @pl.when(pl.program_id(0) == 0)
    def _():
        build_bias(
            source, assign_ref[group], meta_ref[1], segment_ref, column_ref, bias_ref, rows, tok_dev, reach
        )

    acc_ref[...] = jnp.zeros_like(acc_ref) if first else acc_in_ref[...]
    turned = (((1,), (1,)), ((), ()))
    grads = []
    for head in range(HEADS_STEP):
        lanes = slice(head * HD, (head + 1) * HD)

        def stacked(ref):
            start = head * ratio
            return jnp.concatenate(
                [ref[:, r * HD : (r + 1) * HD] for r in range(start, start + ratio)], axis=0
            )

        def windowed(which):
            return kv_ref[pl.ds(block, window // rows), which, :, lanes].reshape(window, HD)

        query, grad = stacked(query_ref), stacked(grad_ref)
        key, value = windowed(0), windowed(1)
        scores = lax.dot_general(key, query, turned, preferred_element_type=jnp.float32)
        scores = scores * (scale * LOG2E) + bias_ref[...]
        top = jnp.max(scores, axis=0, keepdims=True)
        weights = jnp.exp2(scores - top)
        probs = weights * (1.0 / jnp.sum(weights, axis=0, keepdims=True))
        grad_probs = lax.dot_general(value, grad, turned, preferred_element_type=jnp.float32)
        product = probs * grad_probs
        delta = jnp.sum(product, axis=0, keepdims=True)
        grad_scores = (product - probs * delta).astype(jnp.bfloat16)
        grad_value = jnp.dot(
            probs.astype(jnp.bfloat16), grad, preferred_element_type=jnp.float32
        )
        grad_key = jnp.dot(grad_scores, query, preferred_element_type=jnp.float32)
        grad_query = lax.dot_general(
            grad_scores, key, (((0,), (0,)), ((), ())), preferred_element_type=jnp.float32
        )
        grads.append((grad_query * scale).reshape(ratio, rows, HD))
        acc_ref[0, span, lanes] += grad_key
        acc_ref[1, span, lanes] += grad_value
    if last:
        own_ref[0] = acc_ref[0, keys - tok_dev :] * scale
        own_ref[1] = acc_ref[1, keys - tok_dev :]
        for back, halo_ref in enumerate(halo_refs, 1):
            part = slice(keys - (back + 1) * tok_dev, keys - back * tok_dev)
            halo_ref[0] = (acc_ref[0, part] * scale).astype(jnp.bfloat16)
            halo_ref[1] = acc_ref[1, part].astype(jnp.bfloat16)
    query_out_ref[...] = jnp.swapaxes(jnp.concatenate(grads, axis=0), 0, 1).astype(jnp.bfloat16)


def attend(step, base, span, reach, heads, meta, assignment, segments, query, grad, kv, acc, full, last):
    first, filled = acc is None, full is not None
    rows, (blocks, _, _, kv_width) = query[0].shape[1], kv.shape
    ratio = heads // (kv_width // HD)
    keys, tok_dev = blocks * rows, query[0].shape[1] * lax.axis_size("dp")
    pieces, window = keys // tok_dev, reach + rows
    lanes, place = HEADS_STEP * HD, base // HEADS_STEP

    def rows_spec(array, pick):
        start = place if array.shape[2] == heads * HD else 0
        return pl.BlockSpec(
            (None, rows, HEADS_STEP * ratio * HD), lambda c, m, a: (pick(m, a), 0, start + c)
        )

    in_specs = [
        pl.BlockSpec(segments.shape, lambda c, m, a: (0, 0)),
        rows_spec(*query),
        rows_spec(*grad),
    ]
    in_specs.append(pl.BlockSpec((blocks, 2, rows, lanes), lambda c, m, a: (0, 0, 0, place + c)))
    operands = [meta, assignment, segments, query[0], grad[0], kv]
    aliases = {}
    acc_spec = pl.BlockSpec((2, keys, lanes), lambda c, m, a: (0, 0, c))
    if not first:
        if not last:
            aliases[len(operands)] = 1
        operands.append(acc)
        in_specs.append(acc_spec)
    if filled:
        aliases[len(operands)] = 0
        operands.append(full)
        in_specs.append(pl.BlockSpec(memory_space=pl.ANY))
    out_shape = [jax.ShapeDtypeStruct((tok_dev, heads, HD), jnp.bfloat16)]
    out_specs = [
        pl.BlockSpec(
            (rows, HEADS_STEP * ratio, HD),
            lambda c, m, a: (source_of(m[0], step, tok_dev // rows), place + c, 0),
        )
    ]
    if last:
        span_spec = pl.BlockSpec((2, tok_dev, lanes), lambda c, m, a: (0, 0, c))
        out_shape.append(jax.ShapeDtypeStruct((2, tok_dev, span * HD), jnp.float32))
        out_shape += [jax.ShapeDtypeStruct((2, tok_dev, span * HD), jnp.bfloat16)] * (pieces - 1)
        out_specs += [span_spec] * pieces
    else:
        out_shape.append(jax.ShapeDtypeStruct((2, keys, span * HD), jnp.float32))
        out_specs.append(acc_spec)
    pairs = span * ratio * rows * window
    held = (keys, ratio * rows), (window, ratio * rows)
    held += ((2, keys, lanes),) * last
    return pl.pallas_call(
        functools.partial(attend_kernel, step, first, filled, last, tok_dev, reach, ratio),
        out_shape=out_shape,
        grid_spec=pltpu.PrefetchScalarGridSpec(
            num_scalar_prefetch=2,
            grid=(span // HEADS_STEP,),
            in_specs=in_specs,
            out_specs=out_specs,
            scratch_shapes=[pltpu.VMEM(shape, jnp.float32) for shape in held],
        ),
        input_output_aliases=aliases,
        compiler_params=pltpu.CompilerParams(
            dimension_semantics=("arbitrary",), vmem_limit_bytes=VMEM_BYTES
        ),
        cost_estimate=pl.CostEstimate(
            flops=pairs * HD, bytes_accessed=pairs, transcendentals=0
        ),
        name="attend",
    )(*operands)


def shards(queries, keys, values, grad_out, segment_ids, assignment):
    count = lax.axis_size("dp")
    uly = lax.axis_size("uly")
    group = lax.axis_index("dp")
    line = lax.axis_index("blk") * uly + lax.axis_index("uly")
    width, kv_width = queries.shape[2], keys.shape[2]
    heads, kv_heads = width // HD, kv_width // HD
    tok_dev = count * queries.shape[1]
    doc_most = min(512, tok_dev * uly)
    hops = -(-doc_most // tok_dev)
    meta = jnp.stack([group, line]).astype(jnp.int32)

    final, halves = count // 2, kv_heads // HEADS_STEP
    part = width // halves
    others = [step for step in range(1, count) if step != final]
    jobs = [(2, step, 0, kv_width) for step in range(count)]
    order = [*others[1:], final]
    jobs.append((0, others[0], 0, width))
    jobs += [(0, step, half * part, part) for half in range(halves) for step in order]
    kv_own, *staged = stage(assignment, (queries, grad_out, keys, values), jobs)
    kv_arrived = [exchanged(staged[step - 1], "dp", step) for step in range(1, count)]
    ahead, behind = staged[count - 1 : count + len(order)], staged[count + len(order) :]
    ahead, kv_arrived = lax.optimization_barrier((ahead, kv_arrived))
    whole = exchanged(ahead[0], "dp", others[0])
    arrived = [[exchanged(rows, "dp", step) for rows, step in zip(ahead[1:], order)]]
    for step, piece in enumerate(kv_arrived, 1):
        kv_own = lax.dynamic_update_index_in_dim(
            kv_own, piece, source_of(group, step, count), 0
        )
    halos = [shifted(kv_own, ("blk", "uly"), back) for back in range(hops, 0, -1)]
    kv = jnp.concatenate([*halos, kv_own], axis=0)

    fixed = (doc_most, heads, meta, assignment, segment_ids)
    own = (queries, lambda m, a: a[m[0]]), (grad_out, lambda m, a: a[m[0]])
    first = (whole, lambda m, a: 0), (whole, lambda m, a: 1)
    accs, full, totals, returned = [], None, [], []
    for half in range(halves):
        base = half * HEADS_STEP
        full, acc = attend(0, base, HEADS_STEP, *fixed, *own, kv, None, full, False)
        if not half:
            behind, acc = lax.optimization_barrier((behind, acc))
        accs.append(acc)
    for half in range(halves):
        base = half * HEADS_STEP
        full, accs[half] = attend(
            others[0], base, HEADS_STEP, *fixed, *first, kv, accs[half], full, False
        )
    for half in range(halves):
        base = half * HEADS_STEP
        if half:
            rows, full = lax.optimization_barrier((behind[half * len(order) - 1], full))
            arrived[half].append(exchanged(rows, "dp", final))
        if half + 1 < halves:
            rows = behind[half * len(order) : (half + 1) * len(order) - 1]
            arrived.append([exchanged(piece, "dp", step) for piece, step in zip(rows, order)])
        for both, step in zip(arrived[half], order):
            pair = (both, lambda m, a: 0), (both, lambda m, a: 1)
            full, accs[half], *halos = attend(
                step, base, HEADS_STEP, *fixed, *pair, kv, accs[half], full, step == final
            )
        if half:
            halos, returned = lax.optimization_barrier((halos, returned))
        returned = [shifted(halo, ("blk", "uly"), -back) for back, halo in enumerate(halos, 1)]
        total = accs[half]
        for halo in returned:
            total = total + halo.astype(jnp.float32)
        totals.append(total.astype(jnp.bfloat16))
    total = jnp.concatenate(totals, axis=2)
    return full[None], total[0][None], total[1][None]


def solution(mesh):
    in_specs = (
        P(None, ("blk", "uly", "dp"), None),
        P(None, ("blk", "uly", "dp"), None),
        P(None, ("blk", "uly", "dp"), None),
        P(None, ("blk", "uly", "dp"), None),
        P(),
        P(),
    )
    out_specs = (
        P("dp", ("blk", "uly"), None, None),
        P("dp", ("blk", "uly"), None),
        P("dp", ("blk", "uly"), None),
    )
    return jax.shard_map(shards, mesh=mesh, in_specs=in_specs, out_specs=out_specs, check_vma=False)
```

```python
import functools

import jax
import jax.numpy as jnp
from jax import lax
from jax.experimental import pallas as pl
from jax.experimental.pallas import tpu as pltpu
from jax.sharding import PartitionSpec as P

HD = 128
LOG2E = 1.4426950408889634
BIG_NEGATIVE = -1e30
VMEM_BYTES = 32 * 1024 * 1024
HEADS_STEP = 2


def target_of(index, step, count):
    return lax.rem(index + step, count)


def source_of(index, step, count):
    return lax.rem(index + count - step, count)


def exchanged(value, axis, step):
    count = lax.axis_size(axis)
    return lax.ppermute(value, axis, [(i, (i + step) % count) for i in range(count)])


def shifted(value, axis, by):
    length = lax.axis_size(axis)
    pairs = [(i, i + by) for i in range(length) if 0 <= i + by < length]
    return lax.ppermute(value, axis, pairs)


def stage_kernel(count, jobs, outs, assign_ref, *refs):
    group = lax.axis_index("dp")
    sources, refs = refs[:4], refs[4:]
    out_refs, held_refs, (in_sems, out_sems) = refs[:outs], refs[outs : 2 * outs], refs[-2:]
    loads, stores = [], []
    for out, (first, step, start, width) in enumerate(jobs):
        chosen = assign_ref[target_of(group, step, count)]
        for which in range(2):
            origin = sources[first + which].at[chosen, :, start : start + width]
            held, slot = held_refs[out].at[which], 2 * out + which
            loads.append(pltpu.make_async_copy(origin, held, in_sems.at[slot]))
            stores.append(pltpu.make_async_copy(held, out_refs[out].at[which], out_sems.at[slot]))
    for load in loads:
        load.start()
    for load, store in zip(loads, stores):
        load.wait()
        store.start()
    for store in stores:
        store.wait()


def stage(assignment, arrays, jobs):
    count, rows, _ = arrays[0].shape
    shapes = [(2, rows, width) for _, _, _, width in jobs]
    kind = arrays[0].dtype
    far = pl.BlockSpec(memory_space=pltpu.HBM)
    return pl.pallas_call(
        functools.partial(stage_kernel, count, jobs, len(jobs)),
        out_shape=[jax.ShapeDtypeStruct(shape, kind) for shape in shapes],
        in_specs=[pl.BlockSpec(memory_space=pltpu.SMEM)] + [far] * len(arrays),
        out_specs=[far] * len(jobs),
        scratch_shapes=[pltpu.VMEM(shape, kind) for shape in shapes]
        + [pltpu.SemaphoreType.DMA((2 * len(jobs),))] * 2,
        name="stage",
    )(assignment, *arrays)


def build_bias(source, sequence, line, segment_ref, column_ref, bias_ref, rows, tok_dev, reach):
    keys, lanes = column_ref.shape
    pieces = keys // tok_dev
    window = bias_ref.shape[0]
    eye = lax.broadcasted_iota(jnp.int32, (tok_dev, tok_dev), 0) == lax.broadcasted_iota(
        jnp.int32, (tok_dev, tok_dev), 1
    )
    for place in range(pieces):
        back = pieces - 1 - place
        start = pl.multiple_of(jnp.maximum(line - back, 0) * tok_dev, tok_dev)
        every = segment_ref[:, pl.ds(start, tok_dev)].astype(jnp.float32)
        mine = lax.broadcasted_iota(jnp.int32, every.shape, 0) == sequence
        row = jnp.sum(jnp.where(mine, every, 0.0), axis=0, keepdims=True)
        column = jnp.sum(jnp.where(eye, row, 0.0), axis=1, keepdims=True)
        column = jnp.where(line >= back, column, -1.0)
        column_ref[place * tok_dev : (place + 1) * tok_dev, :] = jnp.broadcast_to(
            column, (tok_dev, lanes)
        )

    def token(shape):
        return lax.rem(lax.broadcasted_iota(jnp.int32, shape, 1), jnp.int32(rows))

    here = pl.multiple_of(keys - tok_dev + source * rows, rows)
    asked_rows = column_ref[pl.ds(here, rows), :]
    same = lax.broadcasted_iota(jnp.int32, (rows, lanes), 0) == token((rows, lanes))
    asked = jnp.sum(jnp.where(same, asked_rows, 0.0), axis=0, keepdims=True)
    held = column_ref[pl.ds(pl.multiple_of(here - reach, rows), window), :]
    place = lax.broadcasted_iota(jnp.int32, (window, lanes), 0)
    allowed = (held == asked) & (place <= token((window, lanes)) + reach)
    bias_ref[...] = jnp.where(allowed, 0.0, BIG_NEGATIVE)


def attend_kernel(
    step, first, filled, last, tok_dev, reach, ratio,
    meta_ref, assign_ref, segment_ref, query_ref, grad_ref, kv_ref, *refs,
):
    refs = list(refs)
    if not first:
        acc_in_ref = refs.pop(0)
    if filled:
        refs.pop(0)
    query_out_ref = refs.pop(0)
    column_ref, bias_ref = refs[-2 - last], refs[-1 - last]
    if last:
        own_ref, halo_refs, acc_ref = refs[0], refs[1:-3], refs[-1]
    else:
        acc_ref = refs[0]

    rows = query_ref.shape[0]
    window = bias_ref.shape[0]
    keys = column_ref.shape[0]
    scale = 1.0 / HD**0.5
    group = meta_ref[0]
    source = source_of(group, step, tok_dev // rows)
    block = (keys - tok_dev - reach) // rows + source
    span = pl.ds(pl.multiple_of(block * rows, rows), window)

    @pl.when(pl.program_id(0) == 0)
    def _():
        build_bias(
            source, assign_ref[group], meta_ref[1], segment_ref, column_ref, bias_ref, rows, tok_dev, reach
        )

    acc_ref[...] = jnp.zeros_like(acc_ref) if first else acc_in_ref[...]
    turned = (((1,), (1,)), ((), ()))
    grads = []
    for head in range(HEADS_STEP):
        lanes = slice(head * HD, (head + 1) * HD)

        def stacked(ref):
            start = head * ratio
            return jnp.concatenate(
                [ref[:, r * HD : (r + 1) * HD] for r in range(start, start + ratio)], axis=0
            )

        def windowed(which):
            return kv_ref[pl.ds(block, window // rows), which, :, lanes].reshape(window, HD)

        query, grad = stacked(query_ref), stacked(grad_ref)
        key, value = windowed(0), windowed(1)
        scores = lax.dot_general(key, query, turned, preferred_element_type=jnp.float32)
        scores = scores * (scale * LOG2E) + bias_ref[...]
        top = jnp.max(scores, axis=0, keepdims=True)
        weights = jnp.exp2(scores - top)
        probs = weights * (1.0 / jnp.sum(weights, axis=0, keepdims=True))
        grad_probs = lax.dot_general(value, grad, turned, preferred_element_type=jnp.float32)
        product = probs * grad_probs
        delta = jnp.sum(product, axis=0, keepdims=True)
        grad_scores = (product - probs * delta).astype(jnp.bfloat16)
        grad_value = jnp.dot(
            probs.astype(jnp.bfloat16), grad, preferred_element_type=jnp.float32
        )
        grad_key = jnp.dot(grad_scores, query, preferred_element_type=jnp.float32)
        grad_query = lax.dot_general(
            grad_scores, key, (((0,), (0,)), ((), ())), preferred_element_type=jnp.float32
        )
        grads.append((grad_query * scale).reshape(ratio, rows, HD))
        acc_ref[0, span, lanes] += grad_key
        acc_ref[1, span, lanes] += grad_value
    if last:
        own_ref[0] = acc_ref[0, keys - tok_dev :] * scale
        own_ref[1] = acc_ref[1, keys - tok_dev :]
        for back, halo_ref in enumerate(halo_refs, 1):
            part = slice(keys - (back + 1) * tok_dev, keys - back * tok_dev)
            halo_ref[0] = (acc_ref[0, part] * scale).astype(jnp.bfloat16)
            halo_ref[1] = acc_ref[1, part].astype(jnp.bfloat16)
    query_out_ref[...] = jnp.swapaxes(jnp.concatenate(grads, axis=0), 0, 1).astype(jnp.bfloat16)


def attend(step, base, span, reach, heads, meta, assignment, segments, query, grad, kv, acc, full, last):
    first, filled = acc is None, full is not None
    rows, (blocks, _, _, kv_width) = query[0].shape[1], kv.shape
    ratio = heads // (kv_width // HD)
    keys, tok_dev = blocks * rows, query[0].shape[1] * lax.axis_size("dp")
    pieces, window = keys // tok_dev, reach + rows
    lanes, place = HEADS_STEP * HD, base // HEADS_STEP

    def rows_spec(array, pick):
        start = place if array.shape[2] == heads * HD else 0
        return pl.BlockSpec(
            (None, rows, HEADS_STEP * ratio * HD), lambda c, m, a: (pick(m, a), 0, start + c)
        )

    in_specs = [
        pl.BlockSpec(segments.shape, lambda c, m, a: (0, 0)),
        rows_spec(*query),
        rows_spec(*grad),
    ]
    in_specs.append(pl.BlockSpec((blocks, 2, rows, lanes), lambda c, m, a: (0, 0, 0, place + c)))
    operands = [meta, assignment, segments, query[0], grad[0], kv]
    aliases = {}
    acc_spec = pl.BlockSpec((2, keys, lanes), lambda c, m, a: (0, 0, place + c))
    if not first:
        if not last:
            aliases[len(operands)] = 1
        operands.append(acc)
        in_specs.append(acc_spec)
    if filled:
        aliases[len(operands)] = 0
        operands.append(full)
        in_specs.append(pl.BlockSpec(memory_space=pl.ANY))
    out_shape = [jax.ShapeDtypeStruct((tok_dev, heads, HD), jnp.bfloat16)]
    out_specs = [
        pl.BlockSpec(
            (rows, HEADS_STEP * ratio, HD),
            lambda c, m, a: (source_of(m[0], step, tok_dev // rows), place + c, 0),
        )
    ]
    if last:
        span_spec = pl.BlockSpec((2, tok_dev, lanes), lambda c, m, a: (0, 0, c))
        out_shape.append(jax.ShapeDtypeStruct((2, tok_dev, span * HD), jnp.float32))
        out_shape += [jax.ShapeDtypeStruct((2, tok_dev, span * HD), jnp.bfloat16)] * (pieces - 1)
        out_specs += [span_spec] * pieces
    else:
        out_shape.append(jax.ShapeDtypeStruct((2, keys, kv_width), jnp.float32))
        out_specs.append(acc_spec)
    pairs = span * ratio * rows * window
    held = (keys, ratio * rows), (window, ratio * rows)
    held += ((2, keys, lanes),) * last
    return pl.pallas_call(
        functools.partial(attend_kernel, step, first, filled, last, tok_dev, reach, ratio),
        out_shape=out_shape,
        grid_spec=pltpu.PrefetchScalarGridSpec(
            num_scalar_prefetch=2,
            grid=(span // HEADS_STEP,),
            in_specs=in_specs,
            out_specs=out_specs,
            scratch_shapes=[pltpu.VMEM(shape, jnp.float32) for shape in held],
        ),
        input_output_aliases=aliases,
        compiler_params=pltpu.CompilerParams(
            dimension_semantics=("arbitrary",), vmem_limit_bytes=VMEM_BYTES
        ),
        cost_estimate=pl.CostEstimate(
            flops=pairs * HD, bytes_accessed=pairs, transcendentals=0
        ),
        name="attend",
    )(*operands)


def shards(queries, keys, values, grad_out, segment_ids, assignment):
    count = lax.axis_size("dp")
    uly = lax.axis_size("uly")
    group = lax.axis_index("dp")
    line = lax.axis_index("blk") * uly + lax.axis_index("uly")
    width, kv_width = queries.shape[2], keys.shape[2]
    heads, kv_heads = width // HD, kv_width // HD
    tok_dev = count * queries.shape[1]
    doc_most = min(512, tok_dev * uly)
    hops = -(-doc_most // tok_dev)
    meta = jnp.stack([group, line]).astype(jnp.int32)

    final, halves = count // 2, kv_heads // HEADS_STEP
    part = width // halves
    others = [step for step in range(1, count) if step != final]
    jobs = [(2, step, 0, kv_width) for step in range(count)]
    jobs += [(0, step, 0, width) for step in others]
    jobs += [(0, final, half * part, part) for half in range(halves)]
    staged = stage(assignment, (queries, grad_out, keys, values), jobs)
    kv_staged, staged = staged[:count], list(staged[count:])
    kv_arrived = [exchanged(kv_staged[step], "dp", step) for step in range(1, count)]
    staged, kv_arrived[0] = lax.optimization_barrier((staged, kv_arrived[0]))
    arrived = [exchanged(rows, "dp", step) for rows, step in zip(staged, others)]
    held = staged[len(others) :]
    kv_own = jnp.zeros((count, *kv_staged[0].shape), keys.dtype)
    for step, piece in enumerate([kv_staged[0], *kv_arrived]):
        kv_own = lax.dynamic_update_index_in_dim(
            kv_own, piece, source_of(group, step, count), 0
        )
    halos = [shifted(kv_own, ("blk", "uly"), back) for back in range(hops, 0, -1)]
    kv = jnp.concatenate([*halos, kv_own], axis=0)

    rows, kv = lax.optimization_barrier((held[0], kv))
    split = [exchanged(rows, "dp", final)]
    fixed = (doc_most, heads, meta, assignment, segment_ids)
    query, grad = (queries, lambda m, a: a[m[0]]), (grad_out, lambda m, a: a[m[0]])
    full, acc = attend(0, 0, kv_heads, *fixed, query, grad, kv, None, None, False)
    for step, both in zip(others, arrived):
        query, grad = (both, lambda m, a: 0), (both, lambda m, a: 1)
        full, acc = attend(step, 0, kv_heads, *fixed, query, grad, kv, acc, full, False)
        if len(split) < halves:
            rows, acc = lax.optimization_barrier((held[len(split)], acc))
            split.append(exchanged(rows, "dp", final))
    parts = []
    for half, both in enumerate(split):
        query, grad = (both, lambda m, a: 0), (both, lambda m, a: 1)
        full, *part = attend(
            final, half * HEADS_STEP, HEADS_STEP, *fixed, query, grad, kv, acc, full, True
        )
        parts.append(part)
    total, *halos = [jnp.concatenate(part, axis=2) for part in zip(*parts)]
    for back, halo in enumerate(halos, 1):
        total = total + shifted(halo, ("blk", "uly"), -back).astype(jnp.float32)
    total = total.astype(jnp.bfloat16)
    return full[None], total[0][None], total[1][None]


def solution(mesh):
    in_specs = (
        P(None, ("blk", "uly", "dp"), None),
        P(None, ("blk", "uly", "dp"), None),
        P(None, ("blk", "uly", "dp"), None),
        P(None, ("blk", "uly", "dp"), None),
        P(),
        P(),
    )
    out_specs = (
        P("dp", ("blk", "uly"), None, None),
        P("dp", ("blk", "uly"), None),
        P("dp", ("blk", "uly"), None),
    )
    return jax.shard_map(shards, mesh=mesh, in_specs=in_specs, out_specs=out_specs, check_vma=False)
```

```python
import functools

import jax
import jax.numpy as jnp
from jax import lax
from jax.experimental import pallas as pl
from jax.experimental.pallas import tpu as pltpu
from jax.sharding import PartitionSpec as P

HD = 128
LOG2E = 1.4426950408889634
BIG_NEGATIVE = -1e30
VMEM_BYTES = 32 * 1024 * 1024
HEADS_STEP = 2


def target_of(index, step, count):
    return lax.rem(index + step, count)


def source_of(index, step, count):
    return lax.rem(index + count - step, count)


def exchanged(value, axis, step):
    count = lax.axis_size(axis)
    return lax.ppermute(value, axis, [(i, (i + step) % count) for i in range(count)])


def shifted(value, axis, by):
    length = lax.axis_size(axis)
    pairs = [(i, i + by) for i in range(length) if 0 <= i + by < length]
    return lax.ppermute(value, axis, pairs)


def stage_kernel(count, jobs, outs, assign_ref, *refs):
    group = lax.axis_index("dp")
    sources, refs = refs[:4], refs[4:]
    out_refs, held_refs, (in_sems, out_sems) = refs[:outs], refs[outs : 2 * outs], refs[-2:]
    loads, stores = [], []
    for out, (first, step, start, width) in enumerate(jobs):
        chosen = assign_ref[target_of(group, step, count)]
        for which in range(2):
            origin = sources[first + which].at[chosen, :, start : start + width]
            held, slot = held_refs[out].at[which], 2 * out + which
            loads.append(pltpu.make_async_copy(origin, held, in_sems.at[slot]))
            stores.append(pltpu.make_async_copy(held, out_refs[out].at[which], out_sems.at[slot]))
    for load in loads:
        load.start()
    for load, store in zip(loads, stores):
        load.wait()
        store.start()
    for store in stores:
        store.wait()


def stage(assignment, arrays, jobs):
    count, rows, _ = arrays[0].shape
    shapes = [(2, rows, width) for _, _, _, width in jobs]
    kind = arrays[0].dtype
    far = pl.BlockSpec(memory_space=pltpu.HBM)
    return pl.pallas_call(
        functools.partial(stage_kernel, count, jobs, len(jobs)),
        out_shape=[jax.ShapeDtypeStruct(shape, kind) for shape in shapes],
        in_specs=[pl.BlockSpec(memory_space=pltpu.SMEM)] + [far] * len(arrays),
        out_specs=[far] * len(jobs),
        scratch_shapes=[pltpu.VMEM(shape, kind) for shape in shapes]
        + [pltpu.SemaphoreType.DMA((2 * len(jobs),))] * 2,
        name="stage",
    )(assignment, *arrays)


def build_bias(source, sequence, line, segment_ref, column_ref, bias_ref, rows, tok_dev, reach):
    keys, lanes = column_ref.shape
    pieces = keys // tok_dev
    window = bias_ref.shape[0]
    eye = lax.broadcasted_iota(jnp.int32, (tok_dev, tok_dev), 0) == lax.broadcasted_iota(
        jnp.int32, (tok_dev, tok_dev), 1
    )
    for place in range(pieces):
        back = pieces - 1 - place
        start = pl.multiple_of(jnp.maximum(line - back, 0) * tok_dev, tok_dev)
        every = segment_ref[:, pl.ds(start, tok_dev)].astype(jnp.float32)
        mine = lax.broadcasted_iota(jnp.int32, every.shape, 0) == sequence
        row = jnp.sum(jnp.where(mine, every, 0.0), axis=0, keepdims=True)
        column = jnp.sum(jnp.where(eye, row, 0.0), axis=1, keepdims=True)
        column = jnp.where(line >= back, column, -1.0)
        column_ref[place * tok_dev : (place + 1) * tok_dev, :] = jnp.broadcast_to(
            column, (tok_dev, lanes)
        )

    def token(shape):
        return lax.rem(lax.broadcasted_iota(jnp.int32, shape, 1), jnp.int32(rows))

    here = pl.multiple_of(keys - tok_dev + source * rows, rows)
    asked_rows = column_ref[pl.ds(here, rows), :]
    same = lax.broadcasted_iota(jnp.int32, (rows, lanes), 0) == token((rows, lanes))
    asked = jnp.sum(jnp.where(same, asked_rows, 0.0), axis=0, keepdims=True)
    held = column_ref[pl.ds(pl.multiple_of(here - reach, rows), window), :]
    place = lax.broadcasted_iota(jnp.int32, (window, lanes), 0)
    allowed = (held == asked) & (place <= token((window, lanes)) + reach)
    bias_ref[...] = jnp.where(allowed, 0.0, BIG_NEGATIVE)


def attend_kernel(
    step, first, filled, last, tok_dev, reach, ratio,
    meta_ref, assign_ref, segment_ref, query_ref, grad_ref, kv_ref, *refs,
):
    refs = list(refs)
    if not first:
        acc_in_ref = refs.pop(0)
    if filled:
        refs.pop(0)
    query_out_ref = refs.pop(0)
    column_ref, bias_ref = refs[-2 - last], refs[-1 - last]
    if last:
        own_ref, halo_refs, acc_ref = refs[0], refs[1:-3], refs[-1]
    else:
        acc_ref = refs[0]

    rows = query_ref.shape[0]
    window = bias_ref.shape[0]
    keys = column_ref.shape[0]
    scale = 1.0 / HD**0.5
    group = meta_ref[0]
    source = source_of(group, step, tok_dev // rows)
    block = (keys - tok_dev - reach) // rows + source
    span = pl.ds(pl.multiple_of(block * rows, rows), window)

    @pl.when(pl.program_id(0) == 0)
    def _():
        build_bias(
            source, assign_ref[group], meta_ref[1], segment_ref, column_ref, bias_ref, rows, tok_dev, reach
        )

    acc_ref[...] = jnp.zeros_like(acc_ref) if first else acc_in_ref[...]
    turned = (((1,), (1,)), ((), ()))
    grads = []
    for head in range(HEADS_STEP):
        lanes = slice(head * HD, (head + 1) * HD)

        def stacked(ref):
            start = head * ratio
            return jnp.concatenate(
                [ref[:, r * HD : (r + 1) * HD] for r in range(start, start + ratio)], axis=0
            )

        def windowed(which):
            return kv_ref[pl.ds(block, window // rows), which, :, lanes].reshape(window, HD)

        query, grad = stacked(query_ref), stacked(grad_ref)
        key, value = windowed(0), windowed(1)
        scores = lax.dot_general(key, query, turned, preferred_element_type=jnp.float32)
        scores = scores * (scale * LOG2E) + bias_ref[...]
        top = jnp.max(scores, axis=0, keepdims=True)
        weights = jnp.exp2(scores - top)
        probs = weights * (1.0 / jnp.sum(weights, axis=0, keepdims=True))
        grad_probs = lax.dot_general(value, grad, turned, preferred_element_type=jnp.float32)
        product = probs * grad_probs
        delta = jnp.sum(product, axis=0, keepdims=True)
        grad_scores = (product - probs * delta).astype(jnp.bfloat16)
        grad_value = jnp.dot(
            probs.astype(jnp.bfloat16), grad, preferred_element_type=jnp.float32
        )
        grad_key = jnp.dot(grad_scores, query, preferred_element_type=jnp.float32)
        grad_query = lax.dot_general(
            grad_scores, key, (((0,), (0,)), ((), ())), preferred_element_type=jnp.float32
        )
        grads.append((grad_query * scale).reshape(ratio, rows, HD))
        acc_ref[0, span, lanes] += grad_key
        acc_ref[1, span, lanes] += grad_value
    if last:
        own_ref[0] = acc_ref[0, keys - tok_dev :] * scale
        own_ref[1] = acc_ref[1, keys - tok_dev :]
        for back, halo_ref in enumerate(halo_refs, 1):
            part = slice(keys - (back + 1) * tok_dev, keys - back * tok_dev)
            halo_ref[0] = (acc_ref[0, part] * scale).astype(jnp.bfloat16)
            halo_ref[1] = acc_ref[1, part].astype(jnp.bfloat16)
    query_out_ref[...] = jnp.swapaxes(jnp.concatenate(grads, axis=0), 0, 1).astype(jnp.bfloat16)


def attend(step, base, span, reach, heads, meta, assignment, segments, query, grad, kv, acc, full, last):
    first, filled = acc is None, full is not None
    rows, (blocks, _, _, kv_width) = query[0].shape[1], kv.shape
    ratio = heads // (kv_width // HD)
    keys, tok_dev = blocks * rows, query[0].shape[1] * lax.axis_size("dp")
    pieces, window = keys // tok_dev, reach + rows
    lanes, place = HEADS_STEP * HD, base // HEADS_STEP

    def rows_spec(array, pick):
        start = place if array.shape[2] == heads * HD else 0
        return pl.BlockSpec(
            (None, rows, HEADS_STEP * ratio * HD), lambda c, m, a: (pick(m, a), 0, start + c)
        )

    in_specs = [
        pl.BlockSpec(segments.shape, lambda c, m, a: (0, 0)),
        rows_spec(*query),
        rows_spec(*grad),
    ]
    in_specs.append(pl.BlockSpec((blocks, 2, rows, lanes), lambda c, m, a: (0, 0, 0, place + c)))
    operands = [meta, assignment, segments, query[0], grad[0], kv]
    aliases = {}
    acc_spec = pl.BlockSpec((2, keys, lanes), lambda c, m, a: (0, 0, c))
    if not first:
        if not last:
            aliases[len(operands)] = 1
        operands.append(acc)
        in_specs.append(acc_spec)
    if filled:
        aliases[len(operands)] = 0
        operands.append(full)
        in_specs.append(pl.BlockSpec(memory_space=pl.ANY))
    out_shape = [jax.ShapeDtypeStruct((tok_dev, heads, HD), jnp.bfloat16)]
    out_specs = [
        pl.BlockSpec(
            (rows, HEADS_STEP * ratio, HD),
            lambda c, m, a: (source_of(m[0], step, tok_dev // rows), place + c, 0),
        )
    ]
    if last:
        span_spec = pl.BlockSpec((2, tok_dev, lanes), lambda c, m, a: (0, 0, c))
        out_shape.append(jax.ShapeDtypeStruct((2, tok_dev, span * HD), jnp.float32))
        out_shape += [jax.ShapeDtypeStruct((2, tok_dev, span * HD), jnp.bfloat16)] * (pieces - 1)
        out_specs += [span_spec] * pieces
    else:
        out_shape.append(jax.ShapeDtypeStruct((2, keys, span * HD), jnp.float32))
        out_specs.append(acc_spec)
    pairs = span * ratio * rows * window
    held = (keys, ratio * rows), (window, ratio * rows)
    held += ((2, keys, lanes),) * last
    return pl.pallas_call(
        functools.partial(attend_kernel, step, first, filled, last, tok_dev, reach, ratio),
        out_shape=out_shape,
        grid_spec=pltpu.PrefetchScalarGridSpec(
            num_scalar_prefetch=2,
            grid=(span // HEADS_STEP,),
            in_specs=in_specs,
            out_specs=out_specs,
            scratch_shapes=[pltpu.VMEM(shape, jnp.float32) for shape in held],
        ),
        input_output_aliases=aliases,
        compiler_params=pltpu.CompilerParams(
            dimension_semantics=("arbitrary",), vmem_limit_bytes=VMEM_BYTES
        ),
        cost_estimate=pl.CostEstimate(
            flops=pairs * HD, bytes_accessed=pairs, transcendentals=0
        ),
        name="attend",
    )(*operands)


def shards(queries, keys, values, grad_out, segment_ids, assignment):
    count = lax.axis_size("dp")
    uly = lax.axis_size("uly")
    group = lax.axis_index("dp")
    line = lax.axis_index("blk") * uly + lax.axis_index("uly")
    width, kv_width = queries.shape[2], keys.shape[2]
    heads, kv_heads = width // HD, kv_width // HD
    tok_dev = count * queries.shape[1]
    doc_most = min(512, tok_dev * uly)
    hops = -(-doc_most // tok_dev)
    meta = jnp.stack([group, line]).astype(jnp.int32)

    final, halves = count // 2, kv_heads // HEADS_STEP
    part = width // halves
    others = [step for step in range(1, count) if step != final]
    jobs = [(2, step, 0, kv_width) for step in range(count)]
    order = [*others[1:], final]
    jobs.append((0, others[0], 0, width))
    jobs += [(0, step, half * part, part) for half in range(halves) for step in order]
    staged = stage(assignment, (queries, grad_out, keys, values), jobs)
    kv_staged, staged = staged[:count], list(staged[count:])
    kv_arrived = [exchanged(kv_staged[step], "dp", step) for step in range(1, count)]
    staged, kv_arrived[0] = lax.optimization_barrier((staged, kv_arrived[0]))
    whole = exchanged(staged[0], "dp", others[0])
    arrived = [exchanged(rows, "dp", step) for rows, step in zip(staged[1:], order)]
    behind = staged[1 + len(order) :]
    kv_own = jnp.zeros((count, *kv_staged[0].shape), keys.dtype)
    for step, piece in enumerate([kv_staged[0], *kv_arrived]):
        kv_own = lax.dynamic_update_index_in_dim(
            kv_own, piece, source_of(group, step, count), 0
        )
    halos = [shifted(kv_own, ("blk", "uly"), back) for back in range(hops, 0, -1)]
    kv = jnp.concatenate([*halos, kv_own], axis=0)

    fixed = (doc_most, heads, meta, assignment, segment_ids)
    own = (queries, lambda m, a: a[m[0]]), (grad_out, lambda m, a: a[m[0]])
    first = (whole, lambda m, a: 0), (whole, lambda m, a: 1)
    accs, full, totals, returned = [], None, [], []
    for half in range(halves):
        base = half * HEADS_STEP
        full, acc = attend(0, base, HEADS_STEP, *fixed, *own, kv, None, full, False)
        accs.append(acc)
        if not half:
            behind, full = lax.optimization_barrier((behind, full))
    arrived += [exchanged(rows, "dp", order[at % len(order)]) for at, rows in enumerate(behind)]
    for half in range(halves):
        base = half * HEADS_STEP
        full, accs[half] = attend(
            others[0], base, HEADS_STEP, *fixed, *first, kv, accs[half], full, False
        )
    for half in range(halves):
        base = half * HEADS_STEP
        for both, step in zip(arrived[half * len(order) :], order):
            pair = (both, lambda m, a: 0), (both, lambda m, a: 1)
            full, accs[half], *halos = attend(
                step, base, HEADS_STEP, *fixed, *pair, kv, accs[half], full, step == final
            )
        if half:
            halos, returned = lax.optimization_barrier((halos, returned))
        returned = [shifted(halo, ("blk", "uly"), -back) for back, halo in enumerate(halos, 1)]
        total = accs[half]
        for halo in returned:
            total = total + halo.astype(jnp.float32)
        totals.append(total.astype(jnp.bfloat16))
    total = jnp.concatenate(totals, axis=2)
    return full[None], total[0][None], total[1][None]


def solution(mesh):
    in_specs = (
        P(None, ("blk", "uly", "dp"), None),
        P(None, ("blk", "uly", "dp"), None),
        P(None, ("blk", "uly", "dp"), None),
        P(None, ("blk", "uly", "dp"), None),
        P(),
        P(),
    )
    out_specs = (
        P("dp", ("blk", "uly"), None, None),
        P("dp", ("blk", "uly"), None),
        P("dp", ("blk", "uly"), None),
    )
    return jax.shard_map(shards, mesh=mesh, in_specs=in_specs, out_specs=out_specs, check_vma=False)
```

```python
import functools

import jax
import jax.numpy as jnp
from jax import lax
from jax.experimental import pallas as pl
from jax.experimental.pallas import tpu as pltpu
from jax.sharding import PartitionSpec as P

HD = 128
LOG2E = 1.4426950408889634
BIG_NEGATIVE = -1e30
VMEM_BYTES = 32 * 1024 * 1024
HEADS_STEP = 2


def target_of(index, step, count):
    return lax.rem(index + step, count)


def source_of(index, step, count):
    return lax.rem(index + count - step, count)


def exchanged(value, axis, step):
    count = lax.axis_size(axis)
    return lax.ppermute(value, axis, [(i, (i + step) % count) for i in range(count)])


def shifted(value, axis, by):
    length = lax.axis_size(axis)
    pairs = [(i, i + by) for i in range(length) if 0 <= i + by < length]
    return lax.ppermute(value, axis, pairs)


def stage_kernel(count, jobs, outs, assign_ref, *refs):
    group = lax.axis_index("dp")
    sources, refs = refs[:4], refs[4:]
    out_refs, held_refs, (in_sems, out_sems) = refs[:outs], refs[outs : 2 * outs], refs[-2:]
    loads, stores = [], []
    for out, (first, step, start, width) in enumerate(jobs):
        chosen = assign_ref[target_of(group, step, count)]
        for which in range(2):
            origin = sources[first + which].at[chosen, :, start : start + width]
            held, slot = held_refs[out].at[which], 2 * out + which
            loads.append(pltpu.make_async_copy(origin, held, in_sems.at[slot]))
            stores.append(pltpu.make_async_copy(held, out_refs[out].at[which], out_sems.at[slot]))
    for load in loads:
        load.start()
    for load, store in zip(loads, stores):
        load.wait()
        store.start()
    for store in stores:
        store.wait()


def stage(assignment, arrays, jobs):
    count, rows, _ = arrays[0].shape
    shapes = [(2, rows, width) for _, _, _, width in jobs]
    kind = arrays[0].dtype
    far = pl.BlockSpec(memory_space=pltpu.HBM)
    return pl.pallas_call(
        functools.partial(stage_kernel, count, jobs, len(jobs)),
        out_shape=[jax.ShapeDtypeStruct(shape, kind) for shape in shapes],
        in_specs=[pl.BlockSpec(memory_space=pltpu.SMEM)] + [far] * len(arrays),
        out_specs=[far] * len(jobs),
        scratch_shapes=[pltpu.VMEM(shape, kind) for shape in shapes]
        + [pltpu.SemaphoreType.DMA((2 * len(jobs),))] * 2,
        name="stage",
    )(assignment, *arrays)


def build_bias(source, sequence, line, segment_ref, column_ref, bias_ref, rows, tok_dev, reach):
    keys, lanes = column_ref.shape
    pieces = keys // tok_dev
    window = bias_ref.shape[0]
    eye = lax.broadcasted_iota(jnp.int32, (tok_dev, tok_dev), 0) == lax.broadcasted_iota(
        jnp.int32, (tok_dev, tok_dev), 1
    )
    for place in range(pieces):
        back = pieces - 1 - place
        start = pl.multiple_of(jnp.maximum(line - back, 0) * tok_dev, tok_dev)
        every = segment_ref[:, pl.ds(start, tok_dev)].astype(jnp.float32)
        mine = lax.broadcasted_iota(jnp.int32, every.shape, 0) == sequence
        row = jnp.sum(jnp.where(mine, every, 0.0), axis=0, keepdims=True)
        column = jnp.sum(jnp.where(eye, row, 0.0), axis=1, keepdims=True)
        column = jnp.where(line >= back, column, -1.0)
        column_ref[place * tok_dev : (place + 1) * tok_dev, :] = jnp.broadcast_to(
            column, (tok_dev, lanes)
        )

    def token(shape):
        return lax.rem(lax.broadcasted_iota(jnp.int32, shape, 1), jnp.int32(rows))

    here = pl.multiple_of(keys - tok_dev + source * rows, rows)
    asked_rows = column_ref[pl.ds(here, rows), :]
    same = lax.broadcasted_iota(jnp.int32, (rows, lanes), 0) == token((rows, lanes))
    asked = jnp.sum(jnp.where(same, asked_rows, 0.0), axis=0, keepdims=True)
    held = column_ref[pl.ds(pl.multiple_of(here - reach, rows), window), :]
    place = lax.broadcasted_iota(jnp.int32, (window, lanes), 0)
    allowed = (held == asked) & (place <= token((window, lanes)) + reach)
    bias_ref[...] = jnp.where(allowed, 0.0, BIG_NEGATIVE)


def attend_kernel(
    step, first, filled, last, tok_dev, reach, ratio,
    meta_ref, assign_ref, segment_ref, query_ref, grad_ref, kv_ref, *refs,
):
    refs = list(refs)
    if not first:
        acc_in_ref = refs.pop(0)
    if filled:
        refs.pop(0)
    query_out_ref = refs.pop(0)
    column_ref, bias_ref = refs[-2 - last], refs[-1 - last]
    if last:
        own_ref, halo_refs, acc_ref = refs[0], refs[1:-3], refs[-1]
    else:
        acc_ref = refs[0]

    rows = query_ref.shape[0]
    window = bias_ref.shape[0]
    keys = column_ref.shape[0]
    scale = 1.0 / HD**0.5
    group = meta_ref[0]
    source = source_of(group, step, tok_dev // rows)
    block = (keys - tok_dev - reach) // rows + source
    span = pl.ds(pl.multiple_of(block * rows, rows), window)

    @pl.when(pl.program_id(0) == 0)
    def _():
        build_bias(
            source, assign_ref[group], meta_ref[1], segment_ref, column_ref, bias_ref, rows, tok_dev, reach
        )

    acc_ref[...] = jnp.zeros_like(acc_ref) if first else acc_in_ref[...]
    turned = (((1,), (1,)), ((), ()))
    grads = []
    for head in range(HEADS_STEP):
        lanes = slice(head * HD, (head + 1) * HD)

        def stacked(ref):
            start = head * ratio
            return jnp.concatenate(
                [ref[:, r * HD : (r + 1) * HD] for r in range(start, start + ratio)], axis=0
            )

        def windowed(which):
            return kv_ref[pl.ds(block, window // rows), which, :, lanes].reshape(window, HD)

        query, grad = stacked(query_ref), stacked(grad_ref)
        key, value = windowed(0), windowed(1)
        scores = lax.dot_general(key, query, turned, preferred_element_type=jnp.float32)
        scores = scores * (scale * LOG2E) + bias_ref[...]
        top = jnp.max(scores, axis=0, keepdims=True)
        weights = jnp.exp2(scores - top)
        probs = weights * (1.0 / jnp.sum(weights, axis=0, keepdims=True))
        grad_probs = lax.dot_general(value, grad, turned, preferred_element_type=jnp.float32)
        product = probs * grad_probs
        delta = jnp.sum(product, axis=0, keepdims=True)
        grad_scores = (product - probs * delta).astype(jnp.bfloat16)
        grad_value = jnp.dot(
            probs.astype(jnp.bfloat16), grad, preferred_element_type=jnp.float32
        )
        grad_key = jnp.dot(grad_scores, query, preferred_element_type=jnp.float32)
        grad_query = lax.dot_general(
            grad_scores, key, (((0,), (0,)), ((), ())), preferred_element_type=jnp.float32
        )
        grads.append((grad_query * scale).reshape(ratio, rows, HD))
        acc_ref[0, span, lanes] += grad_key
        acc_ref[1, span, lanes] += grad_value
    if last:
        own_ref[0] = acc_ref[0, keys - tok_dev :] * scale
        own_ref[1] = acc_ref[1, keys - tok_dev :]
        for back, halo_ref in enumerate(halo_refs, 1):
            part = slice(keys - (back + 1) * tok_dev, keys - back * tok_dev)
            halo_ref[0] = (acc_ref[0, part] * scale).astype(jnp.bfloat16)
            halo_ref[1] = acc_ref[1, part].astype(jnp.bfloat16)
    query_out_ref[...] = jnp.swapaxes(jnp.concatenate(grads, axis=0), 0, 1).astype(jnp.bfloat16)


def attend(step, base, span, reach, heads, meta, assignment, segments, query, grad, kv, acc, full, last):
    first, filled = acc is None, full is not None
    rows, (blocks, _, _, kv_width) = query[0].shape[1], kv.shape
    ratio = heads // (kv_width // HD)
    keys, tok_dev = blocks * rows, query[0].shape[1] * lax.axis_size("dp")
    pieces, window = keys // tok_dev, reach + rows
    lanes, place = HEADS_STEP * HD, base // HEADS_STEP

    def rows_spec(array, pick):
        start = place if array.shape[2] == heads * HD else 0
        return pl.BlockSpec(
            (None, rows, HEADS_STEP * ratio * HD), lambda c, m, a: (pick(m, a), 0, start + c)
        )

    in_specs = [
        pl.BlockSpec(segments.shape, lambda c, m, a: (0, 0)),
        rows_spec(*query),
        rows_spec(*grad),
    ]
    in_specs.append(pl.BlockSpec((blocks, 2, rows, lanes), lambda c, m, a: (0, 0, 0, place + c)))
    operands = [meta, assignment, segments, query[0], grad[0], kv]
    aliases = {}
    acc_spec = pl.BlockSpec((2, keys, lanes), lambda c, m, a: (0, 0, place + c))
    if not first:
        if not last:
            aliases[len(operands)] = 1
        operands.append(acc)
        in_specs.append(acc_spec)
    if filled:
        aliases[len(operands)] = 0
        operands.append(full)
        in_specs.append(pl.BlockSpec(memory_space=pl.ANY))
    out_shape = [jax.ShapeDtypeStruct((tok_dev, heads, HD), jnp.bfloat16)]
    out_specs = [
        pl.BlockSpec(
            (rows, HEADS_STEP * ratio, HD),
            lambda c, m, a: (source_of(m[0], step, tok_dev // rows), place + c, 0),
        )
    ]
    if last:
        span_spec = pl.BlockSpec((2, tok_dev, lanes), lambda c, m, a: (0, 0, c))
        out_shape.append(jax.ShapeDtypeStruct((2, tok_dev, span * HD), jnp.float32))
        out_shape += [jax.ShapeDtypeStruct((2, tok_dev, span * HD), jnp.bfloat16)] * (pieces - 1)
        out_specs += [span_spec] * pieces
    else:
        out_shape.append(jax.ShapeDtypeStruct((2, keys, kv_width), jnp.float32))
        out_specs.append(acc_spec)
    pairs = span * ratio * rows * window
    held = (keys, ratio * rows), (window, ratio * rows)
    held += ((2, keys, lanes),) * last
    return pl.pallas_call(
        functools.partial(attend_kernel, step, first, filled, last, tok_dev, reach, ratio),
        out_shape=out_shape,
        grid_spec=pltpu.PrefetchScalarGridSpec(
            num_scalar_prefetch=2,
            grid=(span // HEADS_STEP,),
            in_specs=in_specs,
            out_specs=out_specs,
            scratch_shapes=[pltpu.VMEM(shape, jnp.float32) for shape in held],
        ),
        input_output_aliases=aliases,
        compiler_params=pltpu.CompilerParams(
            dimension_semantics=("arbitrary",), vmem_limit_bytes=VMEM_BYTES
        ),
        cost_estimate=pl.CostEstimate(
            flops=pairs * HD, bytes_accessed=pairs, transcendentals=0
        ),
        name="attend",
    )(*operands)


def shards(queries, keys, values, grad_out, segment_ids, assignment):
    count = lax.axis_size("dp")
    uly = lax.axis_size("uly")
    group = lax.axis_index("dp")
    line = lax.axis_index("blk") * uly + lax.axis_index("uly")
    width, kv_width = queries.shape[2], keys.shape[2]
    heads, kv_heads = width // HD, kv_width // HD
    tok_dev = count * queries.shape[1]
    doc_most = min(512, tok_dev * uly)
    hops = -(-doc_most // tok_dev)
    meta = jnp.stack([group, line]).astype(jnp.int32)

    final, halves = count // 2, kv_heads // HEADS_STEP
    part = width // halves
    others = [step for step in range(1, count) if step != final]
    jobs = [(2, step, 0, kv_width) for step in range(count)]
    jobs += [(0, step, 0, width) for step in others]
    jobs += [(0, final, half * part, part) for half in range(halves)]
    staged = stage(assignment, (queries, grad_out, keys, values), jobs)
    kv_staged, staged = staged[:count], list(staged[count:])
    kv_arrived = [exchanged(kv_staged[step], "dp", step) for step in range(1, count)]
    staged, kv_arrived[0] = lax.optimization_barrier((staged, kv_arrived[0]))
    arrived = [exchanged(rows, "dp", step) for rows, step in zip(staged, others)]
    held = staged[len(others) :]
    kv_own = jnp.zeros((count, *kv_staged[0].shape), keys.dtype)
    for step, piece in enumerate([kv_staged[0], *kv_arrived]):
        kv_own = lax.dynamic_update_index_in_dim(
            kv_own, piece, source_of(group, step, count), 0
        )
    halos = [shifted(kv_own, ("blk", "uly"), back) for back in range(hops, 0, -1)]
    kv = jnp.concatenate([*halos, kv_own], axis=0)

    fixed = (doc_most, heads, meta, assignment, segment_ids)
    query, grad = (queries, lambda m, a: a[m[0]]), (grad_out, lambda m, a: a[m[0]])
    full, acc = attend(0, 0, kv_heads, *fixed, query, grad, kv, None, None, False)
    rows, acc = lax.optimization_barrier((held[0], acc))
    split = [exchanged(rows, "dp", final)]
    for step, both in zip(others, arrived):
        query, grad = (both, lambda m, a: 0), (both, lambda m, a: 1)
        full, acc = attend(step, 0, kv_heads, *fixed, query, grad, kv, acc, full, False)
    for rows in held[1:]:
        rows, acc = lax.optimization_barrier((rows, acc))
        split.append(exchanged(rows, "dp", final))
    totals, returned = [], []
    for half, both in enumerate(split):
        query, grad = (both, lambda m, a: 0), (both, lambda m, a: 1)
        full, total, *halos = attend(
            final, half * HEADS_STEP, HEADS_STEP, *fixed, query, grad, kv, acc, full, True
        )
        if half:
            halos, returned = lax.optimization_barrier((halos, returned))
        returned = [shifted(halo, ("blk", "uly"), -back) for back, halo in enumerate(halos, 1)]
        for halo in returned:
            total = total + halo.astype(jnp.float32)
        totals.append(total.astype(jnp.bfloat16))
    total = jnp.concatenate(totals, axis=2)
    return full[None], total[0][None], total[1][None]


def solution(mesh):
    in_specs = (
        P(None, ("blk", "uly", "dp"), None),
        P(None, ("blk", "uly", "dp"), None),
        P(None, ("blk", "uly", "dp"), None),
        P(None, ("blk", "uly", "dp"), None),
        P(),
        P(),
    )
    out_specs = (
        P("dp", ("blk", "uly"), None, None),
        P("dp", ("blk", "uly"), None),
        P("dp", ("blk", "uly"), None),
    )
    return jax.shard_map(shards, mesh=mesh, in_specs=in_specs, out_specs=out_specs, check_vma=False)
```

```python
import functools

import jax
import jax.numpy as jnp
from jax import lax
from jax.experimental import pallas as pl
from jax.experimental.pallas import tpu as pltpu
from jax.sharding import PartitionSpec as P

HD = 128
LOG2E = 1.4426950408889634
BIG_NEGATIVE = -1e30
VMEM_BYTES = 32 * 1024 * 1024
HEADS_STEP = 2


def target_of(index, step, count):
    return lax.rem(index + step, count)


def source_of(index, step, count):
    return lax.rem(index + count - step, count)


def exchanged(value, axis, step):
    count = lax.axis_size(axis)
    return lax.ppermute(value, axis, [(i, (i + step) % count) for i in range(count)])


def shifted(value, axis, by):
    length = lax.axis_size(axis)
    pairs = [(i, i + by) for i in range(length) if 0 <= i + by < length]
    return lax.ppermute(value, axis, pairs)


def stage_kernel(count, jobs, outs, assign_ref, *refs):
    group = lax.axis_index("dp")
    sources, refs = refs[:4], refs[4:]
    out_refs, held_refs, (in_sems, out_sems) = refs[:outs], refs[outs : 2 * outs], refs[-2:]
    loads, stores = [], []
    for out, (first, step, start, width) in enumerate(jobs):
        chosen = assign_ref[target_of(group, step, count)]
        for which in range(2):
            origin = sources[first + which].at[chosen, :, start : start + width]
            held, slot = held_refs[out].at[which], 2 * out + which
            loads.append(pltpu.make_async_copy(origin, held, in_sems.at[slot]))
            stores.append(pltpu.make_async_copy(held, out_refs[out].at[which], out_sems.at[slot]))
    for load in loads:
        load.start()
    for load, store in zip(loads, stores):
        load.wait()
        store.start()
    for store in stores:
        store.wait()


def stage(assignment, arrays, jobs):
    count, rows, _ = arrays[0].shape
    shapes = [(2, rows, width) for _, _, _, width in jobs]
    kind = arrays[0].dtype
    far = pl.BlockSpec(memory_space=pltpu.HBM)
    return pl.pallas_call(
        functools.partial(stage_kernel, count, jobs, len(jobs)),
        out_shape=[jax.ShapeDtypeStruct(shape, kind) for shape in shapes],
        in_specs=[pl.BlockSpec(memory_space=pltpu.SMEM)] + [far] * len(arrays),
        out_specs=[far] * len(jobs),
        scratch_shapes=[pltpu.VMEM(shape, kind) for shape in shapes]
        + [pltpu.SemaphoreType.DMA((2 * len(jobs),))] * 2,
        name="stage",
    )(assignment, *arrays)


def build_bias(source, sequence, line, segment_ref, column_ref, bias_ref, rows, tok_dev, reach):
    keys, lanes = column_ref.shape
    pieces = keys // tok_dev
    window = bias_ref.shape[0]
    eye = lax.broadcasted_iota(jnp.int32, (tok_dev, tok_dev), 0) == lax.broadcasted_iota(
        jnp.int32, (tok_dev, tok_dev), 1
    )
    for place in range(pieces):
        back = pieces - 1 - place
        start = pl.multiple_of(jnp.maximum(line - back, 0) * tok_dev, tok_dev)
        every = segment_ref[:, pl.ds(start, tok_dev)].astype(jnp.float32)
        mine = lax.broadcasted_iota(jnp.int32, every.shape, 0) == sequence
        row = jnp.sum(jnp.where(mine, every, 0.0), axis=0, keepdims=True)
        column = jnp.sum(jnp.where(eye, row, 0.0), axis=1, keepdims=True)
        column = jnp.where(line >= back, column, -1.0)
        column_ref[place * tok_dev : (place + 1) * tok_dev, :] = jnp.broadcast_to(
            column, (tok_dev, lanes)
        )

    def token(shape):
        return lax.rem(lax.broadcasted_iota(jnp.int32, shape, 1), jnp.int32(rows))

    here = pl.multiple_of(keys - tok_dev + source * rows, rows)
    asked_rows = column_ref[pl.ds(here, rows), :]
    same = lax.broadcasted_iota(jnp.int32, (rows, lanes), 0) == token((rows, lanes))
    asked = jnp.sum(jnp.where(same, asked_rows, 0.0), axis=0, keepdims=True)
    held = column_ref[pl.ds(pl.multiple_of(here - reach, rows), window), :]
    place = lax.broadcasted_iota(jnp.int32, (window, lanes), 0)
    allowed = (held == asked) & (place <= token((window, lanes)) + reach)
    bias_ref[...] = jnp.where(allowed, 0.0, BIG_NEGATIVE)


def attend_kernel(
    step, first, filled, last, tok_dev, reach, ratio,
    meta_ref, assign_ref, segment_ref, query_ref, grad_ref, kv_ref, *refs,
):
    refs = list(refs)
    if not first:
        acc_in_ref = refs.pop(0)
    if filled:
        refs.pop(0)
    query_out_ref = refs.pop(0)
    column_ref, bias_ref, turn_ref = refs[-3 - last : len(refs) - last]
    if last:
        own_ref, halo_refs, acc_ref = refs[0], refs[1:-4], refs[-1]
    else:
        acc_ref = refs[0]

    rows = query_ref.shape[0]
    window = bias_ref.shape[0]
    keys = column_ref.shape[0]
    scale = 1.0 / HD**0.5
    group = meta_ref[0]
    source = source_of(group, step, tok_dev // rows)
    block = (keys - tok_dev - reach) // rows + source
    span = pl.ds(pl.multiple_of(block * rows, rows), window)

    @pl.when(pl.program_id(0) == 0)
    def _():
        build_bias(
            source, assign_ref[group], meta_ref[1], segment_ref, column_ref, bias_ref, rows, tok_dev, reach
        )

    acc_ref[...] = jnp.zeros_like(acc_ref) if first else acc_in_ref[...]
    turned = (((1,), (1,)), ((), ()))
    for head in range(HEADS_STEP):
        lanes = slice(head * HD, (head + 1) * HD)

        def stacked(ref):
            start = head * ratio
            return jnp.concatenate(
                [ref[:, r * HD : (r + 1) * HD] for r in range(start, start + ratio)], axis=0
            )

        def windowed(which):
            return kv_ref[pl.ds(block, window // rows), which, :, lanes].reshape(window, HD)

        query, grad = stacked(query_ref), stacked(grad_ref)
        key, value = windowed(0), windowed(1)
        scores = lax.dot_general(key, query, turned, preferred_element_type=jnp.float32)
        scores = scores * (scale * LOG2E) + bias_ref[...]
        top = jnp.max(scores, axis=0, keepdims=True)
        weights = jnp.exp2(scores - top)
        probs = weights * (1.0 / jnp.sum(weights, axis=0, keepdims=True))
        grad_probs = lax.dot_general(value, grad, turned, preferred_element_type=jnp.float32)
        product = probs * grad_probs
        delta = jnp.sum(product, axis=0, keepdims=True)
        grad_scores = (product - probs * delta).astype(jnp.bfloat16)
        grad_value = jnp.dot(
            probs.astype(jnp.bfloat16), grad, preferred_element_type=jnp.float32
        )
        grad_key = jnp.dot(grad_scores, query, preferred_element_type=jnp.float32)
        grad_query = lax.dot_general(
            grad_scores, key, (((0,), (0,)), ((), ())), preferred_element_type=jnp.float32
        )
        grad_query = (grad_query * scale).reshape(ratio, rows, HD)
        for r in range(ratio):
            turn_ref[:, head * ratio + r, :] = grad_query[r]
        acc_ref[0, span, lanes] += grad_key
        acc_ref[1, span, lanes] += grad_value
    if last:
        own_ref[0] = acc_ref[0, keys - tok_dev :] * scale
        own_ref[1] = acc_ref[1, keys - tok_dev :]
        for back, halo_ref in enumerate(halo_refs, 1):
            part = slice(keys - (back + 1) * tok_dev, keys - back * tok_dev)
            halo_ref[0] = (acc_ref[0, part] * scale).astype(jnp.bfloat16)
            halo_ref[1] = acc_ref[1, part].astype(jnp.bfloat16)
    query_out_ref[...] = turn_ref[...].astype(jnp.bfloat16)


def attend(step, base, span, reach, heads, meta, assignment, segments, query, grad, kv, acc, full, last):
    first, filled = acc is None, full is not None
    rows, (blocks, _, _, kv_width) = query[0].shape[1], kv.shape
    ratio = heads // (kv_width // HD)
    keys, tok_dev = blocks * rows, query[0].shape[1] * lax.axis_size("dp")
    pieces, window = keys // tok_dev, reach + rows
    lanes, place = HEADS_STEP * HD, base // HEADS_STEP

    def rows_spec(array, pick):
        start = place if array.shape[2] == heads * HD else 0
        return pl.BlockSpec(
            (None, rows, HEADS_STEP * ratio * HD), lambda c, m, a: (pick(m, a), 0, start + c)
        )

    in_specs = [
        pl.BlockSpec(segments.shape, lambda c, m, a: (0, 0)),
        rows_spec(*query),
        rows_spec(*grad),
    ]
    in_specs.append(pl.BlockSpec((blocks, 2, rows, lanes), lambda c, m, a: (0, 0, 0, place + c)))
    operands = [meta, assignment, segments, query[0], grad[0], kv]
    aliases = {}
    acc_spec = pl.BlockSpec((2, keys, lanes), lambda c, m, a: (0, 0, place + c))
    if not first:
        if not last:
            aliases[len(operands)] = 1
        operands.append(acc)
        in_specs.append(acc_spec)
    if filled:
        aliases[len(operands)] = 0
        operands.append(full)
        in_specs.append(pl.BlockSpec(memory_space=pl.ANY))
    out_shape = [jax.ShapeDtypeStruct((tok_dev, heads, HD), jnp.bfloat16)]
    out_specs = [
        pl.BlockSpec(
            (rows, HEADS_STEP * ratio, HD),
            lambda c, m, a: (source_of(m[0], step, tok_dev // rows), place + c, 0),
        )
    ]
    if last:
        span_spec = pl.BlockSpec((2, tok_dev, lanes), lambda c, m, a: (0, 0, c))
        out_shape.append(jax.ShapeDtypeStruct((2, tok_dev, span * HD), jnp.float32))
        out_shape += [jax.ShapeDtypeStruct((2, tok_dev, span * HD), jnp.bfloat16)] * (pieces - 1)
        out_specs += [span_spec] * pieces
    else:
        out_shape.append(jax.ShapeDtypeStruct((2, keys, kv_width), jnp.float32))
        out_specs.append(acc_spec)
    pairs = span * ratio * rows * window
    held = (keys, ratio * rows), (window, ratio * rows), (rows, HEADS_STEP * ratio, HD)
    held += ((2, keys, lanes),) * last
    return pl.pallas_call(
        functools.partial(attend_kernel, step, first, filled, last, tok_dev, reach, ratio),
        out_shape=out_shape,
        grid_spec=pltpu.PrefetchScalarGridSpec(
            num_scalar_prefetch=2,
            grid=(span // HEADS_STEP,),
            in_specs=in_specs,
            out_specs=out_specs,
            scratch_shapes=[pltpu.VMEM(shape, jnp.float32) for shape in held],
        ),
        input_output_aliases=aliases,
        compiler_params=pltpu.CompilerParams(
            dimension_semantics=("arbitrary",),
            vmem_limit_bytes=VMEM_BYTES,
            fuse_transposed_lhs_in_matmul=True,
        ),
        cost_estimate=pl.CostEstimate(
            flops=pairs * HD, bytes_accessed=pairs, transcendentals=0
        ),
        name="attend",
    )(*operands)


def shards(queries, keys, values, grad_out, segment_ids, assignment):
    count = lax.axis_size("dp")
    uly = lax.axis_size("uly")
    group = lax.axis_index("dp")
    line = lax.axis_index("blk") * uly + lax.axis_index("uly")
    width, kv_width = queries.shape[2], keys.shape[2]
    heads, kv_heads = width // HD, kv_width // HD
    tok_dev = count * queries.shape[1]
    doc_most = min(512, tok_dev * uly)
    hops = -(-doc_most // tok_dev)
    meta = jnp.stack([group, line]).astype(jnp.int32)

    final, halves = count // 2, kv_heads // HEADS_STEP
    part = width // halves
    others = [step for step in range(1, count) if step != final]
    jobs = [(2, step, 0, kv_width) for step in range(count)]
    jobs += [(0, step, 0, width) for step in others]
    jobs += [(0, final, half * part, part) for half in range(halves)]
    staged = stage(assignment, (queries, grad_out, keys, values), jobs)
    kv_staged, staged = staged[:count], list(staged[count:])
    kv_arrived = [exchanged(kv_staged[step], "dp", step) for step in range(1, count)]
    staged, kv_arrived[0] = lax.optimization_barrier((staged, kv_arrived[0]))
    arrived = [exchanged(rows, "dp", step) for rows, step in zip(staged, others)]
    held = staged[len(others) :]
    kv_own = jnp.zeros((count, *kv_staged[0].shape), keys.dtype)
    for step, piece in enumerate([kv_staged[0], *kv_arrived]):
        kv_own = lax.dynamic_update_index_in_dim(
            kv_own, piece, source_of(group, step, count), 0
        )
    halos = [shifted(kv_own, ("blk", "uly"), back) for back in range(hops, 0, -1)]
    kv = jnp.concatenate([*halos, kv_own], axis=0)

    fixed = (doc_most, heads, meta, assignment, segment_ids)
    query, grad = (queries, lambda m, a: a[m[0]]), (grad_out, lambda m, a: a[m[0]])
    full, acc = attend(0, 0, kv_heads, *fixed, query, grad, kv, None, None, False)
    rows, acc = lax.optimization_barrier((held[0], acc))
    split = [exchanged(rows, "dp", final)]
    for step, both in zip(others, arrived):
        query, grad = (both, lambda m, a: 0), (both, lambda m, a: 1)
        full, acc = attend(step, 0, kv_heads, *fixed, query, grad, kv, acc, full, False)
    for rows in held[1:]:
        rows, acc = lax.optimization_barrier((rows, acc))
        split.append(exchanged(rows, "dp", final))
    totals, returned = [], []
    for half, both in enumerate(split):
        query, grad = (both, lambda m, a: 0), (both, lambda m, a: 1)
        full, total, *halos = attend(
            final, half * HEADS_STEP, HEADS_STEP, *fixed, query, grad, kv, acc, full, True
        )
        if half:
            halos, returned[0] = lax.optimization_barrier((halos, returned[0]))
        returned = [shifted(halo, ("blk", "uly"), -back) for back, halo in enumerate(halos, 1)]
        for halo in returned:
            total = total + halo.astype(jnp.float32)
        totals.append(total.astype(jnp.bfloat16))
    total = jnp.concatenate(totals, axis=2)
    return full[None], total[0][None], total[1][None]


def solution(mesh):
    in_specs = (
        P(None, ("blk", "uly", "dp"), None),
        P(None, ("blk", "uly", "dp"), None),
        P(None, ("blk", "uly", "dp"), None),
        P(None, ("blk", "uly", "dp"), None),
        P(),
        P(),
    )
    out_specs = (
        P("dp", ("blk", "uly"), None, None),
        P("dp", ("blk", "uly"), None),
        P("dp", ("blk", "uly"), None),
    )
    return jax.shard_map(shards, mesh=mesh, in_specs=in_specs, out_specs=out_specs, check_vma=False)
```

```python
import functools

import jax
import jax.numpy as jnp
from jax import lax
from jax.experimental import pallas as pl
from jax.experimental.pallas import tpu as pltpu
from jax.sharding import PartitionSpec as P

HD = 128
LOG2E = 1.4426950408889634
BIG_NEGATIVE = -1e30
VMEM_BYTES = 32 * 1024 * 1024
HEADS_STEP = 2
CALL_COST = 30


def target_of(index, step, count):
    return lax.rem(index + step, count)


def source_of(index, step, count):
    return lax.rem(index + count - step, count)


def exchanged(value, axis, step):
    count = lax.axis_size(axis)
    return lax.ppermute(value, axis, [(i, (i + step) % count) for i in range(count)])


def shifted(value, axis, by):
    length = lax.axis_size(axis)
    pairs = [(i, i + by) for i in range(length) if 0 <= i + by < length]
    return lax.ppermute(value, axis, pairs)


def stage_kernel(count, jobs, outs, assign_ref, *refs):
    group = lax.axis_index("dp")
    sources, refs = refs[:4], refs[4:]
    out_refs, held_refs, (in_sems, out_sems) = refs[:outs], refs[outs : 2 * outs], refs[-2:]
    loads, stores = [], []
    for out, (first, step, start, width) in enumerate(jobs):
        chosen = assign_ref[target_of(group, step, count)]
        for which in range(2):
            origin = sources[first + which].at[chosen, :, start : start + width]
            held, slot = held_refs[out].at[which], 2 * out + which
            loads.append(pltpu.make_async_copy(origin, held, in_sems.at[slot]))
            stores.append(pltpu.make_async_copy(held, out_refs[out].at[which], out_sems.at[slot]))
    for load in loads:
        load.start()
    for load, store in zip(loads, stores):
        load.wait()
        store.start()
    for store in stores:
        store.wait()


def stage(assignment, arrays, jobs):
    count, rows, _ = arrays[0].shape
    shapes = [(2, rows, width) for _, _, _, width in jobs]
    kind = arrays[0].dtype
    far = pl.BlockSpec(memory_space=pltpu.HBM)
    return pl.pallas_call(
        functools.partial(stage_kernel, count, jobs, len(jobs)),
        out_shape=[jax.ShapeDtypeStruct(shape, kind) for shape in shapes],
        in_specs=[pl.BlockSpec(memory_space=pltpu.SMEM)] + [far] * len(arrays),
        out_specs=[far] * len(jobs),
        scratch_shapes=[pltpu.VMEM(shape, kind) for shape in shapes]
        + [pltpu.SemaphoreType.DMA((2 * len(jobs),))] * 2,
        name="stage",
    )(assignment, *arrays)


def build_bias(source, sequence, line, segment_ref, column_ref, bias_ref, rows, tok_dev, reach):
    keys, lanes = column_ref.shape
    pieces = keys // tok_dev
    window = bias_ref.shape[0]
    eye = lax.broadcasted_iota(jnp.int32, (tok_dev, tok_dev), 0) == lax.broadcasted_iota(
        jnp.int32, (tok_dev, tok_dev), 1
    )
    for place in range(pieces):
        back = pieces - 1 - place
        start = pl.multiple_of(jnp.maximum(line - back, 0) * tok_dev, tok_dev)
        every = segment_ref[:, pl.ds(start, tok_dev)].astype(jnp.float32)
        mine = lax.broadcasted_iota(jnp.int32, every.shape, 0) == sequence
        row = jnp.sum(jnp.where(mine, every, 0.0), axis=0, keepdims=True)
        column = jnp.sum(jnp.where(eye, row, 0.0), axis=1, keepdims=True)
        column = jnp.where(line >= back, column, -1.0)
        column_ref[place * tok_dev : (place + 1) * tok_dev, :] = jnp.broadcast_to(
            column, (tok_dev, lanes)
        )

    def token(shape):
        return lax.rem(lax.broadcasted_iota(jnp.int32, shape, 1), jnp.int32(rows))

    here = pl.multiple_of(keys - tok_dev + source * rows, rows)
    asked_rows = column_ref[pl.ds(here, rows), :]
    same = lax.broadcasted_iota(jnp.int32, (rows, lanes), 0) == token((rows, lanes))
    asked = jnp.sum(jnp.where(same, asked_rows, 0.0), axis=0, keepdims=True)
    held = column_ref[pl.ds(pl.multiple_of(here - reach, rows), window), :]
    place = lax.broadcasted_iota(jnp.int32, (window, lanes), 0)
    allowed = (held == asked) & (place <= token((window, lanes)) + reach)
    bias_ref[...] = jnp.where(allowed, 0.0, BIG_NEGATIVE)


def attend_kernel(
    step, first, filled, last, tok_dev, reach, ratio,
    meta_ref, assign_ref, segment_ref, query_ref, grad_ref, kv_ref, *refs,
):
    refs = list(refs)
    if not first:
        acc_in_ref = refs.pop(0)
    if filled:
        refs.pop(0)
    query_out_ref = refs.pop(0)
    column_ref, bias_ref = refs[-2 - last], refs[-1 - last]
    if last:
        own_ref, halo_refs, acc_ref = refs[0], refs[1:-3], refs[-1]
    else:
        acc_ref = refs[0]

    rows = query_ref.shape[0]
    window = bias_ref.shape[0]
    keys = column_ref.shape[0]
    scale = 1.0 / HD**0.5
    group = meta_ref[0]
    source = source_of(group, step, tok_dev // rows)
    block = (keys - tok_dev - reach) // rows + source
    span = pl.ds(pl.multiple_of(block * rows, rows), window)

    @pl.when(pl.program_id(0) == 0)
    def _():
        build_bias(
            source, assign_ref[group], meta_ref[1], segment_ref, column_ref, bias_ref, rows, tok_dev, reach
        )

    acc_ref[...] = jnp.zeros_like(acc_ref) if first else acc_in_ref[...]
    turned = (((1,), (1,)), ((), ()))
    grads = []
    for head in range(HEADS_STEP):
        lanes = slice(head * HD, (head + 1) * HD)

        def stacked(ref):
            start = head * ratio
            return jnp.concatenate(
                [ref[:, r * HD : (r + 1) * HD] for r in range(start, start + ratio)], axis=0
            )

        def windowed(which):
            return kv_ref[pl.ds(block, window // rows), which, :, lanes].reshape(window, HD)

        query, grad = stacked(query_ref), stacked(grad_ref)
        key, value = windowed(0), windowed(1)
        scores = lax.dot_general(key, query, turned, preferred_element_type=jnp.float32)
        scores = scores * (scale * LOG2E) + bias_ref[...]
        top = jnp.max(scores, axis=0, keepdims=True)
        weights = jnp.exp2(scores - top)
        probs = weights * (1.0 / jnp.sum(weights, axis=0, keepdims=True))
        grad_probs = lax.dot_general(value, grad, turned, preferred_element_type=jnp.float32)
        product = probs * grad_probs
        delta = jnp.sum(product, axis=0, keepdims=True)
        grad_scores = (product - probs * delta).astype(jnp.bfloat16)
        grad_value = jnp.dot(
            probs.astype(jnp.bfloat16), grad, preferred_element_type=jnp.float32
        )
        grad_key = jnp.dot(grad_scores, query, preferred_element_type=jnp.float32)
        grad_query = lax.dot_general(
            grad_scores, key, (((0,), (0,)), ((), ())), preferred_element_type=jnp.float32
        )
        grads.append((grad_query * scale).reshape(ratio, rows, HD))
        acc_ref[0, span, lanes] += grad_key
        acc_ref[1, span, lanes] += grad_value
    if last:
        own_ref[0] = acc_ref[0, keys - tok_dev :] * scale
        own_ref[1] = acc_ref[1, keys - tok_dev :]
        for back, halo_ref in enumerate(halo_refs, 1):
            part = slice(keys - (back + 1) * tok_dev, keys - back * tok_dev)
            halo_ref[0] = (acc_ref[0, part] * scale).astype(jnp.bfloat16)
            halo_ref[1] = acc_ref[1, part].astype(jnp.bfloat16)
    query_out_ref[...] = jnp.swapaxes(jnp.concatenate(grads, axis=0), 0, 1).astype(jnp.bfloat16)


def attend(step, base, span, reach, heads, meta, assignment, segments, query, grad, kv, acc, full, last):
    first, filled = acc is None, full is not None
    rows, (blocks, _, _, kv_width) = query[0].shape[1], kv.shape
    ratio = heads // (kv_width // HD)
    keys, tok_dev = blocks * rows, query[0].shape[1] * lax.axis_size("dp")
    pieces, window = keys // tok_dev, reach + rows
    lanes, place = HEADS_STEP * HD, base // HEADS_STEP

    def rows_spec(array, pick):
        start = place if array.shape[2] == heads * HD else 0
        return pl.BlockSpec(
            (None, rows, HEADS_STEP * ratio * HD), lambda c, m, a: (pick(m, a), 0, start + c)
        )

    in_specs = [
        pl.BlockSpec(segments.shape, lambda c, m, a: (0, 0)),
        rows_spec(*query),
        rows_spec(*grad),
    ]
    in_specs.append(pl.BlockSpec((blocks, 2, rows, lanes), lambda c, m, a: (0, 0, 0, place + c)))
    operands = [meta, assignment, segments, query[0], grad[0], kv]
    aliases = {}
    acc_spec = pl.BlockSpec((2, keys, lanes), lambda c, m, a: (0, 0, place + c))
    if not first:
        if not last:
            aliases[len(operands)] = 1
        operands.append(acc)
        in_specs.append(acc_spec)
    if filled:
        aliases[len(operands)] = 0
        operands.append(full)
        in_specs.append(pl.BlockSpec(memory_space=pl.ANY))
    out_shape = [jax.ShapeDtypeStruct((tok_dev, heads, HD), jnp.bfloat16)]
    out_specs = [
        pl.BlockSpec(
            (rows, HEADS_STEP * ratio, HD),
            lambda c, m, a: (source_of(m[0], step, tok_dev // rows), place + c, 0),
        )
    ]
    if last:
        span_spec = pl.BlockSpec((2, tok_dev, lanes), lambda c, m, a: (0, 0, c))
        out_shape.append(jax.ShapeDtypeStruct((2, tok_dev, span * HD), jnp.float32))
        out_shape += [jax.ShapeDtypeStruct((2, tok_dev, span * HD), jnp.bfloat16)] * (pieces - 1)
        out_specs += [span_spec] * pieces
    else:
        out_shape.append(jax.ShapeDtypeStruct((2, keys, kv_width), jnp.float32))
        out_specs.append(acc_spec)
    pairs = span * ratio * rows * window
    cost = CALL_COST if step and not last else 1
    held = (keys, ratio * rows), (window, ratio * rows)
    held += ((2, keys, lanes),) * last
    return pl.pallas_call(
        functools.partial(attend_kernel, step, first, filled, last, tok_dev, reach, ratio),
        out_shape=out_shape,
        grid_spec=pltpu.PrefetchScalarGridSpec(
            num_scalar_prefetch=2,
            grid=(span // HEADS_STEP,),
            in_specs=in_specs,
            out_specs=out_specs,
            scratch_shapes=[pltpu.VMEM(shape, jnp.float32) for shape in held],
        ),
        input_output_aliases=aliases,
        compiler_params=pltpu.CompilerParams(
            dimension_semantics=("arbitrary",), vmem_limit_bytes=VMEM_BYTES
        ),
        cost_estimate=pl.CostEstimate(
            flops=pairs * HD * cost, bytes_accessed=pairs * cost, transcendentals=0
        ),
        name="attend",
    )(*operands)


def shards(queries, keys, values, grad_out, segment_ids, assignment):
    count = lax.axis_size("dp")
    uly = lax.axis_size("uly")
    group = lax.axis_index("dp")
    line = lax.axis_index("blk") * uly + lax.axis_index("uly")
    width, kv_width = queries.shape[2], keys.shape[2]
    heads, kv_heads = width // HD, kv_width // HD
    tok_dev = count * queries.shape[1]
    doc_most = min(512, tok_dev * uly)
    hops = -(-doc_most // tok_dev)
    meta = jnp.stack([group, line]).astype(jnp.int32)

    final, halves = count // 2, kv_heads // HEADS_STEP
    part = width // halves
    others = [step for step in range(1, count) if step != final]
    jobs = [(2, step, 0, kv_width) for step in range(count)]
    jobs += [(0, step, 0, width) for step in others]
    jobs += [(0, final, half * part, part) for half in range(halves)]
    staged = stage(assignment, (queries, grad_out, keys, values), jobs)
    kv_staged, staged = staged[:count], list(staged[count:])
    kv_arrived = [exchanged(kv_staged[step], "dp", step) for step in range(1, count)]
    staged, kv_arrived[0] = lax.optimization_barrier((staged, kv_arrived[0]))
    arrived = [exchanged(rows, "dp", step) for rows, step in zip(staged, others)]
    held = staged[len(others) :]
    kv_own = jnp.zeros((count, *kv_staged[0].shape), keys.dtype)
    for step, piece in enumerate([kv_staged[0], *kv_arrived]):
        kv_own = lax.dynamic_update_index_in_dim(
            kv_own, piece, source_of(group, step, count), 0
        )
    halos = [shifted(kv_own, ("blk", "uly"), back) for back in range(hops, 0, -1)]
    kv = jnp.concatenate([*halos, kv_own], axis=0)

    fixed = (doc_most, heads, meta, assignment, segment_ids)
    query, grad = (queries, lambda m, a: a[m[0]]), (grad_out, lambda m, a: a[m[0]])
    full, acc = attend(0, 0, kv_heads, *fixed, query, grad, kv, None, None, False)
    rows, acc = lax.optimization_barrier((held[0], acc))
    split = [exchanged(rows, "dp", final)]
    for step, both in zip(others, arrived):
        query, grad = (both, lambda m, a: 0), (both, lambda m, a: 1)
        full, acc = attend(step, 0, kv_heads, *fixed, query, grad, kv, acc, full, False)
    for rows in held[1:]:
        rows, split[-1], acc = lax.optimization_barrier((rows, split[-1], acc))
        split.append(exchanged(rows, "dp", final))
    totals, returned = [], []
    for half, both in enumerate(split):
        query, grad = (both, lambda m, a: 0), (both, lambda m, a: 1)
        full, total, *halos = attend(
            final, half * HEADS_STEP, HEADS_STEP, *fixed, query, grad, kv, acc, full, True
        )
        if half:
            halos, returned[0] = lax.optimization_barrier((halos, returned[0]))
        returned = [shifted(halo, ("blk", "uly"), -back) for back, halo in enumerate(halos, 1)]
        for halo in returned:
            total = total + halo.astype(jnp.float32)
        totals.append(total.astype(jnp.bfloat16))
    total = jnp.concatenate(totals, axis=2)
    return full[None], total[0][None], total[1][None]


def solution(mesh):
    in_specs = (
        P(None, ("blk", "uly", "dp"), None),
        P(None, ("blk", "uly", "dp"), None),
        P(None, ("blk", "uly", "dp"), None),
        P(None, ("blk", "uly", "dp"), None),
        P(),
        P(),
    )
    out_specs = (
        P("dp", ("blk", "uly"), None, None),
        P("dp", ("blk", "uly"), None),
        P("dp", ("blk", "uly"), None),
    )
    return jax.shard_map(shards, mesh=mesh, in_specs=in_specs, out_specs=out_specs, check_vma=False)
```

```python
import functools

import jax
import jax.numpy as jnp
from jax import lax
from jax.experimental import pallas as pl
from jax.experimental.pallas import tpu as pltpu
from jax.sharding import PartitionSpec as P

HD = 128
LOG2E = 1.4426950408889634
BIG_NEGATIVE = -1e30
VMEM_BYTES = 32 * 1024 * 1024
HEADS_STEP = 2


def target_of(index, step, count):
    return lax.rem(index + step, count)


def source_of(index, step, count):
    return lax.rem(index + count - step, count)


def exchanged(value, axis, step):
    count = lax.axis_size(axis)
    return lax.ppermute(value, axis, [(i, (i + step) % count) for i in range(count)])


def shifted(value, axis, by):
    length = lax.axis_size(axis)
    pairs = [(i, i + by) for i in range(length) if 0 <= i + by < length]
    return lax.ppermute(value, axis, pairs)


def stage_kernel(count, jobs, outs, assign_ref, *refs):
    group = lax.axis_index("dp")
    sources, refs = refs[:4], refs[4:]
    out_refs, held_refs, (in_sems, out_sems) = refs[:outs], refs[outs : 2 * outs], refs[-2:]
    loads, stores = [], []
    for out, (first, step, start, width) in enumerate(jobs):
        chosen = assign_ref[target_of(group, step, count)]
        for which in range(2):
            origin = sources[first + which].at[chosen, :, start : start + width]
            held, slot = held_refs[out].at[which], 2 * out + which
            loads.append(pltpu.make_async_copy(origin, held, in_sems.at[slot]))
            stores.append(pltpu.make_async_copy(held, out_refs[out].at[which], out_sems.at[slot]))
    for load in loads:
        load.start()
    for load, store in zip(loads, stores):
        load.wait()
        store.start()
    for store in stores:
        store.wait()


def stage(assignment, arrays, jobs):
    count, rows, _ = arrays[0].shape
    shapes = [(2, rows, width) for _, _, _, width in jobs]
    kind = arrays[0].dtype
    far = pl.BlockSpec(memory_space=pltpu.HBM)
    return pl.pallas_call(
        functools.partial(stage_kernel, count, jobs, len(jobs)),
        out_shape=[jax.ShapeDtypeStruct(shape, kind) for shape in shapes],
        in_specs=[pl.BlockSpec(memory_space=pltpu.SMEM)] + [far] * len(arrays),
        out_specs=[far] * len(jobs),
        scratch_shapes=[pltpu.VMEM(shape, kind) for shape in shapes]
        + [pltpu.SemaphoreType.DMA((2 * len(jobs),))] * 2,
        name="stage",
    )(assignment, *arrays)


def build_bias(source, sequence, line, segment_ref, column_ref, bias_ref, rows, tok_dev, reach):
    keys, lanes = column_ref.shape
    pieces = keys // tok_dev
    window = bias_ref.shape[0]
    eye = lax.broadcasted_iota(jnp.int32, (tok_dev, tok_dev), 0) == lax.broadcasted_iota(
        jnp.int32, (tok_dev, tok_dev), 1
    )
    for place in range(pieces):
        back = pieces - 1 - place
        start = pl.multiple_of(jnp.maximum(line - back, 0) * tok_dev, tok_dev)
        every = segment_ref[:, pl.ds(start, tok_dev)].astype(jnp.float32)
        mine = lax.broadcasted_iota(jnp.int32, every.shape, 0) == sequence
        row = jnp.sum(jnp.where(mine, every, 0.0), axis=0, keepdims=True)
        column = jnp.sum(jnp.where(eye, row, 0.0), axis=1, keepdims=True)
        column = jnp.where(line >= back, column, -1.0)
        column_ref[place * tok_dev : (place + 1) * tok_dev, :] = jnp.broadcast_to(
            column, (tok_dev, lanes)
        )

    def token(shape):
        return lax.rem(lax.broadcasted_iota(jnp.int32, shape, 1), jnp.int32(rows))

    here = pl.multiple_of(keys - tok_dev + source * rows, rows)
    asked_rows = column_ref[pl.ds(here, rows), :]
    same = lax.broadcasted_iota(jnp.int32, (rows, lanes), 0) == token((rows, lanes))
    asked = jnp.sum(jnp.where(same, asked_rows, 0.0), axis=0, keepdims=True)
    held = column_ref[pl.ds(pl.multiple_of(here - reach, rows), window), :]
    place = lax.broadcasted_iota(jnp.int32, (window, lanes), 0)
    allowed = (held == asked) & (place <= token((window, lanes)) + reach)
    bias_ref[...] = jnp.where(allowed, 0.0, BIG_NEGATIVE)


def attend_kernel(
    step, first, filled, last, tok_dev, reach, ratio,
    meta_ref, assign_ref, segment_ref, query_ref, grad_ref, kv_ref, *refs,
):
    refs = list(refs)
    if not first:
        acc_in_ref = refs.pop(0)
    if filled:
        refs.pop(0)
    query_out_ref = refs.pop(0)
    column_ref, bias_ref = refs[-2 - last], refs[-1 - last]
    if last:
        own_ref, halo_refs, acc_ref = refs[0], refs[1:-3], refs[-1]
    else:
        acc_ref = refs[0]

    rows = query_ref.shape[0]
    window = bias_ref.shape[0]
    keys = column_ref.shape[0]
    scale = 1.0 / HD**0.5
    group = meta_ref[0]
    source = source_of(group, step, tok_dev // rows)
    block = (keys - tok_dev - reach) // rows + source
    span = pl.ds(pl.multiple_of(block * rows, rows), window)

    @pl.when(pl.program_id(0) == 0)
    def _():
        build_bias(
            source, assign_ref[group], meta_ref[1], segment_ref, column_ref, bias_ref, rows, tok_dev, reach
        )

    acc_ref[...] = jnp.zeros_like(acc_ref) if first else acc_in_ref[...]
    turned = (((1,), (1,)), ((), ()))
    grads = []
    for head in range(HEADS_STEP):
        lanes = slice(head * HD, (head + 1) * HD)

        def stacked(ref):
            start = head * ratio
            return jnp.concatenate(
                [ref[:, r * HD : (r + 1) * HD] for r in range(start, start + ratio)], axis=0
            )

        def windowed(which):
            return kv_ref[pl.ds(block, window // rows), which, :, lanes].reshape(window, HD)

        query, grad = stacked(query_ref), stacked(grad_ref)
        key, value = windowed(0), windowed(1)
        scores = lax.dot_general(key, query, turned, preferred_element_type=jnp.float32)
        scores = scores * (scale * LOG2E) + bias_ref[...]
        top = jnp.max(scores, axis=0, keepdims=True)
        weights = jnp.exp2(scores - top)
        probs = weights * (1.0 / jnp.sum(weights, axis=0, keepdims=True))
        grad_probs = lax.dot_general(value, grad, turned, preferred_element_type=jnp.float32)
        product = probs * grad_probs
        delta = jnp.sum(product, axis=0, keepdims=True)
        grad_scores = (product - probs * delta).astype(jnp.bfloat16)
        grad_value = jnp.dot(
            probs.astype(jnp.bfloat16), grad, preferred_element_type=jnp.float32
        )
        grad_key = jnp.dot(grad_scores, query, preferred_element_type=jnp.float32)
        grad_query = lax.dot_general(
            grad_scores, key, (((0,), (0,)), ((), ())), preferred_element_type=jnp.float32
        )
        grads.append((grad_query * scale).reshape(ratio, rows, HD))
        acc_ref[0, span, lanes] += grad_key
        acc_ref[1, span, lanes] += grad_value
    if last:
        own_ref[0] = acc_ref[0, keys - tok_dev :] * scale
        own_ref[1] = acc_ref[1, keys - tok_dev :]
        for back, halo_ref in enumerate(halo_refs, 1):
            part = slice(keys - (back + 1) * tok_dev, keys - back * tok_dev)
            halo_ref[0] = (acc_ref[0, part] * scale).astype(jnp.bfloat16)
            halo_ref[1] = acc_ref[1, part].astype(jnp.bfloat16)
    query_out_ref[...] = jnp.swapaxes(jnp.concatenate(grads, axis=0), 0, 1).astype(jnp.bfloat16)


def attend(step, base, span, reach, heads, meta, assignment, segments, query, grad, kv, acc, full, last):
    first, filled = acc is None, full is not None
    rows, (blocks, _, _, kv_width) = query[0].shape[1], kv.shape
    ratio = heads // (kv_width // HD)
    keys, tok_dev = blocks * rows, query[0].shape[1] * lax.axis_size("dp")
    pieces, window = keys // tok_dev, reach + rows
    lanes, place = HEADS_STEP * HD, base // HEADS_STEP

    def rows_spec(array, pick):
        start = place if array.shape[2] == heads * HD else 0
        return pl.BlockSpec(
            (None, rows, HEADS_STEP * ratio * HD), lambda c, m, a: (pick(m, a), 0, start + c)
        )

    in_specs = [
        pl.BlockSpec(segments.shape, lambda c, m, a: (0, 0)),
        rows_spec(*query),
        rows_spec(*grad),
    ]
    in_specs.append(pl.BlockSpec((blocks, 2, rows, lanes), lambda c, m, a: (0, 0, 0, place + c)))
    operands = [meta, assignment, segments, query[0], grad[0], kv]
    aliases = {}
    acc_spec = pl.BlockSpec((2, keys, lanes), lambda c, m, a: (0, 0, place + c))
    if not first:
        if not last:
            aliases[len(operands)] = 1
        operands.append(acc)
        in_specs.append(acc_spec)
    if filled:
        aliases[len(operands)] = 0
        operands.append(full)
        in_specs.append(pl.BlockSpec(memory_space=pl.ANY))
    out_shape = [jax.ShapeDtypeStruct((tok_dev, heads, HD), jnp.bfloat16)]
    out_specs = [
        pl.BlockSpec(
            (rows, HEADS_STEP * ratio, HD),
            lambda c, m, a: (source_of(m[0], step, tok_dev // rows), place + c, 0),
        )
    ]
    if last:
        span_spec = pl.BlockSpec((2, tok_dev, lanes), lambda c, m, a: (0, 0, c))
        out_shape.append(jax.ShapeDtypeStruct((2, tok_dev, span * HD), jnp.float32))
        out_shape += [jax.ShapeDtypeStruct((2, tok_dev, span * HD), jnp.bfloat16)] * (pieces - 1)
        out_specs += [span_spec] * pieces
    else:
        out_shape.append(jax.ShapeDtypeStruct((2, keys, kv_width), jnp.float32))
        out_specs.append(acc_spec)
    pairs = span * ratio * rows * window
    held = (keys, ratio * rows), (window, ratio * rows)
    held += ((2, keys, lanes),) * last
    return pl.pallas_call(
        functools.partial(attend_kernel, step, first, filled, last, tok_dev, reach, ratio),
        out_shape=out_shape,
        grid_spec=pltpu.PrefetchScalarGridSpec(
            num_scalar_prefetch=2,
            grid=(span // HEADS_STEP,),
            in_specs=in_specs,
            out_specs=out_specs,
            scratch_shapes=[pltpu.VMEM(shape, jnp.float32) for shape in held],
        ),
        input_output_aliases=aliases,
        compiler_params=pltpu.CompilerParams(
            dimension_semantics=("arbitrary",), vmem_limit_bytes=VMEM_BYTES
        ),
        cost_estimate=pl.CostEstimate(
            flops=pairs * HD, bytes_accessed=pairs, transcendentals=0
        ),
        name="attend",
    )(*operands)


def shards(queries, keys, values, grad_out, segment_ids, assignment):
    count = lax.axis_size("dp")
    uly = lax.axis_size("uly")
    group = lax.axis_index("dp")
    line = lax.axis_index("blk") * uly + lax.axis_index("uly")
    width, kv_width = queries.shape[2], keys.shape[2]
    heads, kv_heads = width // HD, kv_width // HD
    tok_dev = count * queries.shape[1]
    doc_most = min(512, tok_dev * uly)
    hops = -(-doc_most // tok_dev)
    meta = jnp.stack([group, line]).astype(jnp.int32)

    final, halves = count // 2, kv_heads // HEADS_STEP
    part = width // halves
    others = [step for step in range(1, count) if step != final]
    jobs = [(2, step, 0, kv_width) for step in range(count)]
    jobs += [(0, step, 0, width) for step in others]
    jobs += [(0, final, half * part, part) for half in range(halves)]
    staged = stage(assignment, (queries, grad_out, keys, values), jobs)
    kv_staged, staged = staged[:count], list(staged[count:])
    kv_arrived = [exchanged(kv_staged[step], "dp", step) for step in range(1, count)]
    staged, kv_arrived[0] = lax.optimization_barrier((staged, kv_arrived[0]))
    arrived = [exchanged(rows, "dp", step) for rows, step in zip(staged, others)]
    held = staged[len(others) :]
    kv_own = jnp.zeros((count, *kv_staged[0].shape), keys.dtype)
    for step, piece in enumerate([kv_staged[0], *kv_arrived]):
        kv_own = lax.dynamic_update_index_in_dim(
            kv_own, piece, source_of(group, step, count), 0
        )
    halos = [shifted(kv_own, ("blk", "uly"), back) for back in range(hops, 0, -1)]
    kv = jnp.concatenate([*halos, kv_own], axis=0)

    fixed = (doc_most, heads, meta, assignment, segment_ids)
    pairs = [(step, (both, lambda m, a: 0), (both, lambda m, a: 1)) for step, both in zip(others, arrived)]
    pairs.append((0, (queries, lambda m, a: a[m[0]]), (grad_out, lambda m, a: a[m[0]])))
    full, acc, split = None, None, []
    for step, query, grad in pairs:
        full, acc = attend(step, 0, kv_heads, *fixed, query, grad, kv, acc, full, False)
        if not split:
            rows, acc = lax.optimization_barrier((held[0], acc))
            split = [exchanged(rows, "dp", final)]
    for rows in held[1:]:
        rows, acc = lax.optimization_barrier((rows, acc))
        split.append(exchanged(rows, "dp", final))
    totals, returned = [], []
    for half, both in enumerate(split):
        query, grad = (both, lambda m, a: 0), (both, lambda m, a: 1)
        full, total, *halos = attend(
            final, half * HEADS_STEP, HEADS_STEP, *fixed, query, grad, kv, acc, full, True
        )
        if half:
            halos, returned[0] = lax.optimization_barrier((halos, returned[0]))
        returned = [shifted(halo, ("blk", "uly"), -back) for back, halo in enumerate(halos, 1)]
        for halo in returned:
            total = total + halo.astype(jnp.float32)
        totals.append(total.astype(jnp.bfloat16))
    total = jnp.concatenate(totals, axis=2)
    return full[None], total[0][None], total[1][None]


def solution(mesh):
    in_specs = (
        P(None, ("blk", "uly", "dp"), None),
        P(None, ("blk", "uly", "dp"), None),
        P(None, ("blk", "uly", "dp"), None),
        P(None, ("blk", "uly", "dp"), None),
        P(),
        P(),
    )
    out_specs = (
        P("dp", ("blk", "uly"), None, None),
        P("dp", ("blk", "uly"), None),
        P("dp", ("blk", "uly"), None),
    )
    return jax.shard_map(shards, mesh=mesh, in_specs=in_specs, out_specs=out_specs, check_vma=False)
```

```python
import functools

import jax
import jax.numpy as jnp
from jax import lax
from jax.experimental import pallas as pl
from jax.experimental.pallas import tpu as pltpu
from jax.sharding import PartitionSpec as P

HD = 128
LOG2E = 1.4426950408889634
BIG_NEGATIVE = -1e30
VMEM_BYTES = 32 * 1024 * 1024
HEADS_STEP = 2
CALL_COST = (1, 1, 1, 100)


def target_of(index, step, count):
    return lax.rem(index + step, count)


def source_of(index, step, count):
    return lax.rem(index + count - step, count)


def exchanged(value, axis, step):
    count = lax.axis_size(axis)
    return lax.ppermute(value, axis, [(i, (i + step) % count) for i in range(count)])


def shifted(value, axis, by):
    length = lax.axis_size(axis)
    pairs = [(i, i + by) for i in range(length) if 0 <= i + by < length]
    return lax.ppermute(value, axis, pairs)


def stage_kernel(count, jobs, outs, assign_ref, *refs):
    group = lax.axis_index("dp")
    sources, refs = refs[:4], refs[4:]
    out_refs, held_refs, (in_sems, out_sems) = refs[:outs], refs[outs : 2 * outs], refs[-2:]
    loads, stores = [], []
    for out, (first, step, start, width, *_) in enumerate(jobs):
        chosen = assign_ref[target_of(group, step, count)]
        for which in range(out_refs[out].shape[0]):
            origin = sources[first + which].at[chosen, :, start : start + width]
            held, slot = held_refs[out].at[which], 2 * out + which
            loads.append(pltpu.make_async_copy(origin, held, in_sems.at[slot]))
            stores.append(pltpu.make_async_copy(held, out_refs[out].at[which], out_sems.at[slot]))
    for load in loads:
        load.start()
    for load, store in zip(loads, stores):
        load.wait()
        store.start()
    for store in stores:
        store.wait()


def stage(assignment, arrays, jobs):
    count, rows, _ = arrays[0].shape
    shapes = [(job[4] if len(job) > 4 else 2, rows, job[3]) for job in jobs]
    kind = arrays[0].dtype
    far = pl.BlockSpec(memory_space=pltpu.HBM)
    return pl.pallas_call(
        functools.partial(stage_kernel, count, jobs, len(jobs)),
        out_shape=[jax.ShapeDtypeStruct(shape, kind) for shape in shapes],
        in_specs=[pl.BlockSpec(memory_space=pltpu.SMEM)] + [far] * len(arrays),
        out_specs=[far] * len(jobs),
        scratch_shapes=[pltpu.VMEM(shape, kind) for shape in shapes]
        + [pltpu.SemaphoreType.DMA((2 * len(jobs),))] * 2,
        name="stage",
    )(assignment, *arrays)


def build_bias(source, sequence, line, segment_ref, column_ref, bias_ref, rows, tok_dev, reach):
    keys, lanes = column_ref.shape
    pieces = keys // tok_dev
    window = bias_ref.shape[0]
    eye = lax.broadcasted_iota(jnp.int32, (tok_dev, tok_dev), 0) == lax.broadcasted_iota(
        jnp.int32, (tok_dev, tok_dev), 1
    )
    for place in range(pieces):
        back = pieces - 1 - place
        start = pl.multiple_of(jnp.maximum(line - back, 0) * tok_dev, tok_dev)
        every = segment_ref[:, pl.ds(start, tok_dev)].astype(jnp.float32)
        mine = lax.broadcasted_iota(jnp.int32, every.shape, 0) == sequence
        row = jnp.sum(jnp.where(mine, every, 0.0), axis=0, keepdims=True)
        column = jnp.sum(jnp.where(eye, row, 0.0), axis=1, keepdims=True)
        column = jnp.where(line >= back, column, -1.0)
        column_ref[place * tok_dev : (place + 1) * tok_dev, :] = jnp.broadcast_to(
            column, (tok_dev, lanes)
        )

    def token(shape):
        return lax.rem(lax.broadcasted_iota(jnp.int32, shape, 1), jnp.int32(rows))

    here = pl.multiple_of(keys - tok_dev + source * rows, rows)
    asked_rows = column_ref[pl.ds(here, rows), :]
    same = lax.broadcasted_iota(jnp.int32, (rows, lanes), 0) == token((rows, lanes))
    asked = jnp.sum(jnp.where(same, asked_rows, 0.0), axis=0, keepdims=True)
    held = column_ref[pl.ds(pl.multiple_of(here - reach, rows), window), :]
    place = lax.broadcasted_iota(jnp.int32, (window, lanes), 0)
    allowed = (held == asked) & (place <= token((window, lanes)) + reach)
    bias_ref[...] = jnp.where(allowed, 0.0, BIG_NEGATIVE)


def attend_kernel(
    step, first, filled, last, tok_dev, reach, ratio,
    meta_ref, assign_ref, segment_ref, query_ref, grad_ref, kv_ref, *refs,
):
    refs = list(refs)
    if not first:
        acc_in_ref = refs.pop(0)
    if filled:
        refs.pop(0)
    query_out_ref = refs.pop(0)
    column_ref, bias_ref = refs[-2 - last], refs[-1 - last]
    if last:
        own_ref, halo_refs, acc_ref = refs[0], refs[1:-3], refs[-1]
    else:
        acc_ref = refs[0]

    rows = query_ref.shape[0]
    window = bias_ref.shape[0]
    keys = column_ref.shape[0]
    scale = 1.0 / HD**0.5
    group = meta_ref[0]
    source = source_of(group, step, tok_dev // rows)
    block = (keys - tok_dev - reach) // rows + source
    span = pl.ds(pl.multiple_of(block * rows, rows), window)

    @pl.when(pl.program_id(0) == 0)
    def _():
        build_bias(
            source, assign_ref[group], meta_ref[1], segment_ref, column_ref, bias_ref, rows, tok_dev, reach
        )

    acc_ref[...] = jnp.zeros_like(acc_ref) if first else acc_in_ref[...]
    turned = (((1,), (1,)), ((), ()))
    grads = []
    for head in range(HEADS_STEP):
        lanes = slice(head * HD, (head + 1) * HD)

        def stacked(ref):
            start = head * ratio
            return jnp.concatenate(
                [ref[:, r * HD : (r + 1) * HD] for r in range(start, start + ratio)], axis=0
            )

        def windowed(which):
            return kv_ref[pl.ds(block, window // rows), which, :, lanes].reshape(window, HD)

        query, grad = stacked(query_ref), stacked(grad_ref)
        key, value = windowed(0), windowed(1)
        scores = lax.dot_general(key, query, turned, preferred_element_type=jnp.float32)
        scores = scores * (scale * LOG2E) + bias_ref[...]
        top = jnp.max(scores, axis=0, keepdims=True)
        weights = jnp.exp2(scores - top)
        probs = weights * (1.0 / jnp.sum(weights, axis=0, keepdims=True))
        grad_probs = lax.dot_general(value, grad, turned, preferred_element_type=jnp.float32)
        product = probs * grad_probs
        delta = jnp.sum(product, axis=0, keepdims=True)
        grad_scores = (product - probs * delta).astype(jnp.bfloat16)
        grad_value = jnp.dot(
            probs.astype(jnp.bfloat16), grad, preferred_element_type=jnp.float32
        )
        grad_key = jnp.dot(grad_scores, query, preferred_element_type=jnp.float32)
        grad_query = lax.dot_general(
            grad_scores, key, (((0,), (0,)), ((), ())), preferred_element_type=jnp.float32
        )
        grads.append((grad_query * scale).reshape(ratio, rows, HD))
        acc_ref[0, span, lanes] += grad_key
        acc_ref[1, span, lanes] += grad_value
    if last:
        own_ref[0] = acc_ref[0, keys - tok_dev :] * scale
        own_ref[1] = acc_ref[1, keys - tok_dev :]
        for back, halo_ref in enumerate(halo_refs, 1):
            part = slice(keys - (back + 1) * tok_dev, keys - back * tok_dev)
            halo_ref[0] = (acc_ref[0, part] * scale).astype(jnp.bfloat16)
            halo_ref[1] = acc_ref[1, part].astype(jnp.bfloat16)
    query_out_ref[...] = jnp.swapaxes(jnp.concatenate(grads, axis=0), 0, 1).astype(jnp.bfloat16)


def attend(step, base, span, reach, heads, meta, assignment, segments, query, grad, kv, acc, full, last):
    first, filled = acc is None, full is not None
    rows, (blocks, _, _, kv_width) = query[0].shape[1], kv.shape
    ratio = heads // (kv_width // HD)
    keys, tok_dev = blocks * rows, query[0].shape[1] * lax.axis_size("dp")
    pieces, window = keys // tok_dev, reach + rows
    lanes, place = HEADS_STEP * HD, base // HEADS_STEP

    def rows_spec(array, pick):
        start = place if array.shape[2] == heads * HD else 0
        return pl.BlockSpec(
            (None, rows, HEADS_STEP * ratio * HD), lambda c, m, a: (pick(m, a), 0, start + c)
        )

    in_specs = [
        pl.BlockSpec(segments.shape, lambda c, m, a: (0, 0)),
        rows_spec(*query),
        rows_spec(*grad),
    ]
    in_specs.append(pl.BlockSpec((blocks, 2, rows, lanes), lambda c, m, a: (0, 0, 0, place + c)))
    operands = [meta, assignment, segments, query[0], grad[0], kv]
    aliases = {}
    acc_spec = pl.BlockSpec((2, keys, lanes), lambda c, m, a: (0, 0, place + c))
    if not first:
        if not last:
            aliases[len(operands)] = 1
        operands.append(acc)
        in_specs.append(acc_spec)
    if filled:
        aliases[len(operands)] = 0
        operands.append(full)
        in_specs.append(pl.BlockSpec(memory_space=pl.ANY))
    out_shape = [jax.ShapeDtypeStruct((tok_dev, heads, HD), jnp.bfloat16)]
    out_specs = [
        pl.BlockSpec(
            (rows, HEADS_STEP * ratio, HD),
            lambda c, m, a: (source_of(m[0], step, tok_dev // rows), place + c, 0),
        )
    ]
    if last:
        span_spec = pl.BlockSpec((2, tok_dev, lanes), lambda c, m, a: (0, 0, c))
        out_shape.append(jax.ShapeDtypeStruct((2, tok_dev, span * HD), jnp.float32))
        out_shape += [jax.ShapeDtypeStruct((2, tok_dev, span * HD), jnp.bfloat16)] * (pieces - 1)
        out_specs += [span_spec] * pieces
    else:
        out_shape.append(jax.ShapeDtypeStruct((2, keys, kv_width), jnp.float32))
        out_specs.append(acc_spec)
    pairs = span * ratio * rows * window
    cost = CALL_COST[step] if step < len(CALL_COST) and not last else 1
    held = (keys, ratio * rows), (window, ratio * rows)
    held += ((2, keys, lanes),) * last
    return pl.pallas_call(
        functools.partial(attend_kernel, step, first, filled, last, tok_dev, reach, ratio),
        out_shape=out_shape,
        grid_spec=pltpu.PrefetchScalarGridSpec(
            num_scalar_prefetch=2,
            grid=(span // HEADS_STEP,),
            in_specs=in_specs,
            out_specs=out_specs,
            scratch_shapes=[pltpu.VMEM(shape, jnp.float32) for shape in held],
        ),
        input_output_aliases=aliases,
        compiler_params=pltpu.CompilerParams(
            dimension_semantics=("arbitrary",), vmem_limit_bytes=VMEM_BYTES
        ),
        cost_estimate=pl.CostEstimate(
            flops=pairs * HD * cost, bytes_accessed=pairs * cost, transcendentals=0
        ),
        name="attend",
    )(*operands)


def shards(queries, keys, values, grad_out, segment_ids, assignment):
    count = lax.axis_size("dp")
    uly = lax.axis_size("uly")
    group = lax.axis_index("dp")
    line = lax.axis_index("blk") * uly + lax.axis_index("uly")
    width, kv_width = queries.shape[2], keys.shape[2]
    heads, kv_heads = width // HD, kv_width // HD
    tok_dev = count * queries.shape[1]
    doc_most = min(512, tok_dev * uly)
    hops = -(-doc_most // tok_dev)
    meta = jnp.stack([group, line]).astype(jnp.int32)

    final, halves = count // 2, kv_heads // HEADS_STEP
    part = width // halves
    others = [step for step in range(1, count) if step != final]
    jobs = [(2, step, 0, kv_width) for step in range(count)]
    jobs += [(0, step, 0, width) for step in others]
    jobs += [(0, final, half * part, part) for half in range(halves - 1)]
    jobs += [(which, final, (halves - 1) * part, part, 1) for which in range(2)]
    staged = stage(assignment, (queries, grad_out, keys, values), jobs)
    kv_staged, staged = staged[:count], list(staged[count:])
    kv_arrived = [exchanged(kv_staged[step], "dp", step) for step in range(1, count)]
    staged, kv_arrived[0] = lax.optimization_barrier((staged, kv_arrived[0]))
    arrived = [exchanged(rows, "dp", step) for rows, step in zip(staged, others)]
    held = staged[len(others) :]
    kv_own = jnp.zeros((count, *kv_staged[0].shape), keys.dtype)
    for step, piece in enumerate([kv_staged[0], *kv_arrived]):
        kv_own = lax.dynamic_update_index_in_dim(
            kv_own, piece, source_of(group, step, count), 0
        )
    halos = [shifted(kv_own, ("blk", "uly"), back) for back in range(hops, 0, -1)]
    kv = jnp.concatenate([*halos, kv_own], axis=0)

    fixed = (doc_most, heads, meta, assignment, segment_ids)
    query, grad = (queries, lambda m, a: a[m[0]]), (grad_out, lambda m, a: a[m[0]])
    full, acc = attend(0, 0, kv_heads, *fixed, query, grad, kv, None, None, False)
    rows, acc = lax.optimization_barrier((held[0], acc))
    split = [exchanged(rows, "dp", final)]
    for at, (step, both) in enumerate(zip(others, arrived)):
        query, grad = (both, lambda m, a: 0), (both, lambda m, a: 1)
        full, acc = attend(step, 0, kv_heads, *fixed, query, grad, kv, acc, full, False)
        if not at:
            rows, acc = lax.optimization_barrier((held[1:], acc))
            split += [exchanged(piece, "dp", final) for piece in rows]
    totals, returned = [], []
    for half in range(halves):
        both = split[half]
        query, grad = (both, lambda m, a: 0), (both, lambda m, a: 1)
        if half + 1 == halves:
            grad = (split[half + 1], lambda m, a: 0)
        full, total, *halos = attend(
            final, half * HEADS_STEP, HEADS_STEP, *fixed, query, grad, kv, acc, full, True
        )
        if half:
            halos, returned[0] = lax.optimization_barrier((halos, returned[0]))
        returned = [shifted(halo, ("blk", "uly"), -back) for back, halo in enumerate(halos, 1)]
        for halo in returned:
            total = total + halo.astype(jnp.float32)
        totals.append(total.astype(jnp.bfloat16))
    total = jnp.concatenate(totals, axis=2)
    return full[None], total[0][None], total[1][None]


def solution(mesh):
    in_specs = (
        P(None, ("blk", "uly", "dp"), None),
        P(None, ("blk", "uly", "dp"), None),
        P(None, ("blk", "uly", "dp"), None),
        P(None, ("blk", "uly", "dp"), None),
        P(),
        P(),
    )
    out_specs = (
        P("dp", ("blk", "uly"), None, None),
        P("dp", ("blk", "uly"), None),
        P("dp", ("blk", "uly"), None),
    )
    return jax.shard_map(shards, mesh=mesh, in_specs=in_specs, out_specs=out_specs, check_vma=False)
```

```python
import functools

import jax
import jax.numpy as jnp
from jax import lax
from jax.experimental import pallas as pl
from jax.experimental.pallas import tpu as pltpu
from jax.sharding import PartitionSpec as P

HD = 128
LOG2E = 1.4426950408889634
BIG_NEGATIVE = -1e30
VMEM_BYTES = 32 * 1024 * 1024
HEADS_STEP = 2
CALL_COST = (1, 1, 1, 100)


def target_of(index, step, count):
    return lax.rem(index + step, count)


def source_of(index, step, count):
    return lax.rem(index + count - step, count)


def exchanged(value, axis, step):
    count = lax.axis_size(axis)
    return lax.ppermute(value, axis, [(i, (i + step) % count) for i in range(count)])


def shifted(value, axis, by):
    length = lax.axis_size(axis)
    pairs = [(i, i + by) for i in range(length) if 0 <= i + by < length]
    return lax.ppermute(value, axis, pairs)


def stage_kernel(count, jobs, outs, assign_ref, *refs):
    group = lax.axis_index("dp")
    sources, refs = refs[:4], refs[4:]
    out_refs, held_refs, (in_sems, out_sems) = refs[:outs], refs[outs : 2 * outs], refs[-2:]
    loads, stores = [], []
    for out, (first, step, start, width, *_) in enumerate(jobs):
        chosen = assign_ref[target_of(group, step, count)]
        for which in range(out_refs[out].shape[0]):
            origin = sources[first + which].at[chosen, :, start : start + width]
            held, slot = held_refs[out].at[which], 2 * out + which
            loads.append(pltpu.make_async_copy(origin, held, in_sems.at[slot]))
            stores.append(pltpu.make_async_copy(held, out_refs[out].at[which], out_sems.at[slot]))
    for load in loads:
        load.start()
    for load, store in zip(loads, stores):
        load.wait()
        store.start()
    for store in stores:
        store.wait()


def stage(assignment, arrays, jobs):
    count, rows, _ = arrays[0].shape
    shapes = [(job[4] if len(job) > 4 else 2, rows, job[3]) for job in jobs]
    kind = arrays[0].dtype
    far = pl.BlockSpec(memory_space=pltpu.HBM)
    return pl.pallas_call(
        functools.partial(stage_kernel, count, jobs, len(jobs)),
        out_shape=[jax.ShapeDtypeStruct(shape, kind) for shape in shapes],
        in_specs=[pl.BlockSpec(memory_space=pltpu.SMEM)] + [far] * len(arrays),
        out_specs=[far] * len(jobs),
        scratch_shapes=[pltpu.VMEM(shape, kind) for shape in shapes]
        + [pltpu.SemaphoreType.DMA((2 * len(jobs),))] * 2,
        name="stage",
    )(assignment, *arrays)


def build_bias(source, sequence, line, segment_ref, column_ref, bias_ref, rows, tok_dev, reach):
    keys, lanes = column_ref.shape
    pieces = keys // tok_dev
    window = bias_ref.shape[0]
    eye = lax.broadcasted_iota(jnp.int32, (tok_dev, tok_dev), 0) == lax.broadcasted_iota(
        jnp.int32, (tok_dev, tok_dev), 1
    )
    for place in range(pieces):
        back = pieces - 1 - place
        start = pl.multiple_of(jnp.maximum(line - back, 0) * tok_dev, tok_dev)
        every = segment_ref[:, pl.ds(start, tok_dev)].astype(jnp.float32)
        mine = lax.broadcasted_iota(jnp.int32, every.shape, 0) == sequence
        row = jnp.sum(jnp.where(mine, every, 0.0), axis=0, keepdims=True)
        column = jnp.sum(jnp.where(eye, row, 0.0), axis=1, keepdims=True)
        column = jnp.where(line >= back, column, -1.0)
        column_ref[place * tok_dev : (place + 1) * tok_dev, :] = jnp.broadcast_to(
            column, (tok_dev, lanes)
        )

    def token(shape):
        return lax.rem(lax.broadcasted_iota(jnp.int32, shape, 1), jnp.int32(rows))

    here = pl.multiple_of(keys - tok_dev + source * rows, rows)
    asked_rows = column_ref[pl.ds(here, rows), :]
    same = lax.broadcasted_iota(jnp.int32, (rows, lanes), 0) == token((rows, lanes))
    asked = jnp.sum(jnp.where(same, asked_rows, 0.0), axis=0, keepdims=True)
    held = column_ref[pl.ds(pl.multiple_of(here - reach, rows), window), :]
    place = lax.broadcasted_iota(jnp.int32, (window, lanes), 0)
    allowed = (held == asked) & (place <= token((window, lanes)) + reach)
    bias_ref[...] = jnp.where(allowed, 0.0, BIG_NEGATIVE)


def attend_kernel(
    step, place, first, filled, last, tok_dev, reach, ratio,
    meta_ref, assign_ref, segment_ref, query_ref, grad_ref, kv_ref, *refs,
):
    refs = list(refs)
    if not first:
        acc_in_ref = refs.pop(0)
    if filled:
        refs.pop(0)
    query_out_ref = refs.pop(0)
    column_ref, bias_ref, fetch_sem = refs[-3 - last : len(refs) - last]
    if last:
        own_ref, halo_refs, acc_ref = refs[0], refs[1:-4], refs[-1]
    else:
        acc_ref = refs[0]

    rows = query_ref.shape[0]
    window = bias_ref.shape[0]
    keys = column_ref.shape[0]
    scale = 1.0 / HD**0.5
    group = meta_ref[0]
    source = source_of(group, step, tok_dev // rows)
    block = (keys - tok_dev - reach) // rows + source
    span = pl.ds(pl.multiple_of(block * rows, rows), window)

    @pl.when(pl.program_id(0) == 0)
    def _():
        build_bias(
            source, assign_ref[group], meta_ref[1], segment_ref, column_ref, bias_ref, rows, tok_dev, reach
        )

    if first:
        acc_ref[...] = jnp.zeros_like(acc_ref)
    else:
        start = pl.multiple_of((place + pl.program_id(0)) * HEADS_STEP * HD, HEADS_STEP * HD)
        fetch = pltpu.make_async_copy(
            acc_in_ref.at[:, :, pl.ds(start, HEADS_STEP * HD)], acc_ref, fetch_sem
        )
        fetch.start()
    turned, across = (((1,), (1,)), ((), ())), (((0,), (0,)), ((), ()))
    heads = range(HEADS_STEP)
    lanes = [slice(head * HD, (head + 1) * HD) for head in heads]

    def product(left, right, contract):
        return lax.dot_general(left, right, contract, preferred_element_type=jnp.float32)

    def stacked(ref, head):
        start = head * ratio
        return jnp.concatenate(
            [ref[:, r * HD : (r + 1) * HD] for r in range(start, start + ratio)], axis=0
        )

    def windowed(which, head):
        return kv_ref[pl.ds(block, window // rows), which, :, lanes[head]].reshape(window, HD)

    plain = (((1,), (0,)), ((), ()))
    query, key = [stacked(query_ref, head) for head in heads], [windowed(0, head) for head in heads]
    scores = [product(key[head], query[head], turned) for head in heads]
    grad, value = [stacked(grad_ref, head) for head in heads], [windowed(1, head) for head in heads]
    grad_probs = [product(value[head], grad[head], turned) for head in heads]
    probs, grad_scores = [], []
    for head in heads:
        score = scores[head] * (scale * LOG2E) + bias_ref[...]
        weights = jnp.exp2(score - jnp.max(score, axis=0, keepdims=True))
        probs.append(weights * (1.0 / jnp.sum(weights, axis=0, keepdims=True)))
    for head in heads:
        weighted = probs[head] * grad_probs[head]
        delta = jnp.sum(weighted, axis=0, keepdims=True)
        grad_scores.append((weighted - probs[head] * delta).astype(jnp.bfloat16))
    grads = []
    for head in heads:
        grad_query = product(grad_scores[head], key[head], across)
        grads.append((grad_query * scale).reshape(ratio, rows, HD))
    grad_key = [product(grad_scores[head], query[head], plain) for head in heads]
    grad_value = [product(probs[head].astype(jnp.bfloat16), grad[head], plain) for head in heads]
    if not first:
        fetch.wait()
    for head in heads:
        acc_ref[0, span, lanes[head]] += grad_key[head]
        acc_ref[1, span, lanes[head]] += grad_value[head]
    if last:
        own_ref[0] = acc_ref[0, keys - tok_dev :] * scale
        own_ref[1] = acc_ref[1, keys - tok_dev :]
        for back, halo_ref in enumerate(halo_refs, 1):
            part = slice(keys - (back + 1) * tok_dev, keys - back * tok_dev)
            halo_ref[0] = (acc_ref[0, part] * scale).astype(jnp.bfloat16)
            halo_ref[1] = acc_ref[1, part].astype(jnp.bfloat16)
    query_out_ref[...] = jnp.swapaxes(jnp.concatenate(grads, axis=0), 0, 1).astype(jnp.bfloat16)


def attend(step, base, span, reach, heads, meta, assignment, segments, query, grad, kv, acc, full, last):
    first, filled = acc is None, full is not None
    rows, (blocks, _, _, kv_width) = query[0].shape[1], kv.shape
    ratio = heads // (kv_width // HD)
    keys, tok_dev = blocks * rows, query[0].shape[1] * lax.axis_size("dp")
    pieces, window = keys // tok_dev, reach + rows
    lanes, place = HEADS_STEP * HD, base // HEADS_STEP

    def rows_spec(array, pick):
        start = place if array.shape[2] == heads * HD else 0
        return pl.BlockSpec(
            (None, rows, HEADS_STEP * ratio * HD), lambda c, m, a: (pick(m, a), 0, start + c)
        )

    in_specs = [
        pl.BlockSpec(segments.shape, lambda c, m, a: (0, 0)),
        rows_spec(*query),
        rows_spec(*grad),
    ]
    in_specs.append(pl.BlockSpec((blocks, 2, rows, lanes), lambda c, m, a: (0, 0, 0, place + c)))
    operands = [meta, assignment, segments, query[0], grad[0], kv]
    aliases = {}
    acc_spec = pl.BlockSpec((2, keys, lanes), lambda c, m, a: (0, 0, place + c))
    if not first:
        if not last:
            aliases[len(operands)] = 1
        operands.append(acc)
        in_specs.append(pl.BlockSpec(memory_space=pl.ANY))
    if filled:
        aliases[len(operands)] = 0
        operands.append(full)
        in_specs.append(pl.BlockSpec(memory_space=pl.ANY))
    out_shape = [jax.ShapeDtypeStruct((tok_dev, heads, HD), jnp.bfloat16)]
    out_specs = [
        pl.BlockSpec(
            (rows, HEADS_STEP * ratio, HD),
            lambda c, m, a: (source_of(m[0], step, tok_dev // rows), place + c, 0),
        )
    ]
    if last:
        span_spec = pl.BlockSpec((2, tok_dev, lanes), lambda c, m, a: (0, 0, c))
        out_shape.append(jax.ShapeDtypeStruct((2, tok_dev, span * HD), jnp.float32))
        out_shape += [jax.ShapeDtypeStruct((2, tok_dev, span * HD), jnp.bfloat16)] * (pieces - 1)
        out_specs += [span_spec] * pieces
    else:
        out_shape.append(jax.ShapeDtypeStruct((2, keys, kv_width), jnp.float32))
        out_specs.append(acc_spec)
    pairs = span * ratio * rows * window
    cost = CALL_COST[step] if step < len(CALL_COST) and not last else 1
    held = [pltpu.VMEM((held, ratio * rows), jnp.float32) for held in (keys, window)]
    held.append(pltpu.SemaphoreType.DMA)
    held += [pltpu.VMEM((2, keys, lanes), jnp.float32)] * last
    return pl.pallas_call(
        functools.partial(attend_kernel, step, place, first, filled, last, tok_dev, reach, ratio),
        out_shape=out_shape,
        grid_spec=pltpu.PrefetchScalarGridSpec(
            num_scalar_prefetch=2,
            grid=(span // HEADS_STEP,),
            in_specs=in_specs,
            out_specs=out_specs,
            scratch_shapes=held,
        ),
        input_output_aliases=aliases,
        compiler_params=pltpu.CompilerParams(
            dimension_semantics=("arbitrary",), vmem_limit_bytes=VMEM_BYTES
        ),
        cost_estimate=pl.CostEstimate(
            flops=pairs * HD * cost, bytes_accessed=pairs * cost, transcendentals=0
        ),
        name="attend",
    )(*operands)


def shards(queries, keys, values, grad_out, segment_ids, assignment):
    count = lax.axis_size("dp")
    uly = lax.axis_size("uly")
    group = lax.axis_index("dp")
    line = lax.axis_index("blk") * uly + lax.axis_index("uly")
    width, kv_width = queries.shape[2], keys.shape[2]
    heads, kv_heads = width // HD, kv_width // HD
    tok_dev = count * queries.shape[1]
    doc_most = min(512, tok_dev * uly)
    hops = -(-doc_most // tok_dev)
    meta = jnp.stack([group, line]).astype(jnp.int32)

    final, halves = count // 2, kv_heads // HEADS_STEP
    part = width // halves
    others = [step for step in range(1, count) if step != final]
    jobs = [(2, step, 0, kv_width) for step in range(count)]
    jobs += [(0, step, 0, width) for step in others]
    jobs += [(0, final, half * part, part) for half in range(halves - 1)]
    jobs += [(which, final, (halves - 1) * part, part, 1) for which in range(2)]
    staged = stage(assignment, (queries, grad_out, keys, values), jobs)
    kv_staged, staged = staged[:count], list(staged[count:])
    kv_arrived = [exchanged(kv_staged[step], "dp", step) for step in range(1, count)]
    staged, kv_arrived[0] = lax.optimization_barrier((staged, kv_arrived[0]))
    arrived = [exchanged(rows, "dp", step) for rows, step in zip(staged, others)]
    held = staged[len(others) :]
    kv_own = jnp.zeros((count, *kv_staged[0].shape), keys.dtype)
    for step, piece in enumerate([kv_staged[0], *kv_arrived]):
        kv_own = lax.dynamic_update_index_in_dim(
            kv_own, piece, source_of(group, step, count), 0
        )
    halos = [shifted(kv_own, ("blk", "uly"), back) for back in range(hops, 0, -1)]
    kv = jnp.concatenate([*halos, kv_own], axis=0)

    fixed = (doc_most, heads, meta, assignment, segment_ids)
    query, grad = (queries, lambda m, a: a[m[0]]), (grad_out, lambda m, a: a[m[0]])
    full, acc = attend(0, 0, kv_heads, *fixed, query, grad, kv, None, None, False)
    rows, acc = lax.optimization_barrier((held[0], acc))
    split = [exchanged(rows, "dp", final)]
    for at, (step, both) in enumerate(zip(others, arrived)):
        query, grad = (both, lambda m, a: 0), (both, lambda m, a: 1)
        full, acc = attend(step, 0, kv_heads, *fixed, query, grad, kv, acc, full, False)
        if not at:
            rows, acc = lax.optimization_barrier((held[1:], acc))
            split += [exchanged(piece, "dp", final) for piece in rows]
    totals, returned = [], []
    for half in range(halves):
        both = split[half]
        query, grad = (both, lambda m, a: 0), (both, lambda m, a: 1)
        if half + 1 == halves:
            grad = (split[half + 1], lambda m, a: 0)
        full, total, *halos = attend(
            final, half * HEADS_STEP, HEADS_STEP, *fixed, query, grad, kv, acc, full, True
        )
        if half:
            halos, returned[0] = lax.optimization_barrier((halos, returned[0]))
        returned = [shifted(halo, ("blk", "uly"), -back) for back, halo in enumerate(halos, 1)]
        for halo in returned:
            total = total + halo.astype(jnp.float32)
        totals.append(total.astype(jnp.bfloat16))
    total = jnp.concatenate(totals, axis=2)
    return full[None], total[0][None], total[1][None]


def solution(mesh):
    in_specs = (
        P(None, ("blk", "uly", "dp"), None),
        P(None, ("blk", "uly", "dp"), None),
        P(None, ("blk", "uly", "dp"), None),
        P(None, ("blk", "uly", "dp"), None),
        P(),
        P(),
    )
    out_specs = (
        P("dp", ("blk", "uly"), None, None),
        P("dp", ("blk", "uly"), None),
        P("dp", ("blk", "uly"), None),
    )
    return jax.shard_map(shards, mesh=mesh, in_specs=in_specs, out_specs=out_specs, check_vma=False)
```

```python
import functools

import jax
import jax.numpy as jnp
from jax import lax
from jax.experimental import pallas as pl
from jax.experimental.pallas import tpu as pltpu
from jax.sharding import PartitionSpec as P

HD = 128
LOG2E = 1.4426950408889634
BIG_NEGATIVE = -1e30
VMEM_BYTES = 32 * 1024 * 1024
HEADS_STEP = 2
CALL_COST = (1, 1, 1, 100)


def target_of(index, step, count):
    return lax.rem(index + step, count)


def source_of(index, step, count):
    return lax.rem(index + count - step, count)


def exchanged(value, axis, step):
    count = lax.axis_size(axis)
    return lax.ppermute(value, axis, [(i, (i + step) % count) for i in range(count)])


def shifted(value, axis, by):
    length = lax.axis_size(axis)
    pairs = [(i, i + by) for i in range(length) if 0 <= i + by < length]
    return lax.ppermute(value, axis, pairs)


def stage_kernel(count, jobs, outs, assign_ref, *refs):
    group = lax.axis_index("dp")
    sources, refs = refs[:4], refs[4:]
    out_refs, held_refs, (in_sems, out_sems) = refs[:outs], refs[outs : 2 * outs], refs[-2:]
    loads, stores = [], []
    for out, (first, step, start, width, *_) in enumerate(jobs):
        chosen = assign_ref[target_of(group, step, count)]
        for which in range(out_refs[out].shape[0]):
            origin = sources[first + which].at[chosen, :, start : start + width]
            held, slot = held_refs[out].at[which], 2 * out + which
            loads.append(pltpu.make_async_copy(origin, held, in_sems.at[slot]))
            stores.append(pltpu.make_async_copy(held, out_refs[out].at[which], out_sems.at[slot]))
    for load in loads:
        load.start()
    for load, store in zip(loads, stores):
        load.wait()
        store.start()
    for store in stores:
        store.wait()


def stage(assignment, arrays, jobs):
    count, rows, _ = arrays[0].shape
    shapes = [(job[4] if len(job) > 4 else 2, rows, job[3]) for job in jobs]
    kind = arrays[0].dtype
    far = pl.BlockSpec(memory_space=pltpu.HBM)
    return pl.pallas_call(
        functools.partial(stage_kernel, count, jobs, len(jobs)),
        out_shape=[jax.ShapeDtypeStruct(shape, kind) for shape in shapes],
        in_specs=[pl.BlockSpec(memory_space=pltpu.SMEM)] + [far] * len(arrays),
        out_specs=[far] * len(jobs),
        scratch_shapes=[pltpu.VMEM(shape, kind) for shape in shapes]
        + [pltpu.SemaphoreType.DMA((2 * len(jobs),))] * 2,
        name="stage",
    )(assignment, *arrays)


def build_bias(source, sequence, line, segment_ref, column_ref, bias_ref, rows, tok_dev, reach):
    keys, lanes = column_ref.shape
    pieces = keys // tok_dev
    window = bias_ref.shape[0]
    eye = lax.broadcasted_iota(jnp.int32, (tok_dev, tok_dev), 0) == lax.broadcasted_iota(
        jnp.int32, (tok_dev, tok_dev), 1
    )
    for place in range(pieces):
        back = pieces - 1 - place
        start = pl.multiple_of(jnp.maximum(line - back, 0) * tok_dev, tok_dev)
        every = segment_ref[:, pl.ds(start, tok_dev)].astype(jnp.float32)
        mine = lax.broadcasted_iota(jnp.int32, every.shape, 0) == sequence
        row = jnp.sum(jnp.where(mine, every, 0.0), axis=0, keepdims=True)
        column = jnp.sum(jnp.where(eye, row, 0.0), axis=1, keepdims=True)
        column = jnp.where(line >= back, column, -1.0)
        column_ref[place * tok_dev : (place + 1) * tok_dev, :] = jnp.broadcast_to(
            column, (tok_dev, lanes)
        )

    def token(shape):
        return lax.rem(lax.broadcasted_iota(jnp.int32, shape, 1), jnp.int32(rows))

    here = pl.multiple_of(keys - tok_dev + source * rows, rows)
    asked_rows = column_ref[pl.ds(here, rows), :]
    same = lax.broadcasted_iota(jnp.int32, (rows, lanes), 0) == token((rows, lanes))
    asked = jnp.sum(jnp.where(same, asked_rows, 0.0), axis=0, keepdims=True)
    held = column_ref[pl.ds(pl.multiple_of(here - reach, rows), window), :]
    place = lax.broadcasted_iota(jnp.int32, (window, lanes), 0)
    allowed = (held == asked) & (place <= token((window, lanes)) + reach)
    bias_ref[...] = jnp.where(allowed, 0.0, BIG_NEGATIVE)


def attend_kernel(
    step, first, filled, last, tok_dev, reach, ratio,
    meta_ref, assign_ref, segment_ref, query_ref, grad_ref, kv_ref, *refs,
):
    refs = list(refs)
    if not first:
        acc_in_ref = refs.pop(0)
    if filled:
        refs.pop(0)
    query_out_ref = refs.pop(0)
    column_ref, bias_ref = refs[-2 - last], refs[-1 - last]
    if last:
        own_ref, halo_refs, acc_ref = refs[0], refs[1:-3], refs[-1]
    else:
        acc_ref = refs[0]

    rows = query_ref.shape[0]
    window = bias_ref.shape[0]
    keys = column_ref.shape[0]
    scale = 1.0 / HD**0.5
    group = meta_ref[0]
    source = source_of(group, step, tok_dev // rows)
    block = (keys - tok_dev - reach) // rows + source
    span = pl.ds(pl.multiple_of(block * rows, rows), window)

    def mask():
        build_bias(
            source, assign_ref[group], meta_ref[1], segment_ref, column_ref, bias_ref, rows, tok_dev, reach
        )

    if last:
        mask()
    else:
        pl.when(pl.program_id(0) == 0)(mask)

    acc_ref[...] = jnp.zeros_like(acc_ref) if first else acc_in_ref[...]
    turned, across = (((1,), (1,)), ((), ())), (((0,), (0,)), ((), ()))
    heads = range(HEADS_STEP)
    lanes = [slice(head * HD, (head + 1) * HD) for head in heads]

    def product(left, right, contract):
        return lax.dot_general(left, right, contract, preferred_element_type=jnp.float32)

    def stacked(ref, head):
        start = head * ratio
        return jnp.concatenate(
            [ref[:, r * HD : (r + 1) * HD] for r in range(start, start + ratio)], axis=0
        )

    def windowed(which, head):
        return kv_ref[pl.ds(block, window // rows), which, :, lanes[head]].reshape(window, HD)

    plain = (((1,), (0,)), ((), ()))
    query, key = [stacked(query_ref, head) for head in heads], [windowed(0, head) for head in heads]
    scores = [product(key[head], query[head], turned) for head in heads]
    grad, value = [stacked(grad_ref, head) for head in heads], [windowed(1, head) for head in heads]
    grad_probs = [product(value[head], grad[head], turned) for head in heads]
    probs, grad_scores = [], []
    for head in heads:
        score = scores[head] * (scale * LOG2E) + bias_ref[...]
        weights = jnp.exp2(score - jnp.max(score, axis=0, keepdims=True))
        probs.append(weights * (1.0 / jnp.sum(weights, axis=0, keepdims=True)))
    for head in heads:
        weighted = probs[head] * grad_probs[head]
        delta = jnp.sum(weighted, axis=0, keepdims=True)
        grad_scores.append((weighted - probs[head] * delta).astype(jnp.bfloat16))
    grads = []
    for head in heads:
        grad_query = product(grad_scores[head], key[head], across)
        grads.append((grad_query * scale).reshape(ratio, rows, HD))
    grad_key = [product(grad_scores[head], query[head], plain) for head in heads]
    grad_value = [product(probs[head].astype(jnp.bfloat16), grad[head], plain) for head in heads]
    for head in heads:
        acc_ref[0, span, lanes[head]] += grad_key[head]
        acc_ref[1, span, lanes[head]] += grad_value[head]
    if last:
        own_ref[0] = acc_ref[0, keys - tok_dev :] * scale
        own_ref[1] = acc_ref[1, keys - tok_dev :]
        for back, halo_ref in enumerate(halo_refs, 1):
            part = slice(keys - (back + 1) * tok_dev, keys - back * tok_dev)
            halo_ref[0] = (acc_ref[0, part] * scale).astype(jnp.bfloat16)
            halo_ref[1] = acc_ref[1, part].astype(jnp.bfloat16)
    query_out_ref[...] = jnp.swapaxes(jnp.concatenate(grads, axis=0), 0, 1).astype(jnp.bfloat16)


def attend(step, base, span, reach, heads, meta, assignment, segments, query, grad, kv, acc, full, last):
    first, filled = acc is None, full is not None
    rows, (blocks, _, _, kv_width) = query[0].shape[1], kv.shape
    ratio = heads // (kv_width // HD)
    keys, tok_dev = blocks * rows, query[0].shape[1] * lax.axis_size("dp")
    pieces, window = keys // tok_dev, reach + rows
    lanes, place = HEADS_STEP * HD, base // HEADS_STEP

    def rows_spec(array, pick):
        start = place if array.shape[2] == heads * HD else 0
        return pl.BlockSpec(
            (None, rows, HEADS_STEP * ratio * HD), lambda c, m, a: (pick(m, a), 0, start + c)
        )

    in_specs = [
        pl.BlockSpec(segments.shape, lambda c, m, a: (0, 0)),
        rows_spec(*query),
        rows_spec(*grad),
    ]
    in_specs.append(pl.BlockSpec((blocks, 2, rows, lanes), lambda c, m, a: (0, 0, 0, place + c)))
    operands = [meta, assignment, segments, query[0], grad[0], kv]
    aliases = {}
    acc_spec = pl.BlockSpec((2, keys, lanes), lambda c, m, a: (0, 0, place + c))
    if not first:
        if not last:
            aliases[len(operands)] = 1
        operands.append(acc)
        in_specs.append(acc_spec)
    if filled:
        aliases[len(operands)] = 0
        operands.append(full)
        in_specs.append(pl.BlockSpec(memory_space=pl.ANY))
    out_shape = [jax.ShapeDtypeStruct((tok_dev, heads, HD), jnp.bfloat16)]
    out_specs = [
        pl.BlockSpec(
            (rows, HEADS_STEP * ratio, HD),
            lambda c, m, a: (source_of(m[0], step, tok_dev // rows), place + c, 0),
        )
    ]
    if last:
        span_spec = pl.BlockSpec((2, tok_dev, lanes), lambda c, m, a: (0, 0, c))
        out_shape.append(jax.ShapeDtypeStruct((2, tok_dev, span * HD), jnp.float32))
        out_shape += [jax.ShapeDtypeStruct((2, tok_dev, span * HD), jnp.bfloat16)] * (pieces - 1)
        out_specs += [span_spec] * pieces
    else:
        out_shape.append(jax.ShapeDtypeStruct((2, keys, kv_width), jnp.float32))
        out_specs.append(acc_spec)
    pairs = span * ratio * rows * window
    cost = CALL_COST[step] if step < len(CALL_COST) and not last else 1
    held = (keys, ratio * rows), (window, ratio * rows)
    held += ((2, keys, lanes),) * last
    return pl.pallas_call(
        functools.partial(attend_kernel, step, first, filled, last, tok_dev, reach, ratio),
        out_shape=out_shape,
        grid_spec=pltpu.PrefetchScalarGridSpec(
            num_scalar_prefetch=2,
            grid=(span // HEADS_STEP,),
            in_specs=in_specs,
            out_specs=out_specs,
            scratch_shapes=[pltpu.VMEM(shape, jnp.float32) for shape in held],
        ),
        input_output_aliases=aliases,
        compiler_params=pltpu.CompilerParams(
            dimension_semantics=("arbitrary",), vmem_limit_bytes=VMEM_BYTES
        ),
        cost_estimate=pl.CostEstimate(
            flops=pairs * HD * cost, bytes_accessed=pairs * cost, transcendentals=0
        ),
        name="attend",
    )(*operands)


def shards(queries, keys, values, grad_out, segment_ids, assignment):
    count = lax.axis_size("dp")
    uly = lax.axis_size("uly")
    group = lax.axis_index("dp")
    line = lax.axis_index("blk") * uly + lax.axis_index("uly")
    width, kv_width = queries.shape[2], keys.shape[2]
    heads, kv_heads = width // HD, kv_width // HD
    tok_dev = count * queries.shape[1]
    doc_most = min(512, tok_dev * uly)
    hops = -(-doc_most // tok_dev)
    meta = jnp.stack([group, line]).astype(jnp.int32)

    final, halves = count // 2, kv_heads // HEADS_STEP
    part = width // halves
    others = [step for step in range(1, count) if step != final]
    jobs = [(2, step, 0, kv_width) for step in range(count)]
    jobs += [(0, step, 0, width) for step in others]
    jobs += [(0, final, half * part, part) for half in range(halves - 1)]
    jobs += [(which, final, (halves - 1) * part, part, 1) for which in range(2)]
    staged = stage(assignment, (queries, grad_out, keys, values), jobs)
    kv_staged, staged = staged[:count], list(staged[count:])
    kv_arrived = [exchanged(kv_staged[step], "dp", step) for step in range(1, count)]
    staged, kv_arrived[0] = lax.optimization_barrier((staged, kv_arrived[0]))
    arrived = [exchanged(rows, "dp", step) for rows, step in zip(staged, others)]
    held = staged[len(others) :]
    kv_own = jnp.zeros((count, *kv_staged[0].shape), keys.dtype)
    for step, piece in enumerate([kv_staged[0], *kv_arrived]):
        kv_own = lax.dynamic_update_index_in_dim(
            kv_own, piece, source_of(group, step, count), 0
        )
    halos = [shifted(kv_own, ("blk", "uly"), back) for back in range(hops, 0, -1)]
    kv = jnp.concatenate([*halos, kv_own], axis=0)

    fixed = (doc_most, heads, meta, assignment, segment_ids)
    query, grad = (queries, lambda m, a: a[m[0]]), (grad_out, lambda m, a: a[m[0]])
    full, acc = attend(0, 0, kv_heads, *fixed, query, grad, kv, None, None, False)
    rows, acc = lax.optimization_barrier((held[0], acc))
    split = [exchanged(rows, "dp", final)]
    for at, (step, both) in enumerate(zip(others, arrived)):
        query, grad = (both, lambda m, a: 0), (both, lambda m, a: 1)
        full, acc = attend(step, 0, kv_heads, *fixed, query, grad, kv, acc, full, False)
        if not at:
            rows, acc = lax.optimization_barrier((held[1:], acc))
            split += [exchanged(piece, "dp", final) for piece in rows]
    totals, returned = [], []
    for half in range(halves):
        both = split[half]
        query, grad = (both, lambda m, a: 0), (both, lambda m, a: 1)
        if half + 1 == halves:
            grad = (split[half + 1], lambda m, a: 0)
        full, total, *halos = attend(
            final, half * HEADS_STEP, HEADS_STEP, *fixed, query, grad, kv, acc, full, True
        )
        if half:
            halos, returned[0] = lax.optimization_barrier((halos, returned[0]))
        returned = [shifted(halo, ("blk", "uly"), -back) for back, halo in enumerate(halos, 1)]
        for halo in returned:
            total = total + halo.astype(jnp.float32)
        totals.append(total.astype(jnp.bfloat16))
    total = jnp.concatenate(totals, axis=2)
    return full[None], total[0][None], total[1][None]


def solution(mesh):
    in_specs = (
        P(None, ("blk", "uly", "dp"), None),
        P(None, ("blk", "uly", "dp"), None),
        P(None, ("blk", "uly", "dp"), None),
        P(None, ("blk", "uly", "dp"), None),
        P(),
        P(),
    )
    out_specs = (
        P("dp", ("blk", "uly"), None, None),
        P("dp", ("blk", "uly"), None),
        P("dp", ("blk", "uly"), None),
    )
    return jax.shard_map(shards, mesh=mesh, in_specs=in_specs, out_specs=out_specs, check_vma=False)
```

```python
import functools

import jax
import jax.numpy as jnp
from jax import lax
from jax.experimental import pallas as pl
from jax.experimental.pallas import tpu as pltpu
from jax.sharding import PartitionSpec as P

HD = 128
LOG2E = 1.4426950408889634
BIG_NEGATIVE = -1e30
VMEM_BYTES = 32 * 1024 * 1024
HEADS_STEP = 2
CALL_COST = (1, 1, 1, 100)


def target_of(index, step, count):
    return lax.rem(index + step, count)


def source_of(index, step, count):
    return lax.rem(index + count - step, count)


def exchanged(value, axis, step):
    count = lax.axis_size(axis)
    return lax.ppermute(value, axis, [(i, (i + step) % count) for i in range(count)])


def shifted(value, axis, by):
    length = lax.axis_size(axis)
    pairs = [(i, i + by) for i in range(length) if 0 <= i + by < length]
    return lax.ppermute(value, axis, pairs)


def stage_kernel(count, jobs, outs, assign_ref, *refs):
    group = lax.axis_index("dp")
    sources, refs = refs[:4], refs[4:]
    out_refs, held_refs, (in_sems, out_sems) = refs[:outs], refs[outs : 2 * outs], refs[-2:]
    loads, stores = [], []
    for out, (first, step, start, width, *_) in enumerate(jobs):
        chosen = assign_ref[target_of(group, step, count)]
        for which in range(out_refs[out].shape[0]):
            origin = sources[first + which].at[chosen, :, start : start + width]
            held, slot = held_refs[out].at[which], 2 * out + which
            loads.append(pltpu.make_async_copy(origin, held, in_sems.at[slot]))
            stores.append(pltpu.make_async_copy(held, out_refs[out].at[which], out_sems.at[slot]))
    for load in loads:
        load.start()
    for load, store in zip(loads, stores):
        load.wait()
        store.start()
    for store in stores:
        store.wait()


def stage(assignment, arrays, jobs):
    count, rows, _ = arrays[0].shape
    shapes = [(job[4] if len(job) > 4 else 2, rows, job[3]) for job in jobs]
    kind = arrays[0].dtype
    far = pl.BlockSpec(memory_space=pltpu.HBM)
    return pl.pallas_call(
        functools.partial(stage_kernel, count, jobs, len(jobs)),
        out_shape=[jax.ShapeDtypeStruct(shape, kind) for shape in shapes],
        in_specs=[pl.BlockSpec(memory_space=pltpu.SMEM)] + [far] * len(arrays),
        out_specs=[far] * len(jobs),
        scratch_shapes=[pltpu.VMEM(shape, kind) for shape in shapes]
        + [pltpu.SemaphoreType.DMA((2 * len(jobs),))] * 2,
        name="stage",
    )(assignment, *arrays)


def build_bias(source, sequence, line, segment_ref, column_ref, bias_ref, rows, tok_dev, reach):
    keys, lanes = column_ref.shape
    pieces = keys // tok_dev
    window = bias_ref.shape[0]
    eye = lax.broadcasted_iota(jnp.int32, (tok_dev, tok_dev), 0) == lax.broadcasted_iota(
        jnp.int32, (tok_dev, tok_dev), 1
    )
    for place in range(pieces):
        back = pieces - 1 - place
        start = pl.multiple_of(jnp.maximum(line - back, 0) * tok_dev, tok_dev)
        every = segment_ref[:, pl.ds(start, tok_dev)].astype(jnp.float32)
        mine = lax.broadcasted_iota(jnp.int32, every.shape, 0) == sequence
        row = jnp.sum(jnp.where(mine, every, 0.0), axis=0, keepdims=True)
        column = jnp.sum(jnp.where(eye, row, 0.0), axis=1, keepdims=True)
        column = jnp.where(line >= back, column, -1.0)
        column_ref[place * tok_dev : (place + 1) * tok_dev, :] = jnp.broadcast_to(
            column, (tok_dev, lanes)
        )

    def token(shape):
        return lax.rem(lax.broadcasted_iota(jnp.int32, shape, 1), jnp.int32(rows))

    here = pl.multiple_of(keys - tok_dev + source * rows, rows)
    asked_rows = column_ref[pl.ds(here, rows), :]
    same = lax.broadcasted_iota(jnp.int32, (rows, lanes), 0) == token((rows, lanes))
    asked = jnp.sum(jnp.where(same, asked_rows, 0.0), axis=0, keepdims=True)
    held = column_ref[pl.ds(pl.multiple_of(here - reach, rows), window), :]
    place = lax.broadcasted_iota(jnp.int32, (window, lanes), 0)
    allowed = (held == asked) & (place <= token((window, lanes)) + reach)
    bias_ref[...] = jnp.where(allowed, 0.0, BIG_NEGATIVE)


def attend_kernel(
    step, first, filled, last, tok_dev, reach, ratio,
    meta_ref, assign_ref, segment_ref, query_ref, grad_ref, kv_ref, *refs,
):
    refs = list(refs)
    if not first:
        acc_in_ref = refs.pop(0)
    if filled:
        refs.pop(0)
    query_out_ref = refs.pop(0)
    column_ref, bias_ref = refs[-2 - last], refs[-1 - last]
    if last:
        own_ref, halo_refs, acc_ref = refs[0], refs[1:-3], refs[-1]
    else:
        acc_ref = refs[0]

    rows = query_ref.shape[0]
    window = bias_ref.shape[0]
    keys = column_ref.shape[0]
    scale = 1.0 / HD**0.5
    group = meta_ref[0]
    source = source_of(group, step, tok_dev // rows)
    block = (keys - tok_dev - reach) // rows + source
    span = pl.ds(pl.multiple_of(block * rows, rows), window)

    def mask():
        build_bias(
            source, assign_ref[group], meta_ref[1], segment_ref, column_ref, bias_ref, rows, tok_dev, reach
        )

    if last:
        mask()
    else:
        pl.when(pl.program_id(0) == 0)(mask)

    acc_ref[...] = jnp.zeros_like(acc_ref) if first else acc_in_ref[...]
    turned, across = (((1,), (1,)), ((), ())), (((0,), (0,)), ((), ()))
    heads = range(HEADS_STEP)
    lanes = [slice(head * HD, (head + 1) * HD) for head in heads]

    def product(left, right, contract):
        return lax.dot_general(left, right, contract, preferred_element_type=jnp.float32)

    def stacked(ref, head):
        start = head * ratio
        return jnp.concatenate(
            [ref[:, r * HD : (r + 1) * HD] for r in range(start, start + ratio)], axis=0
        )

    def windowed(which, head):
        return kv_ref[pl.ds(block, window // rows), which, :, lanes[head]].reshape(window, HD)

    plain = (((1,), (0,)), ((), ()))
    query, key = [stacked(query_ref, head) for head in heads], [windowed(0, head) for head in heads]
    scores = [product(key[head], query[head], turned) for head in heads]
    grad, value = [stacked(grad_ref, head) for head in heads], [windowed(1, head) for head in heads]
    grad_probs = [product(value[head], grad[head], turned) for head in heads]
    probs, grad_scores = [], []
    for head in heads:
        score = scores[head] * (scale * LOG2E) + bias_ref[...]
        weights = jnp.exp2(score - jnp.max(score, axis=0, keepdims=True))
        probs.append(weights * (1.0 / jnp.sum(weights, axis=0, keepdims=True)))
    for head in heads:
        weighted = probs[head] * grad_probs[head]
        delta = jnp.sum(weighted, axis=0, keepdims=True)
        grad_scores.append((weighted - probs[head] * delta).astype(jnp.bfloat16))
    grads = []
    for head in heads:
        grad_query = product(grad_scores[head], key[head], across)
        grads.append((grad_query * scale).reshape(ratio, rows, HD))
    grad_key = [product(grad_scores[head], query[head], plain) for head in heads]
    grad_value = [product(probs[head].astype(jnp.bfloat16), grad[head], plain) for head in heads]
    for head in heads:
        acc_ref[0, span, lanes[head]] += grad_key[head]
        acc_ref[1, span, lanes[head]] += grad_value[head]
    if last:
        own_ref[0] = acc_ref[0, keys - tok_dev :] * scale
        own_ref[1] = acc_ref[1, keys - tok_dev :]
        for back, halo_ref in enumerate(halo_refs, 1):
            part = slice(keys - (back + 1) * tok_dev, keys - back * tok_dev)
            halo_ref[0] = (acc_ref[0, part] * scale).astype(jnp.bfloat16)
            halo_ref[1] = acc_ref[1, part].astype(jnp.bfloat16)
    query_out_ref[...] = jnp.swapaxes(jnp.concatenate(grads, axis=0), 0, 1).astype(jnp.bfloat16)


def attend(step, base, span, reach, heads, meta, assignment, segments, query, grad, kv, acc, full, last):
    first, filled = acc is None, full is not None
    rows, (blocks, _, _, kv_width) = query[0].shape[1], kv.shape
    ratio = heads // (kv_width // HD)
    keys, tok_dev = blocks * rows, query[0].shape[1] * lax.axis_size("dp")
    pieces, window = keys // tok_dev, reach + rows
    lanes, place = HEADS_STEP * HD, base // HEADS_STEP

    def rows_spec(array, pick):
        start = place if array.shape[2] == heads * HD else 0
        return pl.BlockSpec(
            (None, rows, HEADS_STEP * ratio * HD), lambda c, m, a: (pick(m, a), 0, start + c)
        )

    in_specs = [
        pl.BlockSpec(segments.shape, lambda c, m, a: (0, 0)),
        rows_spec(*query),
        rows_spec(*grad),
    ]
    in_specs.append(pl.BlockSpec((blocks, 2, rows, lanes), lambda c, m, a: (0, 0, 0, place + c)))
    operands = [meta, assignment, segments, query[0], grad[0], kv]
    aliases = {}
    acc_spec = pl.BlockSpec((2, keys, lanes), lambda c, m, a: (0, 0, place + c))
    if not first:
        if not last:
            aliases[len(operands)] = 1
        operands.append(acc)
        in_specs.append(acc_spec)
    if filled:
        aliases[len(operands)] = 0
        operands.append(full)
        in_specs.append(pl.BlockSpec(memory_space=pl.ANY))
    out_shape = [jax.ShapeDtypeStruct((tok_dev, heads, HD), jnp.bfloat16)]
    out_specs = [
        pl.BlockSpec(
            (rows, HEADS_STEP * ratio, HD),
            lambda c, m, a: (source_of(m[0], step, tok_dev // rows), place + c, 0),
        )
    ]
    if last:
        span_spec = pl.BlockSpec((2, tok_dev, lanes), lambda c, m, a: (0, 0, c))
        out_shape.append(jax.ShapeDtypeStruct((2, tok_dev, span * HD), jnp.float32))
        out_shape += [jax.ShapeDtypeStruct((2, tok_dev, span * HD), jnp.bfloat16)] * (pieces - 1)
        out_specs += [span_spec] * pieces
    else:
        out_shape.append(jax.ShapeDtypeStruct((2, keys, kv_width), jnp.float32))
        out_specs.append(acc_spec)
    pairs = span * ratio * rows * window
    cost = CALL_COST[step] if step < len(CALL_COST) and not last else 1
    held = (keys, ratio * rows), (window, ratio * rows)
    held += ((2, keys, lanes),) * last
    return pl.pallas_call(
        functools.partial(attend_kernel, step, first, filled, last, tok_dev, reach, ratio),
        out_shape=out_shape,
        grid_spec=pltpu.PrefetchScalarGridSpec(
            num_scalar_prefetch=2,
            grid=(span // HEADS_STEP,),
            in_specs=in_specs,
            out_specs=out_specs,
            scratch_shapes=[pltpu.VMEM(shape, jnp.float32) for shape in held],
        ),
        input_output_aliases=aliases,
        compiler_params=pltpu.CompilerParams(
            dimension_semantics=("arbitrary",), vmem_limit_bytes=VMEM_BYTES
        ),
        cost_estimate=pl.CostEstimate(
            flops=pairs * HD * cost, bytes_accessed=pairs * cost, transcendentals=0
        ),
        name="attend",
    )(*operands)


def shards(queries, keys, values, grad_out, segment_ids, assignment):
    count = lax.axis_size("dp")
    uly = lax.axis_size("uly")
    group = lax.axis_index("dp")
    line = lax.axis_index("blk") * uly + lax.axis_index("uly")
    width, kv_width = queries.shape[2], keys.shape[2]
    heads, kv_heads = width // HD, kv_width // HD
    tok_dev = count * queries.shape[1]
    doc_most = min(512, tok_dev * uly)
    hops = -(-doc_most // tok_dev)
    meta = jnp.stack([group, line]).astype(jnp.int32)

    final, halves = count // 2, kv_heads // HEADS_STEP
    part = width // halves
    others = [step for step in range(1, count) if step != final]
    jobs = [(2, step, 0, kv_width) for step in range(count)]
    jobs += [(0, step, 0, width) for step in others]
    jobs += [(which, final, half * part, part, 1) for half in range(halves) for which in range(2)]
    staged = stage(assignment, (queries, grad_out, keys, values), jobs)
    kv_staged, staged = staged[:count], list(staged[count:])
    kv_arrived = [exchanged(kv_staged[step], "dp", step) for step in range(1, count)]
    staged, kv_arrived[0] = lax.optimization_barrier((staged, kv_arrived[0]))
    arrived = [exchanged(rows, "dp", step) for rows, step in zip(staged, others)]
    held = staged[len(others) :]
    kv_own = jnp.zeros((count, *kv_staged[0].shape), keys.dtype)
    for step, piece in enumerate([kv_staged[0], *kv_arrived]):
        kv_own = lax.dynamic_update_index_in_dim(
            kv_own, piece, source_of(group, step, count), 0
        )
    halos = [shifted(kv_own, ("blk", "uly"), back) for back in range(hops, 0, -1)]
    kv = jnp.concatenate([*halos, kv_own], axis=0)

    fixed = (doc_most, heads, meta, assignment, segment_ids)
    query, grad = (queries, lambda m, a: a[m[0]]), (grad_out, lambda m, a: a[m[0]])
    full, acc = attend(0, 0, kv_heads, *fixed, query, grad, kv, None, None, False)
    rows, acc = lax.optimization_barrier((held[0], acc))
    split = [exchanged(rows, "dp", final)]
    for at, (step, both) in enumerate(zip(others, arrived)):
        if not at:
            rows, both = lax.optimization_barrier((held[1], both))
            split.append(exchanged(rows, "dp", final))
        query, grad = (both, lambda m, a: 0), (both, lambda m, a: 1)
        full, acc = attend(step, 0, kv_heads, *fixed, query, grad, kv, acc, full, False)
        rows, acc = lax.optimization_barrier((held[2 + at], acc))
        split.append(exchanged(rows, "dp", final))
    totals, returned = [], []
    for half in range(halves):
        query, grad = [(rows, lambda m, a: 0) for rows in split[2 * half : 2 * half + 2]]
        full, total, *halos = attend(
            final, half * HEADS_STEP, HEADS_STEP, *fixed, query, grad, kv, acc, full, True
        )
        if half:
            halos, returned[0] = lax.optimization_barrier((halos, returned[0]))
        returned = [shifted(halo, ("blk", "uly"), -back) for back, halo in enumerate(halos, 1)]
        for halo in returned:
            total = total + halo.astype(jnp.float32)
        totals.append(total.astype(jnp.bfloat16))
    total = jnp.concatenate(totals, axis=2)
    return full[None], total[0][None], total[1][None]


def solution(mesh):
    in_specs = (
        P(None, ("blk", "uly", "dp"), None),
        P(None, ("blk", "uly", "dp"), None),
        P(None, ("blk", "uly", "dp"), None),
        P(None, ("blk", "uly", "dp"), None),
        P(),
        P(),
    )
    out_specs = (
        P("dp", ("blk", "uly"), None, None),
        P("dp", ("blk", "uly"), None),
        P("dp", ("blk", "uly"), None),
    )
    return jax.shard_map(shards, mesh=mesh, in_specs=in_specs, out_specs=out_specs, check_vma=False)
```

```python
import functools

import jax
import jax.numpy as jnp
from jax import lax
from jax.experimental import pallas as pl
from jax.experimental.pallas import tpu as pltpu
from jax.sharding import PartitionSpec as P

HD = 128
LOG2E = 1.4426950408889634
BIG_NEGATIVE = -1e30
VMEM_BYTES = 32 * 1024 * 1024
HEADS_STEP = 2
CALL_COST = 1


def target_of(index, step, count):
    return lax.rem(index + step, count)


def source_of(index, step, count):
    return lax.rem(index + count - step, count)


def exchanged(value, axis, step):
    count = lax.axis_size(axis)
    return lax.ppermute(value, axis, [(i, (i + step) % count) for i in range(count)])


def shifted(value, axis, by):
    length = lax.axis_size(axis)
    pairs = [(i, i + by) for i in range(length) if 0 <= i + by < length]
    return lax.ppermute(value, axis, pairs)


def stage_kernel(count, jobs, outs, assign_ref, *refs):
    group = lax.axis_index("dp")
    sources, refs = refs[:4], refs[4:]
    out_refs, held_refs, (in_sems, out_sems) = refs[:outs], refs[outs : 2 * outs], refs[-2:]
    loads, stores = [], []
    for out, (first, step, start, width, *_) in enumerate(jobs):
        chosen = assign_ref[target_of(group, step, count)]
        for which in range(out_refs[out].shape[0]):
            origin = sources[first + which].at[chosen, :, start : start + width]
            held, slot = held_refs[out].at[which], 2 * out + which
            loads.append(pltpu.make_async_copy(origin, held, in_sems.at[slot]))
            stores.append(pltpu.make_async_copy(held, out_refs[out].at[which], out_sems.at[slot]))
    for load in loads:
        load.start()
    for load, store in zip(loads, stores):
        load.wait()
        store.start()
    for store in stores:
        store.wait()


def stage(assignment, arrays, jobs):
    count, rows, _ = arrays[0].shape
    shapes = [(job[4] if len(job) > 4 else 2, rows, job[3]) for job in jobs]
    kind = arrays[0].dtype
    far = pl.BlockSpec(memory_space=pltpu.HBM)
    return pl.pallas_call(
        functools.partial(stage_kernel, count, jobs, len(jobs)),
        out_shape=[jax.ShapeDtypeStruct(shape, kind) for shape in shapes],
        in_specs=[pl.BlockSpec(memory_space=pltpu.SMEM)] + [far] * len(arrays),
        out_specs=[far] * len(jobs),
        scratch_shapes=[pltpu.VMEM(shape, kind) for shape in shapes]
        + [pltpu.SemaphoreType.DMA((2 * len(jobs),))] * 2,
        name="stage",
    )(assignment, *arrays)


def build_bias(source, sequence, line, segment_ref, column_ref, bias_ref, rows, tok_dev, reach):
    keys, lanes = column_ref.shape
    pieces = keys // tok_dev
    window = bias_ref.shape[0]
    eye = lax.broadcasted_iota(jnp.int32, (tok_dev, tok_dev), 0) == lax.broadcasted_iota(
        jnp.int32, (tok_dev, tok_dev), 1
    )
    for place in range(pieces):
        back = pieces - 1 - place
        start = pl.multiple_of(jnp.maximum(line - back, 0) * tok_dev, tok_dev)
        every = segment_ref[:, pl.ds(start, tok_dev)].astype(jnp.float32)
        mine = lax.broadcasted_iota(jnp.int32, every.shape, 0) == sequence
        row = jnp.sum(jnp.where(mine, every, 0.0), axis=0, keepdims=True)
        column = jnp.sum(jnp.where(eye, row, 0.0), axis=1, keepdims=True)
        column = jnp.where(line >= back, column, -1.0)
        column_ref[place * tok_dev : (place + 1) * tok_dev, :] = jnp.broadcast_to(
            column, (tok_dev, lanes)
        )

    def token(shape):
        return lax.rem(lax.broadcasted_iota(jnp.int32, shape, 1), jnp.int32(rows))

    here = pl.multiple_of(keys - tok_dev + source * rows, rows)
    asked_rows = column_ref[pl.ds(here, rows), :]
    same = lax.broadcasted_iota(jnp.int32, (rows, lanes), 0) == token((rows, lanes))
    asked = jnp.sum(jnp.where(same, asked_rows, 0.0), axis=0, keepdims=True)
    held = column_ref[pl.ds(pl.multiple_of(here - reach, rows), window), :]
    place = lax.broadcasted_iota(jnp.int32, (window, lanes), 0)
    allowed = (held == asked) & (place <= token((window, lanes)) + reach)
    bias_ref[...] = jnp.where(allowed, 0.0, BIG_NEGATIVE)


def attend_kernel(
    step, first, filled, last, tok_dev, reach, ratio,
    meta_ref, assign_ref, segment_ref, query_ref, grad_ref, kv_ref, *refs,
):
    refs = list(refs)
    if not first:
        acc_in_ref = refs.pop(0)
    if filled:
        refs.pop(0)
    query_out_ref = refs.pop(0)
    column_ref, bias_ref = refs[-2 - last], refs[-1 - last]
    if last:
        own_ref, halo_refs, acc_ref = refs[0], refs[1:-3], refs[-1]
    else:
        acc_ref = refs[0]

    rows = query_ref.shape[0]
    window = bias_ref.shape[0]
    keys = column_ref.shape[0]
    scale = 1.0 / HD**0.5
    group = meta_ref[0]
    source = source_of(group, step, tok_dev // rows)
    block = (keys - tok_dev - reach) // rows + source
    span = pl.ds(pl.multiple_of(block * rows, rows), window)

    def mask():
        build_bias(
            source, assign_ref[group], meta_ref[1], segment_ref, column_ref, bias_ref, rows, tok_dev, reach
        )

    if last:
        mask()
    else:
        pl.when(pl.program_id(0) == 0)(mask)

    acc_ref[...] = jnp.zeros_like(acc_ref) if first else acc_in_ref[...]
    turned, across = (((1,), (1,)), ((), ())), (((0,), (0,)), ((), ()))
    heads = range(HEADS_STEP)
    lanes = [slice(head * HD, (head + 1) * HD) for head in heads]

    def product(left, right, contract):
        return lax.dot_general(left, right, contract, preferred_element_type=jnp.float32)

    def stacked(ref, head):
        start = head * ratio
        return jnp.concatenate(
            [ref[:, r * HD : (r + 1) * HD] for r in range(start, start + ratio)], axis=0
        )

    def windowed(which, head):
        return kv_ref[pl.ds(block, window // rows), which, :, lanes[head]].reshape(window, HD)

    plain = (((1,), (0,)), ((), ()))
    query, key = [stacked(query_ref, head) for head in heads], [windowed(0, head) for head in heads]
    scores = [product(key[head], query[head], turned) for head in heads]
    grad, value = [stacked(grad_ref, head) for head in heads], [windowed(1, head) for head in heads]
    grad_probs = [product(value[head], grad[head], turned) for head in heads]
    probs, grad_scores = [], []
    for head in heads:
        score = scores[head] * (scale * LOG2E) + bias_ref[...]
        weights = jnp.exp2(score - jnp.max(score, axis=0, keepdims=True))
        probs.append(weights * (1.0 / jnp.sum(weights, axis=0, keepdims=True)))
    for head in heads:
        weighted = probs[head] * grad_probs[head]
        delta = jnp.sum(weighted, axis=0, keepdims=True)
        grad_scores.append((weighted - probs[head] * delta).astype(jnp.bfloat16))
    grads = []
    for head in heads:
        grad_query = product(grad_scores[head], key[head], across)
        grads.append((grad_query * scale).reshape(ratio, rows, HD))
    grad_key = [product(grad_scores[head], query[head], plain) for head in heads]
    grad_value = [product(probs[head].astype(jnp.bfloat16), grad[head], plain) for head in heads]
    for head in heads:
        acc_ref[0, span, lanes[head]] += grad_key[head]
        acc_ref[1, span, lanes[head]] += grad_value[head]
    if last:
        own_ref[0] = acc_ref[0, keys - tok_dev :] * scale
        own_ref[1] = acc_ref[1, keys - tok_dev :]
        for back, halo_ref in enumerate(halo_refs, 1):
            part = slice(keys - (back + 1) * tok_dev, keys - back * tok_dev)
            halo_ref[0] = (acc_ref[0, part] * scale).astype(jnp.bfloat16)
            halo_ref[1] = acc_ref[1, part].astype(jnp.bfloat16)
    query_out_ref[...] = jnp.swapaxes(jnp.concatenate(grads, axis=0), 0, 1).astype(jnp.bfloat16)


def attend(step, base, span, reach, heads, meta, assignment, segments, query, grad, kv, acc, full, last):
    first, filled = acc is None, full is not None
    rows, (blocks, _, _, kv_width) = query[0].shape[1], kv.shape
    ratio = heads // (kv_width // HD)
    keys, tok_dev = blocks * rows, query[0].shape[1] * lax.axis_size("dp")
    pieces, window = keys // tok_dev, reach + rows
    lanes, place = HEADS_STEP * HD, base // HEADS_STEP

    def rows_spec(array, pick):
        start = place if array.shape[2] == heads * HD else 0
        return pl.BlockSpec(
            (None, rows, HEADS_STEP * ratio * HD), lambda c, m, a: (pick(m, a), 0, start + c)
        )

    in_specs = [
        pl.BlockSpec(segments.shape, lambda c, m, a: (0, 0)),
        rows_spec(*query),
        rows_spec(*grad),
    ]
    in_specs.append(pl.BlockSpec((blocks, 2, rows, lanes), lambda c, m, a: (0, 0, 0, place + c)))
    operands = [meta, assignment, segments, query[0], grad[0], kv]
    aliases = {}
    acc_spec = pl.BlockSpec((2, keys, lanes), lambda c, m, a: (0, 0, c))
    if not first:
        if not last:
            aliases[len(operands)] = 1
        operands.append(acc)
        in_specs.append(acc_spec)
    if filled:
        aliases[len(operands)] = 0
        operands.append(full)
        in_specs.append(pl.BlockSpec(memory_space=pl.ANY))
    out_shape = [jax.ShapeDtypeStruct((tok_dev, heads, HD), jnp.bfloat16)]
    out_specs = [
        pl.BlockSpec(
            (rows, HEADS_STEP * ratio, HD),
            lambda c, m, a: (source_of(m[0], step, tok_dev // rows), place + c, 0),
        )
    ]
    if last:
        span_spec = pl.BlockSpec((2, tok_dev, lanes), lambda c, m, a: (0, 0, c))
        out_shape.append(jax.ShapeDtypeStruct((2, tok_dev, span * HD), jnp.float32))
        out_shape += [jax.ShapeDtypeStruct((2, tok_dev, span * HD), jnp.bfloat16)] * (pieces - 1)
        out_specs += [span_spec] * pieces
    else:
        out_shape.append(jax.ShapeDtypeStruct((2, keys, span * HD), jnp.float32))
        out_specs.append(acc_spec)
    pairs = span * ratio * rows * window
    cost = CALL_COST if step and not last else 1
    held = (keys, ratio * rows), (window, ratio * rows)
    held += ((2, keys, lanes),) * last
    return pl.pallas_call(
        functools.partial(attend_kernel, step, first, filled, last, tok_dev, reach, ratio),
        out_shape=out_shape,
        grid_spec=pltpu.PrefetchScalarGridSpec(
            num_scalar_prefetch=2,
            grid=(span // HEADS_STEP,),
            in_specs=in_specs,
            out_specs=out_specs,
            scratch_shapes=[pltpu.VMEM(shape, jnp.float32) for shape in held],
        ),
        input_output_aliases=aliases,
        compiler_params=pltpu.CompilerParams(
            dimension_semantics=("arbitrary",), vmem_limit_bytes=VMEM_BYTES
        ),
        cost_estimate=pl.CostEstimate(
            flops=pairs * HD * cost, bytes_accessed=pairs * cost, transcendentals=0
        ),
        name="attend",
    )(*operands)


def shards(queries, keys, values, grad_out, segment_ids, assignment):
    count = lax.axis_size("dp")
    uly = lax.axis_size("uly")
    group = lax.axis_index("dp")
    line = lax.axis_index("blk") * uly + lax.axis_index("uly")
    width, kv_width = queries.shape[2], keys.shape[2]
    heads, kv_heads = width // HD, kv_width // HD
    tok_dev = count * queries.shape[1]
    doc_most = min(512, tok_dev * uly)
    hops = -(-doc_most // tok_dev)
    meta = jnp.stack([group, line]).astype(jnp.int32)

    final, halves = count // 2, kv_heads // HEADS_STEP
    part = width // halves
    others = [step for step in range(1, count) if step != final]
    jobs = [(2, step, 0, kv_width) for step in range(count)]
    order = [*others[1:], final]
    jobs.append((0, others[0], 0, width))
    jobs += [(0, step, half * part, part) for half in range(halves) for step in order]
    staged = stage(assignment, (queries, grad_out, keys, values), jobs)
    kv_staged, staged = staged[:count], list(staged[count:])
    kv_arrived = [exchanged(kv_staged[step], "dp", step) for step in range(1, count)]
    staged, mine, kv_arrived[0] = lax.optimization_barrier((staged, kv_staged[0], kv_arrived[0]))
    whole = exchanged(staged[0], "dp", others[0])
    arrived = [exchanged(rows, "dp", step) for rows, step in zip(staged[1:], order)]
    behind = staged[1 + len(order) :]
    kv_own = jnp.zeros((count, *kv_staged[0].shape), keys.dtype)
    for step, piece in enumerate([mine, *kv_arrived]):
        kv_own = lax.dynamic_update_index_in_dim(
            kv_own, piece, source_of(group, step, count), 0
        )
    halos = [shifted(kv_own, ("blk", "uly"), back) for back in range(hops, 0, -1)]
    kv = jnp.concatenate([*halos, kv_own], axis=0)

    fixed = (doc_most, heads, meta, assignment, segment_ids)
    own = (queries, lambda m, a: a[m[0]]), (grad_out, lambda m, a: a[m[0]])
    first = (whole, lambda m, a: 0), (whole, lambda m, a: 1)
    accs, full, totals, returned = [], None, [], []
    for half in range(halves):
        full, acc = attend(0, half * HEADS_STEP, HEADS_STEP, *fixed, *own, kv, None, full, False)
        accs.append(acc)
    rows, full = lax.optimization_barrier((behind[:-1], full))
    arrived += [exchanged(piece, "dp", step) for piece, step in zip(rows, order)]
    for half in range(halves):
        full, accs[half] = attend(
            others[0], half * HEADS_STEP, HEADS_STEP, *fixed, *first, kv, accs[half], full, False
        )
    for half in range(halves):
        base = half * HEADS_STEP
        for at, step in enumerate(order):
            both = arrived[half * len(order) + at]
            pair = (both, lambda m, a: 0), (both, lambda m, a: 1)
            full, accs[half], *halos = attend(
                step, base, HEADS_STEP, *fixed, *pair, kv, accs[half], full, step == final
            )
            if not half and at == len(order) - 2:
                rows, full = lax.optimization_barrier((behind[-1], full))
                arrived.append(exchanged(rows, "dp", final))
        if half:
            halos, returned[0] = lax.optimization_barrier((halos, returned[0]))
        returned = [shifted(halo, ("blk", "uly"), -back) for back, halo in enumerate(halos, 1)]
        total = accs[half]
        for halo in returned:
            total = total + halo.astype(jnp.float32)
        totals.append(total.astype(jnp.bfloat16))
    total = jnp.concatenate(totals, axis=2)
    return full[None], total[0][None], total[1][None]


def solution(mesh):
    in_specs = (
        P(None, ("blk", "uly", "dp"), None),
        P(None, ("blk", "uly", "dp"), None),
        P(None, ("blk", "uly", "dp"), None),
        P(None, ("blk", "uly", "dp"), None),
        P(),
        P(),
    )
    out_specs = (
        P("dp", ("blk", "uly"), None, None),
        P("dp", ("blk", "uly"), None),
        P("dp", ("blk", "uly"), None),
    )
    return jax.shard_map(shards, mesh=mesh, in_specs=in_specs, out_specs=out_specs, check_vma=False)
```

```python
import functools

import jax
import jax.numpy as jnp
from jax import lax
from jax.experimental import pallas as pl
from jax.experimental.pallas import tpu as pltpu
from jax.sharding import PartitionSpec as P

HD = 128
LOG2E = 1.4426950408889634
BIG_NEGATIVE = -1e30
VMEM_BYTES = 32 * 1024 * 1024
HEADS_STEP = 2
CALL_COST = (1, 1, 1, 100)


def target_of(index, step, count):
    return lax.rem(index + step, count)


def source_of(index, step, count):
    return lax.rem(index + count - step, count)


def exchanged(value, axis, step):
    count = lax.axis_size(axis)
    return lax.ppermute(value, axis, [(i, (i + step) % count) for i in range(count)])


def shifted(value, axis, by):
    length = lax.axis_size(axis)
    pairs = [(i, i + by) for i in range(length) if 0 <= i + by < length]
    return lax.ppermute(value, axis, pairs)


def stage_kernel(count, jobs, outs, assign_ref, *refs):
    group = lax.axis_index("dp")
    sources, refs = refs[:4], refs[4:]
    out_refs, held_refs, (in_sems, out_sems) = refs[:outs], refs[outs : 2 * outs], refs[-2:]
    loads, stores = [], []
    for out, (first, step, start, width, *_) in enumerate(jobs):
        chosen = assign_ref[target_of(group, step, count)]
        for which in range(out_refs[out].shape[0]):
            origin = sources[first + which].at[chosen, :, start : start + width]
            held, slot = held_refs[out].at[which], 2 * out + which
            loads.append(pltpu.make_async_copy(origin, held, in_sems.at[slot]))
            stores.append(pltpu.make_async_copy(held, out_refs[out].at[which], out_sems.at[slot]))
    for load in loads:
        load.start()
    for load, store in zip(loads, stores):
        load.wait()
        store.start()
    for store in stores:
        store.wait()


def stage(assignment, arrays, jobs):
    count, rows, _ = arrays[0].shape
    shapes = [(job[4] if len(job) > 4 else 2, rows, job[3]) for job in jobs]
    kind = arrays[0].dtype
    far = pl.BlockSpec(memory_space=pltpu.HBM)
    return pl.pallas_call(
        functools.partial(stage_kernel, count, jobs, len(jobs)),
        out_shape=[jax.ShapeDtypeStruct(shape, kind) for shape in shapes],
        in_specs=[pl.BlockSpec(memory_space=pltpu.SMEM)] + [far] * len(arrays),
        out_specs=[far] * len(jobs),
        scratch_shapes=[pltpu.VMEM(shape, kind) for shape in shapes]
        + [pltpu.SemaphoreType.DMA((2 * len(jobs),))] * 2,
        name="stage",
    )(assignment, *arrays)


def build_bias(source, sequence, line, segment_ref, column_ref, bias_ref, rows, tok_dev, reach):
    keys, lanes = column_ref.shape
    pieces = keys // tok_dev
    window = bias_ref.shape[0]
    eye = lax.broadcasted_iota(jnp.int32, (tok_dev, tok_dev), 0) == lax.broadcasted_iota(
        jnp.int32, (tok_dev, tok_dev), 1
    )
    for place in range(pieces):
        back = pieces - 1 - place
        start = pl.multiple_of(jnp.maximum(line - back, 0) * tok_dev, tok_dev)
        every = segment_ref[:, pl.ds(start, tok_dev)].astype(jnp.float32)
        mine = lax.broadcasted_iota(jnp.int32, every.shape, 0) == sequence
        row = jnp.sum(jnp.where(mine, every, 0.0), axis=0, keepdims=True)
        column = jnp.sum(jnp.where(eye, row, 0.0), axis=1, keepdims=True)
        column = jnp.where(line >= back, column, -1.0)
        column_ref[place * tok_dev : (place + 1) * tok_dev, :] = jnp.broadcast_to(
            column, (tok_dev, lanes)
        )

    def token(shape):
        return lax.rem(lax.broadcasted_iota(jnp.int32, shape, 1), jnp.int32(rows))

    here = pl.multiple_of(keys - tok_dev + source * rows, rows)
    asked_rows = column_ref[pl.ds(here, rows), :]
    same = lax.broadcasted_iota(jnp.int32, (rows, lanes), 0) == token((rows, lanes))
    asked = jnp.sum(jnp.where(same, asked_rows, 0.0), axis=0, keepdims=True)
    held = column_ref[pl.ds(pl.multiple_of(here - reach, rows), window), :]
    place = lax.broadcasted_iota(jnp.int32, (window, lanes), 0)
    allowed = (held == asked) & (place <= token((window, lanes)) + reach)
    bias_ref[...] = jnp.where(allowed, 0.0, BIG_NEGATIVE)


def attend_kernel(
    step, first, filled, last, tok_dev, reach, ratio,
    meta_ref, assign_ref, segment_ref, query_ref, grad_ref, kv_ref, *refs,
):
    refs = list(refs)
    if not first:
        acc_in_ref = refs.pop(0)
    if filled:
        refs.pop(0)
    query_out_ref = refs.pop(0)
    column_ref, bias_ref = refs[-2 - last], refs[-1 - last]
    if last:
        own_ref, halo_refs, acc_ref = refs[0], refs[1:-3], refs[-1]
    else:
        acc_ref = refs[0]

    rows = query_ref.shape[0]
    window = bias_ref.shape[0]
    keys = column_ref.shape[0]
    scale = 1.0 / HD**0.5
    group = meta_ref[0]
    source = source_of(group, step, tok_dev // rows)
    block = (keys - tok_dev - reach) // rows + source
    span = pl.ds(pl.multiple_of(block * rows, rows), window)

    def mask():
        build_bias(
            source, assign_ref[group], meta_ref[1], segment_ref, column_ref, bias_ref, rows, tok_dev, reach
        )

    if last:
        mask()
    else:
        pl.when(pl.program_id(0) == 0)(mask)

    acc_ref[...] = jnp.zeros_like(acc_ref) if first else acc_in_ref[...]
    turned, across = (((1,), (1,)), ((), ())), (((0,), (0,)), ((), ()))
    heads = range(HEADS_STEP)
    lanes = [slice(head * HD, (head + 1) * HD) for head in heads]

    def product(left, right, contract):
        return lax.dot_general(left, right, contract, preferred_element_type=jnp.float32)

    def stacked(ref, head):
        start = head * ratio
        return jnp.concatenate(
            [ref[:, r * HD : (r + 1) * HD] for r in range(start, start + ratio)], axis=0
        )

    def windowed(which, head):
        return kv_ref[pl.ds(block, window // rows), which, :, lanes[head]].reshape(window, HD)

    plain = (((1,), (0,)), ((), ()))
    query, key = [stacked(query_ref, head) for head in heads], [windowed(0, head) for head in heads]
    scores = [product(key[head], query[head], turned) for head in heads]
    grad, value = [stacked(grad_ref, head) for head in heads], [windowed(1, head) for head in heads]
    grad_probs = [product(value[head], grad[head], turned) for head in heads]
    probs, grad_scores = [], []
    for head in heads:
        score = scores[head] * (scale * LOG2E) + bias_ref[...]
        weights = jnp.exp2(score - jnp.max(score, axis=0, keepdims=True))
        probs.append(weights * (1.0 / jnp.sum(weights, axis=0, keepdims=True)))
    for head in heads:
        weighted = probs[head] * grad_probs[head]
        delta = jnp.sum(weighted, axis=0, keepdims=True)
        grad_scores.append((weighted - probs[head] * delta).astype(jnp.bfloat16))
    grads = []
    for head in heads:
        grad_query = product(grad_scores[head], key[head], across)
        grads.append((grad_query * scale).reshape(ratio, rows, HD))
    grad_key = [product(grad_scores[head], query[head], plain) for head in heads]
    grad_value = [product(probs[head].astype(jnp.bfloat16), grad[head], plain) for head in heads]
    for head in heads:
        acc_ref[0, span, lanes[head]] += grad_key[head]
        acc_ref[1, span, lanes[head]] += grad_value[head]
    if last:
        own_ref[0] = acc_ref[0, keys - tok_dev :] * scale
        own_ref[1] = acc_ref[1, keys - tok_dev :]
        for back, halo_ref in enumerate(halo_refs, 1):
            part = slice(keys - (back + 1) * tok_dev, keys - back * tok_dev)
            halo_ref[0] = (acc_ref[0, part] * scale).astype(jnp.bfloat16)
            halo_ref[1] = acc_ref[1, part].astype(jnp.bfloat16)
    query_out_ref[...] = jnp.swapaxes(jnp.concatenate(grads, axis=0), 0, 1).astype(jnp.bfloat16)


def attend(step, base, span, reach, heads, meta, assignment, segments, query, grad, kv, acc, full, last):
    first, filled = acc is None, full is not None
    rows, (blocks, _, _, kv_width) = query[0].shape[1], kv.shape
    ratio = heads // (kv_width // HD)
    keys, tok_dev = blocks * rows, query[0].shape[1] * lax.axis_size("dp")
    pieces, window = keys // tok_dev, reach + rows
    lanes, place = HEADS_STEP * HD, base // HEADS_STEP

    def rows_spec(array, pick):
        start = place if array.shape[2] == heads * HD else 0
        return pl.BlockSpec(
            (None, rows, HEADS_STEP * ratio * HD), lambda c, m, a: (pick(m, a), 0, start + c)
        )

    in_specs = [
        pl.BlockSpec(segments.shape, lambda c, m, a: (0, 0)),
        rows_spec(*query),
        rows_spec(*grad),
    ]
    in_specs.append(pl.BlockSpec((blocks, 2, rows, lanes), lambda c, m, a: (0, 0, 0, place + c)))
    operands = [meta, assignment, segments, query[0], grad[0], kv]
    aliases = {}
    acc_spec = pl.BlockSpec((2, keys, lanes), lambda c, m, a: (0, 0, place + c))
    if not first:
        if not last:
            aliases[len(operands)] = 1
        operands.append(acc)
        in_specs.append(acc_spec)
    if filled:
        aliases[len(operands)] = 0
        operands.append(full)
        in_specs.append(pl.BlockSpec(memory_space=pl.ANY))
    out_shape = [jax.ShapeDtypeStruct((tok_dev, heads, HD), jnp.bfloat16)]
    out_specs = [
        pl.BlockSpec(
            (rows, HEADS_STEP * ratio, HD),
            lambda c, m, a: (source_of(m[0], step, tok_dev // rows), place + c, 0),
        )
    ]
    if last:
        span_spec = pl.BlockSpec((2, tok_dev, lanes), lambda c, m, a: (0, 0, c))
        out_shape.append(jax.ShapeDtypeStruct((2, tok_dev, span * HD), jnp.float32))
        out_shape += [jax.ShapeDtypeStruct((2, tok_dev, span * HD), jnp.bfloat16)] * (pieces - 1)
        out_specs += [span_spec] * pieces
    else:
        out_shape.append(jax.ShapeDtypeStruct((2, keys, kv_width), jnp.float32))
        out_specs.append(acc_spec)
    pairs = span * ratio * rows * window
    cost = CALL_COST[step] if step < len(CALL_COST) and not last else 1
    held = (keys, ratio * rows), (window, ratio * rows)
    held += ((2, keys, lanes),) * last
    return pl.pallas_call(
        functools.partial(attend_kernel, step, first, filled, last, tok_dev, reach, ratio),
        out_shape=out_shape,
        grid_spec=pltpu.PrefetchScalarGridSpec(
            num_scalar_prefetch=2,
            grid=(span // HEADS_STEP,),
            in_specs=in_specs,
            out_specs=out_specs,
            scratch_shapes=[pltpu.VMEM(shape, jnp.float32) for shape in held],
        ),
        input_output_aliases=aliases,
        compiler_params=pltpu.CompilerParams(
            dimension_semantics=("arbitrary",), vmem_limit_bytes=VMEM_BYTES
        ),
        cost_estimate=pl.CostEstimate(
            flops=pairs * HD * cost, bytes_accessed=pairs * cost, transcendentals=0
        ),
        name="attend",
    )(*operands)


def shards(queries, keys, values, grad_out, segment_ids, assignment):
    count = lax.axis_size("dp")
    uly = lax.axis_size("uly")
    group = lax.axis_index("dp")
    line = lax.axis_index("blk") * uly + lax.axis_index("uly")
    width, kv_width = queries.shape[2], keys.shape[2]
    heads, kv_heads = width // HD, kv_width // HD
    tok_dev = count * queries.shape[1]
    doc_most = min(512, tok_dev * uly)
    hops = -(-doc_most // tok_dev)
    meta = jnp.stack([group, line]).astype(jnp.int32)

    final, halves = count // 2, kv_heads // HEADS_STEP
    part = width // halves
    others = [step for step in range(1, count) if step != final]
    jobs = [(2, step, 0, kv_width) for step in range(count)]
    jobs += [(0, step, 0, width) for step in others]
    jobs += [(which, final, half * part, part, 1) for half in range(halves) for which in range(2)]
    staged = stage(assignment, (queries, grad_out, keys, values), jobs)
    kv_staged, staged = staged[:count], list(staged[count:])
    kv_arrived = [exchanged(kv_staged[step], "dp", step) for step in range(1, count)]
    staged, mine, kv_arrived[0] = lax.optimization_barrier((staged, kv_staged[0], kv_arrived[0]))
    arrived = [exchanged(rows, "dp", step) for rows, step in zip(staged, others)]
    held = staged[len(others) :]
    kv_own = jnp.zeros((count, *kv_staged[0].shape), keys.dtype)
    for step, piece in enumerate([mine, *kv_arrived]):
        kv_own = lax.dynamic_update_index_in_dim(
            kv_own, piece, source_of(group, step, count), 0
        )
    halos = [shifted(kv_own, ("blk", "uly"), back) for back in range(hops, 0, -1)]
    kv = jnp.concatenate([*halos, kv_own], axis=0)

    fixed = (doc_most, heads, meta, assignment, segment_ids)
    query, grad = (queries, lambda m, a: a[m[0]]), (grad_out, lambda m, a: a[m[0]])
    full, acc = attend(0, 0, kv_heads, *fixed, query, grad, kv, None, None, False)
    rows, acc = lax.optimization_barrier((held[0], acc))
    split = [exchanged(rows, "dp", final)]
    for at, (step, both) in enumerate(zip(others, arrived)):
        if not at:
            rows, both = lax.optimization_barrier((held[1], both))
            split.append(exchanged(rows, "dp", final))
        query, grad = (both, lambda m, a: 0), (both, lambda m, a: 1)
        full, acc = attend(step, 0, kv_heads, *fixed, query, grad, kv, acc, full, False)
        rows, acc = lax.optimization_barrier((held[2 + at], acc))
        split.append(exchanged(rows, "dp", final))
    totals, returned = [], []
    for half in range(halves):
        query, grad = [(rows, lambda m, a: 0) for rows in split[2 * half : 2 * half + 2]]
        full, total, *halos = attend(
            final, half * HEADS_STEP, HEADS_STEP, *fixed, query, grad, kv, acc, full, True
        )
        if half:
            halos, returned[0] = lax.optimization_barrier((halos, returned[0]))
        returned = [shifted(halo, ("blk", "uly"), -back) for back, halo in enumerate(halos, 1)]
        for halo in returned:
            total = total + halo.astype(jnp.float32)
        totals.append(total.astype(jnp.bfloat16))
    total = jnp.concatenate(totals, axis=2)
    return full[None], total[0][None], total[1][None]


def solution(mesh):
    in_specs = (
        P(None, ("blk", "uly", "dp"), None),
        P(None, ("blk", "uly", "dp"), None),
        P(None, ("blk", "uly", "dp"), None),
        P(None, ("blk", "uly", "dp"), None),
        P(),
        P(),
    )
    out_specs = (
        P("dp", ("blk", "uly"), None, None),
        P("dp", ("blk", "uly"), None),
        P("dp", ("blk", "uly"), None),
    )
    return jax.shard_map(shards, mesh=mesh, in_specs=in_specs, out_specs=out_specs, check_vma=False)
```

```python
import functools

import jax
import jax.numpy as jnp
from jax import lax
from jax.experimental import pallas as pl
from jax.experimental.pallas import tpu as pltpu
from jax.sharding import PartitionSpec as P

HD = 128
LOG2E = 1.4426950408889634
BIG_NEGATIVE = -1e30
VMEM_BYTES = 32 * 1024 * 1024
HEADS_STEP = 2
CALL_COST = 30


def target_of(index, step, count):
    return lax.rem(index + step, count)


def source_of(index, step, count):
    return lax.rem(index + count - step, count)


def exchanged(value, axis, step):
    count = lax.axis_size(axis)
    return lax.ppermute(value, axis, [(i, (i + step) % count) for i in range(count)])


def shifted(value, axis, by):
    length = lax.axis_size(axis)
    pairs = [(i, i + by) for i in range(length) if 0 <= i + by < length]
    return lax.ppermute(value, axis, pairs)


def stage_kernel(count, jobs, outs, assign_ref, *refs):
    group = lax.axis_index("dp")
    sources, refs = refs[:4], refs[4:]
    out_refs, held_refs, (in_sems, out_sems) = refs[:outs], refs[outs : 2 * outs], refs[-2:]
    loads, stores = [], []
    for out, (first, step, start, width, *_) in enumerate(jobs):
        chosen = assign_ref[target_of(group, step, count)]
        for which in range(out_refs[out].shape[0]):
            origin = sources[first + which].at[chosen, :, start : start + width]
            held, slot = held_refs[out].at[which], 2 * out + which
            loads.append(pltpu.make_async_copy(origin, held, in_sems.at[slot]))
            stores.append(pltpu.make_async_copy(held, out_refs[out].at[which], out_sems.at[slot]))
    for load in loads:
        load.start()
    for load, store in zip(loads, stores):
        load.wait()
        store.start()
    for store in stores:
        store.wait()


def stage(assignment, arrays, jobs):
    count, rows, _ = arrays[0].shape
    shapes = [(job[4] if len(job) > 4 else 2, rows, job[3]) for job in jobs]
    kind = arrays[0].dtype
    far = pl.BlockSpec(memory_space=pltpu.HBM)
    return pl.pallas_call(
        functools.partial(stage_kernel, count, jobs, len(jobs)),
        out_shape=[jax.ShapeDtypeStruct(shape, kind) for shape in shapes],
        in_specs=[pl.BlockSpec(memory_space=pltpu.SMEM)] + [far] * len(arrays),
        out_specs=[far] * len(jobs),
        scratch_shapes=[pltpu.VMEM(shape, kind) for shape in shapes]
        + [pltpu.SemaphoreType.DMA((2 * len(jobs),))] * 2,
        name="stage",
    )(assignment, *arrays)


def build_bias(source, sequence, line, segment_ref, column_ref, bias_ref, rows, tok_dev, reach):
    keys, lanes = column_ref.shape
    pieces = keys // tok_dev
    window = bias_ref.shape[0]
    eye = lax.broadcasted_iota(jnp.int32, (tok_dev, tok_dev), 0) == lax.broadcasted_iota(
        jnp.int32, (tok_dev, tok_dev), 1
    )
    for place in range(pieces):
        back = pieces - 1 - place
        start = pl.multiple_of(jnp.maximum(line - back, 0) * tok_dev, tok_dev)
        every = segment_ref[:, pl.ds(start, tok_dev)].astype(jnp.float32)
        mine = lax.broadcasted_iota(jnp.int32, every.shape, 0) == sequence
        row = jnp.sum(jnp.where(mine, every, 0.0), axis=0, keepdims=True)
        column = jnp.sum(jnp.where(eye, row, 0.0), axis=1, keepdims=True)
        column = jnp.where(line >= back, column, -1.0)
        column_ref[place * tok_dev : (place + 1) * tok_dev, :] = jnp.broadcast_to(
            column, (tok_dev, lanes)
        )

    def token(shape):
        return lax.rem(lax.broadcasted_iota(jnp.int32, shape, 1), jnp.int32(rows))

    here = pl.multiple_of(keys - tok_dev + source * rows, rows)
    asked_rows = column_ref[pl.ds(here, rows), :]
    same = lax.broadcasted_iota(jnp.int32, (rows, lanes), 0) == token((rows, lanes))
    asked = jnp.sum(jnp.where(same, asked_rows, 0.0), axis=0, keepdims=True)
    held = column_ref[pl.ds(pl.multiple_of(here - reach, rows), window), :]
    place = lax.broadcasted_iota(jnp.int32, (window, lanes), 0)
    allowed = (held == asked) & (place <= token((window, lanes)) + reach)
    bias_ref[...] = jnp.where(allowed, 0.0, BIG_NEGATIVE)


def attend_kernel(
    step, first, filled, last, tok_dev, reach, ratio,
    meta_ref, assign_ref, segment_ref, query_ref, grad_ref, kv_ref, *refs,
):
    refs = list(refs)
    if not first:
        acc_in_ref = refs.pop(0)
    if filled:
        refs.pop(0)
    query_out_ref = refs.pop(0)
    column_ref, bias_ref = refs[-2 - last], refs[-1 - last]
    if last:
        own_ref, halo_refs, acc_ref = refs[0], refs[1:-3], refs[-1]
    else:
        acc_ref = refs[0]

    rows = query_ref.shape[0]
    window = bias_ref.shape[0]
    keys = column_ref.shape[0]
    scale = 1.0 / HD**0.5
    group = meta_ref[0]
    source = source_of(group, step, tok_dev // rows)
    block = (keys - tok_dev - reach) // rows + source
    span = pl.ds(pl.multiple_of(block * rows, rows), window)

    def mask():
        build_bias(
            source, assign_ref[group], meta_ref[1], segment_ref, column_ref, bias_ref, rows, tok_dev, reach
        )

    if last:
        mask()
    else:
        pl.when(pl.program_id(0) == 0)(mask)

    acc_ref[...] = jnp.zeros_like(acc_ref) if first else acc_in_ref[...]
    turned, across = (((1,), (1,)), ((), ())), (((0,), (0,)), ((), ()))
    heads = range(HEADS_STEP)
    lanes = [slice(head * HD, (head + 1) * HD) for head in heads]

    def product(left, right, contract):
        return lax.dot_general(left, right, contract, preferred_element_type=jnp.float32)

    def stacked(ref, head):
        start = head * ratio
        return jnp.concatenate(
            [ref[:, r * HD : (r + 1) * HD] for r in range(start, start + ratio)], axis=0
        )

    def windowed(which, head):
        return kv_ref[pl.ds(block, window // rows), which, :, lanes[head]].reshape(window, HD)

    plain = (((1,), (0,)), ((), ()))
    query, key = [stacked(query_ref, head) for head in heads], [windowed(0, head) for head in heads]
    scores = [product(key[head], query[head], turned) for head in heads]
    grad, value = [stacked(grad_ref, head) for head in heads], [windowed(1, head) for head in heads]
    grad_probs = [product(value[head], grad[head], turned) for head in heads]
    probs, grad_scores = [], []
    for head in heads:
        score = scores[head] * (scale * LOG2E) + bias_ref[...]
        weights = jnp.exp2(score - jnp.max(score, axis=0, keepdims=True))
        probs.append(weights * (1.0 / jnp.sum(weights, axis=0, keepdims=True)))
    for head in heads:
        weighted = probs[head] * grad_probs[head]
        delta = jnp.sum(weighted, axis=0, keepdims=True)
        grad_scores.append((weighted - probs[head] * delta).astype(jnp.bfloat16))
    grads = []
    for head in heads:
        grad_query = product(grad_scores[head], key[head], across)
        grads.append((grad_query * scale).reshape(ratio, rows, HD))
    grad_key = [product(grad_scores[head], query[head], plain) for head in heads]
    grad_value = [product(probs[head].astype(jnp.bfloat16), grad[head], plain) for head in heads]
    for head in heads:
        acc_ref[0, span, lanes[head]] += grad_key[head]
        acc_ref[1, span, lanes[head]] += grad_value[head]
    if last:
        own_ref[0] = acc_ref[0, keys - tok_dev :] * scale
        own_ref[1] = acc_ref[1, keys - tok_dev :]
        for back, halo_ref in enumerate(halo_refs, 1):
            part = slice(keys - (back + 1) * tok_dev, keys - back * tok_dev)
            halo_ref[0] = (acc_ref[0, part] * scale).astype(jnp.bfloat16)
            halo_ref[1] = acc_ref[1, part].astype(jnp.bfloat16)
    query_out_ref[...] = jnp.swapaxes(jnp.concatenate(grads, axis=0), 0, 1).astype(jnp.bfloat16)


def attend(step, base, span, reach, heads, meta, assignment, segments, query, grad, kv, acc, full, last):
    first, filled = acc is None, full is not None
    rows, (blocks, _, _, kv_width) = query[0].shape[1], kv.shape
    ratio = heads // (kv_width // HD)
    keys, tok_dev = blocks * rows, query[0].shape[1] * lax.axis_size("dp")
    pieces, window = keys // tok_dev, reach + rows
    lanes, place = HEADS_STEP * HD, base // HEADS_STEP

    def rows_spec(array, pick):
        start = place if array.shape[2] == heads * HD else 0
        return pl.BlockSpec(
            (None, rows, HEADS_STEP * ratio * HD), lambda c, m, a: (pick(m, a), 0, start + c)
        )

    in_specs = [
        pl.BlockSpec(segments.shape, lambda c, m, a: (0, 0)),
        rows_spec(*query),
        rows_spec(*grad),
    ]
    in_specs.append(pl.BlockSpec((blocks, 2, rows, lanes), lambda c, m, a: (0, 0, 0, place + c)))
    operands = [meta, assignment, segments, query[0], grad[0], kv]
    aliases = {}
    acc_spec = pl.BlockSpec((2, keys, lanes), lambda c, m, a: (0, 0, place + c))
    if not first:
        if not last:
            aliases[len(operands)] = 1
        operands.append(acc)
        in_specs.append(acc_spec)
    if filled:
        aliases[len(operands)] = 0
        operands.append(full)
        in_specs.append(pl.BlockSpec(memory_space=pl.ANY))
    out_shape = [jax.ShapeDtypeStruct((tok_dev, heads, HD), jnp.bfloat16)]
    out_specs = [
        pl.BlockSpec(
            (rows, HEADS_STEP * ratio, HD),
            lambda c, m, a: (source_of(m[0], step, tok_dev // rows), place + c, 0),
        )
    ]
    if last:
        span_spec = pl.BlockSpec((2, tok_dev, lanes), lambda c, m, a: (0, 0, c))
        out_shape.append(jax.ShapeDtypeStruct((2, tok_dev, span * HD), jnp.float32))
        out_shape += [jax.ShapeDtypeStruct((2, tok_dev, span * HD), jnp.bfloat16)] * (pieces - 1)
        out_specs += [span_spec] * pieces
    else:
        out_shape.append(jax.ShapeDtypeStruct((2, keys, kv_width), jnp.float32))
        out_specs.append(acc_spec)
    pairs = span * ratio * rows * window
    cost = CALL_COST if step and not last else 1
    held = (keys, ratio * rows), (window, ratio * rows)
    held += ((2, keys, lanes),) * last
    return pl.pallas_call(
        functools.partial(attend_kernel, step, first, filled, last, tok_dev, reach, ratio),
        out_shape=out_shape,
        grid_spec=pltpu.PrefetchScalarGridSpec(
            num_scalar_prefetch=2,
            grid=(span // HEADS_STEP,),
            in_specs=in_specs,
            out_specs=out_specs,
            scratch_shapes=[pltpu.VMEM(shape, jnp.float32) for shape in held],
        ),
        input_output_aliases=aliases,
        compiler_params=pltpu.CompilerParams(
            dimension_semantics=("arbitrary",), vmem_limit_bytes=VMEM_BYTES
        ),
        cost_estimate=pl.CostEstimate(
            flops=pairs * HD * cost, bytes_accessed=pairs * cost, transcendentals=0
        ),
        name="attend",
    )(*operands)


def shards(queries, keys, values, grad_out, segment_ids, assignment):
    count = lax.axis_size("dp")
    uly = lax.axis_size("uly")
    group = lax.axis_index("dp")
    line = lax.axis_index("blk") * uly + lax.axis_index("uly")
    width, kv_width = queries.shape[2], keys.shape[2]
    heads, kv_heads = width // HD, kv_width // HD
    tok_dev = count * queries.shape[1]
    doc_most = min(512, tok_dev * uly)
    hops = -(-doc_most // tok_dev)
    meta = jnp.stack([group, line]).astype(jnp.int32)

    final, halves = count // 2, kv_heads // HEADS_STEP
    part = width // halves
    others = [step for step in range(1, count) if step != final]
    jobs = [(2, step, 0, kv_width) for step in range(count)]
    jobs += [(0, step, 0, width) for step in others]
    jobs += [(0, final, half * part, part) for half in range(halves - 1)]
    jobs += [(which, final, (halves - 1) * part, part, 1) for which in range(2)]
    staged = stage(assignment, (queries, grad_out, keys, values), jobs)
    kv_staged, staged = staged[:count], list(staged[count:])
    kv_arrived = [exchanged(kv_staged[step], "dp", step) for step in range(1, count)]
    staged, kv_arrived[0] = lax.optimization_barrier((staged, kv_arrived[0]))
    arrived = [exchanged(rows, "dp", step) for rows, step in zip(staged, others)]
    held = staged[len(others) :]
    kv_own = jnp.zeros((count, *kv_staged[0].shape), keys.dtype)
    for step, piece in enumerate([kv_staged[0], *kv_arrived]):
        kv_own = lax.dynamic_update_index_in_dim(
            kv_own, piece, source_of(group, step, count), 0
        )
    halos = [shifted(kv_own, ("blk", "uly"), back) for back in range(hops, 0, -1)]
    kv = jnp.concatenate([*halos, kv_own], axis=0)

    fixed = (doc_most, heads, meta, assignment, segment_ids)
    query, grad = (queries, lambda m, a: a[m[0]]), (grad_out, lambda m, a: a[m[0]])
    full, acc = attend(0, 0, kv_heads, *fixed, query, grad, kv, None, None, False)
    rows, acc = lax.optimization_barrier((held[0], acc))
    split = [exchanged(rows, "dp", final)]
    for step, both in zip(others, arrived):
        query, grad = (both, lambda m, a: 0), (both, lambda m, a: 1)
        full, acc = attend(step, 0, kv_heads, *fixed, query, grad, kv, acc, full, False)
    rows, acc = lax.optimization_barrier((held[1:], acc))
    split += [exchanged(piece, "dp", final) for piece in rows]
    totals, returned = [], []
    for half in range(halves):
        both = split[half]
        query, grad = (both, lambda m, a: 0), (both, lambda m, a: 1)
        if half + 1 == halves:
            grad = (split[half + 1], lambda m, a: 0)
        full, total, *halos = attend(
            final, half * HEADS_STEP, HEADS_STEP, *fixed, query, grad, kv, acc, full, True
        )
        if half:
            halos, returned[0] = lax.optimization_barrier((halos, returned[0]))
        returned = [shifted(halo, ("blk", "uly"), -back) for back, halo in enumerate(halos, 1)]
        for halo in returned:
            total = total + halo.astype(jnp.float32)
        totals.append(total.astype(jnp.bfloat16))
    total = jnp.concatenate(totals, axis=2)
    return full[None], total[0][None], total[1][None]


def solution(mesh):
    in_specs = (
        P(None, ("blk", "uly", "dp"), None),
        P(None, ("blk", "uly", "dp"), None),
        P(None, ("blk", "uly", "dp"), None),
        P(None, ("blk", "uly", "dp"), None),
        P(),
        P(),
    )
    out_specs = (
        P("dp", ("blk", "uly"), None, None),
        P("dp", ("blk", "uly"), None),
        P("dp", ("blk", "uly"), None),
    )
    return jax.shard_map(shards, mesh=mesh, in_specs=in_specs, out_specs=out_specs, check_vma=False)
```

```python
import functools

import jax
import jax.numpy as jnp
from jax import lax
from jax.experimental import pallas as pl
from jax.experimental.pallas import tpu as pltpu
from jax.sharding import PartitionSpec as P

HD = 128
LOG2E = 1.4426950408889634
BIG_NEGATIVE = -1e30
VMEM_BYTES = 32 * 1024 * 1024
HEADS_STEP = 2
CALL_COST = 30


def target_of(index, step, count):
    return lax.rem(index + step, count)


def source_of(index, step, count):
    return lax.rem(index + count - step, count)


def exchanged(value, axis, step):
    count = lax.axis_size(axis)
    return lax.ppermute(value, axis, [(i, (i + step) % count) for i in range(count)])


def shifted(value, axis, by):
    length = lax.axis_size(axis)
    pairs = [(i, i + by) for i in range(length) if 0 <= i + by < length]
    return lax.ppermute(value, axis, pairs)


def stage_kernel(count, jobs, outs, assign_ref, *refs):
    group = lax.axis_index("dp")
    sources, refs = refs[:4], refs[4:]
    out_refs, held_refs, (in_sems, out_sems) = refs[:outs], refs[outs : 2 * outs], refs[-2:]
    loads, stores = [], []
    for out, (first, step, start, width, *_) in enumerate(jobs):
        chosen = assign_ref[target_of(group, step, count)]
        for which in range(out_refs[out].shape[0]):
            origin = sources[first + which].at[chosen, :, start : start + width]
            held, slot = held_refs[out].at[which], 2 * out + which
            loads.append(pltpu.make_async_copy(origin, held, in_sems.at[slot]))
            stores.append(pltpu.make_async_copy(held, out_refs[out].at[which], out_sems.at[slot]))
    for load in loads:
        load.start()
    for load, store in zip(loads, stores):
        load.wait()
        store.start()
    for store in stores:
        store.wait()


def stage(assignment, arrays, jobs):
    count, rows, _ = arrays[0].shape
    shapes = [(job[4] if len(job) > 4 else 2, rows, job[3]) for job in jobs]
    kind = arrays[0].dtype
    far = pl.BlockSpec(memory_space=pltpu.HBM)
    return pl.pallas_call(
        functools.partial(stage_kernel, count, jobs, len(jobs)),
        out_shape=[jax.ShapeDtypeStruct(shape, kind) for shape in shapes],
        in_specs=[pl.BlockSpec(memory_space=pltpu.SMEM)] + [far] * len(arrays),
        out_specs=[far] * len(jobs),
        scratch_shapes=[pltpu.VMEM(shape, kind) for shape in shapes]
        + [pltpu.SemaphoreType.DMA((2 * len(jobs),))] * 2,
        name="stage",
    )(assignment, *arrays)


def build_bias(source, sequence, line, segment_ref, column_ref, bias_ref, rows, tok_dev, reach):
    keys, lanes = column_ref.shape
    pieces = keys // tok_dev
    window = bias_ref.shape[0]
    eye = lax.broadcasted_iota(jnp.int32, (tok_dev, tok_dev), 0) == lax.broadcasted_iota(
        jnp.int32, (tok_dev, tok_dev), 1
    )
    for place in range(pieces):
        back = pieces - 1 - place
        start = pl.multiple_of(jnp.maximum(line - back, 0) * tok_dev, tok_dev)
        every = segment_ref[:, pl.ds(start, tok_dev)].astype(jnp.float32)
        mine = lax.broadcasted_iota(jnp.int32, every.shape, 0) == sequence
        row = jnp.sum(jnp.where(mine, every, 0.0), axis=0, keepdims=True)
        column = jnp.sum(jnp.where(eye, row, 0.0), axis=1, keepdims=True)
        column = jnp.where(line >= back, column, -1.0)
        column_ref[place * tok_dev : (place + 1) * tok_dev, :] = jnp.broadcast_to(
            column, (tok_dev, lanes)
        )

    def token(shape):
        return lax.rem(lax.broadcasted_iota(jnp.int32, shape, 1), jnp.int32(rows))

    here = pl.multiple_of(keys - tok_dev + source * rows, rows)
    asked_rows = column_ref[pl.ds(here, rows), :]
    same = lax.broadcasted_iota(jnp.int32, (rows, lanes), 0) == token((rows, lanes))
    asked = jnp.sum(jnp.where(same, asked_rows, 0.0), axis=0, keepdims=True)
    held = column_ref[pl.ds(pl.multiple_of(here - reach, rows), window), :]
    place = lax.broadcasted_iota(jnp.int32, (window, lanes), 0)
    allowed = (held == asked) & (place <= token((window, lanes)) + reach)
    bias_ref[...] = jnp.where(allowed, 0.0, BIG_NEGATIVE)


def attend_kernel(
    step, first, filled, last, tok_dev, reach, ratio,
    meta_ref, assign_ref, segment_ref, query_ref, grad_ref, kv_ref, *refs,
):
    refs = list(refs)
    if not first:
        acc_in_ref = refs.pop(0)
    if filled:
        refs.pop(0)
    query_out_ref = refs.pop(0)
    column_ref, bias_ref = refs[-2 - last], refs[-1 - last]
    if last:
        own_ref, halo_refs, acc_ref = refs[0], refs[1:-3], refs[-1]
    else:
        acc_ref = refs[0]

    rows = query_ref.shape[0]
    window = bias_ref.shape[0]
    keys = column_ref.shape[0]
    scale = 1.0 / HD**0.5
    group = meta_ref[0]
    source = source_of(group, step, tok_dev // rows)
    block = (keys - tok_dev - reach) // rows + source
    span = pl.ds(pl.multiple_of(block * rows, rows), window)

    def mask():
        build_bias(
            source, assign_ref[group], meta_ref[1], segment_ref, column_ref, bias_ref, rows, tok_dev, reach
        )

    if last:
        mask()
    else:
        pl.when(pl.program_id(0) == 0)(mask)

    acc_ref[...] = jnp.zeros_like(acc_ref) if first else acc_in_ref[...]
    turned, across = (((1,), (1,)), ((), ())), (((0,), (0,)), ((), ()))
    heads = range(HEADS_STEP)
    lanes = [slice(head * HD, (head + 1) * HD) for head in heads]

    def product(left, right, contract):
        return lax.dot_general(left, right, contract, preferred_element_type=jnp.float32)

    def stacked(ref, head):
        start = head * ratio
        return jnp.concatenate(
            [ref[:, r * HD : (r + 1) * HD] for r in range(start, start + ratio)], axis=0
        )

    def windowed(which, head):
        return kv_ref[pl.ds(block, window // rows), which, :, lanes[head]].reshape(window, HD)

    plain = (((1,), (0,)), ((), ()))
    query, key = [stacked(query_ref, head) for head in heads], [windowed(0, head) for head in heads]
    scores = [product(key[head], query[head], turned) for head in heads]
    grad, value = [stacked(grad_ref, head) for head in heads], [windowed(1, head) for head in heads]
    grad_probs = [product(value[head], grad[head], turned) for head in heads]
    probs, grad_scores = [], []
    for head in heads:
        score = scores[head] * (scale * LOG2E) + bias_ref[...]
        weights = jnp.exp2(score - jnp.max(score, axis=0, keepdims=True))
        probs.append(weights * (1.0 / jnp.sum(weights, axis=0, keepdims=True)))
    for head in heads:
        weighted = probs[head] * grad_probs[head]
        delta = jnp.sum(weighted, axis=0, keepdims=True)
        grad_scores.append((weighted - probs[head] * delta).astype(jnp.bfloat16))
    grads = []
    for head in heads:
        grad_query = product(grad_scores[head], key[head], across)
        grads.append((grad_query * scale).reshape(ratio, rows, HD))
    grad_key = [product(grad_scores[head], query[head], plain) for head in heads]
    grad_value = [product(probs[head].astype(jnp.bfloat16), grad[head], plain) for head in heads]
    for head in heads:
        acc_ref[0, span, lanes[head]] += grad_key[head]
        acc_ref[1, span, lanes[head]] += grad_value[head]
    if last:
        own_ref[0] = acc_ref[0, keys - tok_dev :] * scale
        own_ref[1] = acc_ref[1, keys - tok_dev :]
        for back, halo_ref in enumerate(halo_refs, 1):
            part = slice(keys - (back + 1) * tok_dev, keys - back * tok_dev)
            halo_ref[0] = (acc_ref[0, part] * scale).astype(jnp.bfloat16)
            halo_ref[1] = acc_ref[1, part].astype(jnp.bfloat16)
    query_out_ref[...] = jnp.swapaxes(jnp.concatenate(grads, axis=0), 0, 1).astype(jnp.bfloat16)


def attend(step, base, span, reach, heads, meta, assignment, segments, query, grad, kv, acc, full, last):
    first, filled = acc is None, full is not None
    rows, (blocks, _, _, kv_width) = query[0].shape[1], kv.shape
    ratio = heads // (kv_width // HD)
    keys, tok_dev = blocks * rows, query[0].shape[1] * lax.axis_size("dp")
    pieces, window = keys // tok_dev, reach + rows
    lanes, place = HEADS_STEP * HD, base // HEADS_STEP

    def rows_spec(array, pick):
        start = place if array.shape[2] == heads * HD else 0
        return pl.BlockSpec(
            (None, rows, HEADS_STEP * ratio * HD), lambda c, m, a: (pick(m, a), 0, start + c)
        )

    in_specs = [
        pl.BlockSpec(segments.shape, lambda c, m, a: (0, 0)),
        rows_spec(*query),
        rows_spec(*grad),
    ]
    in_specs.append(pl.BlockSpec((blocks, 2, rows, lanes), lambda c, m, a: (0, 0, 0, place + c)))
    operands = [meta, assignment, segments, query[0], grad[0], kv]
    aliases = {}
    acc_spec = pl.BlockSpec((2, keys, lanes), lambda c, m, a: (0, 0, place + c))
    if not first:
        if not last:
            aliases[len(operands)] = 1
        operands.append(acc)
        in_specs.append(acc_spec)
    if filled:
        aliases[len(operands)] = 0
        operands.append(full)
        in_specs.append(pl.BlockSpec(memory_space=pl.ANY))
    out_shape = [jax.ShapeDtypeStruct((tok_dev, heads, HD), jnp.bfloat16)]
    out_specs = [
        pl.BlockSpec(
            (rows, HEADS_STEP * ratio, HD),
            lambda c, m, a: (source_of(m[0], step, tok_dev // rows), place + c, 0),
        )
    ]
    if last:
        span_spec = pl.BlockSpec((2, tok_dev, lanes), lambda c, m, a: (0, 0, c))
        out_shape.append(jax.ShapeDtypeStruct((2, tok_dev, span * HD), jnp.float32))
        out_shape += [jax.ShapeDtypeStruct((2, tok_dev, span * HD), jnp.bfloat16)] * (pieces - 1)
        out_specs += [span_spec] * pieces
    else:
        out_shape.append(jax.ShapeDtypeStruct((2, keys, kv_width), jnp.float32))
        out_specs.append(acc_spec)
    pairs = span * ratio * rows * window
    cost = CALL_COST if step and not last else 1
    held = (keys, ratio * rows), (window, ratio * rows)
    held += ((2, keys, lanes),) * last
    return pl.pallas_call(
        functools.partial(attend_kernel, step, first, filled, last, tok_dev, reach, ratio),
        out_shape=out_shape,
        grid_spec=pltpu.PrefetchScalarGridSpec(
            num_scalar_prefetch=2,
            grid=(span // HEADS_STEP,),
            in_specs=in_specs,
            out_specs=out_specs,
            scratch_shapes=[pltpu.VMEM(shape, jnp.float32) for shape in held],
        ),
        input_output_aliases=aliases,
        compiler_params=pltpu.CompilerParams(
            dimension_semantics=("arbitrary",), vmem_limit_bytes=VMEM_BYTES
        ),
        cost_estimate=pl.CostEstimate(
            flops=pairs * HD * cost, bytes_accessed=pairs * cost, transcendentals=0
        ),
        name="attend",
    )(*operands)


def shards(queries, keys, values, grad_out, segment_ids, assignment):
    count = lax.axis_size("dp")
    uly = lax.axis_size("uly")
    group = lax.axis_index("dp")
    line = lax.axis_index("blk") * uly + lax.axis_index("uly")
    width, kv_width = queries.shape[2], keys.shape[2]
    heads, kv_heads = width // HD, kv_width // HD
    tok_dev = count * queries.shape[1]
    doc_most = min(512, tok_dev * uly)
    hops = -(-doc_most // tok_dev)
    meta = jnp.stack([group, line]).astype(jnp.int32)

    final, halves = count // 2, kv_heads // HEADS_STEP
    part = width // halves
    others = [step for step in range(1, count) if step != final]
    jobs = [(2, step, 0, kv_width) for step in range(count)]
    jobs += [(0, step, 0, width) for step in others]
    jobs += [(0, final, half * part, part) for half in range(halves - 1)]
    jobs += [(which, final, (halves - 1) * part, part, 1) for which in range(2)]
    staged = stage(assignment, (queries, grad_out, keys, values), jobs)
    kv_staged, staged = staged[:count], list(staged[count:])
    kv_arrived = [exchanged(kv_staged[step], "dp", step) for step in range(1, count)]
    staged, kv_arrived[0] = lax.optimization_barrier((staged, kv_arrived[0]))
    arrived = [exchanged(rows, "dp", step) for rows, step in zip(staged, others)]
    held = staged[len(others) :]
    kv_own = jnp.zeros((count, *kv_staged[0].shape), keys.dtype)
    for step, piece in enumerate([kv_staged[0], *kv_arrived]):
        kv_own = lax.dynamic_update_index_in_dim(
            kv_own, piece, source_of(group, step, count), 0
        )
    halos = [shifted(kv_own, ("blk", "uly"), back) for back in range(hops, 0, -1)]
    kv = jnp.concatenate([*halos, kv_own], axis=0)

    rows, kv = lax.optimization_barrier((held[0], kv))
    split = [exchanged(rows, "dp", final)]
    fixed = (doc_most, heads, meta, assignment, segment_ids)
    query, grad = (queries, lambda m, a: a[m[0]]), (grad_out, lambda m, a: a[m[0]])
    full, acc = attend(0, 0, kv_heads, *fixed, query, grad, kv, None, None, False)
    for step, both in zip(others, arrived):
        query, grad = (both, lambda m, a: 0), (both, lambda m, a: 1)
        full, acc = attend(step, 0, kv_heads, *fixed, query, grad, kv, acc, full, False)
    rows, acc = lax.optimization_barrier((held[1:], acc))
    split += [exchanged(piece, "dp", final) for piece in rows]
    totals, returned = [], []
    for half in range(halves):
        both = split[half]
        query, grad = (both, lambda m, a: 0), (both, lambda m, a: 1)
        if half + 1 == halves:
            grad = (split[half + 1], lambda m, a: 0)
        full, total, *halos = attend(
            final, half * HEADS_STEP, HEADS_STEP, *fixed, query, grad, kv, acc, full, True
        )
        if half:
            halos, returned[0] = lax.optimization_barrier((halos, returned[0]))
        returned = [shifted(halo, ("blk", "uly"), -back) for back, halo in enumerate(halos, 1)]
        for halo in returned:
            total = total + halo.astype(jnp.float32)
        totals.append(total.astype(jnp.bfloat16))
    total = jnp.concatenate(totals, axis=2)
    return full[None], total[0][None], total[1][None]


def solution(mesh):
    in_specs = (
        P(None, ("blk", "uly", "dp"), None),
        P(None, ("blk", "uly", "dp"), None),
        P(None, ("blk", "uly", "dp"), None),
        P(None, ("blk", "uly", "dp"), None),
        P(),
        P(),
    )
    out_specs = (
        P("dp", ("blk", "uly"), None, None),
        P("dp", ("blk", "uly"), None),
        P("dp", ("blk", "uly"), None),
    )
    return jax.shard_map(shards, mesh=mesh, in_specs=in_specs, out_specs=out_specs, check_vma=False)
```

```python
import functools

import jax
import jax.numpy as jnp
from jax import lax
from jax.experimental import pallas as pl
from jax.experimental.pallas import tpu as pltpu
from jax.sharding import PartitionSpec as P

HD = 128
LOG2E = 1.4426950408889634
BIG_NEGATIVE = -1e30
VMEM_BYTES = 32 * 1024 * 1024
HEADS_STEP = 2
CALL_COST = 30


def target_of(index, step, count):
    return lax.rem(index + step, count)


def source_of(index, step, count):
    return lax.rem(index + count - step, count)


def exchanged(value, axis, step):
    count = lax.axis_size(axis)
    return lax.ppermute(value, axis, [(i, (i + step) % count) for i in range(count)])


def shifted(value, axis, by):
    length = lax.axis_size(axis)
    pairs = [(i, i + by) for i in range(length) if 0 <= i + by < length]
    return lax.ppermute(value, axis, pairs)


def stage_kernel(count, jobs, outs, assign_ref, *refs):
    group = lax.axis_index("dp")
    sources, refs = refs[:4], refs[4:]
    out_refs, held_refs, (in_sems, out_sems) = refs[:outs], refs[outs : 2 * outs], refs[-2:]
    loads, stores = [], []
    for out, (first, step, start, width, *_) in enumerate(jobs):
        chosen = assign_ref[target_of(group, step, count)]
        for which in range(out_refs[out].shape[0]):
            origin = sources[first + which].at[chosen, :, start : start + width]
            held, slot = held_refs[out].at[which], 2 * out + which
            loads.append(pltpu.make_async_copy(origin, held, in_sems.at[slot]))
            stores.append(pltpu.make_async_copy(held, out_refs[out].at[which], out_sems.at[slot]))
    for load in loads:
        load.start()
    for load, store in zip(loads, stores):
        load.wait()
        store.start()
    for store in stores:
        store.wait()


def stage(assignment, arrays, jobs):
    count, rows, _ = arrays[0].shape
    shapes = [(job[4] if len(job) > 4 else 2, rows, job[3]) for job in jobs]
    kind = arrays[0].dtype
    far = pl.BlockSpec(memory_space=pltpu.HBM)
    return pl.pallas_call(
        functools.partial(stage_kernel, count, jobs, len(jobs)),
        out_shape=[jax.ShapeDtypeStruct(shape, kind) for shape in shapes],
        in_specs=[pl.BlockSpec(memory_space=pltpu.SMEM)] + [far] * len(arrays),
        out_specs=[far] * len(jobs),
        scratch_shapes=[pltpu.VMEM(shape, kind) for shape in shapes]
        + [pltpu.SemaphoreType.DMA((2 * len(jobs),))] * 2,
        name="stage",
    )(assignment, *arrays)


def build_bias(source, sequence, line, segment_ref, column_ref, bias_ref, rows, tok_dev, reach):
    keys, lanes = column_ref.shape
    pieces = keys // tok_dev
    window = bias_ref.shape[0]
    eye = lax.broadcasted_iota(jnp.int32, (tok_dev, tok_dev), 0) == lax.broadcasted_iota(
        jnp.int32, (tok_dev, tok_dev), 1
    )
    for place in range(pieces):
        back = pieces - 1 - place
        start = pl.multiple_of(jnp.maximum(line - back, 0) * tok_dev, tok_dev)
        every = segment_ref[:, pl.ds(start, tok_dev)].astype(jnp.float32)
        mine = lax.broadcasted_iota(jnp.int32, every.shape, 0) == sequence
        row = jnp.sum(jnp.where(mine, every, 0.0), axis=0, keepdims=True)
        column = jnp.sum(jnp.where(eye, row, 0.0), axis=1, keepdims=True)
        column = jnp.where(line >= back, column, -1.0)
        column_ref[place * tok_dev : (place + 1) * tok_dev, :] = jnp.broadcast_to(
            column, (tok_dev, lanes)
        )

    def token(shape):
        return lax.rem(lax.broadcasted_iota(jnp.int32, shape, 1), jnp.int32(rows))

    here = pl.multiple_of(keys - tok_dev + source * rows, rows)
    asked_rows = column_ref[pl.ds(here, rows), :]
    same = lax.broadcasted_iota(jnp.int32, (rows, lanes), 0) == token((rows, lanes))
    asked = jnp.sum(jnp.where(same, asked_rows, 0.0), axis=0, keepdims=True)
    held = column_ref[pl.ds(pl.multiple_of(here - reach, rows), window), :]
    place = lax.broadcasted_iota(jnp.int32, (window, lanes), 0)
    allowed = (held == asked) & (place <= token((window, lanes)) + reach)
    bias_ref[...] = jnp.where(allowed, 0.0, BIG_NEGATIVE)


def attend_kernel(
    step, first, filled, last, tok_dev, reach, ratio,
    meta_ref, assign_ref, segment_ref, query_ref, grad_ref, kv_ref, *refs,
):
    refs = list(refs)
    if not first:
        acc_in_ref = refs.pop(0)
    if filled:
        refs.pop(0)
    query_out_ref = refs.pop(0)
    column_ref, bias_ref = refs[-2 - last], refs[-1 - last]
    if last:
        own_ref, halo_refs, acc_ref = refs[0], refs[1:-3], refs[-1]
    else:
        acc_ref = refs[0]

    rows = query_ref.shape[0]
    window = bias_ref.shape[0]
    keys = column_ref.shape[0]
    scale = 1.0 / HD**0.5
    group = meta_ref[0]
    source = source_of(group, step, tok_dev // rows)
    block = (keys - tok_dev - reach) // rows + source
    span = pl.ds(pl.multiple_of(block * rows, rows), window)

    def mask():
        build_bias(
            source, assign_ref[group], meta_ref[1], segment_ref, column_ref, bias_ref, rows, tok_dev, reach
        )

    if last:
        mask()
    else:
        pl.when(pl.program_id(0) == 0)(mask)

    acc_ref[...] = jnp.zeros_like(acc_ref) if first else acc_in_ref[...]
    turned, across = (((1,), (1,)), ((), ())), (((0,), (0,)), ((), ()))
    heads = range(HEADS_STEP)
    lanes = [slice(head * HD, (head + 1) * HD) for head in heads]

    def product(left, right, contract):
        return lax.dot_general(left, right, contract, preferred_element_type=jnp.float32)

    def stacked(ref, head):
        start = head * ratio
        return jnp.concatenate(
            [ref[:, r * HD : (r + 1) * HD] for r in range(start, start + ratio)], axis=0
        )

    def windowed(which, head):
        return kv_ref[pl.ds(block, window // rows), which, :, lanes[head]].reshape(window, HD)

    plain = (((1,), (0,)), ((), ()))
    query, key = [stacked(query_ref, head) for head in heads], [windowed(0, head) for head in heads]
    scores = [product(key[head], query[head], turned) for head in heads]
    grad, value = [stacked(grad_ref, head) for head in heads], [windowed(1, head) for head in heads]
    grad_probs = [product(value[head], grad[head], turned) for head in heads]
    probs, grad_scores = [], []
    for head in heads:
        score = scores[head] * (scale * LOG2E) + bias_ref[...]
        weights = jnp.exp2(score - jnp.max(score, axis=0, keepdims=True))
        probs.append(weights * (1.0 / jnp.sum(weights, axis=0, keepdims=True)))
    for head in heads:
        weighted = probs[head] * grad_probs[head]
        delta = jnp.sum(weighted, axis=0, keepdims=True)
        grad_scores.append((weighted - probs[head] * delta).astype(jnp.bfloat16))
    grads = []
    for head in heads:
        if last:
            query_out_ref[head] = grad_scores[head]
            continue
        grad_query = product(grad_scores[head], key[head], across)
        grads.append((grad_query * scale).reshape(ratio, rows, HD))
    grad_key = [product(grad_scores[head], query[head], plain) for head in heads]
    grad_value = [product(probs[head].astype(jnp.bfloat16), grad[head], plain) for head in heads]
    for head in heads:
        acc_ref[0, span, lanes[head]] += grad_key[head]
        acc_ref[1, span, lanes[head]] += grad_value[head]
    if last:
        own_ref[0] = acc_ref[0, keys - tok_dev :] * scale
        own_ref[1] = acc_ref[1, keys - tok_dev :]
        for back, halo_ref in enumerate(halo_refs, 1):
            part = slice(keys - (back + 1) * tok_dev, keys - back * tok_dev)
            halo_ref[0] = (acc_ref[0, part] * scale).astype(jnp.bfloat16)
            halo_ref[1] = acc_ref[1, part].astype(jnp.bfloat16)
    if not last:
        turned_grads = jnp.swapaxes(jnp.concatenate(grads, axis=0), 0, 1)
        query_out_ref[...] = turned_grads.astype(jnp.bfloat16)


def attend(step, base, span, reach, heads, meta, assignment, segments, query, grad, kv, acc, full, last):
    first, filled = acc is None, full is not None and not last
    rows, (blocks, _, _, kv_width) = query[0].shape[1], kv.shape
    ratio = heads // (kv_width // HD)
    keys, tok_dev = blocks * rows, query[0].shape[1] * lax.axis_size("dp")
    pieces, window = keys // tok_dev, reach + rows
    lanes, place = HEADS_STEP * HD, base // HEADS_STEP

    def rows_spec(array, pick):
        start = place if array.shape[2] == heads * HD else 0
        return pl.BlockSpec(
            (None, rows, HEADS_STEP * ratio * HD), lambda c, m, a: (pick(m, a), 0, start + c)
        )

    in_specs = [
        pl.BlockSpec(segments.shape, lambda c, m, a: (0, 0)),
        rows_spec(*query),
        rows_spec(*grad),
    ]
    in_specs.append(pl.BlockSpec((blocks, 2, rows, lanes), lambda c, m, a: (0, 0, 0, place + c)))
    operands = [meta, assignment, segments, query[0], grad[0], kv]
    aliases = {}
    acc_spec = pl.BlockSpec((2, keys, lanes), lambda c, m, a: (0, 0, place + c))
    if not first:
        if not last:
            aliases[len(operands)] = 1
        operands.append(acc)
        in_specs.append(acc_spec)
    if filled:
        aliases[len(operands)] = 0
        operands.append(full)
        in_specs.append(pl.BlockSpec(memory_space=pl.ANY))
    out_shape = [jax.ShapeDtypeStruct((tok_dev, heads, HD), jnp.bfloat16)]
    out_specs = [
        pl.BlockSpec(
            (rows, HEADS_STEP * ratio, HD),
            lambda c, m, a: (source_of(m[0], step, tok_dev // rows), place + c, 0),
        )
    ]
    if last:
        stretch = (HEADS_STEP, window, ratio * rows)
        out_shape = [jax.ShapeDtypeStruct(stretch, jnp.bfloat16)]
        out_specs = [pl.BlockSpec(stretch, lambda c, m, a: (0, 0, 0))]
        span_spec = pl.BlockSpec((2, tok_dev, lanes), lambda c, m, a: (0, 0, c))
        out_shape.append(jax.ShapeDtypeStruct((2, tok_dev, span * HD), jnp.float32))
        out_shape += [jax.ShapeDtypeStruct((2, tok_dev, span * HD), jnp.bfloat16)] * (pieces - 1)
        out_specs += [span_spec] * pieces
    else:
        out_shape.append(jax.ShapeDtypeStruct((2, keys, kv_width), jnp.float32))
        out_specs.append(acc_spec)
    pairs = span * ratio * rows * window
    cost = CALL_COST if step and not last else 1
    held = (keys, ratio * rows), (window, ratio * rows)
    held += ((2, keys, lanes),) * last
    return pl.pallas_call(
        functools.partial(attend_kernel, step, first, filled, last, tok_dev, reach, ratio),
        out_shape=out_shape,
        grid_spec=pltpu.PrefetchScalarGridSpec(
            num_scalar_prefetch=2,
            grid=(span // HEADS_STEP,),
            in_specs=in_specs,
            out_specs=out_specs,
            scratch_shapes=[pltpu.VMEM(shape, jnp.float32) for shape in held],
        ),
        input_output_aliases=aliases,
        compiler_params=pltpu.CompilerParams(
            dimension_semantics=("arbitrary",), vmem_limit_bytes=VMEM_BYTES
        ),
        cost_estimate=pl.CostEstimate(
            flops=pairs * HD * cost, bytes_accessed=pairs * cost, transcendentals=0
        ),
        name="attend",
    )(*operands)


def turn_kernel(step, tok_dev, reach, meta_ref, scores_ref, key_ref, full_ref, out_ref):
    rows, blocks = out_ref.shape[0], key_ref.shape[0]
    window = scores_ref.shape[1]
    source = source_of(meta_ref[0], step, tok_dev // rows)
    block = (blocks * rows - tok_dev - reach) // rows + source
    grads = []
    for head in range(HEADS_STEP):
        key = key_ref[pl.ds(block, window // rows), :, head * HD : (head + 1) * HD]
        grad = lax.dot_general(
            scores_ref[head],
            key.reshape(window, HD),
            (((0,), (0,)), ((), ())),
            preferred_element_type=jnp.float32,
        )
        grads.append((grad * (1.0 / HD**0.5)).reshape(-1, rows, HD))
    out_ref[...] = jnp.swapaxes(jnp.concatenate(grads, axis=0), 0, 1).astype(jnp.bfloat16)


def turn(step, place, reach, meta, scores, kv, full):
    blocks, _, rows, _ = kv.shape
    tok_dev, heads, _ = full.shape
    step_heads = HEADS_STEP * scores.shape[2] // rows
    return pl.pallas_call(
        functools.partial(turn_kernel, step, tok_dev, reach),
        out_shape=jax.ShapeDtypeStruct(full.shape, full.dtype),
        grid_spec=pltpu.PrefetchScalarGridSpec(
            num_scalar_prefetch=1,
            grid=(1,),
            in_specs=[
                pl.BlockSpec(scores.shape, lambda c, m: (0, 0, 0)),
                pl.BlockSpec((blocks, None, rows, HEADS_STEP * HD), lambda c, m: (0, 0, 0, place)),
                pl.BlockSpec(memory_space=pl.ANY),
            ],
            out_specs=pl.BlockSpec(
                (rows, step_heads, HD),
                lambda c, m: (source_of(m[0], step, tok_dev // rows), place, 0),
            ),
        ),
        input_output_aliases={3: 0},
        compiler_params=pltpu.CompilerParams(
            dimension_semantics=("arbitrary",), vmem_limit_bytes=VMEM_BYTES
        ),
        name="turn",
    )(meta, scores, kv, full)


def shards(queries, keys, values, grad_out, segment_ids, assignment):
    count = lax.axis_size("dp")
    uly = lax.axis_size("uly")
    group = lax.axis_index("dp")
    line = lax.axis_index("blk") * uly + lax.axis_index("uly")
    width, kv_width = queries.shape[2], keys.shape[2]
    heads, kv_heads = width // HD, kv_width // HD
    tok_dev = count * queries.shape[1]
    doc_most = min(512, tok_dev * uly)
    hops = -(-doc_most // tok_dev)
    meta = jnp.stack([group, line]).astype(jnp.int32)

    final, halves = count // 2, kv_heads // HEADS_STEP
    part = width // halves
    others = [step for step in range(1, count) if step != final]
    jobs = [(2, step, 0, kv_width) for step in range(count)]
    jobs += [(0, step, 0, width) for step in others]
    jobs += [(0, final, half * part, part) for half in range(halves - 1)]
    jobs += [(which, final, (halves - 1) * part, part, 1) for which in range(2)]
    staged = stage(assignment, (queries, grad_out, keys, values), jobs)
    kv_staged, staged = staged[:count], list(staged[count:])
    kv_arrived = [exchanged(kv_staged[step], "dp", step) for step in range(1, count)]
    staged, kv_arrived[0] = lax.optimization_barrier((staged, kv_arrived[0]))
    arrived = [exchanged(rows, "dp", step) for rows, step in zip(staged, others)]
    held = staged[len(others) :]
    kv_own = jnp.zeros((count, *kv_staged[0].shape), keys.dtype)
    for step, piece in enumerate([kv_staged[0], *kv_arrived]):
        kv_own = lax.dynamic_update_index_in_dim(
            kv_own, piece, source_of(group, step, count), 0
        )
    halos = [shifted(kv_own, ("blk", "uly"), back) for back in range(hops, 0, -1)]
    kv = jnp.concatenate([*halos, kv_own], axis=0)

    rows, kv = lax.optimization_barrier((held[0], kv))
    split = [exchanged(rows, "dp", final)]
    fixed = (doc_most, heads, meta, assignment, segment_ids)
    query, grad = (queries, lambda m, a: a[m[0]]), (grad_out, lambda m, a: a[m[0]])
    full, acc = attend(0, 0, kv_heads, *fixed, query, grad, kv, None, None, False)
    for step, both in zip(others, arrived):
        query, grad = (both, lambda m, a: 0), (both, lambda m, a: 1)
        full, acc = attend(step, 0, kv_heads, *fixed, query, grad, kv, acc, full, False)
    rows, acc = lax.optimization_barrier((held[1:], acc))
    split += [exchanged(piece, "dp", final) for piece in rows]
    totals, returned, held_scores = [], [], []
    for half in range(halves):
        both = split[half]
        query, grad = (both, lambda m, a: 0), (both, lambda m, a: 1)
        if half + 1 == halves:
            grad = (split[half + 1], lambda m, a: 0)
        scores, total, *halos = attend(
            final, half * HEADS_STEP, HEADS_STEP, *fixed, query, grad, kv, acc, full, True
        )
        if half:
            halos, returned[0] = lax.optimization_barrier((halos, returned[0]))
            held_scores, total = lax.optimization_barrier((held_scores, total))
        held_scores.append(scores)
        returned = [shifted(halo, ("blk", "uly"), -back) for back, halo in enumerate(halos, 1)]
        for halo in returned:
            total = total + halo.astype(jnp.float32)
        totals.append(total.astype(jnp.bfloat16))
    for half, scores in enumerate(held_scores):
        full = turn(final, half, doc_most, meta, scores, kv, full)
    total = jnp.concatenate(totals, axis=2)
    return full[None], total[0][None], total[1][None]


def solution(mesh):
    in_specs = (
        P(None, ("blk", "uly", "dp"), None),
        P(None, ("blk", "uly", "dp"), None),
        P(None, ("blk", "uly", "dp"), None),
        P(None, ("blk", "uly", "dp"), None),
        P(),
        P(),
    )
    out_specs = (
        P("dp", ("blk", "uly"), None, None),
        P("dp", ("blk", "uly"), None),
        P("dp", ("blk", "uly"), None),
    )
    return jax.shard_map(shards, mesh=mesh, in_specs=in_specs, out_specs=out_specs, check_vma=False)
```

```python
import functools

import jax
import jax.numpy as jnp
from jax import lax
from jax.experimental import pallas as pl
from jax.experimental.pallas import tpu as pltpu
from jax.sharding import PartitionSpec as P

HD = 128
LOG2E = 1.4426950408889634
BIG_NEGATIVE = -1e30
VMEM_BYTES = 32 * 1024 * 1024
HEADS_STEP = 2
CALL_COST = 30


def target_of(index, step, count):
    return lax.rem(index + step, count)


def source_of(index, step, count):
    return lax.rem(index + count - step, count)


def exchanged(value, axis, step):
    count = lax.axis_size(axis)
    return lax.ppermute(value, axis, [(i, (i + step) % count) for i in range(count)])


def shifted(value, axis, by):
    length = lax.axis_size(axis)
    pairs = [(i, i + by) for i in range(length) if 0 <= i + by < length]
    return lax.ppermute(value, axis, pairs)


def stage_kernel(count, jobs, outs, assign_ref, *refs):
    group = lax.axis_index("dp")
    sources, refs = refs[:4], refs[4:]
    out_refs, held_refs, (in_sems, out_sems) = refs[:outs], refs[outs : 2 * outs], refs[-2:]
    loads, stores = [], []
    for out, (first, step, start, width, *_) in enumerate(jobs):
        chosen = assign_ref[target_of(group, step, count)]
        for which in range(out_refs[out].shape[0]):
            origin = sources[first + which].at[chosen, :, start : start + width]
            held, slot = held_refs[out].at[which], 2 * out + which
            loads.append(pltpu.make_async_copy(origin, held, in_sems.at[slot]))
            stores.append(pltpu.make_async_copy(held, out_refs[out].at[which], out_sems.at[slot]))
    for load in loads:
        load.start()
    for load, store in zip(loads, stores):
        load.wait()
        store.start()
    for store in stores:
        store.wait()


def stage(assignment, arrays, jobs):
    count, rows, _ = arrays[0].shape
    shapes = [(job[4] if len(job) > 4 else 2, rows, job[3]) for job in jobs]
    kind = arrays[0].dtype
    far = pl.BlockSpec(memory_space=pltpu.HBM)
    return pl.pallas_call(
        functools.partial(stage_kernel, count, jobs, len(jobs)),
        out_shape=[jax.ShapeDtypeStruct(shape, kind) for shape in shapes],
        in_specs=[pl.BlockSpec(memory_space=pltpu.SMEM)] + [far] * len(arrays),
        out_specs=[far] * len(jobs),
        scratch_shapes=[pltpu.VMEM(shape, kind) for shape in shapes]
        + [pltpu.SemaphoreType.DMA((2 * len(jobs),))] * 2,
        name="stage",
    )(assignment, *arrays)


def build_bias(source, sequence, line, segment_ref, column_ref, bias_ref, rows, tok_dev, reach):
    keys, lanes = column_ref.shape
    pieces = keys // tok_dev
    window = bias_ref.shape[0]
    eye = lax.broadcasted_iota(jnp.int32, (tok_dev, tok_dev), 0) == lax.broadcasted_iota(
        jnp.int32, (tok_dev, tok_dev), 1
    )
    for place in range(pieces):
        back = pieces - 1 - place
        start = pl.multiple_of(jnp.maximum(line - back, 0) * tok_dev, tok_dev)
        every = segment_ref[:, pl.ds(start, tok_dev)].astype(jnp.float32)
        mine = lax.broadcasted_iota(jnp.int32, every.shape, 0) == sequence
        row = jnp.sum(jnp.where(mine, every, 0.0), axis=0, keepdims=True)
        column = jnp.sum(jnp.where(eye, row, 0.0), axis=1, keepdims=True)
        column = jnp.where(line >= back, column, -1.0)
        column_ref[place * tok_dev : (place + 1) * tok_dev, :] = jnp.broadcast_to(
            column, (tok_dev, lanes)
        )

    def token(shape):
        return lax.rem(lax.broadcasted_iota(jnp.int32, shape, 1), jnp.int32(rows))

    here = pl.multiple_of(keys - tok_dev + source * rows, rows)
    asked_rows = column_ref[pl.ds(here, rows), :]
    same = lax.broadcasted_iota(jnp.int32, (rows, lanes), 0) == token((rows, lanes))
    asked = jnp.sum(jnp.where(same, asked_rows, 0.0), axis=0, keepdims=True)
    held = column_ref[pl.ds(pl.multiple_of(here - reach, rows), window), :]
    place = lax.broadcasted_iota(jnp.int32, (window, lanes), 0)
    allowed = (held == asked) & (place <= token((window, lanes)) + reach)
    bias_ref[...] = jnp.where(allowed, 0.0, BIG_NEGATIVE)


def attend_kernel(
    step, first, filled, last, tok_dev, reach, ratio,
    meta_ref, assign_ref, segment_ref, query_ref, grad_ref, kv_ref, *refs,
):
    refs = list(refs)
    if not first:
        acc_in_ref = refs.pop(0)
    if filled:
        refs.pop(0)
    query_out_ref = refs.pop(0)
    column_ref, bias_ref = refs[-2 - last], refs[-1 - last]
    if last:
        own_ref, halo_refs, acc_ref = refs[0], refs[1:-3], refs[-1]
    else:
        acc_ref = refs[0]

    rows = query_ref.shape[0]
    window = bias_ref.shape[0]
    keys = column_ref.shape[0]
    scale = 1.0 / HD**0.5
    group = meta_ref[0]
    source = source_of(group, step, tok_dev // rows)
    block = (keys - tok_dev - reach) // rows + source
    span = pl.ds(pl.multiple_of(block * rows, rows), window)

    def mask():
        build_bias(
            source, assign_ref[group], meta_ref[1], segment_ref, column_ref, bias_ref, rows, tok_dev, reach
        )

    if last:
        mask()
    else:
        pl.when(pl.program_id(0) == 0)(mask)

    acc_ref[...] = jnp.zeros_like(acc_ref) if first else acc_in_ref[...]
    turned, across = (((1,), (1,)), ((), ())), (((0,), (0,)), ((), ()))
    heads = range(HEADS_STEP)
    lanes = [slice(head * HD, (head + 1) * HD) for head in heads]

    def product(left, right, contract):
        return lax.dot_general(left, right, contract, preferred_element_type=jnp.float32)

    def stacked(ref, head):
        start = head * ratio
        return jnp.concatenate(
            [ref[:, r * HD : (r + 1) * HD] for r in range(start, start + ratio)], axis=0
        )

    def windowed(which, head):
        return kv_ref[pl.ds(block, window // rows), which, :, lanes[head]].reshape(window, HD)

    plain = (((1,), (0,)), ((), ()))
    query, key = [stacked(query_ref, head) for head in heads], [windowed(0, head) for head in heads]
    scores = [product(key[head], query[head], turned) for head in heads]
    grad, value = [stacked(grad_ref, head) for head in heads], [windowed(1, head) for head in heads]
    grad_probs = [product(value[head], grad[head], turned) for head in heads]
    probs, grad_scores = [], []
    for head in heads:
        score = scores[head] * (scale * LOG2E) + bias_ref[...]
        weights = jnp.exp2(score - jnp.max(score, axis=0, keepdims=True))
        probs.append(weights * (1.0 / jnp.sum(weights, axis=0, keepdims=True)))
    for head in heads:
        weighted = probs[head] * grad_probs[head]
        delta = jnp.sum(weighted, axis=0, keepdims=True)
        grad_scores.append((weighted - probs[head] * delta).astype(jnp.bfloat16))
    grads = []
    for head in heads:
        if last:
            query_out_ref[head] = grad_scores[head]
            continue
        grad_query = product(grad_scores[head], key[head], across)
        grads.append((grad_query * scale).reshape(ratio, rows, HD))
    grad_key = [product(grad_scores[head], query[head], plain) for head in heads]
    grad_value = [product(probs[head].astype(jnp.bfloat16), grad[head], plain) for head in heads]
    for head in heads:
        acc_ref[0, span, lanes[head]] += grad_key[head]
        acc_ref[1, span, lanes[head]] += grad_value[head]
    if last:
        own_ref[0] = acc_ref[0, keys - tok_dev :] * scale
        own_ref[1] = acc_ref[1, keys - tok_dev :]
        for back, halo_ref in enumerate(halo_refs, 1):
            part = slice(keys - (back + 1) * tok_dev, keys - back * tok_dev)
            halo_ref[0] = (acc_ref[0, part] * scale).astype(jnp.bfloat16)
            halo_ref[1] = acc_ref[1, part].astype(jnp.bfloat16)
    if not last:
        turned_grads = jnp.swapaxes(jnp.concatenate(grads, axis=0), 0, 1)
        query_out_ref[...] = turned_grads.astype(jnp.bfloat16)


def attend(step, base, span, reach, heads, meta, assignment, segments, query, grad, kv, acc, full, last):
    first, filled = acc is None, full is not None and not last
    rows, (blocks, _, _, kv_width) = query[0].shape[1], kv.shape
    ratio = heads // (kv_width // HD)
    keys, tok_dev = blocks * rows, query[0].shape[1] * lax.axis_size("dp")
    pieces, window = keys // tok_dev, reach + rows
    lanes, place = HEADS_STEP * HD, base // HEADS_STEP

    def rows_spec(array, pick):
        start = place if array.shape[2] == heads * HD else 0
        return pl.BlockSpec(
            (None, rows, HEADS_STEP * ratio * HD), lambda c, m, a: (pick(m, a), 0, start + c)
        )

    in_specs = [
        pl.BlockSpec(segments.shape, lambda c, m, a: (0, 0)),
        rows_spec(*query),
        rows_spec(*grad),
    ]
    in_specs.append(pl.BlockSpec((blocks, 2, rows, lanes), lambda c, m, a: (0, 0, 0, place + c)))
    operands = [meta, assignment, segments, query[0], grad[0], kv]
    aliases = {}
    acc_spec = pl.BlockSpec((2, keys, lanes), lambda c, m, a: (0, 0, place + c))
    if not first:
        if not last:
            aliases[len(operands)] = 1
        operands.append(acc)
        in_specs.append(acc_spec)
    if filled:
        aliases[len(operands)] = 0
        operands.append(full)
        in_specs.append(pl.BlockSpec(memory_space=pl.ANY))
    out_shape = [jax.ShapeDtypeStruct((tok_dev, heads, HD), jnp.bfloat16)]
    out_specs = [
        pl.BlockSpec(
            (rows, HEADS_STEP * ratio, HD),
            lambda c, m, a: (source_of(m[0], step, tok_dev // rows), place + c, 0),
        )
    ]
    if last:
        stretch = (HEADS_STEP, window, ratio * rows)
        out_shape = [jax.ShapeDtypeStruct(stretch, jnp.bfloat16)]
        out_specs = [pl.BlockSpec(stretch, lambda c, m, a: (0, 0, 0))]
        span_spec = pl.BlockSpec((2, tok_dev, lanes), lambda c, m, a: (0, 0, c))
        out_shape.append(jax.ShapeDtypeStruct((2, tok_dev, span * HD), jnp.float32))
        out_shape += [jax.ShapeDtypeStruct((2, tok_dev, span * HD), jnp.bfloat16)] * (pieces - 1)
        out_specs += [span_spec] * pieces
    else:
        out_shape.append(jax.ShapeDtypeStruct((2, keys, kv_width), jnp.float32))
        out_specs.append(acc_spec)
    pairs = span * ratio * rows * window
    cost = CALL_COST if step and not last else 1
    held = (keys, ratio * rows), (window, ratio * rows)
    held += ((2, keys, lanes),) * last
    return pl.pallas_call(
        functools.partial(attend_kernel, step, first, filled, last, tok_dev, reach, ratio),
        out_shape=out_shape,
        grid_spec=pltpu.PrefetchScalarGridSpec(
            num_scalar_prefetch=2,
            grid=(span // HEADS_STEP,),
            in_specs=in_specs,
            out_specs=out_specs,
            scratch_shapes=[pltpu.VMEM(shape, jnp.float32) for shape in held],
        ),
        input_output_aliases=aliases,
        compiler_params=pltpu.CompilerParams(
            dimension_semantics=("arbitrary",), vmem_limit_bytes=VMEM_BYTES
        ),
        cost_estimate=pl.CostEstimate(
            flops=pairs * HD * cost, bytes_accessed=pairs * cost, transcendentals=0
        ),
        name="attend",
    )(*operands)


def turn_kernel(step, tok_dev, reach, meta_ref, key_ref, full_ref, *refs):
    scores_refs, out_ref = refs[:-1], refs[-1]
    rows, blocks = out_ref.shape[0], key_ref.shape[0]
    window = scores_refs[0].shape[1]
    source = source_of(meta_ref[0], step, tok_dev // rows)
    block = (blocks * rows - tok_dev - reach) // rows + source

    def one(scores_ref):
        grads = []
        for head in range(HEADS_STEP):
            key = key_ref[pl.ds(block, window // rows), :, head * HD : (head + 1) * HD]
            grad = lax.dot_general(
                scores_ref[head],
                key.reshape(window, HD),
                (((0,), (0,)), ((), ())),
                preferred_element_type=jnp.float32,
            )
            grads.append((grad * (1.0 / HD**0.5)).reshape(-1, rows, HD))
        turned = jnp.swapaxes(jnp.concatenate(grads, axis=0), 0, 1)
        out_ref[...] = turned.astype(jnp.bfloat16)

    for half, scores_ref in enumerate(scores_refs):
        pl.when(pl.program_id(0) == half)(functools.partial(one, scores_ref))


def turn(step, reach, meta, scores, kv, full):
    blocks, _, rows, _ = kv.shape
    tok_dev, heads, _ = full.shape
    shape = scores[0].shape
    step_heads = HEADS_STEP * shape[2] // rows
    return pl.pallas_call(
        functools.partial(turn_kernel, step, tok_dev, reach),
        out_shape=jax.ShapeDtypeStruct(full.shape, full.dtype),
        grid_spec=pltpu.PrefetchScalarGridSpec(
            num_scalar_prefetch=1,
            grid=(len(scores),),
            in_specs=[
                pl.BlockSpec((blocks, None, rows, HEADS_STEP * HD), lambda c, m: (0, 0, 0, c)),
                pl.BlockSpec(memory_space=pl.ANY),
            ]
            + [pl.BlockSpec(shape, lambda c, m: (0, 0, 0))] * len(scores),
            out_specs=pl.BlockSpec(
                (rows, step_heads, HD),
                lambda c, m: (source_of(m[0], step, tok_dev // rows), c, 0),
            ),
        ),
        input_output_aliases={2: 0},
        compiler_params=pltpu.CompilerParams(
            dimension_semantics=("arbitrary",), vmem_limit_bytes=VMEM_BYTES
        ),
        name="turn",
    )(meta, kv, full, *scores)


def shards(queries, keys, values, grad_out, segment_ids, assignment):
    count = lax.axis_size("dp")
    uly = lax.axis_size("uly")
    group = lax.axis_index("dp")
    line = lax.axis_index("blk") * uly + lax.axis_index("uly")
    width, kv_width = queries.shape[2], keys.shape[2]
    heads, kv_heads = width // HD, kv_width // HD
    tok_dev = count * queries.shape[1]
    doc_most = min(512, tok_dev * uly)
    hops = -(-doc_most // tok_dev)
    meta = jnp.stack([group, line]).astype(jnp.int32)

    final, halves = count // 2, kv_heads // HEADS_STEP
    part = width // halves
    others = [step for step in range(1, count) if step != final]
    jobs = [(2, step, 0, kv_width) for step in range(count)]
    jobs += [(0, step, 0, width) for step in others]
    jobs += [(0, final, half * part, part) for half in range(halves - 1)]
    jobs += [(which, final, (halves - 1) * part, part, 1) for which in range(2)]
    staged = stage(assignment, (queries, grad_out, keys, values), jobs)
    kv_staged, staged = staged[:count], list(staged[count:])
    kv_arrived = [exchanged(kv_staged[step], "dp", step) for step in range(1, count)]
    staged, kv_arrived[0] = lax.optimization_barrier((staged, kv_arrived[0]))
    arrived = [exchanged(rows, "dp", step) for rows, step in zip(staged, others)]
    held = staged[len(others) :]
    kv_own = jnp.zeros((count, *kv_staged[0].shape), keys.dtype)
    for step, piece in enumerate([kv_staged[0], *kv_arrived]):
        kv_own = lax.dynamic_update_index_in_dim(
            kv_own, piece, source_of(group, step, count), 0
        )
    halos = [shifted(kv_own, ("blk", "uly"), back) for back in range(hops, 0, -1)]
    kv = jnp.concatenate([*halos, kv_own], axis=0)

    rows, kv = lax.optimization_barrier((held[0], kv))
    split = [exchanged(rows, "dp", final)]
    fixed = (doc_most, heads, meta, assignment, segment_ids)
    query, grad = (queries, lambda m, a: a[m[0]]), (grad_out, lambda m, a: a[m[0]])
    full, acc = attend(0, 0, kv_heads, *fixed, query, grad, kv, None, None, False)
    for step, both in zip(others, arrived):
        query, grad = (both, lambda m, a: 0), (both, lambda m, a: 1)
        full, acc = attend(step, 0, kv_heads, *fixed, query, grad, kv, acc, full, False)
    rows, acc = lax.optimization_barrier((held[1:], acc))
    split += [exchanged(piece, "dp", final) for piece in rows]
    totals, returned, held_scores = [], [], []
    for half in range(halves):
        both = split[half]
        query, grad = (both, lambda m, a: 0), (both, lambda m, a: 1)
        if half + 1 == halves:
            grad = (split[half + 1], lambda m, a: 0)
        scores, total, *halos = attend(
            final, half * HEADS_STEP, HEADS_STEP, *fixed, query, grad, kv, acc, full, True
        )
        if half:
            halos, returned[0] = lax.optimization_barrier((halos, returned[0]))
            held_scores, total = lax.optimization_barrier((held_scores, total))
        held_scores.append(scores)
        returned = [shifted(halo, ("blk", "uly"), -back) for back, halo in enumerate(halos, 1)]
        for halo in returned:
            total = total + halo.astype(jnp.float32)
        totals.append(total.astype(jnp.bfloat16))
    full = turn(final, doc_most, meta, held_scores, kv, full)
    total = jnp.concatenate(totals, axis=2)
    return full[None], total[0][None], total[1][None]


def solution(mesh):
    in_specs = (
        P(None, ("blk", "uly", "dp"), None),
        P(None, ("blk", "uly", "dp"), None),
        P(None, ("blk", "uly", "dp"), None),
        P(None, ("blk", "uly", "dp"), None),
        P(),
        P(),
    )
    out_specs = (
        P("dp", ("blk", "uly"), None, None),
        P("dp", ("blk", "uly"), None),
        P("dp", ("blk", "uly"), None),
    )
    return jax.shard_map(shards, mesh=mesh, in_specs=in_specs, out_specs=out_specs, check_vma=False)
```

```python
import functools

import jax
import jax.numpy as jnp
from jax import lax
from jax.experimental import pallas as pl
from jax.experimental.pallas import tpu as pltpu
from jax.sharding import PartitionSpec as P

HD = 128
LOG2E = 1.4426950408889634
BIG_NEGATIVE = -1e30
VMEM_BYTES = 32 * 1024 * 1024
HEADS_STEP = 2
CALL_COST = 30


def target_of(index, step, count):
    return lax.rem(index + step, count)


def source_of(index, step, count):
    return lax.rem(index + count - step, count)


def exchanged(value, axis, step):
    count = lax.axis_size(axis)
    return lax.ppermute(value, axis, [(i, (i + step) % count) for i in range(count)])


def shifted(value, axis, by):
    length = lax.axis_size(axis)
    pairs = [(i, i + by) for i in range(length) if 0 <= i + by < length]
    return lax.ppermute(value, axis, pairs)


def stage_kernel(count, jobs, outs, assign_ref, *refs):
    group = lax.axis_index("dp")
    sources, refs = refs[:4], refs[4:]
    out_refs, held_refs, (in_sems, out_sems) = refs[:outs], refs[outs : 2 * outs], refs[-2:]
    loads, stores = [], []
    for out, (first, step, start, width, *_) in enumerate(jobs):
        chosen = assign_ref[target_of(group, step, count)]
        for which in range(out_refs[out].shape[0]):
            origin = sources[first + which].at[chosen, :, start : start + width]
            held, slot = held_refs[out].at[which], 2 * out + which
            loads.append(pltpu.make_async_copy(origin, held, in_sems.at[slot]))
            stores.append(pltpu.make_async_copy(held, out_refs[out].at[which], out_sems.at[slot]))
    for load in loads:
        load.start()
    for load, store in zip(loads, stores):
        load.wait()
        store.start()
    for store in stores:
        store.wait()


def stage(assignment, arrays, jobs):
    count, rows, _ = arrays[0].shape
    shapes = [(job[4] if len(job) > 4 else 2, rows, job[3]) for job in jobs]
    kind = arrays[0].dtype
    far = pl.BlockSpec(memory_space=pltpu.HBM)
    return pl.pallas_call(
        functools.partial(stage_kernel, count, jobs, len(jobs)),
        out_shape=[jax.ShapeDtypeStruct(shape, kind) for shape in shapes],
        in_specs=[pl.BlockSpec(memory_space=pltpu.SMEM)] + [far] * len(arrays),
        out_specs=[far] * len(jobs),
        scratch_shapes=[pltpu.VMEM(shape, kind) for shape in shapes]
        + [pltpu.SemaphoreType.DMA((2 * len(jobs),))] * 2,
        name="stage",
    )(assignment, *arrays)


def build_bias(source, sequence, line, segment_ref, column_ref, bias_ref, rows, tok_dev, reach):
    keys, lanes = column_ref.shape
    pieces = keys // tok_dev
    window = bias_ref.shape[0]
    eye = lax.broadcasted_iota(jnp.int32, (tok_dev, tok_dev), 0) == lax.broadcasted_iota(
        jnp.int32, (tok_dev, tok_dev), 1
    )
    for place in range(pieces):
        back = pieces - 1 - place
        start = pl.multiple_of(jnp.maximum(line - back, 0) * tok_dev, tok_dev)
        every = segment_ref[:, pl.ds(start, tok_dev)].astype(jnp.float32)
        mine = lax.broadcasted_iota(jnp.int32, every.shape, 0) == sequence
        row = jnp.sum(jnp.where(mine, every, 0.0), axis=0, keepdims=True)
        column = jnp.sum(jnp.where(eye, row, 0.0), axis=1, keepdims=True)
        column = jnp.where(line >= back, column, -1.0)
        column_ref[place * tok_dev : (place + 1) * tok_dev, :] = jnp.broadcast_to(
            column, (tok_dev, lanes)
        )

    def token(shape):
        return lax.rem(lax.broadcasted_iota(jnp.int32, shape, 1), jnp.int32(rows))

    here = pl.multiple_of(keys - tok_dev + source * rows, rows)
    asked_rows = column_ref[pl.ds(here, rows), :]
    same = lax.broadcasted_iota(jnp.int32, (rows, lanes), 0) == token((rows, lanes))
    asked = jnp.sum(jnp.where(same, asked_rows, 0.0), axis=0, keepdims=True)
    held = column_ref[pl.ds(pl.multiple_of(here - reach, rows), window), :]
    place = lax.broadcasted_iota(jnp.int32, (window, lanes), 0)
    allowed = (held == asked) & (place <= token((window, lanes)) + reach)
    bias_ref[...] = jnp.where(allowed, 0.0, BIG_NEGATIVE)


def attend_kernel(
    step, first, filled, last, tok_dev, reach, ratio,
    meta_ref, assign_ref, segment_ref, query_ref, grad_ref, kv_ref, *refs,
):
    refs = list(refs)
    if not first:
        acc_in_ref = refs.pop(0)
    if filled:
        refs.pop(0)
    query_out_ref = refs.pop(0)
    column_ref, bias_ref = refs[-2 - last], refs[-1 - last]
    if last:
        own_ref, halo_refs, acc_ref = refs[0], refs[1:-3], refs[-1]
    else:
        acc_ref = refs[0]

    rows = query_ref.shape[0]
    window = bias_ref.shape[0]
    keys = column_ref.shape[0]
    scale = 1.0 / HD**0.5
    group = meta_ref[0]
    source = source_of(group, step, tok_dev // rows)
    block = (keys - tok_dev - reach) // rows + source
    span = pl.ds(pl.multiple_of(block * rows, rows), window)

    def mask():
        build_bias(
            source, assign_ref[group], meta_ref[1], segment_ref, column_ref, bias_ref, rows, tok_dev, reach
        )

    if last:
        mask()
    else:
        pl.when(pl.program_id(0) == 0)(mask)

    acc_ref[...] = jnp.zeros_like(acc_ref) if first else acc_in_ref[...]
    turned, across = (((1,), (1,)), ((), ())), (((0,), (0,)), ((), ()))
    heads = range(HEADS_STEP)
    lanes = [slice(head * HD, (head + 1) * HD) for head in heads]

    def product(left, right, contract):
        return lax.dot_general(left, right, contract, preferred_element_type=jnp.float32)

    def stacked(ref, head):
        start = head * ratio
        return jnp.concatenate(
            [ref[:, r * HD : (r + 1) * HD] for r in range(start, start + ratio)], axis=0
        )

    def windowed(which, head):
        return kv_ref[pl.ds(block, window // rows), which, :, lanes[head]].reshape(window, HD)

    plain = (((1,), (0,)), ((), ()))
    query, key = [stacked(query_ref, head) for head in heads], [windowed(0, head) for head in heads]
    scores = [product(key[head], query[head], turned) for head in heads]
    grad, value = [stacked(grad_ref, head) for head in heads], [windowed(1, head) for head in heads]
    grad_probs = [product(value[head], grad[head], turned) for head in heads]
    probs, grad_scores = [], []
    for head in heads:
        score = scores[head] * (scale * LOG2E) + bias_ref[...]
        weights = jnp.exp2(score - jnp.max(score, axis=0, keepdims=True))
        probs.append(weights * (1.0 / jnp.sum(weights, axis=0, keepdims=True)))
    for head in heads:
        weighted = probs[head] * grad_probs[head]
        delta = jnp.sum(weighted, axis=0, keepdims=True)
        grad_scores.append((weighted - probs[head] * delta).astype(jnp.bfloat16))
    grads = []
    for head in heads:
        if last:
            query_out_ref[head] = grad_scores[head]
            continue
        grad_query = product(grad_scores[head], key[head], across)
        grads.append((grad_query * scale).reshape(ratio, rows, HD))
    grad_key = [product(grad_scores[head], query[head], plain) for head in heads]
    grad_value = [product(probs[head].astype(jnp.bfloat16), grad[head], plain) for head in heads]
    for head in heads:
        acc_ref[0, span, lanes[head]] += grad_key[head]
        acc_ref[1, span, lanes[head]] += grad_value[head]
    if last:
        own_ref[0] = acc_ref[0, keys - tok_dev :] * scale
        own_ref[1] = acc_ref[1, keys - tok_dev :]
        for back, halo_ref in enumerate(halo_refs, 1):
            part = slice(keys - (back + 1) * tok_dev, keys - back * tok_dev)
            halo_ref[0] = (acc_ref[0, part] * scale).astype(jnp.bfloat16)
            halo_ref[1] = acc_ref[1, part].astype(jnp.bfloat16)
    if not last:
        turned_grads = jnp.swapaxes(jnp.concatenate(grads, axis=0), 0, 1)
        query_out_ref[...] = turned_grads.astype(jnp.bfloat16)


def attend(step, base, span, reach, heads, meta, assignment, segments, query, grad, kv, acc, full, last):
    first, filled = acc is None, full is not None and not last
    rows, (blocks, _, _, kv_width) = query[0].shape[1], kv.shape
    ratio = heads // (kv_width // HD)
    keys, tok_dev = blocks * rows, query[0].shape[1] * lax.axis_size("dp")
    pieces, window = keys // tok_dev, reach + rows
    lanes, place = HEADS_STEP * HD, base // HEADS_STEP

    def rows_spec(array, pick):
        start = place if array.shape[2] == heads * HD else 0
        return pl.BlockSpec(
            (None, rows, HEADS_STEP * ratio * HD), lambda c, m, a: (pick(m, a), 0, start + c)
        )

    in_specs = [
        pl.BlockSpec(segments.shape, lambda c, m, a: (0, 0)),
        rows_spec(*query),
        rows_spec(*grad),
    ]
    in_specs.append(pl.BlockSpec((blocks, 2, rows, lanes), lambda c, m, a: (0, 0, 0, place + c)))
    operands = [meta, assignment, segments, query[0], grad[0], kv]
    aliases = {}
    acc_spec = pl.BlockSpec((2, keys, lanes), lambda c, m, a: (0, 0, place + c))
    if not first:
        if not last:
            aliases[len(operands)] = 1
        operands.append(acc)
        in_specs.append(acc_spec)
    if filled:
        aliases[len(operands)] = 0
        operands.append(full)
        in_specs.append(pl.BlockSpec(memory_space=pl.ANY))
    out_shape = [jax.ShapeDtypeStruct((tok_dev, heads, HD), jnp.bfloat16)]
    out_specs = [
        pl.BlockSpec(
            (rows, HEADS_STEP * ratio, HD),
            lambda c, m, a: (source_of(m[0], step, tok_dev // rows), place + c, 0),
        )
    ]
    if last:
        stretch = (HEADS_STEP, window, ratio * rows)
        out_shape = [jax.ShapeDtypeStruct(stretch, jnp.bfloat16)]
        out_specs = [pl.BlockSpec(stretch, lambda c, m, a: (0, 0, 0))]
        span_spec = pl.BlockSpec((2, tok_dev, lanes), lambda c, m, a: (0, 0, c))
        out_shape.append(jax.ShapeDtypeStruct((2, tok_dev, span * HD), jnp.float32))
        out_shape += [jax.ShapeDtypeStruct((2, tok_dev, span * HD), jnp.bfloat16)] * (pieces - 1)
        out_specs += [span_spec] * pieces
    else:
        out_shape.append(jax.ShapeDtypeStruct((2, keys, kv_width), jnp.float32))
        out_specs.append(acc_spec)
    pairs = span * ratio * rows * window
    cost = CALL_COST if step and not last else 1
    held = (keys, ratio * rows), (window, ratio * rows)
    held += ((2, keys, lanes),) * last
    return pl.pallas_call(
        functools.partial(attend_kernel, step, first, filled, last, tok_dev, reach, ratio),
        out_shape=out_shape,
        grid_spec=pltpu.PrefetchScalarGridSpec(
            num_scalar_prefetch=2,
            grid=(span // HEADS_STEP,),
            in_specs=in_specs,
            out_specs=out_specs,
            scratch_shapes=[pltpu.VMEM(shape, jnp.float32) for shape in held],
        ),
        input_output_aliases=aliases,
        compiler_params=pltpu.CompilerParams(
            dimension_semantics=("arbitrary",), vmem_limit_bytes=VMEM_BYTES
        ),
        cost_estimate=pl.CostEstimate(
            flops=pairs * HD * cost, bytes_accessed=pairs * cost, transcendentals=0
        ),
        name="attend",
    )(*operands)


def turn_kernel(step, tok_dev, reach, meta_ref, key_ref, full_ref, *refs):
    scores_refs, out_ref = refs[:-1], refs[-1]
    rows, blocks = out_ref.shape[0], key_ref.shape[0]
    window = scores_refs[0].shape[1]
    source = source_of(meta_ref[0], step, tok_dev // rows)
    block = (blocks * rows - tok_dev - reach) // rows + source

    def one(scores_ref):
        grads = []
        for head in range(HEADS_STEP):
            key = key_ref[pl.ds(block, window // rows), :, head * HD : (head + 1) * HD]
            grad = lax.dot_general(
                scores_ref[head],
                key.reshape(window, HD),
                (((0,), (0,)), ((), ())),
                preferred_element_type=jnp.float32,
            )
            grads.append((grad * (1.0 / HD**0.5)).reshape(-1, rows, HD))
        turned = jnp.swapaxes(jnp.concatenate(grads, axis=0), 0, 1)
        out_ref[...] = turned.astype(jnp.bfloat16)

    for half, scores_ref in enumerate(scores_refs):
        pl.when(pl.program_id(0) == half)(functools.partial(one, scores_ref))


def turn(step, reach, meta, scores, kv, full):
    blocks, _, rows, _ = kv.shape
    tok_dev, heads, _ = full.shape
    shape = scores[0].shape
    step_heads = HEADS_STEP * shape[2] // rows
    return pl.pallas_call(
        functools.partial(turn_kernel, step, tok_dev, reach),
        out_shape=jax.ShapeDtypeStruct(full.shape, full.dtype),
        grid_spec=pltpu.PrefetchScalarGridSpec(
            num_scalar_prefetch=1,
            grid=(len(scores),),
            in_specs=[
                pl.BlockSpec((blocks, None, rows, HEADS_STEP * HD), lambda c, m: (0, 0, 0, c)),
                pl.BlockSpec(memory_space=pl.ANY),
            ]
            + [pl.BlockSpec(shape, lambda c, m: (0, 0, 0))] * len(scores),
            out_specs=pl.BlockSpec(
                (rows, step_heads, HD),
                lambda c, m: (source_of(m[0], step, tok_dev // rows), c, 0),
            ),
        ),
        input_output_aliases={2: 0},
        compiler_params=pltpu.CompilerParams(
            dimension_semantics=("arbitrary",), vmem_limit_bytes=VMEM_BYTES
        ),
        name="turn",
    )(meta, kv, full, *scores)


def shards(queries, keys, values, grad_out, segment_ids, assignment):
    count = lax.axis_size("dp")
    uly = lax.axis_size("uly")
    group = lax.axis_index("dp")
    line = lax.axis_index("blk") * uly + lax.axis_index("uly")
    width, kv_width = queries.shape[2], keys.shape[2]
    heads, kv_heads = width // HD, kv_width // HD
    tok_dev = count * queries.shape[1]
    doc_most = min(512, tok_dev * uly)
    hops = -(-doc_most // tok_dev)
    meta = jnp.stack([group, line]).astype(jnp.int32)

    final, halves = count // 2, kv_heads // HEADS_STEP
    part = width // halves
    others = [step for step in range(1, count) if step != final]
    jobs = [(2, step, 0, kv_width) for step in range(count)]
    jobs += [(0, step, 0, width) for step in others]
    jobs += [(0, final, half * part, part) for half in range(halves - 1)]
    jobs += [(which, final, (halves - 1) * part, part, 1) for which in range(2)]
    staged = stage(assignment, (queries, grad_out, keys, values), jobs)
    kv_staged, staged = staged[:count], list(staged[count:])
    kv_arrived = [exchanged(kv_staged[step], "dp", step) for step in range(1, count)]
    staged, kv_arrived[0] = lax.optimization_barrier((staged, kv_arrived[0]))
    arrived = [exchanged(rows, "dp", step) for rows, step in zip(staged, others)]
    held = staged[len(others) :]
    kv_own = jnp.zeros((count, *kv_staged[0].shape), keys.dtype)
    for step, piece in enumerate([kv_staged[0], *kv_arrived]):
        kv_own = lax.dynamic_update_index_in_dim(
            kv_own, piece, source_of(group, step, count), 0
        )
    halos = [shifted(kv_own, ("blk", "uly"), back) for back in range(hops, 0, -1)]
    kv = jnp.concatenate([*halos, kv_own], axis=0)

    rows, kv = lax.optimization_barrier((held[0], kv))
    split = [exchanged(rows, "dp", final)]
    fixed = (doc_most, heads, meta, assignment, segment_ids)
    query, grad = (queries, lambda m, a: a[m[0]]), (grad_out, lambda m, a: a[m[0]])
    full, acc = attend(0, 0, kv_heads, *fixed, query, grad, kv, None, None, False)
    for step, both in zip(others, arrived):
        query, grad = (both, lambda m, a: 0), (both, lambda m, a: 1)
        full, acc = attend(step, 0, kv_heads, *fixed, query, grad, kv, acc, full, False)
    rows, acc = lax.optimization_barrier((held[1:], acc))
    split += [exchanged(piece, "dp", final) for piece in rows]
    totals, returned, held_scores = [], [], []
    for half in range(halves):
        both = split[half]
        query, grad = (both, lambda m, a: 0), (both, lambda m, a: 1)
        if half + 1 == halves:
            grad = (split[half + 1], lambda m, a: 0)
        scores, total, *halos = attend(
            final, half * HEADS_STEP, HEADS_STEP, *fixed, query, grad, kv, acc, full, True
        )
        if half:
            halos, returned[-1] = lax.optimization_barrier((halos, returned[-1]))
            held_scores, total = lax.optimization_barrier((held_scores, total))
        held_scores.append(scores)
        returned = [shifted(halo, ("blk", "uly"), -back) for back, halo in enumerate(halos, 1)]
        for halo in returned:
            total = total + halo.astype(jnp.float32)
        totals.append(total.astype(jnp.bfloat16))
    full = turn(final, doc_most, meta, held_scores, kv, full)
    total = jnp.concatenate(totals, axis=2)
    return full[None], total[0][None], total[1][None]


def solution(mesh):
    in_specs = (
        P(None, ("blk", "uly", "dp"), None),
        P(None, ("blk", "uly", "dp"), None),
        P(None, ("blk", "uly", "dp"), None),
        P(None, ("blk", "uly", "dp"), None),
        P(),
        P(),
    )
    out_specs = (
        P("dp", ("blk", "uly"), None, None),
        P("dp", ("blk", "uly"), None),
        P("dp", ("blk", "uly"), None),
    )
    return jax.shard_map(shards, mesh=mesh, in_specs=in_specs, out_specs=out_specs, check_vma=False)
```

```python
import functools

import jax
import jax.numpy as jnp
from jax import lax
from jax.experimental import pallas as pl
from jax.experimental.pallas import tpu as pltpu
from jax.sharding import PartitionSpec as P

HD = 128
LOG2E = 1.4426950408889634
BIG_NEGATIVE = -1e30
VMEM_BYTES = 32 * 1024 * 1024
HEADS_STEP = 2
CALL_COST = 30


def target_of(index, step, count):
    return lax.rem(index + step, count)


def source_of(index, step, count):
    return lax.rem(index + count - step, count)


def exchanged(value, axis, step):
    count = lax.axis_size(axis)
    return lax.ppermute(value, axis, [(i, (i + step) % count) for i in range(count)])


def shifted(value, axis, by):
    length = lax.axis_size(axis)
    pairs = [(i, i + by) for i in range(length) if 0 <= i + by < length]
    return lax.ppermute(value, axis, pairs)


def stage_kernel(count, jobs, outs, assign_ref, *refs):
    group = lax.axis_index("dp")
    sources, refs = refs[:4], refs[4:]
    out_refs, held_refs, (in_sems, out_sems) = refs[:outs], refs[outs : 2 * outs], refs[-2:]
    loads, stores = [], []
    for out, (first, step, start, width, *_) in enumerate(jobs):
        chosen = assign_ref[target_of(group, step, count)]
        for which in range(out_refs[out].shape[0]):
            origin = sources[first + which].at[chosen, :, start : start + width]
            held, slot = held_refs[out].at[which], 2 * out + which
            loads.append(pltpu.make_async_copy(origin, held, in_sems.at[slot]))
            stores.append(pltpu.make_async_copy(held, out_refs[out].at[which], out_sems.at[slot]))
    for load in loads:
        load.start()
    for load, store in zip(loads, stores):
        load.wait()
        store.start()
    for store in stores:
        store.wait()


def stage(assignment, arrays, jobs):
    count, rows, _ = arrays[0].shape
    shapes = [(job[4] if len(job) > 4 else 2, rows, job[3]) for job in jobs]
    kind = arrays[0].dtype
    far = pl.BlockSpec(memory_space=pltpu.HBM)
    return pl.pallas_call(
        functools.partial(stage_kernel, count, jobs, len(jobs)),
        out_shape=[jax.ShapeDtypeStruct(shape, kind) for shape in shapes],
        in_specs=[pl.BlockSpec(memory_space=pltpu.SMEM)] + [far] * len(arrays),
        out_specs=[far] * len(jobs),
        scratch_shapes=[pltpu.VMEM(shape, kind) for shape in shapes]
        + [pltpu.SemaphoreType.DMA((2 * len(jobs),))] * 2,
        name="stage",
    )(assignment, *arrays)


def build_bias(source, sequence, line, segment_ref, column_ref, bias_ref, rows, tok_dev, reach):
    keys, lanes = column_ref.shape
    pieces = keys // tok_dev
    window = bias_ref.shape[0]
    eye = lax.broadcasted_iota(jnp.int32, (tok_dev, tok_dev), 0) == lax.broadcasted_iota(
        jnp.int32, (tok_dev, tok_dev), 1
    )
    for place in range(pieces):
        back = pieces - 1 - place
        start = pl.multiple_of(jnp.maximum(line - back, 0) * tok_dev, tok_dev)
        every = segment_ref[:, pl.ds(start, tok_dev)].astype(jnp.float32)
        mine = lax.broadcasted_iota(jnp.int32, every.shape, 0) == sequence
        row = jnp.sum(jnp.where(mine, every, 0.0), axis=0, keepdims=True)
        column = jnp.sum(jnp.where(eye, row, 0.0), axis=1, keepdims=True)
        column = jnp.where(line >= back, column, -1.0)
        column_ref[place * tok_dev : (place + 1) * tok_dev, :] = jnp.broadcast_to(
            column, (tok_dev, lanes)
        )

    def token(shape):
        return lax.rem(lax.broadcasted_iota(jnp.int32, shape, 1), jnp.int32(rows))

    here = pl.multiple_of(keys - tok_dev + source * rows, rows)
    asked_rows = column_ref[pl.ds(here, rows), :]
    same = lax.broadcasted_iota(jnp.int32, (rows, lanes), 0) == token((rows, lanes))
    asked = jnp.sum(jnp.where(same, asked_rows, 0.0), axis=0, keepdims=True)
    held = column_ref[pl.ds(pl.multiple_of(here - reach, rows), window), :]
    place = lax.broadcasted_iota(jnp.int32, (window, lanes), 0)
    allowed = (held == asked) & (place <= token((window, lanes)) + reach)
    bias_ref[...] = jnp.where(allowed, 0.0, BIG_NEGATIVE)


def attend_kernel(
    step, first, filled, last, tok_dev, reach, ratio,
    meta_ref, assign_ref, segment_ref, query_ref, grad_ref, kv_ref, *refs,
):
    refs = list(refs)
    if not first:
        acc_in_ref = refs.pop(0)
    if filled:
        refs.pop(0)
    query_out_ref = refs.pop(0)
    column_ref, bias_ref = refs[-2 - last], refs[-1 - last]
    if last:
        own_ref, halo_refs, acc_ref = refs[0], refs[1:-3], refs[-1]
    else:
        acc_ref = refs[0]

    rows = query_ref.shape[0]
    window = bias_ref.shape[0]
    keys = column_ref.shape[0]
    scale = 1.0 / HD**0.5
    group = meta_ref[0]
    source = source_of(group, step, tok_dev // rows)
    block = (keys - tok_dev - reach) // rows + source
    span = pl.ds(pl.multiple_of(block * rows, rows), window)

    def mask():
        build_bias(
            source, assign_ref[group], meta_ref[1], segment_ref, column_ref, bias_ref, rows, tok_dev, reach
        )

    if last:
        mask()
    else:
        pl.when(pl.program_id(0) == 0)(mask)

    acc_ref[...] = jnp.zeros_like(acc_ref) if first else acc_in_ref[...]
    turned, across = (((1,), (1,)), ((), ())), (((0,), (0,)), ((), ()))
    heads = range(HEADS_STEP)
    lanes = [slice(head * HD, (head + 1) * HD) for head in heads]

    def product(left, right, contract):
        return lax.dot_general(left, right, contract, preferred_element_type=jnp.float32)

    def stacked(ref, head):
        start = head * ratio
        return jnp.concatenate(
            [ref[:, r * HD : (r + 1) * HD] for r in range(start, start + ratio)], axis=0
        )

    def windowed(which, head):
        return kv_ref[pl.ds(block, window // rows), which, :, lanes[head]].reshape(window, HD)

    plain = (((1,), (0,)), ((), ()))
    query, key = [stacked(query_ref, head) for head in heads], [windowed(0, head) for head in heads]
    scores = [product(key[head], query[head], turned) for head in heads]
    grad, value = [stacked(grad_ref, head) for head in heads], [windowed(1, head) for head in heads]
    grad_probs = [product(value[head], grad[head], turned) for head in heads]
    probs, grad_scores = [], []
    for head in heads:
        score = scores[head] * (scale * LOG2E) + bias_ref[...]
        weights = jnp.exp2(score - jnp.max(score, axis=0, keepdims=True))
        probs.append(weights * (1.0 / jnp.sum(weights, axis=0, keepdims=True)))
    for head in heads:
        weighted = probs[head] * grad_probs[head]
        delta = jnp.sum(weighted, axis=0, keepdims=True)
        grad_scores.append((weighted - probs[head] * delta).astype(jnp.bfloat16))
    grads = []
    for head in heads:
        if last:
            query_out_ref[head] = grad_scores[head]
            continue
        grad_query = product(grad_scores[head], key[head], across)
        grads.append((grad_query * scale).reshape(ratio, rows, HD))
    grad_key = [product(grad_scores[head], query[head], plain) for head in heads]
    grad_value = [product(probs[head].astype(jnp.bfloat16), grad[head], plain) for head in heads]
    for head in heads:
        acc_ref[0, span, lanes[head]] += grad_key[head]
        acc_ref[1, span, lanes[head]] += grad_value[head]
    if last:
        own_ref[0] = acc_ref[0, keys - tok_dev :] * scale
        own_ref[1] = acc_ref[1, keys - tok_dev :]
        for back, halo_ref in enumerate(halo_refs, 1):
            part = slice(keys - (back + 1) * tok_dev, keys - back * tok_dev)
            halo_ref[0] = (acc_ref[0, part] * scale).astype(jnp.bfloat16)
            halo_ref[1] = acc_ref[1, part].astype(jnp.bfloat16)
    if not last:
        turned_grads = jnp.swapaxes(jnp.concatenate(grads, axis=0), 0, 1)
        query_out_ref[...] = turned_grads.astype(jnp.bfloat16)


def attend(step, base, span, reach, heads, meta, assignment, segments, query, grad, kv, acc, full, last):
    first, filled = acc is None, full is not None and not last
    rows, (blocks, _, _, kv_width) = query[0].shape[1], kv.shape
    ratio = heads // (kv_width // HD)
    keys, tok_dev = blocks * rows, query[0].shape[1] * lax.axis_size("dp")
    pieces, window = keys // tok_dev, reach + rows
    lanes, place = HEADS_STEP * HD, base // HEADS_STEP

    def rows_spec(array, pick):
        start = place if array.shape[2] == heads * HD else 0
        return pl.BlockSpec(
            (None, rows, HEADS_STEP * ratio * HD), lambda c, m, a: (pick(m, a), 0, start + c)
        )

    in_specs = [
        pl.BlockSpec(segments.shape, lambda c, m, a: (0, 0)),
        rows_spec(*query),
        rows_spec(*grad),
    ]
    in_specs.append(pl.BlockSpec((blocks, 2, rows, lanes), lambda c, m, a: (0, 0, 0, place + c)))
    operands = [meta, assignment, segments, query[0], grad[0], kv]
    aliases = {}
    acc_spec = pl.BlockSpec((2, keys, lanes), lambda c, m, a: (0, 0, place + c))
    if not first:
        if not last:
            aliases[len(operands)] = 1
        operands.append(acc)
        in_specs.append(acc_spec)
    if filled:
        aliases[len(operands)] = 0
        operands.append(full)
        in_specs.append(pl.BlockSpec(memory_space=pl.ANY))
    out_shape = [jax.ShapeDtypeStruct((tok_dev, heads, HD), jnp.bfloat16)]
    out_specs = [
        pl.BlockSpec(
            (rows, HEADS_STEP * ratio, HD),
            lambda c, m, a: (source_of(m[0], step, tok_dev // rows), place + c, 0),
        )
    ]
    if last:
        stretch = (HEADS_STEP, window, ratio * rows)
        out_shape = [jax.ShapeDtypeStruct(stretch, jnp.bfloat16)]
        out_specs = [pl.BlockSpec(stretch, lambda c, m, a: (0, 0, 0))]
        span_spec = pl.BlockSpec((2, tok_dev, lanes), lambda c, m, a: (0, 0, c))
        out_shape.append(jax.ShapeDtypeStruct((2, tok_dev, span * HD), jnp.float32))
        out_shape += [jax.ShapeDtypeStruct((2, tok_dev, span * HD), jnp.bfloat16)] * (pieces - 1)
        out_specs += [span_spec] * pieces
    else:
        out_shape.append(jax.ShapeDtypeStruct((2, keys, kv_width), jnp.float32))
        out_specs.append(acc_spec)
    pairs = span * ratio * rows * window
    cost = CALL_COST if step and not last else 1
    held = (keys, ratio * rows), (window, ratio * rows)
    held += ((2, keys, lanes),) * last
    return pl.pallas_call(
        functools.partial(attend_kernel, step, first, filled, last, tok_dev, reach, ratio),
        out_shape=out_shape,
        grid_spec=pltpu.PrefetchScalarGridSpec(
            num_scalar_prefetch=2,
            grid=(span // HEADS_STEP,),
            in_specs=in_specs,
            out_specs=out_specs,
            scratch_shapes=[pltpu.VMEM(shape, jnp.float32) for shape in held],
        ),
        input_output_aliases=aliases,
        compiler_params=pltpu.CompilerParams(
            dimension_semantics=("arbitrary",), vmem_limit_bytes=VMEM_BYTES
        ),
        cost_estimate=pl.CostEstimate(
            flops=pairs * HD * cost, bytes_accessed=pairs * cost, transcendentals=0
        ),
        name="attend",
    )(*operands)


def turn_kernel(step, tok_dev, reach, meta_ref, key_ref, full_ref, *refs):
    scores_refs, out_ref = refs[:-1], refs[-1]
    rows, blocks = out_ref.shape[0], key_ref.shape[0]
    window = scores_refs[0].shape[1]
    source = source_of(meta_ref[0], step, tok_dev // rows)
    block = (blocks * rows - tok_dev - reach) // rows + source

    def one(scores_ref):
        grads = []
        for head in range(HEADS_STEP):
            key = key_ref[pl.ds(block, window // rows), :, head * HD : (head + 1) * HD]
            grad = lax.dot_general(
                scores_ref[head],
                key.reshape(window, HD),
                (((0,), (0,)), ((), ())),
                preferred_element_type=jnp.float32,
            )
            grads.append((grad * (1.0 / HD**0.5)).reshape(-1, rows, HD))
        turned = jnp.swapaxes(jnp.concatenate(grads, axis=0), 0, 1)
        out_ref[...] = turned.astype(jnp.bfloat16)

    for half, scores_ref in enumerate(scores_refs):
        pl.when(pl.program_id(0) == half)(functools.partial(one, scores_ref))


def turn(step, reach, meta, scores, kv, full):
    blocks, _, rows, _ = kv.shape
    tok_dev, heads, _ = full.shape
    shape = scores[0].shape
    step_heads = HEADS_STEP * shape[2] // rows
    return pl.pallas_call(
        functools.partial(turn_kernel, step, tok_dev, reach),
        out_shape=jax.ShapeDtypeStruct(full.shape, full.dtype),
        grid_spec=pltpu.PrefetchScalarGridSpec(
            num_scalar_prefetch=1,
            grid=(len(scores),),
            in_specs=[
                pl.BlockSpec((blocks, None, rows, HEADS_STEP * HD), lambda c, m: (0, 0, 0, c)),
                pl.BlockSpec(memory_space=pl.ANY),
            ]
            + [pl.BlockSpec(shape, lambda c, m: (0, 0, 0))] * len(scores),
            out_specs=pl.BlockSpec(
                (rows, step_heads, HD),
                lambda c, m: (source_of(m[0], step, tok_dev // rows), c, 0),
            ),
        ),
        input_output_aliases={2: 0},
        compiler_params=pltpu.CompilerParams(
            dimension_semantics=("arbitrary",), vmem_limit_bytes=VMEM_BYTES
        ),
        name="turn",
    )(meta, kv, full, *scores)


def shards(queries, keys, values, grad_out, segment_ids, assignment):
    count = lax.axis_size("dp")
    uly = lax.axis_size("uly")
    group = lax.axis_index("dp")
    line = lax.axis_index("blk") * uly + lax.axis_index("uly")
    width, kv_width = queries.shape[2], keys.shape[2]
    heads, kv_heads = width // HD, kv_width // HD
    tok_dev = count * queries.shape[1]
    doc_most = min(512, tok_dev * uly)
    hops = -(-doc_most // tok_dev)
    meta = jnp.stack([group, line]).astype(jnp.int32)

    final, halves = count // 2, kv_heads // HEADS_STEP
    part = width // halves
    others = [step for step in range(1, count) if step != final]
    jobs = [(2, step, 0, kv_width) for step in range(count)]
    jobs += [(0, step, 0, width) for step in others]
    jobs += [(0, final, half * part, part) for half in range(halves - 1)]
    jobs += [(which, final, (halves - 1) * part, part, 1) for which in range(2)]
    staged = stage(assignment, (queries, grad_out, keys, values), jobs)
    kv_staged, staged = staged[:count], list(staged[count:])
    kv_arrived = [exchanged(kv_staged[step], "dp", step) for step in range(1, count)]
    staged, kv_arrived[0] = lax.optimization_barrier((staged, kv_arrived[0]))
    arrived = [exchanged(rows, "dp", step) for rows, step in zip(staged, others)]
    held = staged[len(others) :]
    kv_own = jnp.zeros((count, *kv_staged[0].shape), keys.dtype)
    for step, piece in enumerate([kv_staged[0], *kv_arrived]):
        kv_own = lax.dynamic_update_index_in_dim(
            kv_own, piece, source_of(group, step, count), 0
        )
    halos = [shifted(kv_own, ("blk", "uly"), back) for back in range(hops, 0, -1)]
    kv = jnp.concatenate([*halos, kv_own], axis=0)

    rows, kv = lax.optimization_barrier((held[0], kv))
    split = [exchanged(rows, "dp", final)]
    fixed = (doc_most, heads, meta, assignment, segment_ids)
    query, grad = (queries, lambda m, a: a[m[0]]), (grad_out, lambda m, a: a[m[0]])
    full, acc = attend(0, 0, kv_heads, *fixed, query, grad, kv, None, None, False)
    for step, both in zip(others, arrived):
        query, grad = (both, lambda m, a: 0), (both, lambda m, a: 1)
        full, acc = attend(step, 0, kv_heads, *fixed, query, grad, kv, acc, full, False)
    rows, acc = lax.optimization_barrier((held[1:], acc))
    split += [exchanged(piece, "dp", final) for piece in rows]
    totals, returned, held_scores = [], [], []
    for half in range(halves):
        both = split[half]
        query, grad = (both, lambda m, a: 0), (both, lambda m, a: 1)
        if half + 1 == halves:
            grad = (split[half + 1], lambda m, a: 0)
        scores, total, *halos = attend(
            final, half * HEADS_STEP, HEADS_STEP, *fixed, query, grad, kv, acc, full, True
        )
        if half:
            held_scores, halos = lax.optimization_barrier((held_scores, halos))
            held_scores, total = lax.optimization_barrier((held_scores, total))
        held_scores.append(scores)
        returned = [shifted(halo, ("blk", "uly"), -back) for back, halo in enumerate(halos, 1)]
        for halo in returned:
            total = total + halo.astype(jnp.float32)
        totals.append(total.astype(jnp.bfloat16))
    full = turn(final, doc_most, meta, held_scores, kv, full)
    total = jnp.concatenate(totals, axis=2)
    return full[None], total[0][None], total[1][None]


def solution(mesh):
    in_specs = (
        P(None, ("blk", "uly", "dp"), None),
        P(None, ("blk", "uly", "dp"), None),
        P(None, ("blk", "uly", "dp"), None),
        P(None, ("blk", "uly", "dp"), None),
        P(),
        P(),
    )
    out_specs = (
        P("dp", ("blk", "uly"), None, None),
        P("dp", ("blk", "uly"), None),
        P("dp", ("blk", "uly"), None),
    )
    return jax.shard_map(shards, mesh=mesh, in_specs=in_specs, out_specs=out_specs, check_vma=False)
```
